128 devices in a mesh: seq: 8 (over z_hi, y), fsdp: 16 (over z_lo, x, core).
Axes of the slice: x: 4, y: 4, z: 4 (z_hi: 2, z_lo: 2; z = z_hi * 2 + z_lo), core: 2. Of those that a mesh axis runs over, the one named last changes fastest.
Arguments:
- tokens: bfloat16 [16, 1024, 2048], P('fsdp', 'seq'), may hold values from -6 to 6
- segment_ids: int32 [16, 1024], P('fsdp'), may hold values from 0 to 1, as said below
- query_weight: bfloat16 [2048, 2048], P('fsdp'), may hold values from -0.25 to 0.25
- key_matrix: bfloat16 [2048, 512], P('fsdp'), may hold values from -0.125 to 0.125
- value_matrix: bfloat16 [2048, 512], P('fsdp'), may hold values from -0.125 to 0.125
- output_weight: bfloat16 [2048, 2048], P('fsdp'), may hold values from -0.75 to 0.75
- gate_weight: bfloat16 [2048, 8192], P('fsdp'), may hold values from -0.125 to 0.125
- up_weight: bfloat16 [2048, 8192], P('fsdp'), may hold values from -0.125 to 0.125
- down_weight: bfloat16 [8192, 2048], P('fsdp'), may hold values from -0.0625 to 0.0625
- attention_gain: bfloat16 [2048], P('fsdp'), may hold values from 0.099609375 to 1.8984375
- feed_gain: bfloat16 [2048], P('fsdp'), may hold values from 0.099609375 to 1.8984375
- cotangent: bfloat16 [16, 1024, 2048], P('fsdp', 'seq'), may hold values from -6 to 6
Outputs:
- layer_out: bfloat16 [16, 1024, 2048], P('fsdp', 'seq')
- grad_tokens: bfloat16 [16, 1024, 2048], P('fsdp', 'seq')
- grad_query: float32 [2048, 2048], P('fsdp')
- grad_key: float32 [2048, 512], P('fsdp')
- grad_value: float32 [2048, 512], P('fsdp')
- grad_output: float32 [2048, 2048], P('fsdp')
- grad_gate: float32 [2048, 8192], P('fsdp')
- grad_up: float32 [2048, 8192], P('fsdp')
- grad_down: float32 [8192, 2048], P('fsdp')
- grad_attention_gain: float32 [2048], P('fsdp')
- grad_feed_gain: float32 [2048], P('fsdp')
The draws below stay inside these ranges and needn't reach their ends.
Inputs may be any that keep to these rules, and one draw needn't show every extreme that they name: `segment_ids`: each sequence holds two documents, 0 then 1; document 0 ends within the last 128 tokens.
All inputs are finite; a program needn't handle non-finite values.
Results may differ from the reference program's by a relative error of at most 0.025.
Values may be sent and summed in bfloat16 or wider, within the bound.
A program may use at most 448 MiB of HBM per device.

```python
import math
import jax
import jax.numpy as jnp
from jax import lax

MODEL_WIDTH = 2048
QUERY_HEADS = 32
KEY_VALUE_HEADS = 8
HEAD_SIZE = 64
FF = 8192
LEN = 1024
BLK = 512
TOK_DEV = 128
ROWS = 16


def draw_segment_ids(key, part):
    key = jax.random.fold_in(key, 11)
    boundary = jax.random.randint(key, (ROWS, 1), LEN - TOK_DEV + 1, LEN)
    indices = jnp.arange(LEN, dtype=jnp.int32)[None, :]
    return (indices >= boundary).astype(jnp.int32)


def levels(key, extent, shards, low, largest):
    level = 1.0
    for position, shards_of in shards:
        steps = jax.random.uniform(jax.random.fold_in(jax.random.fold_in(key, 6), position), (shards_of,), jnp.float32, low / len(shards), largest / len(shards))
        level = level * jnp.repeat(jnp.exp(steps), extent[position] // shards_of).reshape((-1,) + (1,) * (len(extent) - 1 - position))
    return level


def scatter_about(own_key, shape, spread, most, shards=(), kind=jnp.bfloat16):
    values = spread * jax.random.normal(own_key, shape, jnp.float32)
    if shards:
        values = values * levels(own_key, shape, shards, -0.22, 0.18)
    return jnp.clip(values, -most, most).astype(kind)


def setup_inputs(seed: int = 0) -> dict:
    streams_of = jax.random.split(jax.random.key(seed), 13)
    tokens = scatter_about(streams_of[0], (ROWS, LEN, MODEL_WIDTH), 1.0, 6.0, ((0, 16), (1, 8)))
    segment_ids = draw_segment_ids(jax.random.fold_in(streams_of[12], 71), 0)
    query_weight = scatter_about(streams_of[2], (MODEL_WIDTH, QUERY_HEADS * HEAD_SIZE), (MODEL_WIDTH // 4) ** -0.5, 0.25, ((0, 16),))
    key_matrix = scatter_about(streams_of[3], (MODEL_WIDTH, KEY_VALUE_HEADS * HEAD_SIZE), MODEL_WIDTH ** -0.5, 0.125, ((0, 16),))
    value_matrix = scatter_about(streams_of[4], (MODEL_WIDTH, KEY_VALUE_HEADS * HEAD_SIZE), MODEL_WIDTH ** -0.5, 0.125, ((0, 16),))
    output_weight = scatter_about(streams_of[5], (QUERY_HEADS * HEAD_SIZE, MODEL_WIDTH), (MODEL_WIDTH // 32) ** -0.5, 0.75, ((0, 16),))
    gate_weight = scatter_about(streams_of[6], (MODEL_WIDTH, FF), MODEL_WIDTH ** -0.5, 0.125, ((0, 16),))
    up_weight = scatter_about(streams_of[7], (MODEL_WIDTH, FF), MODEL_WIDTH ** -0.5, 0.125, ((0, 16),))
    down_weight = scatter_about(streams_of[8], (FF, MODEL_WIDTH), FF ** -0.5, 0.0625, ((0, 16),))
    attention_gain = jnp.clip(1.0 + 0.18 * jax.random.normal(streams_of[9], (MODEL_WIDTH,), jnp.float32), 0.099609375, 1.8984375).astype(jnp.bfloat16)
    feed_gain = jnp.clip(1.0 + 0.18 * jax.random.normal(streams_of[10], (MODEL_WIDTH,), jnp.float32), 0.099609375, 1.8984375).astype(jnp.bfloat16)
    cotangent = scatter_about(streams_of[11], (ROWS, LEN, MODEL_WIDTH), 1.0, 6.0, ((0, 16), (1, 8)))
    return dict(tokens=tokens, segment_ids=segment_ids, query_weight=query_weight, key_matrix=key_matrix, value_matrix=value_matrix, output_weight=output_weight, gate_weight=gate_weight, up_weight=up_weight, down_weight=down_weight, attention_gain=attention_gain, feed_gain=feed_gain, cotangent=cotangent)


EPS = 1e-05
ROPE_BASE = 500000.0
NEG = -1e+30
HIGH = lax.Precision.HIGHEST

@jax.custom_vjp
def lower_bound(v):
    return lax.optimization_barrier(v.astype(jnp.bfloat16)).astype(jnp.float32)

@jax.custom_vjp
def low_back(v):
    return v

def low_keep(v):
    return (lower_bound(v), None)

def low_pass(kept, grad):
    return (grad,)

def back_keep(v):
    return (v, None)

def back_low(kept, grad):
    return (lower_bound(grad),)
lower_bound.defvjp(low_keep, low_pass)
low_back.defvjp(back_keep, back_low)

def rope_freqs(head_dim):
    half_dim = head_dim // 2
    table = []
    for index in range(half_dim):
        inverse = 1.0 / ROPE_BASE ** (index * 2.0 / head_dim)
        wavelen = 2.0 * math.pi / inverse
        blend = (8192.0 / wavelen - 1.0) / 3.0
        mixed = (1.0 - blend) * inverse / 32.0 + blend * inverse
        entry = inverse if wavelen < 2048.0 else inverse / 32.0 if wavelen > 8192.0 else mixed
        table.append(entry)
    return jnp.asarray(table, dtype=jnp.float32)

def positions_of(segment_row):
    indices = jnp.arange(segment_row.shape[0], dtype=jnp.int32)
    begins = jnp.concatenate([jnp.ones((1,), dtype=jnp.int32), (segment_row[1:] != segment_row[:-1]).astype(jnp.int32)])
    starts_at = lax.cummax(jnp.where(begins > 0, indices, 0), axis=0)
    return indices - starts_at

def angles_of(segment_row, head_dim):
    positions = positions_of(segment_row)
    phase = positions.astype(jnp.float32)[:, None] * rope_freqs(head_dim)[None, :]
    return (jnp.cos(phase), jnp.sin(phase))

def apply_rotation(values_in, cosine_table, sine_table):
    half_dim = values_in.shape[-1] // 2
    first_half = values_in[..., :half_dim]
    second_half = values_in[..., half_dim:]
    return jnp.concatenate([first_half * cosine_table - second_half * sine_table, second_half * cosine_table + first_half * sine_table], axis=-1)

def rms(values_in, gain):
    factor = lax.rsqrt(lax.optimization_barrier(jnp.mean(values_in * values_in, axis=-1, keepdims=True)) + EPS)
    return values_in * factor * gain

def attend(rotated_queries, rotated_keys, heads_of_values, segment_row):
    token_length = rotated_queries.shape[0]
    key_index = jnp.arange(token_length, dtype=jnp.int32)

    def one_block(offset):
        query_rows = lax.dynamic_slice_in_dim(rotated_queries, offset, BLK, 0)
        raw_scores = jnp.einsum('qkgd,skd->kgqs', query_rows, rotated_keys, precision=HIGH)
        scores = low_back(raw_scores) * 0.125
        query_index = offset + jnp.arange(BLK, dtype=jnp.int32)
        query_segment = lax.dynamic_slice_in_dim(segment_row, offset, BLK, 0)
        allowed = (key_index[None, :] <= query_index[:, None]) & (segment_row[None, :] == query_segment[:, None])
        masked = jnp.where(allowed, scores, NEG)
        highest = lax.optimization_barrier(jnp.max(masked, axis=-1, keepdims=True))
        weights = jnp.exp(masked - highest)
        probs = weights / lax.optimization_barrier(jnp.sum(weights, axis=-1, keepdims=True))
        return jnp.einsum('kgqs,skd->qkgd', lower_bound(probs), heads_of_values, precision=HIGH)
    offsets = jnp.arange(token_length // BLK, dtype=jnp.int32) * BLK
    blocks = lax.map(jax.checkpoint(one_block), offsets)
    return blocks.reshape(rotated_queries.shape)

def layer(inputs, segment_row, params):
    query_w, key_w, value_w, output_w, gate_w, up_w, down_w, gain_one, gain_two = params
    token_length = inputs.shape[0]
    group_width = QUERY_HEADS // KEY_VALUE_HEADS
    hidden_one = lower_bound(rms(inputs, gain_one))
    query_rows_in = low_back(lower_bound(jnp.dot(hidden_one, query_w, precision=HIGH)))
    projected_keys = low_back(lower_bound(jnp.dot(hidden_one, key_w, precision=HIGH)))
    projected_values = low_back(lower_bound(jnp.dot(hidden_one, value_w, precision=HIGH)))
    cosine_table, sine_table = angles_of(segment_row, HEAD_SIZE)
    rotated_queries = lower_bound(apply_rotation(query_rows_in.reshape(token_length, KEY_VALUE_HEADS, group_width, HEAD_SIZE), cosine_table[:, None, None, :], sine_table[:, None, None, :]))
    rotated_keys = lower_bound(apply_rotation(projected_keys.reshape(token_length, KEY_VALUE_HEADS, HEAD_SIZE), cosine_table[:, None, :], sine_table[:, None, :]))
    heads_of_values = projected_values.reshape(token_length, KEY_VALUE_HEADS, HEAD_SIZE)
    attended = attend(rotated_queries, rotated_keys, heads_of_values, segment_row)
    attended = low_back(lower_bound(attended.reshape(token_length, QUERY_HEADS * HEAD_SIZE)))
    middle = inputs + low_back(jnp.dot(attended, output_w, precision=HIGH))
    hidden_two = lower_bound(rms(middle, gain_two))
    gate = low_back(jnp.dot(hidden_two, gate_w, precision=HIGH))
    up_proj = low_back(jnp.dot(hidden_two, up_w, precision=HIGH))
    act = lower_bound(jax.nn.silu(gate) * up_proj)
    return middle + low_back(jnp.dot(act, down_w, precision=HIGH))

def reference(tokens, segment_ids, query_weight, key_matrix, value_matrix, output_weight, gate_weight, up_weight, down_weight, attention_gain, feed_gain, cotangent):
    params = tuple((weight.astype(jnp.float32) for weight in (query_weight, key_matrix, value_matrix, output_weight, gate_weight, up_weight, down_weight, attention_gain, feed_gain)))

    def forward(inputs_all, param_set):

        def one_row(carry, row_data):
            row_inputs, segment_row = row_data
            return (carry, layer(row_inputs, segment_row, param_set))
        _, outputs = lax.scan(one_row, jnp.zeros((), jnp.float32), (inputs_all, segment_ids))
        return outputs
    outputs, pullback = jax.vjp(forward, tokens.astype(jnp.float32), params)
    grad_inputs, grads = pullback(cotangent.astype(jnp.float32))
    return (outputs.astype(jnp.bfloat16), grad_inputs.astype(jnp.bfloat16), grads[0], grads[1], grads[2], grads[3], grads[4], grads[5], grads[6], grads[7], grads[8])
```

```python
import math

import jax
import jax.numpy as jnp
from jax import lax
from jax.experimental import pallas as pl
from jax.experimental.pallas import tpu as pltpu
from jax.sharding import PartitionSpec as P

HEAD_SIZE = 64
EPS = 1e-05
ROPE_BASE = 500000.0
NEG = -1e30


def rope_freqs(head_dim):
    half_dim = head_dim // 2
    table = []
    for index in range(half_dim):
        inverse = 1.0 / ROPE_BASE ** (index * 2.0 / head_dim)
        wavelen = 2.0 * math.pi / inverse
        blend = (8192.0 / wavelen - 1.0) / 3.0
        mixed = (1.0 - blend) * inverse / 32.0 + blend * inverse
        entry = inverse if wavelen < 2048.0 else inverse / 32.0 if wavelen > 8192.0 else mixed
        table.append(entry)
    return jnp.asarray(table, dtype=jnp.float32)


def positions_of(segment_row):
    indices = jnp.arange(segment_row.shape[0], dtype=jnp.int32)
    begins = jnp.concatenate(
        [jnp.ones((1,), dtype=jnp.int32), (segment_row[1:] != segment_row[:-1]).astype(jnp.int32)]
    )
    starts_at = lax.cummax(jnp.where(begins > 0, indices, 0), axis=0)
    return indices - starts_at


def angles_of(segment_row, head_dim):
    positions = positions_of(segment_row)
    phase = positions.astype(jnp.float32)[:, None] * rope_freqs(head_dim)[None, :]
    return (jnp.cos(phase), jnp.sin(phase))


MESH = pl.DeviceIdType.MESH
CHUNKS = 4
TILE = 256


def ring():
    rank, owner = lax.axis_index("seq"), lax.axis_index("fsdp")
    side = lax.axis_size("seq") // 2
    row, col = lax.div(rank, side), lax.rem(rank, side)

    def at(which, step):
        return which * side + lax.rem(col + step, side)

    near = [at(row, step) for step in range(side)]
    far = [at(1 - row, step) for step in range(side)]
    return owner, near, far


def greet(owner, peers):
    barrier = pltpu.get_barrier_semaphore()
    for peer in peers:
        pl.semaphore_signal(barrier, inc=1, device_id=(peer, owner), device_id_type=MESH)
    pl.semaphore_wait(barrier, len(peers))


class Copies:
    def __init__(self, owner, send, recv):
        self.owner, self.send, self.recv = owner, send, recv
        self.made = []

    def start(self, source, target, peer):
        number = len(self.made)
        copy = pltpu.make_async_remote_copy(
            src_ref=source,
            dst_ref=target,
            send_sem=self.send.at[number],
            recv_sem=self.recv.at[number],
            device_id=(peer, self.owner),
            device_id_type=MESH,
        )
        copy.start()
        self.made.append(copy)
        return copy

    def finish(self):
        for copy in self.made:
            copy.wait_send()


def gather_blocks(ids, copies, own, out, rows, chunks):
    _, near, far = ids
    me, right, opposite, left = near
    partner = far[0]
    size = rows // chunks
    half = chunks // 2

    def part(index):
        return pl.ds(index * size, size)

    to_right, to_left, to_far = {}, {}, {}
    for step in range(chunks):
        back = chunks - 1 - step
        to_right[step] = copies.start(own.at[part(step)], out.at[me, part(step)], right)
        to_left[back] = copies.start(own.at[part(back)], out.at[me, part(back)], left)
        to_far[step] = copies.start(own.at[part(step)], out.at[me, part(step)], partner)
    on = {}
    for step in range(half):
        back = chunks - 1 - step
        to_right[step].wait_recv()
        on[step] = copies.start(out.at[left, part(step)], out.at[left, part(step)], right)
        to_left[back].wait_recv()
        on[back] = copies.start(out.at[right, part(back)], out.at[right, part(back)], left)
    rest = []
    for step in range(chunks):
        to_far[step].wait_recv()
        block = out.at[partner, part(step)]
        rest.append(copies.start(block, block, right))
        rest.append(copies.start(block, block, left))
    for step in range(half):
        for index in (step, chunks - 1 - step):
            on[index].wait_recv()
            block = out.at[opposite, part(index)]
            rest.append(copies.start(block, block, partner))
    for step in range(half):
        to_right[chunks - 1 - step].wait_recv()
        to_left[step].wait_recv()
    for copy in rest:
        copy.wait_recv()


def gather_copies(chunks):
    return 3 * chunks + chunks + 2 * chunks + chunks


def reduce_blocks(ids, copies, part_of, bufs, rows, chunks, done):
    _, near, far = ids
    me, right, opposite, left = near
    partner, far_right, far_opposite, far_left = far
    from_left, from_right, from_far, mid, end_left, end_right, end_far = bufs
    size = rows // chunks
    half = chunks // 2

    def part(index):
        return pl.ds(index * size, size)

    def wide(ref):
        return ref.astype(jnp.float32)

    order = [x for step in range(half) for x in (step, chunks - 1 - step)]
    one_right, one_left, one_far = {}, {}, {}
    for index in order:
        rows_of = part(index)
        one_far[index] = copies.start(
            part_of.at[far_opposite, rows_of], from_far.at[rows_of], partner
        )
        one_right[index] = copies.start(
            part_of.at[far_right, rows_of], from_left.at[rows_of], right
        )
        one_left[index] = copies.start(part_of.at[far_left, rows_of], from_right.at[rows_of], left)
    last_right, last_left, last_far = {}, {}, {}
    for index in range(half):
        rows_of = part(index)
        last_right[index] = copies.start(part_of.at[right, rows_of], end_left.at[rows_of], right)
        rows_of = part(chunks - 1 - index)
        last_left[chunks - 1 - index] = copies.start(
            part_of.at[left, rows_of], end_right.at[rows_of], left
        )
    two = {}
    for index in order:
        rows_of = part(index)
        one_far[index].wait_recv()
        from_far[rows_of] = (wide(from_far[rows_of]) + wide(part_of[opposite, rows_of])).astype(
            jnp.bfloat16
        )
        two[index] = copies.start(
            from_far.at[rows_of], mid.at[rows_of], left if index < half else right
        )
    for index in order:
        rows_of = part(index)
        one_right[index].wait_recv()
        one_left[index].wait_recv()
        from_left[rows_of] = (
            wide(from_left[rows_of]) + wide(from_right[rows_of]) + wide(part_of[partner, rows_of])
        ).astype(jnp.bfloat16)
        last_far[index] = copies.start(from_left.at[rows_of], end_far.at[rows_of], partner)
    for index in order:
        rows_of = part(index)
        two[index].wait_recv()
        if index < half:
            mid[rows_of] = (wide(mid[rows_of]) + wide(part_of[left, rows_of])).astype(jnp.bfloat16)
            last_left[index] = copies.start(mid.at[rows_of], end_right.at[rows_of], left)
        else:
            mid[rows_of] = (wide(mid[rows_of]) + wide(part_of[right, rows_of])).astype(
                jnp.bfloat16
            )
            last_right[index] = copies.start(mid.at[rows_of], end_left.at[rows_of], right)
    for index in order:
        rows_of = part(index)
        last_far[index].wait_recv()
        last_left[index].wait_recv()
        last_right[index].wait_recv()
        done(
            rows_of,
            wide(part_of[me, rows_of])
            + wide(end_left[rows_of])
            + wide(end_right[rows_of])
            + wide(end_far[rows_of]),
        )


def reduce_copies(chunks):
    return 3 * chunks + 2 * chunks + chunks + chunks


def reduce_scratch(rows, width):
    return [pltpu.VMEM((rows, width), jnp.bfloat16) for _ in range(7)]


def semaphores(count):
    return [pltpu.SemaphoreType.DMA((count,)), pltpu.SemaphoreType.DMA((count,))]


def params(number, limit):
    return pltpu.CompilerParams(
        collective_id=number, has_side_effects=True, vmem_limit_bytes=limit * 2**20
    )


VMEM = pl.BlockSpec(memory_space=pltpu.VMEM)
ANYWHERE = pl.BlockSpec(memory_space=pl.ANY)


def gather_many(blocks, number):
    count = len(blocks)
    rows, width = blocks[0].shape
    ranks = lax.axis_size("seq")
    each = gather_copies(CHUNKS)

    def kernel(*refs):
        own, out = refs[:count], refs[count : 2 * count]
        local, send, recv = refs[2 * count :]
        ids = ring()
        owner, near, far = ids
        greet(owner, (near[1], near[3], far[0]))
        kept = [
            pltpu.make_async_copy(own[i], out[i].at[near[0]], local.at[i]) for i in range(count)
        ]
        for copy in kept:
            copy.start()
        copies = Copies(owner, send, recv)
        for i in range(count):
            gather_blocks(ids, copies, own[i], out[i], rows, CHUNKS)
        copies.finish()
        for copy in kept:
            copy.wait()

    moved = count * ranks * rows * width * 2
    return pl.pallas_call(
        kernel,
        out_shape=[jax.ShapeDtypeStruct((ranks, rows, width), jnp.bfloat16)] * count,
        in_specs=[ANYWHERE] * count,
        out_specs=[ANYWHERE] * count,
        scratch_shapes=[pltpu.SemaphoreType.DMA((count,))] + semaphores(count * each),
        compiler_params=params(number, 32),
        cost_estimate=pl.CostEstimate(flops=0, bytes_accessed=moved * 16, transcendentals=0),
        name="gather_many",
    )(*blocks)


def mean_square(values):
    return jnp.mean(values * values, axis=-1, keepdims=True)


def branch_kernel(part_of, tokens, gain, middle, hidden, block, local, send, recv, *bufs):
    ids = ring()
    owner, near, far = ids
    rows = tokens.shape[0]
    greet(owner, (near[1], near[3], far[0]))
    copies = Copies(owner, send, recv)

    def done(rows_of, total):
        values = tokens[rows_of].astype(jnp.float32) + total
        middle[rows_of] = values
        factor = lax.rsqrt(mean_square(values) + EPS)
        block[rows_of] = (values * factor * gain[...]).astype(jnp.bfloat16)

    reduce_blocks(ids, copies, part_of, bufs, rows, CHUNKS, done)
    kept = pltpu.make_async_copy(block, hidden.at[near[0]], local)
    kept.start()
    gather_blocks(ids, copies, block, hidden, rows, CHUNKS)
    copies.finish()
    kept.wait()


def add_branch(partial, tokens, gain, number):
    rows, width = tokens.shape
    ranks = lax.axis_size("seq")
    count = reduce_copies(CHUNKS) + gather_copies(CHUNKS)
    return pl.pallas_call(
        branch_kernel,
        out_shape=[
            jax.ShapeDtypeStruct((rows, width), jnp.float32),
            jax.ShapeDtypeStruct((ranks, rows, width), jnp.bfloat16),
        ],
        in_specs=[VMEM] * 3,
        out_specs=[VMEM, ANYWHERE],
        scratch_shapes=[pltpu.VMEM((rows, width), jnp.bfloat16), pltpu.SemaphoreType.DMA]
        + semaphores(count)
        + reduce_scratch(rows, width),
        compiler_params=params(number, 32),
        cost_estimate=pl.CostEstimate(
            flops=0, bytes_accessed=ranks * rows * width * 64, transcendentals=0
        ),
        name="add_branch",
    )(partial.reshape(ranks, rows, width), tokens, gain)


def norm_back_rows(grad, gain, values):
    factor = lax.rsqrt(mean_square(values) + EPS)
    normed = values * factor
    weighted = grad * gain
    back = factor * (weighted - normed * jnp.mean(weighted * normed, axis=-1, keepdims=True))
    return back, grad * normed


def middle_kernel(
    part_of, middle, gain, cotangent, grad_middle, grad_gain, branch, block, local, send, recv, *bufs
):
    ids = ring()
    owner, near, far = ids
    rows = middle.shape[0]
    greet(owner, (near[1], near[3], far[0]))
    copies = Copies(owner, send, recv)
    grad_gain[...] = jnp.zeros_like(grad_gain)

    def done(rows_of, total):
        back, terms = norm_back_rows(total, gain[...], middle[rows_of])
        grad_gain[...] += jnp.sum(terms, axis=0, keepdims=True)
        values = cotangent[rows_of].astype(jnp.float32) + back
        grad_middle[rows_of] = values
        block[rows_of] = values.astype(jnp.bfloat16)

    reduce_blocks(ids, copies, part_of, bufs, rows, CHUNKS, done)
    kept = pltpu.make_async_copy(block, branch.at[near[0]], local)
    kept.start()
    gather_blocks(ids, copies, block, branch, rows, CHUNKS)
    copies.finish()
    kept.wait()


def back_to_middle(partial, middle, gain, cotangent, number):
    rows, width = middle.shape
    ranks = lax.axis_size("seq")
    count = reduce_copies(CHUNKS) + gather_copies(CHUNKS)
    return pl.pallas_call(
        middle_kernel,
        out_shape=[
            jax.ShapeDtypeStruct((rows, width), jnp.float32),
            jax.ShapeDtypeStruct((1, width), jnp.float32),
            jax.ShapeDtypeStruct((ranks, rows, width), jnp.bfloat16),
        ],
        in_specs=[VMEM] * 4,
        out_specs=[VMEM, VMEM, ANYWHERE],
        scratch_shapes=[pltpu.VMEM((rows, width), jnp.bfloat16), pltpu.SemaphoreType.DMA]
        + semaphores(count)
        + reduce_scratch(rows, width),
        compiler_params=params(number, 32),
        cost_estimate=pl.CostEstimate(
            flops=0, bytes_accessed=ranks * rows * width * 64, transcendentals=0
        ),
        name="back_to_middle",
    )(partial.reshape(ranks, rows, width), middle, gain, cotangent)


def tokens_kernel(part_of, tokens, gain, grad_middle, out, grad_gain, send, recv, *bufs):
    ids = ring()
    owner, near, far = ids
    rows = tokens.shape[0]
    greet(owner, (near[1], near[3], far[0]))
    copies = Copies(owner, send, recv)
    grad_gain[...] = jnp.zeros_like(grad_gain)

    def done(rows_of, total):
        back, terms = norm_back_rows(total, gain[...], tokens[rows_of].astype(jnp.float32))
        grad_gain[...] += jnp.sum(terms, axis=0, keepdims=True)
        out[rows_of] = (grad_middle[rows_of] + back).astype(jnp.bfloat16)

    reduce_blocks(ids, copies, part_of, bufs, rows, CHUNKS, done)
    copies.finish()


def back_to_tokens(partial, tokens, gain, grad_middle, number):
    rows, width = tokens.shape
    ranks = lax.axis_size("seq")
    return pl.pallas_call(
        tokens_kernel,
        out_shape=[
            jax.ShapeDtypeStruct((rows, width), jnp.bfloat16),
            jax.ShapeDtypeStruct((1, width), jnp.float32),
        ],
        in_specs=[VMEM] * 4,
        out_specs=[VMEM, VMEM],
        scratch_shapes=semaphores(reduce_copies(CHUNKS)) + reduce_scratch(rows, width),
        compiler_params=params(number, 32),
        cost_estimate=pl.CostEstimate(
            flops=0, bytes_accessed=ranks * rows * width * 32, transcendentals=0
        ),
        name="back_to_tokens",
    )(partial.reshape(ranks, rows, width), tokens, gain, grad_middle)


def layer_kernel(part_of, middle, out, send, recv, *bufs):
    ids = ring()
    owner, near, far = ids
    greet(owner, (near[1], near[3], far[0]))
    copies = Copies(owner, send, recv)

    def done(rows_of, total):
        out[rows_of] = (middle[rows_of] + total).astype(jnp.bfloat16)

    reduce_blocks(ids, copies, part_of, bufs, middle.shape[0], CHUNKS, done)
    copies.finish()


def finish_layer(partial, middle, number):
    rows, width = middle.shape
    ranks = lax.axis_size("seq")
    return pl.pallas_call(
        layer_kernel,
        out_shape=jax.ShapeDtypeStruct((rows, width), jnp.bfloat16),
        in_specs=[VMEM] * 2,
        out_specs=VMEM,
        scratch_shapes=semaphores(reduce_copies(CHUNKS)) + reduce_scratch(rows, width),
        compiler_params=params(number, 32),
        cost_estimate=pl.CostEstimate(
            flops=0, bytes_accessed=ranks * rows * width * 32, transcendentals=0
        ),
        name="finish_layer",
    )(partial.reshape(ranks, rows, width), middle)


def rotate_rows(first, second, cosine, sine):
    return jnp.concatenate([first * cosine - second * sine, second * cosine + first * sine], axis=0)


def bias_tile(start_row, key_tile, query_tile, diagonal):
    keys = key_tile * TILE + lax.broadcasted_iota(jnp.int32, (TILE, TILE), 0)
    seen = keys >= start_row
    if diagonal:
        queries = query_tile * TILE + lax.broadcasted_iota(jnp.int32, (TILE, TILE), 1)
        seen = seen & (keys <= queries)
    return jnp.where(seen, 0.0, NEG)


def forward_kernel(qkv, cosine, sine, starts, attended, lse, queries, keys, key_rows, bias):
    group = queries.shape[0] // HEAD_SIZE
    half = HEAD_SIZE // 2
    tiles = qkv.shape[1] // TILE
    cos, sin = cosine[...], sine[...]

    def rotated(first):
        return rotate_rows(
            qkv[pl.ds(first, half)].astype(jnp.float32),
            qkv[pl.ds(first + half, half)].astype(jnp.float32),
            cos,
            sin,
        ).astype(jnp.bfloat16)

    for head in range(group):
        queries[pl.ds(head * HEAD_SIZE, HEAD_SIZE)] = rotated(head * HEAD_SIZE) * jnp.bfloat16(0.125)
    keys[...] = rotated(group * HEAD_SIZE)
    key_rows[...] = keys[...].T
    for tile in range(tiles):
        lanes = pl.ds(tile * TILE, TILE)
        starts_here = starts[:, lanes]
        for low in range(tile + 1):
            bias[pl.ds(low * TILE, TILE)] = bias_tile(starts_here, low, tile, low == tile)
        count = (tile + 1) * TILE

        def one_head(head, _, lanes=lanes, count=count):
            rows = pl.ds(pl.multiple_of(head * HEAD_SIZE, HEAD_SIZE), HEAD_SIZE)
            scores = jnp.dot(
                key_rows[:count], queries[rows, lanes], preferred_element_type=jnp.float32
            )
            scores += bias[:count]
            highest = jnp.max(scores, axis=0, keepdims=True)
            weights = jnp.exp(scores - highest)
            total = jnp.sum(weights, axis=0, keepdims=True)
            out = jnp.dot(
                qkv[pl.ds((group + 1) * HEAD_SIZE, HEAD_SIZE), :count],
                weights.astype(jnp.bfloat16),
                preferred_element_type=jnp.float32,
            )
            attended[rows, lanes] = (out / total).astype(jnp.bfloat16)
            lse[head, :, lanes] = jnp.broadcast_to(highest + jnp.log(total), (8, TILE))
            return 0

        lax.fori_loop(0, group, one_head, 0)


def attend(qkv, cosine, sine, starts, group):
    length = qkv.shape[1]
    return pl.pallas_call(
        forward_kernel,
        out_shape=[
            jax.ShapeDtypeStruct((group * HEAD_SIZE, length), jnp.bfloat16),
            jax.ShapeDtypeStruct((group, 8, length), jnp.float32),
            jax.ShapeDtypeStruct((group * HEAD_SIZE, length), jnp.bfloat16),
            jax.ShapeDtypeStruct((HEAD_SIZE, length), jnp.bfloat16),
        ],
        in_specs=[VMEM] * 4,
        out_specs=[VMEM] * 4,
        scratch_shapes=[
            pltpu.VMEM((length, HEAD_SIZE), jnp.bfloat16),
            pltpu.VMEM((length, TILE), jnp.float32),
        ],
        compiler_params=pltpu.CompilerParams(vmem_limit_bytes=32 * 2**20),
        cost_estimate=pl.CostEstimate(
            flops=4 * group * length * length * HEAD_SIZE,
            bytes_accessed=group * length * length,
            transcendentals=group * length * length,
        ),
        name="attend",
    )(qkv, cosine, sine, starts)


def backward_kernel(
    qkv,
    queries,
    keys,
    attended,
    lse,
    grads,
    cosine,
    sine,
    starts,
    out,
    key_rows,
    value_rows,
    query_rows,
    grad_rows,
    row_dots,
    key_grad,
    value_grad,
    query_grad,
    bias,
):
    group = queries.shape[0] // HEAD_SIZE
    half = HEAD_SIZE // 2
    tiles = qkv.shape[1] // TILE
    key_rows[...] = keys[...].T
    value_rows[...] = qkv[pl.ds((group + 1) * HEAD_SIZE, HEAD_SIZE)].T
    for head in range(group):
        rows = pl.ds(head * HEAD_SIZE, HEAD_SIZE)
        query_rows[head] = queries[rows].T
        grad_rows[head] = grads[rows].T
        row_dots[head] = jnp.broadcast_to(
            jnp.sum(
                grads[rows].astype(jnp.float32) * attended[rows].astype(jnp.float32),
                axis=0,
                keepdims=True,
            ),
            row_dots.shape[1:],
        )
    key_grad[...] = jnp.zeros_like(key_grad)
    value_grad[...] = jnp.zeros_like(value_grad)
    for tile in range(tiles):
        lanes = pl.ds(tile * TILE, TILE)
        starts_here = starts[:, lanes]
        for low in range(tile + 1):
            bias[low] = bias_tile(starts_here, low, tile, low == tile)

        def one_head(head, _, lanes=lanes, tile=tile):
            rows = pl.ds(pl.multiple_of(head * HEAD_SIZE, HEAD_SIZE), HEAD_SIZE)
            query, grad = queries[rows, lanes], grads[rows, lanes]
            query_row, grad_row = query_rows[head, lanes], grad_rows[head, lanes]
            lse_row = lse[head, 0:1, lanes]
            dot_row = row_dots[head, 0:1, lanes]
            total = jnp.zeros((HEAD_SIZE, TILE), jnp.float32)
            for low in range(tile + 1):
                part = pl.ds(low * TILE, TILE)
                scores = jnp.dot(key_rows[part], query, preferred_element_type=jnp.float32)
                probs = jnp.exp(scores + bias[low] - lse_row)
                grad_probs = jnp.dot(value_rows[part], grad, preferred_element_type=jnp.float32)
                grad_scores = (probs * (grad_probs - dot_row)).astype(jnp.bfloat16)
                value_grad[part] += jnp.dot(
                    probs.astype(jnp.bfloat16), grad_row, preferred_element_type=jnp.float32
                )
                key_grad[part] += jnp.dot(
                    grad_scores, query_row, preferred_element_type=jnp.float32
                )
                total += jnp.dot(keys[:, part], grad_scores, preferred_element_type=jnp.float32)
            query_grad[rows, lanes] = total * 0.125
            return 0

        lax.fori_loop(0, group, one_head, 0)
    cos, sin = cosine[...], sine[...]
    for head in range(group):
        first = head * HEAD_SIZE
        out[pl.ds(first, HEAD_SIZE)] = rotate_rows(
            query_grad[pl.ds(first, half)], query_grad[pl.ds(first + half, half)], cos, -sin
        ).astype(jnp.bfloat16)
    turned = key_grad[...].T
    out[pl.ds(group * HEAD_SIZE, HEAD_SIZE)] = rotate_rows(
        turned[:half], turned[half:], cos, -sin
    ).astype(jnp.bfloat16)
    out[pl.ds((group + 1) * HEAD_SIZE, HEAD_SIZE)] = value_grad[...].T.astype(jnp.bfloat16)


def attend_back(qkv, queries, keys, attended, lse, grads, cosine, sine, starts):
    length = qkv.shape[1]
    group = queries.shape[0] // HEAD_SIZE
    tiles = length // TILE
    return pl.pallas_call(
        backward_kernel,
        out_shape=jax.ShapeDtypeStruct(qkv.shape, jnp.bfloat16),
        in_specs=[VMEM] * 9,
        out_specs=VMEM,
        scratch_shapes=[
            pltpu.VMEM((length, HEAD_SIZE), jnp.bfloat16),
            pltpu.VMEM((length, HEAD_SIZE), jnp.bfloat16),
            pltpu.VMEM((group, length, HEAD_SIZE), jnp.bfloat16),
            pltpu.VMEM((group, length, HEAD_SIZE), jnp.bfloat16),
            pltpu.VMEM((group, 8, length), jnp.float32),
            pltpu.VMEM((length, HEAD_SIZE), jnp.float32),
            pltpu.VMEM((length, HEAD_SIZE), jnp.float32),
            pltpu.VMEM((group * HEAD_SIZE, length), jnp.float32),
            pltpu.VMEM((tiles, TILE, TILE), jnp.float32),
        ],
        compiler_params=pltpu.CompilerParams(vmem_limit_bytes=40 * 2**20),
        cost_estimate=pl.CostEstimate(
            flops=10 * group * length * length * HEAD_SIZE,
            bytes_accessed=2 * group * length * length,
            transcendentals=group * length * length,
        ),
        name="attend_back",
    )(qkv, queries, keys, attended, lse, grads, cosine, sine, starts)


def contract_rows(left, right):
    return jnp.einsum("ta,tb->ab", left, right, preferred_element_type=jnp.float32)


def contract_cols(left, right):
    return jnp.einsum("ta,ba->tb", left, right, preferred_element_type=jnp.float32)


def matmul(left, right):
    return jnp.dot(left, right, preferred_element_type=jnp.float32)


def swap_heads(block):
    pairs = [(t * 16 + g, (g // 2) * 16 + 2 * t + g % 2) for t in range(8) for g in range(16)]
    return lax.ppermute(block, ("seq", "fsdp"), pairs)


def swap_heads_back(block):
    pairs = [((g // 2) * 16 + 2 * t + g % 2, t * 16 + g) for t in range(8) for g in range(16)]
    return lax.ppermute(block, ("seq", "fsdp"), pairs)


def swap_cores(block):
    return lax.ppermute(block, "fsdp", [(f, f ^ 1) for f in range(16)])


def shards(
    tokens,
    segment_ids,
    query_weight,
    key_matrix,
    value_matrix,
    output_weight,
    gate_weight,
    up_weight,
    down_weight,
    attention_gain,
    feed_gain,
    cotangent,
):
    rank = lax.axis_index("seq")
    owner = lax.axis_index("fsdp")
    ranks = lax.axis_size("seq")
    owners = lax.axis_size("fsdp")
    rows, width = query_weight.shape
    kv_cols = key_matrix.shape[1] // ranks
    q_cols = width // ranks
    group = q_cols // kv_cols
    ff = gate_weight.shape[1]
    ff_chunk = ff // owners // ranks
    segment_row = segment_ids[0]
    length = segment_row.shape[0]

    def columns(weight, size):
        return lax.dynamic_slice_in_dim(weight, rank * size, size, 1)

    def ff_columns(weight):
        split = weight.reshape(rows, owners, ranks, ff_chunk)
        return lax.dynamic_slice_in_dim(split, rank, 1, 2).reshape(rows, owners * ff_chunk)

    gains_in = jnp.zeros((16, q_cols + 2 * kv_cols), jnp.bfloat16)
    gains_in = gains_in.at[0, :rows].set(attention_gain).at[1, :rows].set(feed_gain)
    qkv_in = jnp.concatenate(
        [columns(query_weight, q_cols), columns(key_matrix, kv_cols), columns(value_matrix, kv_cols)],
        axis=1,
    )
    qkv_got = lax.all_gather(jnp.concatenate([qkv_in, gains_in], axis=0), "fsdp", axis=0)
    qkv_all = qkv_got[:, :rows].reshape(owners * rows, -1)
    gain_one = qkv_got[:, rows, :rows].reshape(1, -1).astype(jnp.float32)
    gain_two = qkv_got[:, rows + 1, :rows].reshape(1, -1).astype(jnp.float32)
    half = swap_heads(output_weight)
    other = swap_cores(half)
    first = owner % 2 == 0
    output_all = jnp.concatenate(
        [jnp.where(first, half, other), jnp.where(first, other, half)], axis=0
    )
    gate_up_all = lax.all_gather(
        jnp.concatenate([ff_columns(gate_weight), ff_columns(up_weight)], axis=1),
        "fsdp",
        axis=0,
        tiled=True,
    )
    ff_local = owners * ff_chunk
    down_all = lax.all_gather(
        lax.dynamic_slice_in_dim(down_weight, rank * ff_chunk, ff_chunk, 0),
        "fsdp",
        axis=0,
        tiled=True,
    )

    starts = (jnp.arange(length, dtype=jnp.int32) - positions_of(segment_row))[None]
    cosine, sine = (table.T for table in angles_of(segment_row, HEAD_SIZE))
    whole, grad_out = gather_many([tokens[0], cotangent[0]], 0)
    whole = whole.reshape(length, width).astype(jnp.float32)
    grad_out = grad_out.reshape(length, width)
    hidden_one = (whole * lax.rsqrt(mean_square(whole) + EPS) * gain_one).astype(jnp.bfloat16)
    qkv = jnp.einsum("tm,mc->ct", hidden_one, qkv_all, preferred_element_type=jnp.float32)
    qkv = qkv.astype(jnp.bfloat16)
    attended, lse, queries, keys = attend(qkv, cosine, sine, starts, group)
    middle, hidden_two = add_branch(
        contract_rows(attended, output_all).astype(jnp.bfloat16), tokens[0], gain_two, 1
    )
    hidden_two = hidden_two.reshape(length, width)

    gate = matmul(hidden_two, gate_up_all[:, :ff_local])
    up_proj = matmul(hidden_two, gate_up_all[:, ff_local:])
    sig_gate = jax.nn.sigmoid(gate)
    silu_gate = gate * sig_gate
    act = (silu_gate * up_proj).astype(jnp.bfloat16)
    grad_act = contract_cols(grad_out, down_all)
    grad_gate = (grad_act * up_proj * (sig_gate * (1.0 + gate * (1.0 - sig_gate)))).astype(
        jnp.bfloat16
    )
    grad_up = (grad_act * silu_gate).astype(jnp.bfloat16)
    gate_up_grads = jnp.concatenate([grad_gate, grad_up], axis=1)
    down_grad = contract_rows(act, grad_out).astype(jnp.bfloat16)
    down_share = lax.psum_scatter(down_grad, "fsdp", scatter_dimension=0, tiled=True)
    gate_up_grad = contract_rows(hidden_two, gate_up_grads).astype(jnp.bfloat16)
    gate_up_share = lax.psum_scatter(gate_up_grad, "fsdp", scatter_dimension=0, tiled=True)
    ff_whole = lax.all_gather(
        jnp.concatenate([gate_up_share, down_share], axis=0), "seq", axis=0
    )
    gate_up_whole = ff_whole[:, :rows]
    down_whole = ff_whole[:, rows:].reshape(-1, width).astype(jnp.float32)
    grad_middle, grad_gain_two, grad_branch = back_to_middle(
        contract_cols(gate_up_grads, gate_up_all).astype(jnp.bfloat16),
        middle,
        gain_two,
        cotangent[0],
        2,
    )
    grad_branch = grad_branch.reshape(length, width)

    grad_attended = jnp.einsum(
        "tm,fm->ft", grad_branch, output_all, preferred_element_type=jnp.float32
    ).astype(jnp.bfloat16)
    qkv_grads = attend_back(
        qkv, queries, keys, attended, lse, grad_attended, cosine, sine, starts
    )
    output_grad = matmul(attended, grad_branch).astype(jnp.bfloat16)
    output_grad = output_grad.reshape(2, ranks, -1, width).swapaxes(0, 1).reshape(-1, width)
    output_share = swap_heads_back(
        lax.psum_scatter(output_grad, "fsdp", scatter_dimension=0, tiled=True)
    )
    output_whole = lax.all_gather(output_share, "seq", axis=0, tiled=True).astype(jnp.float32)
    grad_inputs, grad_gain_one = back_to_tokens(
        jnp.einsum("ct,mc->tm", qkv_grads, qkv_all, preferred_element_type=jnp.float32).astype(
            jnp.bfloat16
        ),
        tokens[0],
        gain_one,
        grad_middle,
        3,
    )
    qkv_share = lax.psum_scatter(
        jnp.einsum(
            "tm,ct->mc", hidden_one, qkv_grads, preferred_element_type=jnp.float32
        ).astype(jnp.bfloat16),
        "fsdp",
        scatter_dimension=0,
        tiled=True,
    )
    qkv_whole = lax.all_gather(qkv_share, "seq", axis=0)
    layer_out = finish_layer(matmul(act, down_all).astype(jnp.bfloat16), middle, 4)
    gain_totals = lax.psum(jnp.concatenate([grad_gain_one, grad_gain_two]), ("seq", "fsdp"))
    gain_totals = lax.dynamic_slice_in_dim(gain_totals, owner * rows, rows, 1)

    def spread(part):
        return part.swapaxes(0, 1).reshape(rows, -1).astype(jnp.float32)

    def ff_spread(part):
        return (
            part.reshape(ranks, rows, owners, ff_chunk)
            .transpose(1, 2, 0, 3)
            .reshape(rows, ff)
            .astype(jnp.float32)
        )

    return (
        layer_out[None],
        grad_inputs[None],
        spread(qkv_whole[:, :, :q_cols]),
        spread(qkv_whole[:, :, q_cols : q_cols + kv_cols]),
        spread(qkv_whole[:, :, q_cols + kv_cols :]),
        output_whole,
        ff_spread(gate_up_whole[:, :, :ff_local]),
        ff_spread(gate_up_whole[:, :, ff_local:]),
        down_whole,
        gain_totals[0],
        gain_totals[1],
    )


def solution(mesh):
    placed = (
        P("fsdp", "seq", None),
        P("fsdp", None),
        P("fsdp", None),
        P("fsdp", None),
        P("fsdp", None),
        P("fsdp", None),
        P("fsdp", None),
        P("fsdp", None),
        P("fsdp", None),
        P("fsdp"),
        P("fsdp"),
        P("fsdp", "seq", None),
    )
    return jax.shard_map(
        shards,
        mesh=mesh,
        in_specs=placed,
        out_specs=(
            P("fsdp", "seq", None),
            P("fsdp", "seq", None),
            P("fsdp", None),
            P("fsdp", None),
            P("fsdp", None),
            P("fsdp", None),
            P("fsdp", None),
            P("fsdp", None),
            P("fsdp", None),
            P("fsdp"),
            P("fsdp"),
        ),
        check_vma=False,
    )
```

```python
import math

import jax
import jax.numpy as jnp
from jax import lax
from jax.experimental import pallas as pl
from jax.experimental.pallas import tpu as pltpu
from jax.sharding import PartitionSpec as P

HEAD_SIZE = 64
EPS = 1e-05
ROPE_BASE = 500000.0
NEG = -1e30


def rope_freqs(head_dim):
    half_dim = head_dim // 2
    table = []
    for index in range(half_dim):
        inverse = 1.0 / ROPE_BASE ** (index * 2.0 / head_dim)
        wavelen = 2.0 * math.pi / inverse
        blend = (8192.0 / wavelen - 1.0) / 3.0
        mixed = (1.0 - blend) * inverse / 32.0 + blend * inverse
        entry = inverse if wavelen < 2048.0 else inverse / 32.0 if wavelen > 8192.0 else mixed
        table.append(entry)
    return jnp.asarray(table, dtype=jnp.float32)


def positions_of(segment_row):
    indices = jnp.arange(segment_row.shape[0], dtype=jnp.int32)
    begins = jnp.concatenate(
        [jnp.ones((1,), dtype=jnp.int32), (segment_row[1:] != segment_row[:-1]).astype(jnp.int32)]
    )
    starts_at = lax.cummax(jnp.where(begins > 0, indices, 0), axis=0)
    return indices - starts_at


def angles_of(segment_row, head_dim):
    positions = positions_of(segment_row)
    phase = positions.astype(jnp.float32)[:, None] * rope_freqs(head_dim)[None, :]
    return (jnp.cos(phase), jnp.sin(phase))


MESH = pl.DeviceIdType.MESH
CHUNKS = 4
TILE = 256


def ring():
    rank, owner = lax.axis_index("seq"), lax.axis_index("fsdp")
    side = lax.axis_size("seq") // 2
    row, col = lax.div(rank, side), lax.rem(rank, side)

    def at(which, step):
        return which * side + lax.rem(col + step, side)

    near = [at(row, step) for step in range(side)]
    far = [at(1 - row, step) for step in range(side)]
    return owner, near, far


def greet(peers):
    barrier = pltpu.get_barrier_semaphore()
    for peer in peers:
        pl.semaphore_signal(barrier, inc=1, device_id=peer, device_id_type=MESH)
    pl.semaphore_wait(barrier, len(peers))


def along_seq(ids):
    owner, near, far = ids
    return [(near[1], owner), (near[3], owner), (far[0], owner)]


def along_fsdp(ids):
    owner, near, _ = ids
    core, place = lax.rem(owner, 2), lax.div(owner, 2)
    count = lax.axis_size("fsdp") // 2
    places = [lax.rem(place + step, count) for step in range(count)]
    mate = (near[0], owner + 1 - 2 * core)
    return core, mate, places, [(near[0], 2 * other + core) for other in places]


class Copies:
    def __init__(self, send, recv):
        self.send, self.recv = send, recv
        self.made = []

    def start(self, source, target, peer):
        number = len(self.made)
        copy = pltpu.make_async_remote_copy(
            src_ref=source,
            dst_ref=target,
            send_sem=self.send.at[number],
            recv_sem=self.recv.at[number],
            device_id=peer,
            device_id_type=MESH,
        )
        copy.start()
        self.made.append(copy)
        return copy

    def finish(self):
        for copy in self.made:
            copy.wait_send()


def by_rows(rows, chunks):
    size = rows // chunks
    return lambda ref, index: ref.at[pl.ds(index * size, size)]


def by_columns(columns, chunks):
    size = columns // chunks
    return lambda ref, index: ref.at[:, pl.ds(index * size, size)]


def gather_blocks(ids, copies, arrays, chunks, meanwhile=None):
    peers = along_seq(ids)
    to_right_of, to_left_of, to_far_of = peers
    _, near, far = ids
    me, right, opposite, left = near
    partner = far[0]
    half = chunks // 2
    to_right, to_left, to_far, on = {}, {}, {}, {}
    for key, (own, out, cut) in enumerate(arrays):
        for step in range(chunks):
            back = chunks - 1 - step
            to_right[key, step] = copies.start(cut(own, step), cut(out.at[me], step), to_right_of)
            to_left[key, back] = copies.start(cut(own, back), cut(out.at[me], back), to_left_of)
            to_far[key, step] = copies.start(cut(own, step), cut(out.at[me], step), to_far_of)
    if meanwhile is not None:
        meanwhile()
    for key, (_, out, cut) in enumerate(arrays):
        for step in range(half):
            back = chunks - 1 - step
            to_right[key, step].wait_recv()
            block = cut(out.at[left], step)
            on[key, step] = copies.start(block, block, to_right_of)
            to_left[key, back].wait_recv()
            block = cut(out.at[right], back)
            on[key, back] = copies.start(block, block, to_left_of)
    rest = []
    for key, (_, out, cut) in enumerate(arrays):
        for step in range(chunks):
            to_far[key, step].wait_recv()
            block = cut(out.at[partner], step)
            rest.append(copies.start(block, block, to_right_of))
            rest.append(copies.start(block, block, to_left_of))
    for key, (_, out, cut) in enumerate(arrays):
        for step in range(half):
            for index in (step, chunks - 1 - step):
                on[key, index].wait_recv()
                block = cut(out.at[opposite], index)
                rest.append(copies.start(block, block, to_far_of))
    for key in range(len(arrays)):
        for step in range(half):
            to_right[key, chunks - 1 - step].wait_recv()
            to_left[key, step].wait_recv()
    for copy in rest:
        copy.wait_recv()


def gather_copies(chunks):
    return 3 * chunks + chunks + 2 * chunks + chunks


def reduce_blocks(ids, copies, part_of, bufs, rows, chunks, done, meanwhile=None, later=None):
    to_right_of, to_left_of, to_far_of = along_seq(ids)
    _, near, far = ids
    me, right, opposite, left = near
    partner, far_right, far_opposite, far_left = far
    from_left, from_right, from_far, mid, end_left, end_right, end_far = bufs
    size = rows // chunks
    half = chunks // 2

    def part(index):
        return pl.ds(index * size, size)

    def wide(ref):
        return ref.astype(jnp.float32)

    order = [x for step in range(half) for x in (step, chunks - 1 - step)]
    one_right, one_left, one_far = {}, {}, {}
    for index in order:
        rows_of = part(index)
        one_far[index] = copies.start(
            part_of.at[far_opposite, rows_of], from_far.at[rows_of], to_far_of
        )
        one_right[index] = copies.start(
            part_of.at[far_right, rows_of], from_left.at[rows_of], to_right_of
        )
        one_left[index] = copies.start(
            part_of.at[far_left, rows_of], from_right.at[rows_of], to_left_of
        )
    last_right, last_left, last_far = {}, {}, {}
    for index in range(half):
        rows_of = part(index)
        last_right[index] = copies.start(
            part_of.at[right, rows_of], end_left.at[rows_of], to_right_of
        )
        rows_of = part(chunks - 1 - index)
        last_left[chunks - 1 - index] = copies.start(
            part_of.at[left, rows_of], end_right.at[rows_of], to_left_of
        )
    if meanwhile is not None:
        meanwhile()
    two = {}
    for index in order:
        rows_of = part(index)
        one_far[index].wait_recv()
        from_far[rows_of] = (wide(from_far[rows_of]) + wide(part_of[opposite, rows_of])).astype(
            jnp.bfloat16
        )
        two[index] = copies.start(
            from_far.at[rows_of], mid.at[rows_of], to_left_of if index < half else to_right_of
        )
    for index in order:
        rows_of = part(index)
        one_right[index].wait_recv()
        one_left[index].wait_recv()
        from_left[rows_of] = (
            wide(from_left[rows_of]) + wide(from_right[rows_of]) + wide(part_of[partner, rows_of])
        ).astype(jnp.bfloat16)
        last_far[index] = copies.start(
            from_left.at[rows_of], end_far.at[rows_of], to_far_of
        )
    for index in order:
        rows_of = part(index)
        two[index].wait_recv()
        if index < half:
            mid[rows_of] = (wide(mid[rows_of]) + wide(part_of[left, rows_of])).astype(jnp.bfloat16)
            last_left[index] = copies.start(mid.at[rows_of], end_right.at[rows_of], to_left_of)
        else:
            mid[rows_of] = (wide(mid[rows_of]) + wide(part_of[right, rows_of])).astype(
                jnp.bfloat16
            )
            last_right[index] = copies.start(mid.at[rows_of], end_left.at[rows_of], to_right_of)
    if later is not None:
        later()
    for index in order:
        rows_of = part(index)
        last_far[index].wait_recv()
        last_left[index].wait_recv()
        last_right[index].wait_recv()
        done(
            rows_of,
            wide(part_of[me, rows_of])
            + wide(end_left[rows_of])
            + wide(end_right[rows_of])
            + wide(end_far[rows_of]),
        )


def reduce_copies(chunks):
    return 3 * chunks + 2 * chunks + chunks + chunks


def reduce_scratch(rows, width):
    return [pltpu.VMEM((rows, width), jnp.bfloat16) for _ in range(7)]


def semaphores(count):
    return [pltpu.SemaphoreType.DMA((count,)), pltpu.SemaphoreType.DMA((count,))]


def params(number, limit):
    return pltpu.CompilerParams(
        collective_id=number, has_side_effects=True, vmem_limit_bytes=limit * 2**20
    )


VMEM = pl.BlockSpec(memory_space=pltpu.VMEM)
ANYWHERE = pl.BlockSpec(memory_space=pl.ANY)


def gather_tokens(tokens, number):
    rows, width = tokens.shape
    ranks = lax.axis_size("seq")

    def kernel(own, out, local, send, recv):
        ids = ring()
        greet(along_seq(ids))
        kept = pltpu.make_async_copy(own, out.at[ids[1][0]], local)
        kept.start()
        copies = Copies(send, recv)
        gather_blocks(ids, copies, [(own, out, by_rows(rows, CHUNKS))], CHUNKS)
        copies.finish()
        kept.wait()

    return pl.pallas_call(
        kernel,
        out_shape=jax.ShapeDtypeStruct((ranks, rows, width), jnp.bfloat16),
        in_specs=[ANYWHERE],
        out_specs=ANYWHERE,
        scratch_shapes=[pltpu.SemaphoreType.DMA] + semaphores(gather_copies(CHUNKS)),
        compiler_params=params(number, 32),
        cost_estimate=pl.CostEstimate(
            flops=0, bytes_accessed=ranks * rows * width * 32, transcendentals=0
        ),
        name="gather_tokens",
    )(tokens)


def mean_square(values):
    return jnp.mean(values * values, axis=-1, keepdims=True)


def branch_kernel(part_of, tokens, gain, middle, hidden, block, local, send, recv, *bufs):
    ids = ring()
    rows = tokens.shape[0]
    greet(along_seq(ids))
    copies = Copies(send, recv)

    def done(rows_of, total):
        values = tokens[rows_of].astype(jnp.float32) + total
        middle[rows_of] = values
        factor = lax.rsqrt(mean_square(values) + EPS)
        block[rows_of] = (values * factor * gain[...]).astype(jnp.bfloat16)

    reduce_blocks(ids, copies, part_of, bufs, rows, CHUNKS, done)
    kept = pltpu.make_async_copy(block, hidden.at[ids[1][0]], local)
    kept.start()
    gather_blocks(ids, copies, [(block, hidden, by_rows(rows, CHUNKS))], CHUNKS)
    copies.finish()
    kept.wait()


def add_branch(partial, tokens, gain, number):
    rows, width = tokens.shape
    ranks = lax.axis_size("seq")
    count = reduce_copies(CHUNKS) + gather_copies(CHUNKS)
    return pl.pallas_call(
        branch_kernel,
        out_shape=[
            jax.ShapeDtypeStruct((rows, width), jnp.float32),
            jax.ShapeDtypeStruct((ranks, rows, width), jnp.bfloat16),
        ],
        in_specs=[VMEM] * 3,
        out_specs=[VMEM, ANYWHERE],
        scratch_shapes=[pltpu.VMEM((rows, width), jnp.bfloat16), pltpu.SemaphoreType.DMA]
        + semaphores(count)
        + reduce_scratch(rows, width),
        compiler_params=params(number, 32),
        cost_estimate=pl.CostEstimate(
            flops=0, bytes_accessed=ranks * rows * width * 64, transcendentals=0
        ),
        name="add_branch",
    )(partial.reshape(ranks, rows, width), tokens, gain)


def norm_back_rows(grad, gain, values):
    factor = lax.rsqrt(mean_square(values) + EPS)
    normed = values * factor
    weighted = grad * gain
    back = factor * (weighted - normed * jnp.mean(weighted * normed, axis=-1, keepdims=True))
    return back, grad * normed


def middle_kernel(
    part_of, middle, gain, cotangent, grad_middle, grad_gain, branch, block, local, send, recv, *bufs
):
    ids = ring()
    rows = middle.shape[0]
    greet(along_seq(ids))
    copies = Copies(send, recv)
    grad_gain[...] = jnp.zeros_like(grad_gain)

    def done(rows_of, total):
        back, terms = norm_back_rows(total, gain[...], middle[rows_of])
        grad_gain[...] += jnp.sum(terms, axis=0, keepdims=True)
        values = cotangent[rows_of].astype(jnp.float32) + back
        grad_middle[rows_of] = values
        block[rows_of] = values.astype(jnp.bfloat16)

    reduce_blocks(ids, copies, part_of, bufs, rows, CHUNKS, done)
    kept = pltpu.make_async_copy(block, branch.at[ids[1][0]], local)
    kept.start()
    gather_blocks(ids, copies, [(block, branch, by_rows(rows, CHUNKS))], CHUNKS)
    copies.finish()
    kept.wait()


def back_to_middle(partial, middle, gain, cotangent, number):
    rows, width = middle.shape
    ranks = lax.axis_size("seq")
    count = reduce_copies(CHUNKS) + gather_copies(CHUNKS)
    return pl.pallas_call(
        middle_kernel,
        out_shape=[
            jax.ShapeDtypeStruct((rows, width), jnp.float32),
            jax.ShapeDtypeStruct((1, width), jnp.float32),
            jax.ShapeDtypeStruct((ranks, rows, width), jnp.bfloat16),
        ],
        in_specs=[VMEM] * 4,
        out_specs=[VMEM, VMEM, ANYWHERE],
        scratch_shapes=[pltpu.VMEM((rows, width), jnp.bfloat16), pltpu.SemaphoreType.DMA]
        + semaphores(count)
        + reduce_scratch(rows, width),
        compiler_params=params(number, 32),
        cost_estimate=pl.CostEstimate(
            flops=0, bytes_accessed=ranks * rows * width * 64, transcendentals=0
        ),
        name="back_to_middle",
    )(partial.reshape(ranks, rows, width), middle, gain, cotangent)


def transposed(ids):
    owner, near, _ = ids
    return lax.div(owner, 2), 2 * near[0] + lax.rem(owner, 2)


def tokens_kernel(
    part_of,
    tokens,
    gain,
    grad_middle,
    qkv_parts,
    heads_parts,
    out,
    grad_gain,
    qkv_share,
    heads_share,
    qkv_mate,
    heads_mate,
    qkv_got,
    heads_got,
    heads_block,
    heads_here,
    send,
    recv,
    *bufs,
):
    ids = ring()
    rows = tokens.shape[0]
    core, mate, places, others = along_fsdp(ids)
    place = places[0]
    swap = transposed(ids)
    stays = swap[0] == ids[1][0]
    barrier = pltpu.get_barrier_semaphore()
    peers = along_seq(ids) + [mate] + others[1:]
    for peer in peers:
        pl.semaphore_signal(barrier, inc=1, device_id=peer, device_id_type=MESH)

    @pl.when(jnp.logical_not(stays))
    def _():
        pl.semaphore_signal(barrier, inc=1, device_id=swap, device_id_type=MESH)
        pl.semaphore_wait(barrier, len(peers) + 1)

    @pl.when(stays)
    def _():
        pl.semaphore_wait(barrier, len(peers))

    copies = Copies(send, recv)
    grad_gain[...] = jnp.zeros_like(grad_gain)
    pair = [
        copies.start(qkv_parts.at[:, 1 - core], qkv_mate, mate),
        copies.start(heads_parts.at[1 - core], heads_mate, mate),
    ]
    pushed = []

    def meanwhile():
        for copy in pair:
            copy.wait_recv()

        def add(index, _):
            qkv_mate[index] = (
                qkv_mate[index].astype(jnp.float32) + qkv_parts[index, core].astype(jnp.float32)
            ).astype(jnp.bfloat16)
            heads_mate[index] = (
                heads_mate[index].astype(jnp.float32)
                + heads_parts[core, index].astype(jnp.float32)
            ).astype(jnp.bfloat16)
            return 0

        lax.fori_loop(0, len(places), add, 0)
        for step in range(1, len(places)):
            pushed.append(
                copies.start(qkv_mate.at[places[step]], qkv_got.at[step], others[step])
            )
            pushed.append(
                copies.start(heads_mate.at[places[step]], heads_got.at[step], others[step])
            )

    def later():
        for copy in pushed:
            copy.wait_recv()
        total = qkv_mate[place].astype(jnp.float32)
        heads_total = heads_mate[place].astype(jnp.float32)
        for step in range(1, len(places)):
            total += qkv_got[step].astype(jnp.float32)
            heads_total += heads_got[step].astype(jnp.float32)
        qkv_share[...] = total.astype(jnp.bfloat16)
        heads_block[...] = heads_total.astype(jnp.bfloat16)

        @pl.when(jnp.logical_not(stays))
        def _():
            copy = pltpu.make_async_remote_copy(
                src_ref=heads_block,
                dst_ref=heads_here,
                send_sem=send.at[send.shape[0] - 1],
                recv_sem=recv.at[recv.shape[0] - 1],
                device_id=swap,
                device_id_type=MESH,
            )
            copy.start()

    def done(rows_of, total):
        back, terms = norm_back_rows(total, gain[...], tokens[rows_of].astype(jnp.float32))
        grad_gain[...] += jnp.sum(terms, axis=0, keepdims=True)
        out[rows_of] = (grad_middle[rows_of] + back).astype(jnp.bfloat16)

    reduce_blocks(ids, copies, part_of, bufs, rows, CHUNKS, done, meanwhile, later)
    copies.finish()

    @pl.when(stays)
    def _():
        heads_share[...] = heads_block[...]

    @pl.when(jnp.logical_not(stays))
    def _():
        pltpu.make_async_remote_copy(
            src_ref=heads_block,
            dst_ref=heads_here,
            send_sem=send.at[send.shape[0] - 1],
            recv_sem=recv.at[recv.shape[0] - 1],
            device_id=swap,
            device_id_type=MESH,
        ).wait()
        heads_share[...] = heads_here[...]


def back_to_tokens(partial, tokens, gain, grad_middle, qkv_grad, heads_grad, number):
    rows, width = tokens.shape
    ranks, owners = lax.axis_size("seq"), lax.axis_size("fsdp")
    places = owners // 2
    qkv_cols, head_rows = qkv_grad.shape[1], heads_grad.shape[0] // owners
    count = reduce_copies(CHUNKS) + 2 + 2 * (places - 1) + 1
    return pl.pallas_call(
        tokens_kernel,
        out_shape=[
            jax.ShapeDtypeStruct((rows, width), jnp.bfloat16),
            jax.ShapeDtypeStruct((1, width), jnp.float32),
            jax.ShapeDtypeStruct((rows, qkv_cols), jnp.bfloat16),
            jax.ShapeDtypeStruct((head_rows, width), jnp.bfloat16),
        ],
        in_specs=[VMEM] * 6,
        out_specs=[VMEM] * 4,
        scratch_shapes=[
            pltpu.VMEM((places, rows, qkv_cols), jnp.bfloat16),
            pltpu.VMEM((places, head_rows, width), jnp.bfloat16),
            pltpu.VMEM((places, rows, qkv_cols), jnp.bfloat16),
            pltpu.VMEM((places, head_rows, width), jnp.bfloat16),
            pltpu.VMEM((head_rows, width), jnp.bfloat16),
            pltpu.VMEM((head_rows, width), jnp.bfloat16),
        ]
        + semaphores(count)
        + reduce_scratch(rows, width),
        compiler_params=params(number, 40),
        cost_estimate=pl.CostEstimate(
            flops=0, bytes_accessed=ranks * rows * width * 32, transcendentals=0
        ),
        name="back_to_tokens",
    )(
        partial.reshape(ranks, rows, width),
        tokens,
        gain,
        grad_middle,
        qkv_grad.reshape(places, 2, rows, qkv_cols),
        heads_grad.reshape(2, places, head_rows, width),
    )


def finish_kernel(
    gate_up,
    down,
    qkv,
    heads,
    gain_one,
    gain_two,
    gate_up_all,
    down_all,
    qkv_all,
    heads_all,
    gains,
    given,
    from_mate,
    summed,
    from_places,
    for_partner,
    from_partner,
    by_column,
    local,
    send,
    recv,
):
    ids = ring()
    _, near, _ = ids
    me = near[0]
    side = lax.axis_size("seq") // 2
    column = lax.rem(me, side)
    core, mate, places, others = along_fsdp(ids)
    to_right_of, to_left_of, to_far_of = along_seq(ids)
    greet(along_seq(ids) + [mate] + others[1:])
    copies = Copies(send, recv)
    arrays = [
        (gate_up, gate_up_all, by_rows(gate_up.shape[0], CHUNKS)),
        (down, down_all, by_rows(down.shape[0], CHUNKS)),
        (qkv, qkv_all, by_rows(qkv.shape[0], CHUNKS)),
        (heads, heads_all, by_columns(heads.shape[1], CHUNKS)),
    ]
    kept = [
        pltpu.make_async_copy(own, out.at[me], local.at[i]) for i, (own, out, _) in enumerate(arrays)
    ]
    for copy in kept:
        copy.start()

    def sum_gains():
        lanes = given.shape[3]
        for index in range(2 * len(places)):
            cols = pl.ds(index * lanes, lanes)
            given[index // 2, index % 2, 0:1] = gain_one[:, cols]
            given[index // 2, index % 2, 1:2] = gain_two[:, cols]
            given[index // 2, index % 2, 2:8] = jnp.zeros((6, lanes), jnp.float32)
        copy = copies.start(given.at[:, 1 - core], from_mate, mate)
        copy.wait_recv()
        summed[...] = given[:, core] + from_mate[...]
        pushed = [
            copies.start(summed.at[places[step]], from_places.at[step], others[step])
            for step in range(1, len(places))
        ]
        for copy in pushed:
            copy.wait_recv()
        total = summed[places[0]]
        for step in range(1, len(places)):
            total += from_places[step]
        for_partner[...] = total
        copy = copies.start(for_partner, from_partner, to_far_of)
        copy.wait_recv()
        by_column[column] = for_partner[...] + from_partner[...]
        to_right = copies.start(by_column.at[column], by_column.at[column], to_right_of)
        to_left = copies.start(by_column.at[column], by_column.at[column], to_left_of)
        to_right.wait_recv()
        to_left.wait_recv()
        after = lax.rem(column + 1, side)
        copies.start(by_column.at[after], by_column.at[after], to_left_of).wait_recv()
        gains[...] = (by_column[0] + by_column[1]) + (by_column[2] + by_column[3])

    gather_blocks(ids, copies, arrays, CHUNKS, sum_gains)
    copies.finish()
    for copy in kept:
        copy.wait()


def finish_grads(gate_up, down, qkv, heads, gain_one, gain_two, number):
    ranks, owners = lax.axis_size("seq"), lax.axis_size("fsdp")
    blocks = (gate_up, down, qkv, heads)
    places = owners // 2
    lanes = gain_one.shape[1] // owners
    size = sum(block.size for block in blocks)
    count = len(blocks) * gather_copies(CHUNKS) + 1 + (places - 1) + 1 + 3

    def table(*shape):
        return pltpu.VMEM((*shape, 8, lanes), jnp.float32)

    return pl.pallas_call(
        finish_kernel,
        out_shape=[jax.ShapeDtypeStruct((ranks, *block.shape), block.dtype) for block in blocks]
        + [jax.ShapeDtypeStruct((8, lanes), jnp.float32)],
        in_specs=[ANYWHERE] * 4 + [VMEM] * 2,
        out_specs=[ANYWHERE] * 4 + [VMEM],
        scratch_shapes=[
            table(places, 2),
            table(places),
            table(places),
            table(places),
            table(),
            table(),
            table(ranks // 2),
            pltpu.SemaphoreType.DMA((len(blocks),)),
        ]
        + semaphores(count),
        compiler_params=params(number, 32),
        cost_estimate=pl.CostEstimate(
            flops=0, bytes_accessed=ranks * size * 32, transcendentals=0
        ),
        name="finish_grads",
    )(*blocks, gain_one, gain_two)


def merge_lanes(first, second):
    half = first.shape[1] // 2
    low = lax.broadcasted_iota(jnp.int32, first.shape, 1) < half
    return (
        jnp.where(low, first, pltpu.roll(second, half, 1)),
        jnp.where(low, pltpu.roll(first, half, 1), second),
    )


def place_kernel(gate, up, down, query, pair, heads, gate_out, up_out, down_out, query_out, key_out, value_out, heads_out):
    lanes = gate.shape[2]
    blocks = gate.shape[0] // 2
    for part, out in ((gate, gate_out), (up, up_out)):
        for index in range(blocks):
            low, high = merge_lanes(
                part[2 * index].astype(jnp.float32), part[2 * index + 1].astype(jnp.float32)
            )
            out[:, pl.ds(index * lanes, lanes)] = low
            out[:, pl.ds((blocks + index) * lanes, lanes)] = high
    key, value = merge_lanes(pair[0].astype(jnp.float32), pair[1].astype(jnp.float32))
    key_out[...] = key
    value_out[...] = value
    down_out[...] = down[0].astype(jnp.float32)
    query_out[...] = query[0].astype(jnp.float32)
    heads_out[...] = heads[0].astype(jnp.float32)


def place_grads(gate_up, down, qkv, heads):
    ranks, rows, both = gate_up.shape
    lanes = 128
    steps = both // 2 // lanes
    down_rows, width = down.shape[1:]
    head_rows = heads.shape[1]
    query_cols = qkv.shape[2] - lanes
    assert steps == ranks and lanes == 2 * HEAD_SIZE
    real = jnp.float32
    return pl.pallas_call(
        place_kernel,
        grid=(steps,),
        out_shape=[
            jax.ShapeDtypeStruct((rows, ranks * both // 2), real),
            jax.ShapeDtypeStruct((rows, ranks * both // 2), real),
            jax.ShapeDtypeStruct((ranks * down_rows, width), real),
            jax.ShapeDtypeStruct((rows, ranks * query_cols), real),
            jax.ShapeDtypeStruct((rows, ranks * HEAD_SIZE), real),
            jax.ShapeDtypeStruct((rows, ranks * HEAD_SIZE), real),
            jax.ShapeDtypeStruct((ranks * head_rows, width), real),
        ],
        in_specs=[
            pl.BlockSpec((ranks, rows, lanes), lambda i: (0, 0, i)),
            pl.BlockSpec((ranks, rows, lanes), lambda i: (0, 0, steps + i)),
            pl.BlockSpec((1, down_rows, width), lambda i: (i, 0, 0)),
            pl.BlockSpec((1, rows, query_cols), lambda i: (i, 0, 0)),
            pl.BlockSpec((2, rows, lanes), lambda i: (i // 2, 0, query_cols // lanes)),
            pl.BlockSpec((1, head_rows, width), lambda i: (i, 0, 0)),
        ],
        out_specs=[
            pl.BlockSpec((rows, ranks * lanes), lambda i: (0, i)),
            pl.BlockSpec((rows, ranks * lanes), lambda i: (0, i)),
            pl.BlockSpec((down_rows, width), lambda i: (i, 0)),
            pl.BlockSpec((rows, query_cols), lambda i: (0, i)),
            pl.BlockSpec((rows, lanes), lambda i: (0, i // 2)),
            pl.BlockSpec((rows, lanes), lambda i: (0, i // 2)),
            pl.BlockSpec((head_rows, width), lambda i: (i, 0)),
        ],
        compiler_params=pltpu.CompilerParams(vmem_limit_bytes=32 * 2**20),
        name="place_grads",
    )(gate_up, gate_up, down, qkv, qkv, heads)


def pick_kernel(
    query, key, value, gate, up, gain_one, gain_two, qkv_out, gate_up_out, wide, narrow, sems
):
    rank, ranks = lax.axis_index("seq"), lax.axis_size("seq")
    rows = query.shape[0]
    lanes = 128
    owners = wide.shape[1]
    pair = lax.div(rank, 2)
    odd = lax.rem(rank, 2)
    query_cols = query.shape[1] // ranks
    stride = gate.shape[1] // owners
    count = 0
    made = []

    def fetch(source, target):
        nonlocal count
        copy = pltpu.make_async_copy(source, target, sems.at[count])
        copy.start()
        made.append(copy)
        count += 1

    fetch(
        query.at[:, pl.ds(pl.multiple_of(rank * query_cols, lanes), query_cols)],
        qkv_out.at[pl.ds(0, rows), pl.ds(0, query_cols)],
    )
    for index, source in enumerate((key, value)):
        fetch(source.at[:, pl.ds(pl.multiple_of(pair * lanes, lanes), lanes)], narrow.at[index])
    for which, source in enumerate((gate, up)):
        for owner in range(owners):
            first = pl.multiple_of(owner * stride + pair * lanes, lanes)
            fetch(source.at[:, pl.ds(first, lanes)], wide.at[which, owner])
    line = lax.broadcasted_iota(jnp.int32, (16, rows), 0)
    first, second = (gain[...].astype(jnp.float32) for gain in (gain_one, gain_two))
    gains = jnp.where(line == 0, first, jnp.where(line == 1, second, 0.0))
    qkv_out[pl.ds(rows, 16)] = jnp.zeros((16, qkv_out.shape[1]), jnp.bfloat16)
    qkv_out[pl.ds(rows, 16), pl.ds(0, rows)] = gains.astype(jnp.bfloat16)
    for copy in made:
        copy.wait()

    def chosen(first, second):
        low, high = merge_lanes(first.astype(jnp.float32), second.astype(jnp.float32))
        return jnp.where(odd == 0, low, high).astype(jnp.bfloat16)

    qkv_out[pl.ds(0, rows), pl.ds(query_cols, lanes)] = chosen(narrow[0], narrow[1])
    for which in range(2):
        for index in range(owners // 2):
            cols = pl.ds((which * (owners // 2) + index) * lanes, lanes)
            gate_up_out[:, cols] = chosen(wide[which, 2 * index], wide[which, 2 * index + 1])


def pick_columns(query, key, value, gate, up, gain_one, gain_two):
    rows, width = query.shape
    ranks, owners = lax.axis_size("seq"), lax.axis_size("fsdp")
    lanes = 128
    assert gate.shape[1] // owners // ranks == HEAD_SIZE == lanes // 2
    return pl.pallas_call(
        pick_kernel,
        out_shape=[
            jax.ShapeDtypeStruct((rows + 16, width // ranks + lanes), jnp.bfloat16),
            jax.ShapeDtypeStruct((rows, owners * lanes), jnp.bfloat16),
        ],
        in_specs=[ANYWHERE] * 5 + [VMEM] * 2,
        out_specs=[VMEM] * 2,
        scratch_shapes=[
            pltpu.VMEM((2, owners, rows, lanes), jnp.bfloat16),
            pltpu.VMEM((2, rows, lanes), jnp.bfloat16),
            pltpu.SemaphoreType.DMA((2 * owners + 3,)),
        ],
        compiler_params=pltpu.CompilerParams(vmem_limit_bytes=32 * 2**20),
        name="pick_columns",
    )(query, key, value, gate, up, gain_one[None], gain_two[None])


def rotate_rows(first, second, cosine, sine):
    return jnp.concatenate([first * cosine - second * sine, second * cosine + first * sine], axis=0)


def bias_tile(start_row, key_tile, query_tile, diagonal):
    keys = key_tile * TILE + lax.broadcasted_iota(jnp.int32, (TILE, TILE), 0)
    seen = keys >= start_row
    if diagonal:
        queries = query_tile * TILE + lax.broadcasted_iota(jnp.int32, (TILE, TILE), 1)
        seen = seen & (keys <= queries)
    return jnp.where(seen, 0.0, NEG)


def attend_tiles(qkv, cosine, sine, starts, attended, lse, queries, keys, key_rows, bias):
    group = queries.shape[0] // HEAD_SIZE
    half = HEAD_SIZE // 2
    tiles = qkv.shape[1] // TILE
    cos, sin = cosine[...], sine[...]

    def rotated(first):
        return rotate_rows(
            qkv[pl.ds(first, half)].astype(jnp.float32),
            qkv[pl.ds(first + half, half)].astype(jnp.float32),
            cos,
            sin,
        ).astype(jnp.bfloat16)

    for head in range(group):
        queries[pl.ds(head * HEAD_SIZE, HEAD_SIZE)] = rotated(head * HEAD_SIZE) * jnp.bfloat16(0.125)
    keys[...] = rotated(group * HEAD_SIZE)
    key_rows[...] = keys[...].T
    for tile in range(tiles):
        lanes = pl.ds(tile * TILE, TILE)
        starts_here = starts[:, lanes]
        for low in range(tile + 1):
            bias[pl.ds(low * TILE, TILE)] = bias_tile(starts_here, low, tile, low == tile)
        count = (tile + 1) * TILE

        def one_head(head, _, lanes=lanes, count=count):
            rows = pl.ds(pl.multiple_of(head * HEAD_SIZE, HEAD_SIZE), HEAD_SIZE)
            scores = jnp.dot(
                key_rows[:count], queries[rows, lanes], preferred_element_type=jnp.float32
            )
            scores += bias[:count]
            highest = jnp.max(scores, axis=0, keepdims=True)
            weights = jnp.exp(scores - highest)
            total = jnp.sum(weights, axis=0, keepdims=True)
            out = jnp.dot(
                qkv[pl.ds((group + 1) * HEAD_SIZE, HEAD_SIZE), :count],
                weights.astype(jnp.bfloat16),
                preferred_element_type=jnp.float32,
            )
            attended[rows, lanes] = (out / total).astype(jnp.bfloat16)
            lse[head, :, lanes] = jnp.broadcast_to(highest + jnp.log(total), (8, TILE))
            return 0

        lax.fori_loop(0, group, one_head, 0)


def forward_kernel(
    qkv,
    cosine,
    sine,
    starts,
    cotangent,
    heads,
    attended,
    lse,
    queries,
    keys,
    gathered,
    heads_all,
    key_rows,
    bias,
    local,
    send,
    recv,
):
    ids = ring()
    rows = cotangent.shape[0]
    core, mate, _, _ = along_fsdp(ids)
    swap = transposed(ids)
    stays = swap[0] == ids[1][0]
    barrier = pltpu.get_barrier_semaphore()
    peers = along_seq(ids) + [mate]
    for peer in peers:
        pl.semaphore_signal(barrier, inc=1, device_id=peer, device_id_type=MESH)

    @pl.when(jnp.logical_not(stays))
    def _():
        pl.semaphore_signal(barrier, inc=1, device_id=swap, device_id_type=MESH)
        pl.semaphore_wait(barrier, len(peers) + 1)

    @pl.when(stays)
    def _():
        pl.semaphore_wait(barrier, len(peers))

    last = send.shape[0] - 1

    def exchange():
        return pltpu.make_async_remote_copy(
            src_ref=heads,
            dst_ref=heads_all.at[core],
            send_sem=send.at[last],
            recv_sem=recv.at[last],
            device_id=swap,
            device_id_type=MESH,
        )

    def keep():
        return pltpu.make_async_copy(heads, heads_all.at[core], local.at[1])

    @pl.when(jnp.logical_not(stays))
    def _():
        exchange().start()

    @pl.when(stays)
    def _():
        keep().start()

    kept = pltpu.make_async_copy(cotangent, gathered.at[ids[1][0]], local.at[0])
    kept.start()
    copies = Copies(send, recv)

    def meanwhile():
        attend_tiles(qkv, cosine, sine, starts, attended, lse, queries, keys, key_rows, bias)

        @pl.when(jnp.logical_not(stays))
        def _():
            exchange().wait()

        @pl.when(stays)
        def _():
            keep().wait()

        passed.append(copies.start(heads_all.at[core], heads_all.at[core], mate))

    passed = []
    gather_blocks(ids, copies, [(cotangent, gathered, by_rows(rows, CHUNKS))], CHUNKS, meanwhile)
    passed[0].wait_recv()
    copies.finish()
    kept.wait()


def attend(qkv, cosine, sine, starts, cotangent, heads, group, number):
    length = qkv.shape[1]
    rows, width = cotangent.shape
    ranks = lax.axis_size("seq")
    return pl.pallas_call(
        forward_kernel,
        out_shape=[
            jax.ShapeDtypeStruct((group * HEAD_SIZE, length), jnp.bfloat16),
            jax.ShapeDtypeStruct((group, 8, length), jnp.float32),
            jax.ShapeDtypeStruct((group * HEAD_SIZE, length), jnp.bfloat16),
            jax.ShapeDtypeStruct((HEAD_SIZE, length), jnp.bfloat16),
            jax.ShapeDtypeStruct((ranks, rows, width), jnp.bfloat16),
            jax.ShapeDtypeStruct((2, *heads.shape), jnp.bfloat16),
        ],
        in_specs=[VMEM] * 4 + [ANYWHERE] * 2,
        out_specs=[VMEM] * 4 + [ANYWHERE] * 2,
        scratch_shapes=[
            pltpu.VMEM((length, HEAD_SIZE), jnp.bfloat16),
            pltpu.VMEM((length, TILE), jnp.float32),
            pltpu.SemaphoreType.DMA((2,)),
        ]
        + semaphores(gather_copies(CHUNKS) + 2),
        compiler_params=params(number, 40),
        cost_estimate=pl.CostEstimate(
            flops=4 * group * length * length * HEAD_SIZE,
            bytes_accessed=ranks * rows * width * 32,
            transcendentals=group * length * length,
        ),
        name="attend",
    )(qkv, cosine, sine, starts, cotangent, heads)


def back_tiles(
    qkv,
    queries,
    keys,
    attended,
    lse,
    grads,
    cosine,
    sine,
    starts,
    out,
    key_rows,
    value_rows,
    query_rows,
    grad_rows,
    row_dots,
    key_grad,
    value_grad,
    query_grad,
    bias,
):
    group = queries.shape[0] // HEAD_SIZE
    half = HEAD_SIZE // 2
    tiles = qkv.shape[1] // TILE
    key_rows[...] = keys[...].T
    value_rows[...] = qkv[pl.ds((group + 1) * HEAD_SIZE, HEAD_SIZE)].T
    for head in range(group):
        rows = pl.ds(head * HEAD_SIZE, HEAD_SIZE)
        query_rows[head] = queries[rows].T
        grad_rows[head] = grads[rows].T
        row_dots[head] = jnp.broadcast_to(
            jnp.sum(
                grads[rows].astype(jnp.float32) * attended[rows].astype(jnp.float32),
                axis=0,
                keepdims=True,
            ),
            row_dots.shape[1:],
        )
    key_grad[...] = jnp.zeros_like(key_grad)
    value_grad[...] = jnp.zeros_like(value_grad)
    for tile in range(tiles):
        lanes = pl.ds(tile * TILE, TILE)
        starts_here = starts[:, lanes]
        for low in range(tile + 1):
            bias[low] = bias_tile(starts_here, low, tile, low == tile)

        def one_head(head, _, lanes=lanes, tile=tile):
            rows = pl.ds(pl.multiple_of(head * HEAD_SIZE, HEAD_SIZE), HEAD_SIZE)
            query, grad = queries[rows, lanes], grads[rows, lanes]
            query_row, grad_row = query_rows[head, lanes], grad_rows[head, lanes]
            lse_row = lse[head, 0:1, lanes]
            dot_row = row_dots[head, 0:1, lanes]
            total = jnp.zeros((HEAD_SIZE, TILE), jnp.float32)
            for low in range(tile + 1):
                part = pl.ds(low * TILE, TILE)
                scores = jnp.dot(key_rows[part], query, preferred_element_type=jnp.float32)
                probs = jnp.exp(scores + bias[low] - lse_row)
                grad_probs = jnp.dot(value_rows[part], grad, preferred_element_type=jnp.float32)
                grad_scores = (probs * (grad_probs - dot_row)).astype(jnp.bfloat16)
                value_grad[part] += jnp.dot(
                    probs.astype(jnp.bfloat16), grad_row, preferred_element_type=jnp.float32
                )
                key_grad[part] += jnp.dot(
                    grad_scores, query_row, preferred_element_type=jnp.float32
                )
                total += jnp.dot(keys[:, part], grad_scores, preferred_element_type=jnp.float32)
            query_grad[rows, lanes] = total * 0.125
            return 0

        lax.fori_loop(0, group, one_head, 0)
    cos, sin = cosine[...], sine[...]
    for head in range(group):
        first = head * HEAD_SIZE
        out[pl.ds(first, HEAD_SIZE)] = rotate_rows(
            query_grad[pl.ds(first, half)], query_grad[pl.ds(first + half, half)], cos, -sin
        ).astype(jnp.bfloat16)
    turned = key_grad[...].T
    out[pl.ds(group * HEAD_SIZE, HEAD_SIZE)] = rotate_rows(
        turned[:half], turned[half:], cos, -sin
    ).astype(jnp.bfloat16)
    out[pl.ds((group + 1) * HEAD_SIZE, HEAD_SIZE)] = value_grad[...].T.astype(jnp.bfloat16)


def backward_kernel(*refs):
    ins, (part_of, middle), (out, layer_out) = refs[:9], refs[9:11], refs[11:13]
    scratch, (send, recv), bufs = refs[13:22], refs[22:24], refs[24:]
    ids = ring()
    greet(along_seq(ids))
    copies = Copies(send, recv)

    def meanwhile():
        back_tiles(*ins, out, *scratch)

    def done(rows_of, total):
        layer_out[rows_of] = (middle[rows_of] + total).astype(jnp.bfloat16)

    reduce_blocks(ids, copies, part_of, bufs, middle.shape[0], CHUNKS, done, meanwhile)
    copies.finish()


def attend_back(
    qkv, queries, keys, attended, lse, grads, cosine, sine, starts, partial, middle, number
):
    length = qkv.shape[1]
    group = queries.shape[0] // HEAD_SIZE
    tiles = length // TILE
    rows, width = middle.shape
    ranks = lax.axis_size("seq")
    return pl.pallas_call(
        backward_kernel,
        out_shape=[
            jax.ShapeDtypeStruct(qkv.shape, jnp.bfloat16),
            jax.ShapeDtypeStruct((rows, width), jnp.bfloat16),
        ],
        in_specs=[VMEM] * 11,
        out_specs=[VMEM] * 2,
        scratch_shapes=[
            pltpu.VMEM((length, HEAD_SIZE), jnp.bfloat16),
            pltpu.VMEM((length, HEAD_SIZE), jnp.bfloat16),
            pltpu.VMEM((group, length, HEAD_SIZE), jnp.bfloat16),
            pltpu.VMEM((group, length, HEAD_SIZE), jnp.bfloat16),
            pltpu.VMEM((group, 8, length), jnp.float32),
            pltpu.VMEM((length, HEAD_SIZE), jnp.float32),
            pltpu.VMEM((length, HEAD_SIZE), jnp.float32),
            pltpu.VMEM((group * HEAD_SIZE, length), jnp.float32),
            pltpu.VMEM((tiles, TILE, TILE), jnp.float32),
        ]
        + semaphores(reduce_copies(CHUNKS))
        + reduce_scratch(rows, width),
        compiler_params=params(number, 48),
        cost_estimate=pl.CostEstimate(
            flops=10 * group * length * length * HEAD_SIZE,
            bytes_accessed=ranks * rows * width * 32,
            transcendentals=group * length * length,
        ),
        name="attend_back",
    )(
        qkv,
        queries,
        keys,
        attended,
        lse,
        grads,
        cosine,
        sine,
        starts,
        partial.reshape(ranks, rows, width),
        middle,
    )


def contract_rows(left, right):
    return jnp.einsum("ta,tb->ab", left, right, preferred_element_type=jnp.float32)


def contract_cols(left, right):
    return jnp.einsum("ta,ba->tb", left, right, preferred_element_type=jnp.float32)


def matmul(left, right):
    return jnp.dot(left, right, preferred_element_type=jnp.float32)


def shards(
    tokens,
    segment_ids,
    query_weight,
    key_matrix,
    value_matrix,
    output_weight,
    gate_weight,
    up_weight,
    down_weight,
    attention_gain,
    feed_gain,
    cotangent,
):
    rank = lax.axis_index("seq")
    owner = lax.axis_index("fsdp")
    ranks = lax.axis_size("seq")
    owners = lax.axis_size("fsdp")
    rows, width = query_weight.shape
    kv_cols = key_matrix.shape[1] // ranks
    q_cols = width // ranks
    group = q_cols // kv_cols
    ff = gate_weight.shape[1]
    ff_chunk = ff // owners // ranks
    segment_row = segment_ids[0]
    length = segment_row.shape[0]

    qkv_in, gate_up_in = pick_columns(
        query_weight, key_matrix, value_matrix, gate_weight, up_weight, attention_gain, feed_gain
    )
    qkv_got = lax.all_gather(qkv_in, "fsdp", axis=0)
    qkv_all = qkv_got[:, :rows].reshape(owners * rows, -1)
    gain_one = qkv_got[:, rows, :rows].reshape(1, -1).astype(jnp.float32)
    gain_two = qkv_got[:, rows + 1, :rows].reshape(1, -1).astype(jnp.float32)
    gate_up_all = lax.all_gather(gate_up_in, "fsdp", axis=0, tiled=True)
    ff_local = owners * ff_chunk
    down_all = lax.all_gather(
        lax.dynamic_slice_in_dim(down_weight, rank * ff_chunk, ff_chunk, 0),
        "fsdp",
        axis=0,
        tiled=True,
    )

    starts = (jnp.arange(length, dtype=jnp.int32) - positions_of(segment_row))[None]
    cosine, sine = (table.T for table in angles_of(segment_row, HEAD_SIZE))
    whole = gather_tokens(tokens[0], 0).reshape(length, width).astype(jnp.float32)
    hidden_one = (whole * lax.rsqrt(mean_square(whole) + EPS) * gain_one).astype(jnp.bfloat16)
    qkv = jnp.einsum("tm,mc->ct", hidden_one, qkv_all, preferred_element_type=jnp.float32)
    qkv = qkv.astype(jnp.bfloat16)
    attended, lse, queries, keys, grad_out, output_all = attend(
        qkv, cosine, sine, starts, cotangent[0], output_weight, group, 1
    )
    grad_out = grad_out.reshape(length, width)
    output_all = output_all.reshape(q_cols, width)
    middle, hidden_two = add_branch(
        contract_rows(attended, output_all).astype(jnp.bfloat16), tokens[0], gain_two, 2
    )
    hidden_two = hidden_two.reshape(length, width)

    gate = matmul(hidden_two, gate_up_all[:, :ff_local])
    up_proj = matmul(hidden_two, gate_up_all[:, ff_local:])
    sig_gate = jax.nn.sigmoid(gate)
    silu_gate = gate * sig_gate
    act = (silu_gate * up_proj).astype(jnp.bfloat16)
    grad_act = contract_cols(grad_out, down_all)
    grad_gate = (grad_act * up_proj * (sig_gate * (1.0 + gate * (1.0 - sig_gate)))).astype(
        jnp.bfloat16
    )
    grad_up = (grad_act * silu_gate).astype(jnp.bfloat16)
    gate_up_grads = jnp.concatenate([grad_gate, grad_up], axis=1)
    down_grad = contract_rows(act, grad_out).astype(jnp.bfloat16)
    down_share = lax.psum_scatter(down_grad, "fsdp", scatter_dimension=0, tiled=True)
    gate_up_grad = contract_rows(hidden_two, gate_up_grads).astype(jnp.bfloat16)
    gate_up_share = lax.psum_scatter(gate_up_grad, "fsdp", scatter_dimension=0, tiled=True)
    layer_partial = matmul(act, down_all).astype(jnp.bfloat16)
    grad_middle, grad_gain_two, grad_branch = back_to_middle(
        contract_cols(gate_up_grads, gate_up_all).astype(jnp.bfloat16),
        middle,
        gain_two,
        cotangent[0],
        3,
    )
    grad_branch = grad_branch.reshape(length, width)

    grad_attended = jnp.einsum(
        "tm,fm->ft", grad_branch, output_all, preferred_element_type=jnp.float32
    ).astype(jnp.bfloat16)
    qkv_grads, layer_out = attend_back(
        qkv,
        queries,
        keys,
        attended,
        lse,
        grad_attended,
        cosine,
        sine,
        starts,
        layer_partial,
        middle,
        4,
    )
    heads_grad = matmul(attended, grad_branch).astype(jnp.bfloat16)
    qkv_grad = jnp.einsum(
        "tm,ct->mc", hidden_one, qkv_grads, preferred_element_type=jnp.float32
    ).astype(jnp.bfloat16)
    grad_inputs, grad_gain_one, qkv_share, heads_share = back_to_tokens(
        jnp.einsum("ct,mc->tm", qkv_grads, qkv_all, preferred_element_type=jnp.float32).astype(
            jnp.bfloat16
        ),
        tokens[0],
        gain_one,
        grad_middle,
        qkv_grad,
        heads_grad,
        5,
    )
    *gathered, gains = finish_grads(
        gate_up_share, down_share, qkv_share, heads_share, grad_gain_one, grad_gain_two, 6
    )
    gate_grad, up_grad, down_total, query_grad, key_grad, value_grad, heads_total = place_grads(
        *gathered
    )
    return (
        layer_out[None],
        grad_inputs[None],
        query_grad,
        key_grad,
        value_grad,
        heads_total,
        gate_grad,
        up_grad,
        down_total,
        gains[0],
        gains[1],
    )


def solution(mesh):
    placed = (
        P("fsdp", "seq", None),
        P("fsdp", None),
        P("fsdp", None),
        P("fsdp", None),
        P("fsdp", None),
        P("fsdp", None),
        P("fsdp", None),
        P("fsdp", None),
        P("fsdp", None),
        P("fsdp"),
        P("fsdp"),
        P("fsdp", "seq", None),
    )
    return jax.shard_map(
        shards,
        mesh=mesh,
        in_specs=placed,
        out_specs=(
            P("fsdp", "seq", None),
            P("fsdp", "seq", None),
            P("fsdp", None),
            P("fsdp", None),
            P("fsdp", None),
            P("fsdp", None),
            P("fsdp", None),
            P("fsdp", None),
            P("fsdp", None),
            P("fsdp"),
            P("fsdp"),
        ),
        check_vma=False,
    )
```

```python
import math

import jax
import jax.numpy as jnp
from jax import lax
from jax.experimental import pallas as pl
from jax.experimental.pallas import tpu as pltpu
from jax.sharding import PartitionSpec as P

HEAD_SIZE = 64
EPS = 1e-05
ROPE_BASE = 500000.0
NEG = -1e30


def rope_freqs(head_dim):
    half_dim = head_dim // 2
    table = []
    for index in range(half_dim):
        inverse = 1.0 / ROPE_BASE ** (index * 2.0 / head_dim)
        wavelen = 2.0 * math.pi / inverse
        blend = (8192.0 / wavelen - 1.0) / 3.0
        mixed = (1.0 - blend) * inverse / 32.0 + blend * inverse
        entry = inverse if wavelen < 2048.0 else inverse / 32.0 if wavelen > 8192.0 else mixed
        table.append(entry)
    return jnp.asarray(table, dtype=jnp.float32)


def positions_of(segment_row):
    indices = jnp.arange(segment_row.shape[0], dtype=jnp.int32)
    begins = jnp.concatenate(
        [jnp.ones((1,), dtype=jnp.int32), (segment_row[1:] != segment_row[:-1]).astype(jnp.int32)]
    )
    starts_at = lax.cummax(jnp.where(begins > 0, indices, 0), axis=0)
    return indices - starts_at


def angles_of(segment_row, head_dim):
    positions = positions_of(segment_row)
    phase = positions.astype(jnp.float32)[:, None] * rope_freqs(head_dim)[None, :]
    return (jnp.cos(phase), jnp.sin(phase))


MESH = pl.DeviceIdType.MESH
CHUNKS = 4
TILE = 256


class Ring:
    def __init__(self, place, count, index_of, device_of):
        side = count // 2
        row, col = lax.div(place, side), lax.rem(place, side)

        def at(which, step):
            return index_of(which * side + lax.rem(col + step, side))

        self.near = [at(row, step) for step in range(side)]
        self.far = [at(1 - row, step) for step in range(side)]
        self.right = device_of(self.near[1])
        self.left = device_of(self.near[3])
        self.partner = device_of(self.far[0])
        self.peers = [self.right, self.left, self.partner]


def seq_ring():
    rank, owner = lax.axis_index("seq"), lax.axis_index("fsdp")
    return Ring(rank, lax.axis_size("seq"), lambda place: place, lambda index: (index, owner))


def fsdp_ring():
    rank, owner = lax.axis_index("seq"), lax.axis_index("fsdp")
    core = lax.rem(owner, 2)
    ring = Ring(
        lax.div(owner, 2),
        lax.axis_size("fsdp") // 2,
        lambda place: 2 * place + core,
        lambda index: (rank, index),
    )
    return ring, core, (rank, owner + 1 - 2 * core)


def greet(peers):
    barrier = pltpu.get_barrier_semaphore()
    for peer in peers:
        pl.semaphore_signal(barrier, inc=1, device_id=peer, device_id_type=MESH)
    pl.semaphore_wait(barrier, len(peers))


def greet_also(peers, other, apart):
    barrier = pltpu.get_barrier_semaphore()
    for peer in peers:
        pl.semaphore_signal(barrier, inc=1, device_id=peer, device_id_type=MESH)

    @pl.when(apart)
    def _():
        pl.semaphore_signal(barrier, inc=1, device_id=other, device_id_type=MESH)
        pl.semaphore_wait(barrier, len(peers) + 1)

    @pl.when(jnp.logical_not(apart))
    def _():
        pl.semaphore_wait(barrier, len(peers))


def transposed():
    rank, owner = lax.axis_index("seq"), lax.axis_index("fsdp")
    other = (lax.div(owner, 2), 2 * rank + lax.rem(owner, 2))
    return other, other[0] != rank


def along_fsdp():
    rank, owner = lax.axis_index("seq"), lax.axis_index("fsdp")
    core, place = lax.rem(owner, 2), lax.div(owner, 2)
    count = lax.axis_size("fsdp") // 2
    places = [lax.rem(place + step, count) for step in range(count)]
    mate = (rank, owner + 1 - 2 * core)
    return core, mate, places, [(rank, 2 * other + core) for other in places]


def in_turn(*walks):
    left = list(walks)
    while left:
        left = [walk for walk in left if next(walk, walk) is not walk]


class Copies:
    def __init__(self, send, recv):
        self.send, self.recv = send, recv
        self.made = []

    def start(self, source, target, peer):
        number = len(self.made)
        copy = pltpu.make_async_remote_copy(
            src_ref=source,
            dst_ref=target,
            send_sem=self.send.at[number],
            recv_sem=self.recv.at[number],
            device_id=peer,
            device_id_type=MESH,
        )
        copy.start()
        self.made.append(copy)
        return copy

    def finish(self):
        for copy in self.made:
            copy.wait_send()


def by_rows(rows, chunks):
    size = rows // chunks
    return lambda ref, index: ref.at[pl.ds(index * size, size)]


def by_columns(columns, chunks):
    size = columns // chunks
    return lambda ref, index: ref.at[:, pl.ds(index * size, size)]


def gather_walk(ring, copies, own, out, cut, chunks, deep=False, mate=None):
    me, right, opposite, left = ring.near
    partner, far_right, _, far_left = ring.far
    half = chunks // 2
    passed = []

    def share(place, index):
        if mate is not None:
            block = cut(out.at[place], index)
            passed.append(copies.start(block, block, mate))

    to_right, to_left, to_far, on = {}, {}, {}, {}
    for step in range(chunks):
        back = chunks - 1 - step
        to_far[step] = copies.start(cut(own, step), cut(out.at[me], step), ring.partner)
        to_right[step] = copies.start(cut(own, step), cut(out.at[me], step), ring.right)
        to_left[back] = copies.start(cut(own, back), cut(out.at[me], back), ring.left)
        if mate is not None:
            passed.append(copies.start(cut(own, step), cut(out.at[me], step), mate))
    yield
    for step in range(half):
        back = chunks - 1 - step
        to_right[step].wait_recv()
        block = cut(out.at[left], step)
        on[step] = copies.start(block, block, ring.right)
        share(left, step)
        to_left[back].wait_recv()
        block = cut(out.at[right], back)
        on[back] = copies.start(block, block, ring.left)
        share(right, back)
        yield
    far_on, rest = {}, []
    for step in range(chunks):
        to_far[step].wait_recv()
        block = cut(out.at[partner], step)
        far_on[0, step] = copies.start(block, block, ring.right)
        far_on[1, step] = copies.start(block, block, ring.left)
        share(partner, step)
        yield
    if deep:
        for step in range(half):
            back = chunks - 1 - step
            far_on[0, step].wait_recv()
            block = cut(out.at[far_left], step)
            rest.append((step, copies.start(block, block, ring.right)))
            share(far_left, step)
            far_on[1, back].wait_recv()
            block = cut(out.at[far_right], back)
            rest.append((back, copies.start(block, block, ring.left)))
            share(far_right, back)
            yield
    for step in range(half):
        for index in (step, chunks - 1 - step):
            on[index].wait_recv()
            if not deep:
                block = cut(out.at[opposite], index)
                rest.append((index, copies.start(block, block, ring.partner)))
            share(opposite, index)
        yield
    for step in range(half):
        back = chunks - 1 - step
        to_right[back].wait_recv()
        share(left, back)
        to_left[step].wait_recv()
        share(right, step)
        if deep:
            far_on[0, back].wait_recv()
            share(far_left, back)
            far_on[1, step].wait_recv()
            share(far_right, step)
        yield
    if not deep:
        for copy in far_on.values():
            copy.wait_recv()
    for index, copy in rest:
        copy.wait_recv()
        share(ring.far[2], index)
    yield
    for copy in passed:
        copy.wait_recv()


def gather_copies(chunks, mate=False):
    return 7 * chunks + (8 * chunks if mate else 0)


def reduce_walk(ring, copies, part_of, bufs, rows, chunks, done):
    me, right, opposite, left = ring.near
    partner, far_right, far_opposite, far_left = ring.far
    from_left, from_right, from_far, mid, end_left, end_right, end_far = bufs
    size = rows // chunks
    half = chunks // 2

    def part(index):
        return pl.ds(index * size, size)

    def wide(ref):
        return ref.astype(jnp.float32)

    order = [x for step in range(half) for x in (step, chunks - 1 - step)]
    one_right, one_left, one_far = {}, {}, {}
    for index in order:
        rows_of = part(index)
        one_far[index] = copies.start(
            part_of.at[far_opposite, rows_of], from_far.at[rows_of], ring.partner
        )
        one_right[index] = copies.start(
            part_of.at[far_right, rows_of], from_left.at[rows_of], ring.right
        )
        one_left[index] = copies.start(
            part_of.at[far_left, rows_of], from_right.at[rows_of], ring.left
        )
    last_right, last_left, last_far = {}, {}, {}
    for index in range(half):
        rows_of = part(index)
        last_right[index] = copies.start(
            part_of.at[right, rows_of], end_left.at[rows_of], ring.right
        )
        rows_of = part(chunks - 1 - index)
        last_left[chunks - 1 - index] = copies.start(
            part_of.at[left, rows_of], end_right.at[rows_of], ring.left
        )
    yield
    two = {}
    for index in order:
        rows_of = part(index)
        one_far[index].wait_recv()
        from_far[rows_of] = (wide(from_far[rows_of]) + wide(part_of[opposite, rows_of])).astype(
            jnp.bfloat16
        )
        two[index] = copies.start(
            from_far.at[rows_of], mid.at[rows_of], ring.left if index < half else ring.right
        )
        yield
    for index in order:
        rows_of = part(index)
        one_right[index].wait_recv()
        one_left[index].wait_recv()
        from_left[rows_of] = (
            wide(from_left[rows_of]) + wide(from_right[rows_of]) + wide(part_of[partner, rows_of])
        ).astype(jnp.bfloat16)
        last_far[index] = copies.start(
            from_left.at[rows_of], end_far.at[rows_of], ring.partner
        )
        yield
    for index in order:
        rows_of = part(index)
        two[index].wait_recv()
        if index < half:
            mid[rows_of] = (wide(mid[rows_of]) + wide(part_of[left, rows_of])).astype(jnp.bfloat16)
            last_left[index] = copies.start(mid.at[rows_of], end_right.at[rows_of], ring.left)
        else:
            mid[rows_of] = (wide(mid[rows_of]) + wide(part_of[right, rows_of])).astype(
                jnp.bfloat16
            )
            last_right[index] = copies.start(mid.at[rows_of], end_left.at[rows_of], ring.right)
        yield
    for index in order:
        rows_of = part(index)
        last_far[index].wait_recv()
        last_left[index].wait_recv()
        last_right[index].wait_recv()
        done(
            rows_of,
            wide(part_of[me, rows_of])
            + wide(end_left[rows_of])
            + wide(end_right[rows_of])
            + wide(end_far[rows_of]),
        )
        yield


def reduce_copies(chunks):
    return 3 * chunks + 2 * chunks + chunks + chunks


def owners_walk(ring, core, mate, copies, grads, own, other, sems, bufs, rows, done):
    mids, from_lefts, from_rights, from_far = bufs[:2], bufs[2:4], bufs[4:6], bufs[6]
    half = rows // 2
    low, high = pl.ds(0, half), pl.ds(half, half)
    near, far = ([lax.div(index, 2) for index in row] for row in (ring.near, ring.far))
    order = [far[2], near[2], far[1], far[3], near[1], near[3], far[0], near[0]]
    got, kept = [], []
    for number, place in enumerate(order):
        got.append(copies.start(grads.at[place, 1 - core], other.at[place], mate))
        copy = pltpu.make_async_copy(grads.at[place, core], own.at[place], sems.at[number])
        copy.start()
        kept.append(copy)
    yield

    def wide(ref):
        return ref.astype(jnp.float32)

    def add(*numbers):
        for number in numbers:
            got[number].wait_recv()
            kept[number].wait()
            place = order[number]
            own[place] = (wide(own[place]) + wide(other[place])).astype(jnp.bfloat16)

    add(0, 1)
    on = []
    for which, row in enumerate((far, near)):
        block = own.at[row[2]]
        on.append(copies.start(block.at[low], mids[which].at[low], ring.left))
        on.append(copies.start(block.at[high], mids[which].at[high], ring.right))
    yield
    ends = []
    for which, row in enumerate((far, near)):
        add(2 + 2 * which, 3 + 2 * which)
        ends.append(
            copies.start(own.at[row[1], low], from_lefts[which].at[low], ring.right)
        )
        ends.append(
            copies.start(own.at[row[3], high], from_rights[which].at[high], ring.left)
        )
        yield
    add(6, 7)
    yield
    for which, row in enumerate((far, near)):
        mid = mids[which]
        on[2 * which].wait_recv()
        mid[low] = (wide(mid[low]) + wide(own[row[3], low])).astype(jnp.bfloat16)
        ends.append(copies.start(mid.at[low], from_rights[which].at[low], ring.left))
        yield
        on[2 * which + 1].wait_recv()
        mid[high] = (wide(mid[high]) + wide(own[row[1], high])).astype(jnp.bfloat16)
        ends.append(copies.start(mid.at[high], from_lefts[which].at[high], ring.right))
        yield
    last = []
    for rows_of, numbers in ((low, (0, 4, 1, 5)), (high, (0, 4, 1, 5))):
        if not last:
            for number in numbers:
                ends[number].wait_recv()
        total = (
            wide(from_lefts[0][rows_of])
            + wide(from_rights[0][rows_of])
            + wide(own[far[0], rows_of])
        )
        from_lefts[0][rows_of] = total.astype(jnp.bfloat16)
        last.append(
            copies.start(from_lefts[0].at[rows_of], from_far.at[rows_of], ring.partner)
        )
    yield
    for number in (2, 6, 3, 7):
        ends[number].wait_recv()
    yield
    for rows_of, copy in zip((low, high), last):
        copy.wait_recv()
        done(
            rows_of,
            wide(from_lefts[1][rows_of])
            + wide(from_rights[1][rows_of])
            + wide(own[near[0], rows_of])
            + wide(from_far[rows_of]),
        )
        yield


OWNERS_COPIES = 8 + 4 + 4 + 4 + 2


def owners_scratch(places, rows, width):
    return (
        [pltpu.VMEM((places, rows, width), jnp.bfloat16) for _ in range(2)]
        + [pltpu.SemaphoreType.DMA((places,))]
        + [pltpu.VMEM((rows, width), jnp.bfloat16) for _ in range(7)]
    )


def reduce_scratch(rows, width):
    return [pltpu.VMEM((rows, width), jnp.bfloat16) for _ in range(7)]


def semaphores(count):
    return [pltpu.SemaphoreType.DMA((count,)), pltpu.SemaphoreType.DMA((count,))]


def params(number, limit):
    return pltpu.CompilerParams(
        collective_id=number, has_side_effects=True, vmem_limit_bytes=limit * 2**20
    )


VMEM = pl.BlockSpec(memory_space=pltpu.VMEM)
ANYWHERE = pl.BlockSpec(memory_space=pl.ANY)


def gather_first(tokens, qkv, gate_up, number):
    blocks = (tokens, qkv, gate_up)
    ranks, owners = lax.axis_size("seq"), lax.axis_size("fsdp")

    def kernel(tokens, qkv, gate_up, tokens_all, qkv_all, gate_up_all, local, send, recv):
        ring = seq_ring()
        weights_ring, _, mate = fsdp_ring()
        greet(ring.peers + weights_ring.peers + [mate])
        copies = Copies(send, recv)
        kept = [
            pltpu.make_async_copy(own, out.at[at.near[0]], local.at[index])
            for index, (own, out, at) in enumerate(
                (
                    (tokens, tokens_all, ring),
                    (qkv, qkv_all, weights_ring),
                    (gate_up, gate_up_all, weights_ring),
                )
            )
        ]
        for copy in kept:
            copy.start()
        in_turn(
            gather_walk(
                weights_ring, copies, qkv, qkv_all, by_rows(qkv.shape[0], 2), 2, True, mate
            ),
            gather_walk(
                ring, copies, tokens, tokens_all, by_rows(tokens.shape[0], CHUNKS), CHUNKS
            ),
            gather_walk(
                weights_ring,
                copies,
                gate_up,
                gate_up_all,
                by_rows(gate_up.shape[0], CHUNKS),
                CHUNKS,
                True,
                mate,
            ),
        )
        copies.finish()
        for copy in kept:
            copy.wait()

    count = gather_copies(CHUNKS) + gather_copies(CHUNKS, True) + gather_copies(2, True)
    return pl.pallas_call(
        kernel,
        out_shape=[
            jax.ShapeDtypeStruct((size, *block.shape), jnp.bfloat16)
            for size, block in zip((ranks, owners, owners), blocks)
        ],
        in_specs=[ANYWHERE] * 3,
        out_specs=[ANYWHERE] * 3,
        scratch_shapes=[pltpu.SemaphoreType.DMA((3,))] + semaphores(count),
        compiler_params=params(number, 32),
        name="gather_first",
    )(*blocks)


def mean_square(values):
    return jnp.mean(values * values, axis=-1, keepdims=True)


def branch_kernel(part_of, tokens, gain, middle, hidden, block, local, send, recv, *bufs):
    ring = seq_ring()
    rows = tokens.shape[0]
    greet(ring.peers)
    copies = Copies(send, recv)

    def done(rows_of, total):
        values = tokens[rows_of].astype(jnp.float32) + total
        middle[rows_of] = values
        factor = lax.rsqrt(mean_square(values) + EPS)
        block[rows_of] = (values * factor * gain[...]).astype(jnp.bfloat16)

    in_turn(reduce_walk(ring, copies, part_of, bufs, rows, CHUNKS, done))
    kept = pltpu.make_async_copy(block, hidden.at[ring.near[0]], local)
    kept.start()
    in_turn(gather_walk(ring, copies, block, hidden, by_rows(rows, CHUNKS), CHUNKS))
    copies.finish()
    kept.wait()


def add_branch(partial, tokens, gain, number):
    rows, width = tokens.shape
    ranks = lax.axis_size("seq")
    count = reduce_copies(CHUNKS) + gather_copies(CHUNKS)
    return pl.pallas_call(
        branch_kernel,
        out_shape=[
            jax.ShapeDtypeStruct((rows, width), jnp.float32),
            jax.ShapeDtypeStruct((ranks, rows, width), jnp.bfloat16),
        ],
        in_specs=[VMEM] * 3,
        out_specs=[VMEM, ANYWHERE],
        scratch_shapes=[pltpu.VMEM((rows, width), jnp.bfloat16), pltpu.SemaphoreType.DMA]
        + semaphores(count)
        + reduce_scratch(rows, width),
        compiler_params=params(number, 32),
        name="add_branch",
    )(partial.reshape(ranks, rows, width), tokens, gain)


def norm_back_rows(grad, gain, values):
    factor = lax.rsqrt(mean_square(values) + EPS)
    normed = values * factor
    weighted = grad * gain
    back = factor * (weighted - normed * jnp.mean(weighted * normed, axis=-1, keepdims=True))
    return back, grad * normed


def middle_kernel(
    part_of,
    middle,
    gain,
    cotangent,
    grads,
    grad_middle,
    grad_gain,
    branch,
    grads_share,
    block,
    local,
    send,
    recv,
    own,
    other,
    sems,
    *bufs,
):
    ring = seq_ring()
    weights_ring, core, mate = fsdp_ring()
    rows = middle.shape[0]
    greet(ring.peers + weights_ring.peers + [mate])
    copies = Copies(send, recv)
    grad_gain[...] = jnp.zeros_like(grad_gain)

    def done(rows_of, total):
        back, terms = norm_back_rows(total, gain[...], middle[rows_of])
        grad_gain[...] += jnp.sum(terms, axis=0, keepdims=True)
        values = cotangent[rows_of].astype(jnp.float32) + back
        grad_middle[rows_of] = values
        block[rows_of] = values.astype(jnp.bfloat16)

    def owned(rows_of, total):
        grads_share[rows_of] = total.astype(jnp.bfloat16)

    kept = pltpu.make_async_copy(block, branch.at[ring.near[0]], local)

    def walk():
        yield from reduce_walk(ring, copies, part_of, bufs[7:], rows, CHUNKS, done)
        kept.start()
        yield from gather_walk(ring, copies, block, branch, by_rows(rows, CHUNKS), CHUNKS)

    in_turn(
        owners_walk(
            weights_ring,
            core,
            mate,
            copies,
            grads,
            own,
            other,
            sems,
            bufs[:7],
            grads_share.shape[0],
            owned,
        ),
        walk(),
    )
    copies.finish()
    kept.wait()


def back_to_middle(partial, middle, gain, cotangent, grads, number):
    rows, width = middle.shape
    ranks, owners = lax.axis_size("seq"), lax.axis_size("fsdp")
    places = owners // 2
    grad_rows, grad_cols = grads.shape[0] // owners, grads.shape[1]
    count = reduce_copies(CHUNKS) + gather_copies(CHUNKS) + OWNERS_COPIES
    return pl.pallas_call(
        middle_kernel,
        out_shape=[
            jax.ShapeDtypeStruct((rows, width), jnp.float32),
            jax.ShapeDtypeStruct((1, width), jnp.float32),
            jax.ShapeDtypeStruct((ranks, rows, width), jnp.bfloat16),
            jax.ShapeDtypeStruct((grad_rows, grad_cols), jnp.bfloat16),
        ],
        in_specs=[VMEM] * 4 + [ANYWHERE],
        out_specs=[VMEM, VMEM, ANYWHERE, VMEM],
        scratch_shapes=[pltpu.VMEM((rows, width), jnp.bfloat16), pltpu.SemaphoreType.DMA]
        + semaphores(count)
        + owners_scratch(places, grad_rows, grad_cols)
        + reduce_scratch(rows, width),
        compiler_params=params(number, 48),
        name="back_to_middle",
    )(
        partial.reshape(ranks, rows, width),
        middle,
        gain,
        cotangent,
        grads.reshape(places, 2, grad_rows, grad_cols),
    )


def tokens_kernel(
    part_of,
    tokens,
    gain,
    grad_middle,
    qkv_parts,
    heads_parts,
    out,
    grad_gain,
    qkv_share,
    heads_share,
    qkv_mate,
    heads_mate,
    qkv_got,
    heads_got,
    heads_block,
    heads_here,
    send,
    recv,
    *bufs,
):
    ring = seq_ring()
    rows = tokens.shape[0]
    core, mate, places, others = along_fsdp()
    place = places[0]
    swap, apart = transposed()
    greet_also(ring.peers + [mate] + others[1:], swap, apart)
    copies = Copies(send, recv)
    grad_gain[...] = jnp.zeros_like(grad_gain)
    pair = [
        copies.start(qkv_parts.at[:, 1 - core], qkv_mate, mate),
        copies.start(heads_parts.at[1 - core], heads_mate, mate),
    ]
    pushed = []

    def meanwhile():
        for copy in pair:
            copy.wait_recv()

        def add(index, _):
            qkv_mate[index] = (
                qkv_mate[index].astype(jnp.float32) + qkv_parts[index, core].astype(jnp.float32)
            ).astype(jnp.bfloat16)
            heads_mate[index] = (
                heads_mate[index].astype(jnp.float32)
                + heads_parts[core, index].astype(jnp.float32)
            ).astype(jnp.bfloat16)
            return 0

        lax.fori_loop(0, len(places), add, 0)
        for step in range(1, len(places)):
            pushed.append(
                copies.start(qkv_mate.at[places[step]], qkv_got.at[step], others[step])
            )
            pushed.append(
                copies.start(heads_mate.at[places[step]], heads_got.at[step], others[step])
            )

    def later():
        for copy in pushed:
            copy.wait_recv()
        total = qkv_mate[place].astype(jnp.float32)
        heads_total = heads_mate[place].astype(jnp.float32)
        for step in range(1, len(places)):
            total += qkv_got[step].astype(jnp.float32)
            heads_total += heads_got[step].astype(jnp.float32)
        qkv_share[...] = total.astype(jnp.bfloat16)
        heads_block[...] = heads_total.astype(jnp.bfloat16)

        @pl.when(apart)
        def _():
            copy = pltpu.make_async_remote_copy(
                src_ref=heads_block,
                dst_ref=heads_here,
                send_sem=send.at[send.shape[0] - 1],
                recv_sem=recv.at[recv.shape[0] - 1],
                device_id=swap,
                device_id_type=MESH,
            )
            copy.start()

    def done(rows_of, total):
        back, terms = norm_back_rows(total, gain[...], tokens[rows_of].astype(jnp.float32))
        grad_gain[...] += jnp.sum(terms, axis=0, keepdims=True)
        out[rows_of] = (grad_middle[rows_of] + back).astype(jnp.bfloat16)

    def weights():
        yield
        meanwhile()
        for _ in range(2 * CHUNKS):
            yield
        later()

    in_turn(reduce_walk(ring, copies, part_of, bufs, rows, CHUNKS, done), weights())
    copies.finish()

    @pl.when(jnp.logical_not(apart))
    def _():
        heads_share[...] = heads_block[...]

    @pl.when(apart)
    def _():
        pltpu.make_async_remote_copy(
            src_ref=heads_block,
            dst_ref=heads_here,
            send_sem=send.at[send.shape[0] - 1],
            recv_sem=recv.at[recv.shape[0] - 1],
            device_id=swap,
            device_id_type=MESH,
        ).wait()
        heads_share[...] = heads_here[...]


def back_to_tokens(partial, tokens, gain, grad_middle, qkv_grad, heads_grad, number):
    rows, width = tokens.shape
    ranks, owners = lax.axis_size("seq"), lax.axis_size("fsdp")
    places = owners // 2
    qkv_cols, head_rows = qkv_grad.shape[1], heads_grad.shape[0] // owners
    count = reduce_copies(CHUNKS) + 2 + 2 * (places - 1) + 1
    return pl.pallas_call(
        tokens_kernel,
        out_shape=[
            jax.ShapeDtypeStruct((rows, width), jnp.bfloat16),
            jax.ShapeDtypeStruct((1, width), jnp.float32),
            jax.ShapeDtypeStruct((rows, qkv_cols), jnp.bfloat16),
            jax.ShapeDtypeStruct((head_rows, width), jnp.bfloat16),
        ],
        in_specs=[VMEM] * 6,
        out_specs=[VMEM] * 4,
        scratch_shapes=[
            pltpu.VMEM((places, rows, qkv_cols), jnp.bfloat16),
            pltpu.VMEM((places, head_rows, width), jnp.bfloat16),
            pltpu.VMEM((places, rows, qkv_cols), jnp.bfloat16),
            pltpu.VMEM((places, head_rows, width), jnp.bfloat16),
            pltpu.VMEM((head_rows, width), jnp.bfloat16),
            pltpu.VMEM((head_rows, width), jnp.bfloat16),
        ]
        + semaphores(count)
        + reduce_scratch(rows, width),
        compiler_params=params(number, 40),
        name="back_to_tokens",
    )(
        partial.reshape(ranks, rows, width),
        tokens,
        gain,
        grad_middle,
        qkv_grad.reshape(places, 2, rows, qkv_cols),
        heads_grad.reshape(2, places, head_rows, width),
    )


def finish_kernel(
    gate_up,
    down,
    qkv,
    heads,
    gain_one,
    gain_two,
    gate_up_all,
    down_all,
    qkv_all,
    heads_all,
    gains,
    given,
    from_mate,
    summed,
    from_places,
    for_partner,
    from_partner,
    by_column,
    local,
    send,
    recv,
):
    ring = seq_ring()
    me = ring.near[0]
    side = lax.axis_size("seq") // 2
    column = lax.rem(me, side)
    core, mate, places, others = along_fsdp()
    greet(ring.peers + [mate] + others[1:])
    copies = Copies(send, recv)
    arrays = [
        (gate_up, gate_up_all, by_rows(gate_up.shape[0], CHUNKS)),
        (down, down_all, by_rows(down.shape[0], CHUNKS)),
        (qkv, qkv_all, by_rows(qkv.shape[0], CHUNKS)),
        (heads, heads_all, by_columns(heads.shape[1], CHUNKS)),
    ]
    kept = [
        pltpu.make_async_copy(own, out.at[me], local.at[i]) for i, (own, out, _) in enumerate(arrays)
    ]
    for copy in kept:
        copy.start()

    def sum_gains():
        lanes = given.shape[3]
        for index in range(2 * len(places)):
            cols = pl.ds(index * lanes, lanes)
            given[index // 2, index % 2, 0:1] = gain_one[:, cols]
            given[index // 2, index % 2, 1:2] = gain_two[:, cols]
            given[index // 2, index % 2, 2:8] = jnp.zeros((6, lanes), jnp.float32)
        copy = copies.start(given.at[:, 1 - core], from_mate, mate)
        yield
        copy.wait_recv()
        summed[...] = given[:, core] + from_mate[...]
        pushed = [
            copies.start(summed.at[places[step]], from_places.at[step], others[step])
            for step in range(1, len(places))
        ]
        yield
        for copy in pushed:
            copy.wait_recv()
        total = summed[places[0]]
        for step in range(1, len(places)):
            total += from_places[step]
        for_partner[...] = total
        copy = copies.start(for_partner, from_partner, ring.partner)
        yield
        copy.wait_recv()
        by_column[column] = for_partner[...] + from_partner[...]
        to_right = copies.start(by_column.at[column], by_column.at[column], ring.right)
        to_left = copies.start(by_column.at[column], by_column.at[column], ring.left)
        yield
        to_right.wait_recv()
        to_left.wait_recv()
        after = lax.rem(column + 1, side)
        copy = copies.start(by_column.at[after], by_column.at[after], ring.left)
        yield
        copy.wait_recv()
        gains[...] = (by_column[0] + by_column[1]) + (by_column[2] + by_column[3])

    in_turn(
        *(gather_walk(ring, copies, own, out, cut, CHUNKS) for own, out, cut in arrays), sum_gains()
    )
    copies.finish()
    for copy in kept:
        copy.wait()


def finish_grads(gate_up, down, qkv, heads, gain_one, gain_two, number):
    ranks, owners = lax.axis_size("seq"), lax.axis_size("fsdp")
    blocks = (gate_up, down, qkv, heads)
    places = owners // 2
    lanes = gain_one.shape[1] // owners
    size = sum(block.size for block in blocks)
    count = len(blocks) * gather_copies(CHUNKS) + 1 + (places - 1) + 1 + 3

    def table(*shape):
        return pltpu.VMEM((*shape, 8, lanes), jnp.float32)

    return pl.pallas_call(
        finish_kernel,
        out_shape=[jax.ShapeDtypeStruct((ranks, *block.shape), block.dtype) for block in blocks]
        + [jax.ShapeDtypeStruct((8, lanes), jnp.float32)],
        in_specs=[ANYWHERE] * 4 + [VMEM] * 2,
        out_specs=[ANYWHERE] * 4 + [VMEM],
        scratch_shapes=[
            table(places, 2),
            table(places),
            table(places),
            table(places),
            table(),
            table(),
            table(ranks // 2),
            pltpu.SemaphoreType.DMA((len(blocks),)),
        ]
        + semaphores(count),
        compiler_params=params(number, 32),
        name="finish_grads",
    )(*blocks, gain_one, gain_two)


def merge_lanes(first, second):
    half = first.shape[1] // 2
    low = lax.broadcasted_iota(jnp.int32, first.shape, 1) < half
    return (
        jnp.where(low, first, pltpu.roll(second, half, 1)),
        jnp.where(low, pltpu.roll(first, half, 1), second),
    )


def place_kernel(gate, up, down, query, pair, heads, gate_out, up_out, down_out, query_out, key_out, value_out, heads_out):
    lanes = gate.shape[2]
    blocks = gate.shape[0] // 2
    for part, out in ((gate, gate_out), (up, up_out)):
        for index in range(blocks):
            low, high = merge_lanes(
                part[2 * index].astype(jnp.float32), part[2 * index + 1].astype(jnp.float32)
            )
            out[:, pl.ds(index * lanes, lanes)] = low
            out[:, pl.ds((blocks + index) * lanes, lanes)] = high
    key, value = merge_lanes(pair[0].astype(jnp.float32), pair[1].astype(jnp.float32))
    key_out[...] = key
    value_out[...] = value
    down_out[...] = down[0].astype(jnp.float32)
    query_out[...] = query[0].astype(jnp.float32)
    heads_out[...] = heads[0].astype(jnp.float32)


def place_grads(gate_up, down, qkv, heads):
    ranks, rows, both = gate_up.shape
    lanes = 128
    steps = both // 2 // lanes
    down_rows, width = down.shape[1:]
    head_rows = heads.shape[1]
    query_cols = qkv.shape[2] - lanes
    assert steps == ranks and lanes == 2 * HEAD_SIZE
    real = jnp.float32
    return pl.pallas_call(
        place_kernel,
        grid=(steps,),
        out_shape=[
            jax.ShapeDtypeStruct((rows, ranks * both // 2), real),
            jax.ShapeDtypeStruct((rows, ranks * both // 2), real),
            jax.ShapeDtypeStruct((ranks * down_rows, width), real),
            jax.ShapeDtypeStruct((rows, ranks * query_cols), real),
            jax.ShapeDtypeStruct((rows, ranks * HEAD_SIZE), real),
            jax.ShapeDtypeStruct((rows, ranks * HEAD_SIZE), real),
            jax.ShapeDtypeStruct((ranks * head_rows, width), real),
        ],
        in_specs=[
            pl.BlockSpec((ranks, rows, lanes), lambda i: (0, 0, i)),
            pl.BlockSpec((ranks, rows, lanes), lambda i: (0, 0, steps + i)),
            pl.BlockSpec((1, down_rows, width), lambda i: (i, 0, 0)),
            pl.BlockSpec((1, rows, query_cols), lambda i: (i, 0, 0)),
            pl.BlockSpec((2, rows, lanes), lambda i: (i // 2, 0, query_cols // lanes)),
            pl.BlockSpec((1, head_rows, width), lambda i: (i, 0, 0)),
        ],
        out_specs=[
            pl.BlockSpec((rows, ranks * lanes), lambda i: (0, i)),
            pl.BlockSpec((rows, ranks * lanes), lambda i: (0, i)),
            pl.BlockSpec((down_rows, width), lambda i: (i, 0)),
            pl.BlockSpec((rows, query_cols), lambda i: (0, i)),
            pl.BlockSpec((rows, lanes), lambda i: (0, i // 2)),
            pl.BlockSpec((rows, lanes), lambda i: (0, i // 2)),
            pl.BlockSpec((head_rows, width), lambda i: (i, 0)),
        ],
        compiler_params=pltpu.CompilerParams(vmem_limit_bytes=32 * 2**20),
        name="place_grads",
    )(gate_up, gate_up, down, qkv, qkv, heads)


def pick_kernel(
    query, key, value, gate, up, gain_one, gain_two, qkv_out, gate_up_out, wide, narrow, sems
):
    rank, ranks = lax.axis_index("seq"), lax.axis_size("seq")
    rows = query.shape[0]
    lanes = 128
    owners = wide.shape[1]
    pair = lax.div(rank, 2)
    odd = lax.rem(rank, 2)
    query_cols = query.shape[1] // ranks
    stride = gate.shape[1] // owners
    count = 0
    made = []

    def fetch(source, target):
        nonlocal count
        copy = pltpu.make_async_copy(source, target, sems.at[count])
        copy.start()
        made.append(copy)
        count += 1

    fetch(
        query.at[:, pl.ds(pl.multiple_of(rank * query_cols, lanes), query_cols)],
        qkv_out.at[pl.ds(0, rows), pl.ds(0, query_cols)],
    )
    for index, source in enumerate((key, value)):
        fetch(source.at[:, pl.ds(pl.multiple_of(pair * lanes, lanes), lanes)], narrow.at[index])
    for which, source in enumerate((gate, up)):
        for owner in range(owners):
            first = pl.multiple_of(owner * stride + pair * lanes, lanes)
            fetch(source.at[:, pl.ds(first, lanes)], wide.at[which, owner])
    line = lax.broadcasted_iota(jnp.int32, (16, rows), 0)
    first, second = (gain[...].astype(jnp.float32) for gain in (gain_one, gain_two))
    gains = jnp.where(line == 0, first, jnp.where(line == 1, second, 0.0))
    qkv_out[pl.ds(rows, 32)] = jnp.zeros((32, qkv_out.shape[1]), jnp.bfloat16)
    qkv_out[pl.ds(rows, 16), pl.ds(0, rows)] = gains.astype(jnp.bfloat16)
    for copy in made:
        copy.wait()

    def chosen(first, second):
        low, high = merge_lanes(first.astype(jnp.float32), second.astype(jnp.float32))
        return jnp.where(odd == 0, low, high).astype(jnp.bfloat16)

    qkv_out[pl.ds(0, rows), pl.ds(query_cols, lanes)] = chosen(narrow[0], narrow[1])
    for which in range(2):
        for index in range(owners // 2):
            cols = pl.ds((which * (owners // 2) + index) * lanes, lanes)
            gate_up_out[:, cols] = chosen(wide[which, 2 * index], wide[which, 2 * index + 1])


def pick_columns(query, key, value, gate, up, gain_one, gain_two):
    rows, width = query.shape
    ranks, owners = lax.axis_size("seq"), lax.axis_size("fsdp")
    lanes = 128
    assert gate.shape[1] // owners // ranks == HEAD_SIZE == lanes // 2
    return pl.pallas_call(
        pick_kernel,
        out_shape=[
            jax.ShapeDtypeStruct((rows + 32, width // ranks + lanes), jnp.bfloat16),
            jax.ShapeDtypeStruct((rows, owners * lanes), jnp.bfloat16),
        ],
        in_specs=[ANYWHERE] * 5 + [VMEM] * 2,
        out_specs=[VMEM] * 2,
        scratch_shapes=[
            pltpu.VMEM((2, owners, rows, lanes), jnp.bfloat16),
            pltpu.VMEM((2, rows, lanes), jnp.bfloat16),
            pltpu.SemaphoreType.DMA((2 * owners + 3,)),
        ],
        compiler_params=pltpu.CompilerParams(vmem_limit_bytes=32 * 2**20),
        name="pick_columns",
    )(query, key, value, gate, up, gain_one[None], gain_two[None])


def rotate_rows(first, second, cosine, sine):
    return jnp.concatenate([first * cosine - second * sine, second * cosine + first * sine], axis=0)


def bias_tile(start_row, key_tile, query_tile, diagonal):
    keys = key_tile * TILE + lax.broadcasted_iota(jnp.int32, (TILE, TILE), 0)
    seen = keys >= start_row
    if diagonal:
        queries = query_tile * TILE + lax.broadcasted_iota(jnp.int32, (TILE, TILE), 1)
        seen = seen & (keys <= queries)
    return jnp.where(seen, 0.0, NEG)


def attend_tiles(qkv, cosine, sine, starts, attended, lse, queries, keys, key_rows, bias):
    group = queries.shape[0] // HEAD_SIZE
    half = HEAD_SIZE // 2
    tiles = qkv.shape[1] // TILE
    cos, sin = cosine[...], sine[...]

    def rotated(first):
        return rotate_rows(
            qkv[pl.ds(first, half)].astype(jnp.float32),
            qkv[pl.ds(first + half, half)].astype(jnp.float32),
            cos,
            sin,
        ).astype(jnp.bfloat16)

    for head in range(group):
        queries[pl.ds(head * HEAD_SIZE, HEAD_SIZE)] = rotated(head * HEAD_SIZE) * jnp.bfloat16(0.125)
    keys[...] = rotated(group * HEAD_SIZE)
    key_rows[...] = keys[...].T
    for tile in range(tiles):
        lanes = pl.ds(tile * TILE, TILE)
        starts_here = starts[:, lanes]
        for low in range(tile + 1):
            bias[pl.ds(low * TILE, TILE)] = bias_tile(starts_here, low, tile, low == tile)
        count = (tile + 1) * TILE

        def one_head(head, _, lanes=lanes, count=count):
            rows = pl.ds(pl.multiple_of(head * HEAD_SIZE, HEAD_SIZE), HEAD_SIZE)
            scores = jnp.dot(
                key_rows[:count], queries[rows, lanes], preferred_element_type=jnp.float32
            )
            scores += bias[:count]
            highest = jnp.max(scores, axis=0, keepdims=True)
            weights = jnp.exp(scores - highest)
            total = jnp.sum(weights, axis=0, keepdims=True)
            out = jnp.dot(
                qkv[pl.ds((group + 1) * HEAD_SIZE, HEAD_SIZE), :count],
                weights.astype(jnp.bfloat16),
                preferred_element_type=jnp.float32,
            )
            attended[rows, lanes] = (out / total).astype(jnp.bfloat16)
            lse[head, :, lanes] = jnp.broadcast_to(highest + jnp.log(total), (8, TILE))
            return 0

        lax.fori_loop(0, group, one_head, 0)


def forward_kernel(
    qkv,
    cosine,
    sine,
    starts,
    cotangent,
    heads,
    down,
    attended,
    lse,
    queries,
    keys,
    gathered,
    heads_all,
    down_all,
    key_rows,
    bias,
    local,
    send,
    recv,
):
    ring = seq_ring()
    weights_ring, core, mate = fsdp_ring()
    swap, apart = transposed()
    greet_also(ring.peers + weights_ring.peers + [mate], swap, apart)
    last = send.shape[0] - 1

    def exchange():
        return pltpu.make_async_remote_copy(
            src_ref=heads,
            dst_ref=heads_all.at[core],
            send_sem=send.at[last],
            recv_sem=recv.at[last],
            device_id=swap,
            device_id_type=MESH,
        )

    def keep():
        return pltpu.make_async_copy(heads, heads_all.at[core], local.at[2])

    kept = [
        pltpu.make_async_copy(cotangent, gathered.at[ring.near[0]], local.at[0]),
        pltpu.make_async_copy(down, down_all.at[weights_ring.near[0]], local.at[1]),
    ]
    for copy in kept:
        copy.start()
    copies = Copies(send, recv)

    def heads_walk():
        @pl.when(apart)
        def _():
            exchange().start()

        @pl.when(jnp.logical_not(apart))
        def _():
            keep().start()

        yield
        attend_tiles(qkv, cosine, sine, starts, attended, lse, queries, keys, key_rows, bias)
        yield

        @pl.when(apart)
        def _():
            exchange().wait()

        @pl.when(jnp.logical_not(apart))
        def _():
            keep().wait()

        copy = copies.start(heads_all.at[core], heads_all.at[core], mate)
        for _ in range(2 * CHUNKS):
            yield
        copy.wait_recv()

    in_turn(
        gather_walk(
            ring, copies, cotangent, gathered, by_rows(cotangent.shape[0], CHUNKS), CHUNKS
        ),
        gather_walk(
            weights_ring,
            copies,
            down,
            down_all,
            by_rows(down.shape[0], CHUNKS),
            CHUNKS,
            True,
            mate,
        ),
        heads_walk(),
    )
    copies.finish()
    for copy in kept:
        copy.wait()


def attend(qkv, cosine, sine, starts, cotangent, heads, down, group, number):
    length = qkv.shape[1]
    rows, width = cotangent.shape
    ranks = lax.axis_size("seq")
    return pl.pallas_call(
        forward_kernel,
        out_shape=[
            jax.ShapeDtypeStruct((group * HEAD_SIZE, length), jnp.bfloat16),
            jax.ShapeDtypeStruct((group, 8, length), jnp.float32),
            jax.ShapeDtypeStruct((group * HEAD_SIZE, length), jnp.bfloat16),
            jax.ShapeDtypeStruct((HEAD_SIZE, length), jnp.bfloat16),
            jax.ShapeDtypeStruct((ranks, rows, width), jnp.bfloat16),
            jax.ShapeDtypeStruct((2, *heads.shape), jnp.bfloat16),
            jax.ShapeDtypeStruct((lax.axis_size("fsdp"), *down.shape), jnp.bfloat16),
        ],
        in_specs=[VMEM] * 4 + [ANYWHERE] * 3,
        out_specs=[VMEM] * 4 + [ANYWHERE] * 3,
        scratch_shapes=[
            pltpu.VMEM((length, HEAD_SIZE), jnp.bfloat16),
            pltpu.VMEM((length, TILE), jnp.float32),
            pltpu.SemaphoreType.DMA((3,)),
        ]
        + semaphores(gather_copies(CHUNKS) + gather_copies(CHUNKS, True) + 2),
        compiler_params=params(number, 40),
        name="attend",
    )(qkv, cosine, sine, starts, cotangent, heads, down)


def back_tiles(
    qkv,
    queries,
    keys,
    attended,
    lse,
    grads,
    cosine,
    sine,
    starts,
    out,
    key_rows,
    value_rows,
    query_rows,
    grad_rows,
    row_dots,
    key_grad,
    value_grad,
    query_grad,
    bias,
):
    group = queries.shape[0] // HEAD_SIZE
    half = HEAD_SIZE // 2
    tiles = qkv.shape[1] // TILE
    key_rows[...] = keys[...].T
    value_rows[...] = qkv[pl.ds((group + 1) * HEAD_SIZE, HEAD_SIZE)].T
    for head in range(group):
        rows = pl.ds(head * HEAD_SIZE, HEAD_SIZE)
        query_rows[head] = queries[rows].T
        grad_rows[head] = grads[rows].T
        row_dots[head] = jnp.broadcast_to(
            jnp.sum(
                grads[rows].astype(jnp.float32) * attended[rows].astype(jnp.float32),
                axis=0,
                keepdims=True,
            ),
            row_dots.shape[1:],
        )
    key_grad[...] = jnp.zeros_like(key_grad)
    value_grad[...] = jnp.zeros_like(value_grad)
    for tile in range(tiles):
        lanes = pl.ds(tile * TILE, TILE)
        starts_here = starts[:, lanes]
        for low in range(tile + 1):
            bias[low] = bias_tile(starts_here, low, tile, low == tile)

        def one_head(head, _, lanes=lanes, tile=tile):
            rows = pl.ds(pl.multiple_of(head * HEAD_SIZE, HEAD_SIZE), HEAD_SIZE)
            query, grad = queries[rows, lanes], grads[rows, lanes]
            query_row, grad_row = query_rows[head, lanes], grad_rows[head, lanes]
            lse_row = lse[head, 0:1, lanes]
            dot_row = row_dots[head, 0:1, lanes]
            total = jnp.zeros((HEAD_SIZE, TILE), jnp.float32)
            for low in range(tile + 1):
                part = pl.ds(low * TILE, TILE)
                scores = jnp.dot(key_rows[part], query, preferred_element_type=jnp.float32)
                probs = jnp.exp(scores + bias[low] - lse_row)
                grad_probs = jnp.dot(value_rows[part], grad, preferred_element_type=jnp.float32)
                grad_scores = (probs * (grad_probs - dot_row)).astype(jnp.bfloat16)
                value_grad[part] += jnp.dot(
                    probs.astype(jnp.bfloat16), grad_row, preferred_element_type=jnp.float32
                )
                key_grad[part] += jnp.dot(
                    grad_scores, query_row, preferred_element_type=jnp.float32
                )
                total += jnp.dot(keys[:, part], grad_scores, preferred_element_type=jnp.float32)
            query_grad[rows, lanes] = total * 0.125
            return 0

        lax.fori_loop(0, group, one_head, 0)
    cos, sin = cosine[...], sine[...]
    for head in range(group):
        first = head * HEAD_SIZE
        out[pl.ds(first, HEAD_SIZE)] = rotate_rows(
            query_grad[pl.ds(first, half)], query_grad[pl.ds(first + half, half)], cos, -sin
        ).astype(jnp.bfloat16)
    turned = key_grad[...].T
    out[pl.ds(group * HEAD_SIZE, HEAD_SIZE)] = rotate_rows(
        turned[:half], turned[half:], cos, -sin
    ).astype(jnp.bfloat16)
    out[pl.ds((group + 1) * HEAD_SIZE, HEAD_SIZE)] = value_grad[...].T.astype(jnp.bfloat16)


def backward_kernel(*refs):
    ins, (part_of, middle, grads), (out, layer_out, grads_share) = (
        refs[:9],
        refs[9:12],
        refs[12:15],
    )
    scratch, (send, recv), (own, other, sems) = refs[15:24], refs[24:26], refs[26:29]
    bufs = refs[29:]
    ring = seq_ring()
    weights_ring, core, mate = fsdp_ring()
    greet(ring.peers + weights_ring.peers + [mate])
    copies = Copies(send, recv)

    def compute():
        yield
        back_tiles(*ins, out, *scratch)

    def done(rows_of, total):
        layer_out[rows_of] = (middle[rows_of] + total).astype(jnp.bfloat16)

    def owned(rows_of, total):
        grads_share[rows_of] = total.astype(jnp.bfloat16)

    in_turn(
        owners_walk(
            weights_ring,
            core,
            mate,
            copies,
            grads,
            own,
            other,
            sems,
            bufs[:7],
            grads_share.shape[0],
            owned,
        ),
        reduce_walk(ring, copies, part_of, bufs[7:], middle.shape[0], CHUNKS, done),
        compute(),
    )
    copies.finish()


def attend_back(
    qkv,
    queries,
    keys,
    attended,
    lse,
    grads,
    cosine,
    sine,
    starts,
    partial,
    middle,
    down_grad,
    number,
):
    length = qkv.shape[1]
    group = queries.shape[0] // HEAD_SIZE
    tiles = length // TILE
    rows, width = middle.shape
    ranks, owners = lax.axis_size("seq"), lax.axis_size("fsdp")
    places = owners // 2
    grad_rows = down_grad.shape[0] // owners
    return pl.pallas_call(
        backward_kernel,
        out_shape=[
            jax.ShapeDtypeStruct(qkv.shape, jnp.bfloat16),
            jax.ShapeDtypeStruct((rows, width), jnp.bfloat16),
            jax.ShapeDtypeStruct((grad_rows, width), jnp.bfloat16),
        ],
        in_specs=[VMEM] * 11 + [ANYWHERE],
        out_specs=[VMEM] * 3,
        scratch_shapes=[
            pltpu.VMEM((length, HEAD_SIZE), jnp.bfloat16),
            pltpu.VMEM((length, HEAD_SIZE), jnp.bfloat16),
            pltpu.VMEM((group, length, HEAD_SIZE), jnp.bfloat16),
            pltpu.VMEM((group, length, HEAD_SIZE), jnp.bfloat16),
            pltpu.VMEM((group, 8, length), jnp.float32),
            pltpu.VMEM((length, HEAD_SIZE), jnp.float32),
            pltpu.VMEM((length, HEAD_SIZE), jnp.float32),
            pltpu.VMEM((group * HEAD_SIZE, length), jnp.float32),
            pltpu.VMEM((tiles, TILE, TILE), jnp.float32),
        ]
        + semaphores(reduce_copies(CHUNKS) + OWNERS_COPIES)
        + owners_scratch(places, grad_rows, width)
        + reduce_scratch(rows, width),
        compiler_params=params(number, 48),
        name="attend_back",
    )(
        qkv,
        queries,
        keys,
        attended,
        lse,
        grads,
        cosine,
        sine,
        starts,
        partial.reshape(ranks, rows, width),
        middle,
        down_grad.reshape(places, 2, grad_rows, width),
    )


def contract_rows(left, right):
    return jnp.einsum("ta,tb->ab", left, right, preferred_element_type=jnp.float32)


def contract_cols(left, right):
    return jnp.einsum("ta,ba->tb", left, right, preferred_element_type=jnp.float32)


def matmul(left, right):
    return jnp.dot(left, right, preferred_element_type=jnp.float32)


def shards(
    tokens,
    segment_ids,
    query_weight,
    key_matrix,
    value_matrix,
    output_weight,
    gate_weight,
    up_weight,
    down_weight,
    attention_gain,
    feed_gain,
    cotangent,
):
    rank = lax.axis_index("seq")
    owner = lax.axis_index("fsdp")
    ranks = lax.axis_size("seq")
    owners = lax.axis_size("fsdp")
    rows, width = query_weight.shape
    kv_cols = key_matrix.shape[1] // ranks
    q_cols = width // ranks
    group = q_cols // kv_cols
    ff = gate_weight.shape[1]
    ff_chunk = ff // owners // ranks
    segment_row = segment_ids[0]
    length = segment_row.shape[0]

    qkv_in, gate_up_in = pick_columns(
        query_weight, key_matrix, value_matrix, gate_weight, up_weight, attention_gain, feed_gain
    )
    whole, qkv_got, gate_up_all = gather_first(tokens[0], qkv_in, gate_up_in, 0)
    gate_up_all = gate_up_all.reshape(width, -1)
    qkv_all = qkv_got[:, :rows].reshape(owners * rows, -1)
    gain_one = qkv_got[:, rows, :rows].reshape(1, -1).astype(jnp.float32)
    gain_two = qkv_got[:, rows + 1, :rows].reshape(1, -1).astype(jnp.float32)
    ff_local = owners * ff_chunk
    down_in = lax.dynamic_slice_in_dim(down_weight, rank * ff_chunk, ff_chunk, 0)

    starts = (jnp.arange(length, dtype=jnp.int32) - positions_of(segment_row))[None]
    cosine, sine = (table.T for table in angles_of(segment_row, HEAD_SIZE))
    whole = whole.reshape(length, width).astype(jnp.float32)
    hidden_one = (whole * lax.rsqrt(mean_square(whole) + EPS) * gain_one).astype(jnp.bfloat16)
    qkv = jnp.einsum("tm,mc->ct", hidden_one, qkv_all, preferred_element_type=jnp.float32)
    qkv = qkv.astype(jnp.bfloat16)
    attended, lse, queries, keys, grad_out, output_all, down_all = attend(
        qkv, cosine, sine, starts, cotangent[0], output_weight, down_in, group, 1
    )
    down_all = down_all.reshape(ff_local, width)
    grad_out = grad_out.reshape(length, width)
    output_all = output_all.reshape(q_cols, width)
    middle, hidden_two = add_branch(
        contract_rows(attended, output_all).astype(jnp.bfloat16), tokens[0], gain_two, 2
    )
    hidden_two = hidden_two.reshape(length, width)

    gate = matmul(hidden_two, gate_up_all[:, :ff_local])
    up_proj = matmul(hidden_two, gate_up_all[:, ff_local:])
    sig_gate = jax.nn.sigmoid(gate)
    silu_gate = gate * sig_gate
    act = (silu_gate * up_proj).astype(jnp.bfloat16)
    grad_act = contract_cols(grad_out, down_all)
    grad_gate = (grad_act * up_proj * (sig_gate * (1.0 + gate * (1.0 - sig_gate)))).astype(
        jnp.bfloat16
    )
    grad_up = (grad_act * silu_gate).astype(jnp.bfloat16)
    gate_up_grads = jnp.concatenate([grad_gate, grad_up], axis=1)
    down_grad = contract_rows(act, grad_out).astype(jnp.bfloat16)
    gate_up_grad = contract_rows(hidden_two, gate_up_grads).astype(jnp.bfloat16)
    layer_partial = matmul(act, down_all).astype(jnp.bfloat16)
    grad_middle, grad_gain_two, grad_branch, gate_up_share = back_to_middle(
        contract_cols(gate_up_grads, gate_up_all).astype(jnp.bfloat16),
        middle,
        gain_two,
        cotangent[0],
        gate_up_grad,
        3,
    )
    grad_branch = grad_branch.reshape(length, width)

    grad_attended = jnp.einsum(
        "tm,fm->ft", grad_branch, output_all, preferred_element_type=jnp.float32
    ).astype(jnp.bfloat16)
    qkv_grads, layer_out, down_share = attend_back(
        qkv,
        queries,
        keys,
        attended,
        lse,
        grad_attended,
        cosine,
        sine,
        starts,
        layer_partial,
        middle,
        down_grad,
        4,
    )
    heads_grad = matmul(attended, grad_branch).astype(jnp.bfloat16)
    qkv_grad = jnp.einsum(
        "tm,ct->mc", hidden_one, qkv_grads, preferred_element_type=jnp.float32
    ).astype(jnp.bfloat16)
    grad_inputs, grad_gain_one, qkv_share, heads_share = back_to_tokens(
        jnp.einsum("ct,mc->tm", qkv_grads, qkv_all, preferred_element_type=jnp.float32).astype(
            jnp.bfloat16
        ),
        tokens[0],
        gain_one,
        grad_middle,
        qkv_grad,
        heads_grad,
        5,
    )
    *gathered, gains = finish_grads(
        gate_up_share, down_share, qkv_share, heads_share, grad_gain_one, grad_gain_two, 6
    )
    gate_grad, up_grad, down_total, query_grad, key_grad, value_grad, heads_total = place_grads(
        *gathered
    )
    return (
        layer_out[None],
        grad_inputs[None],
        query_grad,
        key_grad,
        value_grad,
        heads_total,
        gate_grad,
        up_grad,
        down_total,
        gains[0],
        gains[1],
    )


def solution(mesh):
    placed = (
        P("fsdp", "seq", None),
        P("fsdp", None),
        P("fsdp", None),
        P("fsdp", None),
        P("fsdp", None),
        P("fsdp", None),
        P("fsdp", None),
        P("fsdp", None),
        P("fsdp", None),
        P("fsdp"),
        P("fsdp"),
        P("fsdp", "seq", None),
    )
    return jax.shard_map(
        shards,
        mesh=mesh,
        in_specs=placed,
        out_specs=(
            P("fsdp", "seq", None),
            P("fsdp", "seq", None),
            P("fsdp", None),
            P("fsdp", None),
            P("fsdp", None),
            P("fsdp", None),
            P("fsdp", None),
            P("fsdp", None),
            P("fsdp", None),
            P("fsdp"),
            P("fsdp"),
        ),
        check_vma=False,
    )
```

```python
import math

import jax
import jax.numpy as jnp
from jax import lax
from jax.experimental import pallas as pl
from jax.experimental.pallas import tpu as pltpu
from jax.sharding import PartitionSpec as P

HEAD_SIZE = 64
EPS = 1e-05
ROPE_BASE = 500000.0
NEG = -1e30


def rope_freqs(head_dim):
    half_dim = head_dim // 2
    table = []
    for index in range(half_dim):
        inverse = 1.0 / ROPE_BASE ** (index * 2.0 / head_dim)
        wavelen = 2.0 * math.pi / inverse
        blend = (8192.0 / wavelen - 1.0) / 3.0
        mixed = (1.0 - blend) * inverse / 32.0 + blend * inverse
        entry = inverse if wavelen < 2048.0 else inverse / 32.0 if wavelen > 8192.0 else mixed
        table.append(entry)
    return jnp.asarray(table, dtype=jnp.float32)


def positions_of(segment_row):
    indices = jnp.arange(segment_row.shape[0], dtype=jnp.int32)
    begins = jnp.concatenate(
        [jnp.ones((1,), dtype=jnp.int32), (segment_row[1:] != segment_row[:-1]).astype(jnp.int32)]
    )
    starts_at = lax.cummax(jnp.where(begins > 0, indices, 0), axis=0)
    return indices - starts_at


def angles_of(segment_row, head_dim):
    positions = positions_of(segment_row)
    phase = positions.astype(jnp.float32)[:, None] * rope_freqs(head_dim)[None, :]
    return (jnp.cos(phase), jnp.sin(phase))


MESH = pl.DeviceIdType.MESH
CHUNKS = 4
TILE = 256


class Ring:
    def __init__(self, place, count, index_of, device_of):
        side = count // 2
        self.place = place
        row, col = lax.div(place, side), lax.rem(place, side)

        def at(which, step):
            return index_of(which * side + lax.rem(col + step, side))

        self.near = [at(row, step) for step in range(side)]
        self.far = [at(1 - row, step) for step in range(side)]
        self.right = device_of(self.near[1])
        self.left = device_of(self.near[3])
        self.partner = device_of(self.far[0])
        self.peers = [self.right, self.left, self.partner]


def seq_ring():
    rank, owner = lax.axis_index("seq"), lax.axis_index("fsdp")
    return Ring(rank, lax.axis_size("seq"), lambda place: place, lambda index: (index, owner))


def fsdp_ring():
    rank, owner = lax.axis_index("seq"), lax.axis_index("fsdp")
    core = lax.rem(owner, 2)
    ring = Ring(
        lax.div(owner, 2),
        lax.axis_size("fsdp") // 2,
        lambda place: 2 * place + core,
        lambda index: (rank, index),
    )
    return ring, core, (rank, owner + 1 - 2 * core)


def greet(peers):
    barrier = pltpu.get_barrier_semaphore()
    for peer in peers:
        pl.semaphore_signal(barrier, inc=1, device_id=peer, device_id_type=MESH)
    pl.semaphore_wait(barrier, len(peers))


def greet_also(peers, other, apart):
    barrier = pltpu.get_barrier_semaphore()
    for peer in peers:
        pl.semaphore_signal(barrier, inc=1, device_id=peer, device_id_type=MESH)

    @pl.when(apart)
    def _():
        pl.semaphore_signal(barrier, inc=1, device_id=other, device_id_type=MESH)
        pl.semaphore_wait(barrier, len(peers) + 1)

    @pl.when(jnp.logical_not(apart))
    def _():
        pl.semaphore_wait(barrier, len(peers))


def transposed():
    rank, owner = lax.axis_index("seq"), lax.axis_index("fsdp")
    other = (lax.div(owner, 2), 2 * rank + lax.rem(owner, 2))
    return other, other[0] != rank


def in_step(*walks):
    left = list(walks)
    while left:
        left = [walk for walk in left if next(walk, walk) is not walk]
        yield


def beside(main, *sides):
    sides = [(walk, list(places)) for walk, places in sides]
    step = 0
    for _ in main:
        for walk, places in sides:
            while places and places[0] <= step:
                places.pop(0)
                next(walk, None)
        step += 1
    for walk, _ in sides:
        for _ in walk:
            pass


class Copies:
    def __init__(self, send, recv):
        self.send, self.recv = send, recv
        self.made = []

    def start(self, source, target, peer):
        number = len(self.made)
        copy = pltpu.make_async_remote_copy(
            src_ref=source,
            dst_ref=target,
            send_sem=self.send.at[number],
            recv_sem=self.recv.at[number],
            device_id=peer,
            device_id_type=MESH,
        )
        copy.start()
        self.made.append(copy)
        return copy

    def finish(self):
        for copy in self.made:
            copy.wait_send()


def by_rows(rows, chunks):
    size = rows // chunks
    return lambda ref, index: ref.at[pl.ds(index * size, size)]


def by_columns(columns, chunks):
    size = columns // chunks
    return lambda ref, index: ref.at[:, pl.ds(index * size, size)]


def gather_walk(ring, copies, own, out, cut, chunks, deep=False, mate=None):
    me, right, opposite, left = ring.near
    partner, far_right, _, far_left = ring.far
    half = chunks // 2
    passed = []

    def share(place, index):
        if mate is not None:
            block = cut(out.at[place], index)
            passed.append(copies.start(block, block, mate))

    to_right, to_left, to_far, on = {}, {}, {}, {}
    for step in range(chunks):
        back = chunks - 1 - step
        to_far[step] = copies.start(cut(own, step), cut(out.at[me], step), ring.partner)
        to_right[step] = copies.start(cut(own, step), cut(out.at[me], step), ring.right)
        to_left[back] = copies.start(cut(own, back), cut(out.at[me], back), ring.left)
        if mate is not None:
            passed.append(copies.start(cut(own, step), cut(out.at[me], step), mate))
    yield
    for step in range(half):
        back = chunks - 1 - step
        to_right[step].wait_recv()
        block = cut(out.at[left], step)
        on[step] = copies.start(block, block, ring.right)
        share(left, step)
        to_left[back].wait_recv()
        block = cut(out.at[right], back)
        on[back] = copies.start(block, block, ring.left)
        share(right, back)
        yield
    far_on, rest = {}, []
    for step in range(chunks):
        to_far[step].wait_recv()
        block = cut(out.at[partner], step)
        far_on[0, step] = copies.start(block, block, ring.right)
        far_on[1, step] = copies.start(block, block, ring.left)
        share(partner, step)
        yield
    if deep:
        for step in range(half):
            back = chunks - 1 - step
            far_on[0, step].wait_recv()
            block = cut(out.at[far_left], step)
            rest.append((step, copies.start(block, block, ring.right)))
            share(far_left, step)
            far_on[1, back].wait_recv()
            block = cut(out.at[far_right], back)
            rest.append((back, copies.start(block, block, ring.left)))
            share(far_right, back)
            yield
    for step in range(half):
        for index in (step, chunks - 1 - step):
            on[index].wait_recv()
            if not deep:
                block = cut(out.at[opposite], index)
                rest.append((index, copies.start(block, block, ring.partner)))
            share(opposite, index)
        yield
    for step in range(half):
        back = chunks - 1 - step
        to_right[back].wait_recv()
        share(left, back)
        to_left[step].wait_recv()
        share(right, step)
        if deep:
            far_on[0, back].wait_recv()
            share(far_left, back)
            far_on[1, step].wait_recv()
            share(far_right, step)
        yield
    if not deep:
        for copy in far_on.values():
            copy.wait_recv()
    for index, copy in rest:
        copy.wait_recv()
        share(ring.far[2], index)
    yield
    for copy in passed:
        copy.wait_recv()


def gather_copies(chunks, mate=False):
    return 7 * chunks + (8 * chunks if mate else 0)


def reduce_walk(ring, copies, part_of, bufs, rows, chunks, done):
    me, right, opposite, left = ring.near
    partner, far_right, far_opposite, far_left = ring.far
    from_left, from_right, from_far, mid, end_left, end_right, end_far = bufs
    size = rows // chunks
    half = chunks // 2

    def part(index):
        return pl.ds(index * size, size)

    def wide(ref):
        return ref.astype(jnp.float32)

    order = [x for step in range(half) for x in (step, chunks - 1 - step)]
    one_right, one_left, one_far = {}, {}, {}
    for index in order:
        rows_of = part(index)
        one_far[index] = copies.start(
            part_of.at[far_opposite, rows_of], from_far.at[rows_of], ring.partner
        )
        one_right[index] = copies.start(
            part_of.at[far_right, rows_of], from_left.at[rows_of], ring.right
        )
        one_left[index] = copies.start(
            part_of.at[far_left, rows_of], from_right.at[rows_of], ring.left
        )
    last_right, last_left, last_far = {}, {}, {}
    for index in range(half):
        rows_of = part(index)
        last_right[index] = copies.start(
            part_of.at[right, rows_of], end_left.at[rows_of], ring.right
        )
        rows_of = part(chunks - 1 - index)
        last_left[chunks - 1 - index] = copies.start(
            part_of.at[left, rows_of], end_right.at[rows_of], ring.left
        )
    yield
    two = {}
    for index in order:
        rows_of = part(index)
        one_far[index].wait_recv()
        from_far[rows_of] = (wide(from_far[rows_of]) + wide(part_of[opposite, rows_of])).astype(
            jnp.bfloat16
        )
        two[index] = copies.start(
            from_far.at[rows_of], mid.at[rows_of], ring.left if index < half else ring.right
        )
        yield
    for index in order:
        rows_of = part(index)
        one_right[index].wait_recv()
        one_left[index].wait_recv()
        from_left[rows_of] = (
            wide(from_left[rows_of]) + wide(from_right[rows_of]) + wide(part_of[partner, rows_of])
        ).astype(jnp.bfloat16)
        last_far[index] = copies.start(
            from_left.at[rows_of], end_far.at[rows_of], ring.partner
        )
        yield
    for index in order:
        rows_of = part(index)
        two[index].wait_recv()
        if index < half:
            mid[rows_of] = (wide(mid[rows_of]) + wide(part_of[left, rows_of])).astype(jnp.bfloat16)
            last_left[index] = copies.start(mid.at[rows_of], end_right.at[rows_of], ring.left)
        else:
            mid[rows_of] = (wide(mid[rows_of]) + wide(part_of[right, rows_of])).astype(
                jnp.bfloat16
            )
            last_right[index] = copies.start(mid.at[rows_of], end_left.at[rows_of], ring.right)
        yield
    for index in order:
        rows_of = part(index)
        last_far[index].wait_recv()
        last_left[index].wait_recv()
        last_right[index].wait_recv()
        done(
            rows_of,
            wide(part_of[me, rows_of])
            + wide(end_left[rows_of])
            + wide(end_right[rows_of])
            + wide(end_far[rows_of]),
        )
        yield


def reduce_copies(chunks):
    return 3 * chunks + 2 * chunks + chunks + chunks


def owners_walk(ring, mate, copies, produce, own, other, bufs, rows, done):
    mids, from_lefts, from_rights, from_far = bufs[:2], bufs[2:4], bufs[4:6], bufs[6]
    half = rows // 2
    low, high = pl.ds(0, half), pl.ds(half, half)
    near, far = ([lax.div(index, 2) for index in row] for row in (ring.near, ring.far))
    order = [far[2], near[2], far[1], far[3], near[1], near[3], far[0], near[0]]
    awaited = []
    for place in order:
        awaited.append(produce(place))
        yield

    def wide(ref):
        return ref.astype(jnp.float32)

    def add(*numbers):
        for number in numbers:
            for wait in awaited[number]:
                wait()
            place = order[number]
            own[place] = (wide(own[place]) + wide(other[place])).astype(jnp.bfloat16)

    add(0, 1)
    on = []
    for which, row in enumerate((far, near)):
        block = own.at[row[2]]
        on.append(copies.start(block.at[low], mids[which].at[low], ring.left))
        on.append(copies.start(block.at[high], mids[which].at[high], ring.right))
    yield
    ends = []
    for which, row in enumerate((far, near)):
        add(2 + 2 * which, 3 + 2 * which)
        ends.append(
            copies.start(own.at[row[1], low], from_lefts[which].at[low], ring.right)
        )
        ends.append(
            copies.start(own.at[row[3], high], from_rights[which].at[high], ring.left)
        )
        yield
    add(6, 7)
    yield
    for which, row in enumerate((far, near)):
        mid = mids[which]
        on[2 * which].wait_recv()
        mid[low] = (wide(mid[low]) + wide(own[row[3], low])).astype(jnp.bfloat16)
        ends.append(copies.start(mid.at[low], from_rights[which].at[low], ring.left))
        yield
        on[2 * which + 1].wait_recv()
        mid[high] = (wide(mid[high]) + wide(own[row[1], high])).astype(jnp.bfloat16)
        ends.append(copies.start(mid.at[high], from_lefts[which].at[high], ring.right))
        yield
    last = []
    for rows_of, numbers in ((low, (0, 4, 1, 5)), (high, (0, 4, 1, 5))):
        if not last:
            for number in numbers:
                ends[number].wait_recv()
        total = (
            wide(from_lefts[0][rows_of])
            + wide(from_rights[0][rows_of])
            + wide(own[far[0], rows_of])
        )
        from_lefts[0][rows_of] = total.astype(jnp.bfloat16)
        last.append(
            copies.start(from_lefts[0].at[rows_of], from_far.at[rows_of], ring.partner)
        )
    yield
    for number in (2, 6, 3, 7):
        ends[number].wait_recv()
    yield
    for rows_of, copy in zip((low, high), last):
        copy.wait_recv()
        done(
            rows_of,
            wide(from_lefts[1][rows_of])
            + wide(from_rights[1][rows_of])
            + wide(own[near[0], rows_of])
            + wide(from_far[rows_of]),
        )
        yield


OWNERS_COPIES = 4 + 4 + 4 + 2


def owners_scratch(places, rows, width):
    return [pltpu.VMEM((places, rows, width), jnp.bfloat16) for _ in range(2)] + [
        pltpu.VMEM((rows, width), jnp.bfloat16) for _ in range(7)
    ]


def fetched(copies, core, mate, pieces, own, other, sems):
    count = 0

    def produce(place):
        nonlocal count
        waits = []
        for piece, part in pieces:
            sent = copies.start(piece(place, 1 - core), part(other.at[place]), mate)
            copy = pltpu.make_async_copy(piece(place, core), part(own.at[place]), sems.at[count])
            copy.start()
            count += 1
            waits += [sent.wait_recv, copy.wait]
        return waits

    return produce


def reduce_scratch(rows, width):
    return [pltpu.VMEM((rows, width), jnp.bfloat16) for _ in range(7)]


def semaphores(count):
    return [pltpu.SemaphoreType.DMA((count,)), pltpu.SemaphoreType.DMA((count,))]


def params(number, limit):
    return pltpu.CompilerParams(
        collective_id=number, has_side_effects=True, vmem_limit_bytes=limit * 2**20
    )


VMEM = pl.BlockSpec(memory_space=pltpu.VMEM)
ANYWHERE = pl.BlockSpec(memory_space=pl.ANY)


def gather_first(tokens, qkv, number):
    blocks = (tokens, qkv)
    ranks, owners = lax.axis_size("seq"), lax.axis_size("fsdp")

    def kernel(tokens, qkv, tokens_all, qkv_all, local, send, recv):
        ring = seq_ring()
        weights_ring, _, mate = fsdp_ring()
        greet(ring.peers + weights_ring.peers + [mate])
        copies = Copies(send, recv)
        kept = [
            pltpu.make_async_copy(tokens, tokens_all.at[ring.near[0]], local.at[0]),
            pltpu.make_async_copy(qkv, qkv_all.at[weights_ring.near[0]], local.at[1]),
        ]
        for copy in kept:
            copy.start()
        rows, weight_rows = tokens.shape[0], qkv.shape[0]
        beside(
            gather_walk(ring, copies, tokens, tokens_all, by_rows(rows, CHUNKS), CHUNKS),
            (
                gather_walk(
                    weights_ring, copies, qkv, qkv_all, by_rows(weight_rows, 2), 2, True, mate
                ),
                (0, 0, 2, 2, 4, 6, 6, 8),
            ),
        )
        copies.finish()
        for copy in kept:
            copy.wait()

    count = gather_copies(CHUNKS) + gather_copies(2, True)
    return pl.pallas_call(
        kernel,
        out_shape=[
            jax.ShapeDtypeStruct((size, *block.shape), jnp.bfloat16)
            for size, block in zip((ranks, owners), blocks)
        ],
        in_specs=[ANYWHERE] * 2,
        out_specs=[ANYWHERE] * 2,
        scratch_shapes=[pltpu.SemaphoreType.DMA((2,))] + semaphores(count),
        compiler_params=params(number, 32),
        name="gather_first",
    )(*blocks)


def mean_square(values):
    return jnp.mean(values * values, axis=-1, keepdims=True)


BESIDE_BOTH = (0, 4, 4, 8, 8, 9, 10, 17, 18, 20, 21, 22, 23, 24)
BESIDE_GATHER = (0, 1, 2, 3, 4, 5, 6, 7, 8, 8, 9, 9, 10, 10)


def branch_kernel(
    part_of,
    tokens,
    gain,
    up,
    down,
    middle,
    hidden,
    up_all,
    down_all,
    block,
    local,
    send,
    recv,
    *bufs,
):
    ring = seq_ring()
    weights_ring, _, mate = fsdp_ring()
    rows = tokens.shape[0]
    greet(ring.peers + weights_ring.peers + [mate])
    copies = Copies(send, recv)

    def done(rows_of, total):
        values = tokens[rows_of].astype(jnp.float32) + total
        middle[rows_of] = values
        factor = lax.rsqrt(mean_square(values) + EPS)
        block[rows_of] = (values * factor * gain[...]).astype(jnp.bfloat16)

    kept = [
        pltpu.make_async_copy(up, up_all.at[weights_ring.near[0]], local.at[0]),
        pltpu.make_async_copy(down, down_all.at[weights_ring.near[0]], local.at[1]),
        pltpu.make_async_copy(block, hidden.at[ring.near[0]], local.at[2]),
    ]
    kept[0].start()
    kept[1].start()

    def walk():
        yield from reduce_walk(ring, copies, part_of, bufs, rows, CHUNKS, done)
        kept[2].start()
        yield from gather_walk(ring, copies, block, hidden, by_rows(rows, CHUNKS), CHUNKS)

    def weights(own, out):
        cut = by_rows(own.shape[0], CHUNKS)
        return gather_walk(weights_ring, copies, own, out, cut, CHUNKS, True, mate)

    beside(walk(), (weights(up, up_all), BESIDE_BOTH), (weights(down, down_all), BESIDE_BOTH))
    copies.finish()
    for copy in kept:
        copy.wait()


def add_branch(partial, tokens, gain, up, down, number):
    rows, width = tokens.shape
    ranks, owners = lax.axis_size("seq"), lax.axis_size("fsdp")
    count = reduce_copies(CHUNKS) + gather_copies(CHUNKS) + 2 * gather_copies(CHUNKS, True)
    return pl.pallas_call(
        branch_kernel,
        out_shape=[
            jax.ShapeDtypeStruct((rows, width), jnp.float32),
            jax.ShapeDtypeStruct((ranks, rows, width), jnp.bfloat16),
            jax.ShapeDtypeStruct((owners, *up.shape), jnp.bfloat16),
            jax.ShapeDtypeStruct((owners, *down.shape), jnp.bfloat16),
        ],
        in_specs=[VMEM] * 3 + [ANYWHERE] * 2,
        out_specs=[VMEM] + [ANYWHERE] * 3,
        scratch_shapes=[pltpu.VMEM((rows, width), jnp.bfloat16), pltpu.SemaphoreType.DMA((3,))]
        + semaphores(count)
        + reduce_scratch(rows, width),
        compiler_params=params(number, 32),
        name="add_branch",
    )(partial.reshape(ranks, rows, width), tokens, gain, up, down)


def norm_back_rows(grad, gain, values):
    factor = lax.rsqrt(mean_square(values) + EPS)
    normed = values * factor
    weighted = grad * gain
    back = factor * (weighted - normed * jnp.mean(weighted * normed, axis=-1, keepdims=True))
    return back, grad * normed


PRODUCT = 512


def product(left, right, store):
    def columns(index, _):
        cols = pl.ds(pl.multiple_of(index * PRODUCT, PRODUCT), PRODUCT)
        store(cols, jnp.dot(left, right[:, cols], preferred_element_type=jnp.float32))
        return 0

    lax.fori_loop(0, right.shape[1] // PRODUCT, columns, 0)


def middle_kernel(
    part_of,
    middle,
    gain,
    cotangent,
    hidden,
    gate_grads,
    up_grads,
    act,
    grad_out,
    down,
    grad_middle,
    grad_gain,
    branch,
    grads_share,
    down_grad,
    layer_part,
    block,
    local,
    send,
    recv,
    left_wide,
    right_wide,
    act_here,
    turned,
    for_mate,
    staged,
    loads,
    stores,
    own,
    other,
    *bufs,
):
    ring = seq_ring()
    weights_ring, core, mate = fsdp_ring()
    rows = middle.shape[0]
    greet(ring.peers + weights_ring.peers + [mate])
    copies = Copies(send, recv)
    grad_gain[...] = jnp.zeros_like(grad_gain)

    def load(source, target, number):
        return pltpu.make_async_copy(source, target, loads.at[number])

    units = gate_grads.shape[1]
    first = [
        load(hidden, left_wide, 0),
        load(gate_grads, right_wide.at[:, pl.ds(0, units)], 1),
        load(up_grads, right_wide.at[:, pl.ds(units, units)], 2),
        load(act, act_here, 3),
    ]
    second = [load(grad_out, left_wide, 4), load(down, right_wide, 5)]
    for copy in first:
        copy.start()

    def done(rows_of, total):
        back, terms = norm_back_rows(total, gain[...], middle[rows_of])
        grad_gain[...] += jnp.sum(terms, axis=0, keepdims=True)
        values = cotangent[rows_of].astype(jnp.float32) + back
        grad_middle[rows_of] = values
        block[rows_of] = values.astype(jnp.bfloat16)

    def owned(rows_of, total):
        grads_share[rows_of] = total.astype(jnp.bfloat16)

    kept = pltpu.make_async_copy(block, branch.at[ring.near[0]], local)

    def walk():
        yield from reduce_walk(ring, copies, part_of, bufs[7:], rows, CHUNKS, done)
        kept.start()
        yield from gather_walk(ring, copies, block, branch, by_rows(rows, CHUNKS), CHUNKS)

    def produce(place):
        if first:
            for _ in range(3):
                first.pop(0).wait()
            waited.append(first.pop(0))
        lanes = pl.ds(pl.multiple_of(place * 2 * rows, 2 * rows), 2 * rows)
        turned[...] = left_wide[:, lanes].T
        here, there = pl.ds(core * rows, rows), pl.ds((1 - core) * rows, rows)

        def store_own(cols, value):
            own[place, :, cols] = value.astype(jnp.bfloat16)

        def store_mate(cols, value):
            for_mate[place, :, cols] = value.astype(jnp.bfloat16)

        product(turned[there], right_wide, store_mate)
        sent = copies.start(for_mate.at[place], other.at[place], mate)
        product(turned[here], right_wide, store_own)
        return [sent.wait_recv]

    waited = []

    def others():
        for copy in second:
            copy.start()
        waited[0].wait()
        yield
        second[0].wait()
        flights = [None, None]

        def flush(slot, target):
            copy = pltpu.make_async_copy(staged.at[slot], target, stores.at[slot])
            copy.start()
            flights[slot] = copy

        def store(slot):
            def put(cols, value):
                staged[slot, :, cols] = value.astype(jnp.bfloat16)

            return put

        pieces = act_here.shape[1] // rows
        for index in range(pieces):
            slot = index % 2
            if flights[slot] is not None:
                flights[slot].wait()
            product(act_here[:, pl.ds(index * rows, rows)].T, left_wide, store(slot))
            flush(slot, down_grad.at[index])
            yield
        second[1].wait()
        for index in range(part_of.shape[0]):
            slot = index % 2
            flights[slot].wait()
            product(act_here[pl.ds(index * rows, rows)], right_wide, store(slot))
            flush(slot, layer_part.at[index])
            yield
        for copy in flights:
            copy.wait()

    beside(
        walk(),
        (
            owners_walk(
                weights_ring,
                mate,
                copies,
                produce,
                own,
                other,
                bufs[:7],
                grads_share.shape[0],
                owned,
            ),
            (0,) * 8 + (0, 0, 0, 0, 8, 8, 8, 8, 17, 19, 24, 24),
        ),
        (
            others(),
            (8, 9, 10, 11, 12, 13, 14, 15, 16, 18, 19, 20, 21, 22, 23, 24, 25),
        ),
    )
    copies.finish()
    kept.wait()


def back_to_middle(
    partial, middle, gain, cotangent, hidden, gate_grads, up_grads, act, grad_out, down, number
):
    rows, width = middle.shape
    length = hidden.shape[0]
    ranks, owners = lax.axis_size("seq"), lax.axis_size("fsdp")
    places = owners // 2
    grad_rows, grad_cols = width // owners, 2 * gate_grads.shape[1]
    pieces = act.shape[1] // rows
    count = reduce_copies(CHUNKS) + gather_copies(CHUNKS) + OWNERS_COPIES + places
    return pl.pallas_call(
        middle_kernel,
        out_shape=[
            jax.ShapeDtypeStruct((rows, width), jnp.float32),
            jax.ShapeDtypeStruct((1, width), jnp.float32),
            jax.ShapeDtypeStruct((ranks, rows, width), jnp.bfloat16),
            jax.ShapeDtypeStruct((grad_rows, grad_cols), jnp.bfloat16),
            jax.ShapeDtypeStruct((pieces, rows, width), jnp.bfloat16),
            jax.ShapeDtypeStruct((ranks, rows, width), jnp.bfloat16),
        ],
        in_specs=[VMEM] * 4 + [ANYWHERE] * 6,
        out_specs=[VMEM, VMEM, ANYWHERE, VMEM, ANYWHERE, ANYWHERE],
        scratch_shapes=[pltpu.VMEM((rows, width), jnp.bfloat16), pltpu.SemaphoreType.DMA]
        + semaphores(count)
        + [
            pltpu.VMEM((length, width), jnp.bfloat16),
            pltpu.VMEM((length, width), jnp.bfloat16),
            pltpu.VMEM(act.shape, jnp.bfloat16),
            pltpu.VMEM((2 * grad_rows, length), jnp.bfloat16),
            pltpu.VMEM((places, grad_rows, grad_cols), jnp.bfloat16),
            pltpu.VMEM((2, rows, width), jnp.bfloat16),
            pltpu.SemaphoreType.DMA((6,)),
            pltpu.SemaphoreType.DMA((2,)),
        ]
        + owners_scratch(places, grad_rows, grad_cols)
        + reduce_scratch(rows, width),
        compiler_params=params(number, 52),
        name="back_to_middle",
    )(
        partial.reshape(ranks, rows, width),
        middle,
        gain,
        cotangent,
        hidden,
        gate_grads,
        up_grads,
        act,
        grad_out,
        down,
    )


def tokens_kernel(
    part_of,
    tokens,
    gain,
    grad_middle,
    qkv_grad,
    heads_grad,
    out,
    grad_gain,
    share,
    heads_block,
    heads_here,
    fetches,
    send,
    recv,
    own,
    other,
    *bufs,
):
    ring = seq_ring()
    weights_ring, core, mate = fsdp_ring()
    rows = tokens.shape[0]
    swap, apart = transposed()
    greet_also(ring.peers + weights_ring.peers + [mate], swap, apart)
    copies = Copies(send, recv)
    grad_gain[...] = jnp.zeros_like(grad_gain)
    qkv_cols = qkv_grad.shape[3]
    heads_cols = share.shape[1] - qkv_cols
    qkv_part, heads_part = pl.ds(0, qkv_cols), pl.ds(qkv_cols, heads_cols)

    def heads_of(place, which):
        first = pl.multiple_of(place * heads_cols, heads_cols)
        return heads_grad.at[which, :, pl.ds(first, heads_cols)]

    pieces = (
        (lambda place, which: qkv_grad.at[place, which], lambda ref: ref.at[:, qkv_part]),
        (heads_of, lambda ref: ref.at[:, heads_part]),
    )

    def exchange():
        return pltpu.make_async_remote_copy(
            src_ref=heads_block,
            dst_ref=heads_here,
            send_sem=send.at[send.shape[0] - 1],
            recv_sem=recv.at[recv.shape[0] - 1],
            device_id=swap,
            device_id_type=MESH,
        )

    def owned(rows_of, total):
        share[rows_of, qkv_part] = total[:, :qkv_cols].astype(jnp.bfloat16)
        heads_block[rows_of] = total[:, qkv_cols:].astype(jnp.bfloat16)

    def done(rows_of, total):
        back, terms = norm_back_rows(total, gain[...], tokens[rows_of].astype(jnp.float32))
        grad_gain[...] += jnp.sum(terms, axis=0, keepdims=True)
        out[rows_of] = (grad_middle[rows_of] + back).astype(jnp.bfloat16)

    def weights():
        yield from owners_walk(
            weights_ring,
            mate,
            copies,
            fetched(copies, core, mate, pieces, own, other, fetches),
            own,
            other,
            bufs[:7],
            rows,
            owned,
        )

        @pl.when(apart)
        def _():
            exchange().start()

        yield

        @pl.when(apart)
        def _():
            exchange().wait()
            share[:, heads_part] = heads_here[...]

        @pl.when(jnp.logical_not(apart))
        def _():
            share[:, heads_part] = heads_block[...]

    beside(
        reduce_walk(ring, copies, part_of, bufs[7:], rows, CHUNKS, done),
        (weights(), (0,) * 8 + (0, 1, 2, 3, 4, 4, 8, 8, 9, 10, 11, 12, 13)),
    )
    copies.finish()


def back_to_tokens(partial, tokens, gain, grad_middle, qkv_grad, heads_grad, number):
    rows, width = tokens.shape
    ranks, owners = lax.axis_size("seq"), lax.axis_size("fsdp")
    places = owners // 2
    qkv_cols, heads_cols = qkv_grad.shape[1], width // places
    count = reduce_copies(CHUNKS) + OWNERS_COPIES + 2 * places + 1
    return pl.pallas_call(
        tokens_kernel,
        out_shape=[
            jax.ShapeDtypeStruct((rows, width), jnp.bfloat16),
            jax.ShapeDtypeStruct((1, width), jnp.float32),
            jax.ShapeDtypeStruct((rows, qkv_cols + heads_cols), jnp.bfloat16),
        ],
        in_specs=[VMEM] * 4 + [ANYWHERE] * 2,
        out_specs=[VMEM] * 3,
        scratch_shapes=[
            pltpu.VMEM((rows, heads_cols), jnp.bfloat16),
            pltpu.VMEM((rows, heads_cols), jnp.bfloat16),
            pltpu.SemaphoreType.DMA((2 * places,)),
        ]
        + semaphores(count)
        + owners_scratch(places, rows, qkv_cols + heads_cols)
        + reduce_scratch(rows, width),
        compiler_params=params(number, 40),
        name="back_to_tokens",
    )(
        partial.reshape(ranks, rows, width),
        tokens,
        gain,
        grad_middle,
        qkv_grad.reshape(places, 2, rows, qkv_cols),
        heads_grad.reshape(2, rows, width),
    )


def finish_kernel(
    gate_up,
    down,
    small,
    gain_one,
    gain_two,
    gate_up_all,
    down_all,
    small_all,
    gains,
    given,
    from_mate,
    pair,
    from_partner,
    by_place,
    for_partner,
    partners,
    by_column,
    local,
    send,
    recv,
):
    ring = seq_ring()
    me = ring.near[0]
    side = lax.axis_size("seq") // 2
    weights_ring, core, mate = fsdp_ring()
    greet(ring.peers + weights_ring.peers + [mate])
    copies = Copies(send, recv)
    arrays = [
        (gate_up, gate_up_all, by_rows(gate_up.shape[0], CHUNKS)),
        (down, down_all, by_rows(down.shape[0], CHUNKS)),
        (small, small_all, by_rows(small.shape[0], CHUNKS)),
    ]
    kept = [
        pltpu.make_async_copy(own, out.at[me], local.at[i]) for i, (own, out, _) in enumerate(arrays)
    ]
    for copy in kept:
        copy.start()

    def around(table, ring_of):
        place = lax.rem(ring_of.place, side)
        after = lax.rem(place + 1, side)
        mine = table.at[place]
        to_right = copies.start(mine, mine, ring_of.right)
        to_left = copies.start(mine, mine, ring_of.left)
        yield
        to_right.wait_recv()
        to_left.wait_recv()
        copy = copies.start(table.at[after], table.at[after], ring_of.left)
        yield
        copy.wait_recv()

    def sum_gains():
        lanes = given.shape[2]
        for index in range(given.shape[0]):
            cols = pl.ds(index * lanes, lanes)
            given[index, 0:1] = gain_one[:, cols]
            given[index, 1:2] = gain_two[:, cols]
            given[index, 2:8] = jnp.zeros((6, lanes), jnp.float32)
        copy = copies.start(given, from_mate, mate)
        yield
        copy.wait_recv()
        pair[...] = given[...] + from_mate[...]
        copy = copies.start(pair, from_partner, weights_ring.partner)
        yield
        copy.wait_recv()
        by_place[lax.rem(weights_ring.place, side)] = pair[...] + from_partner[...]
        yield from around(by_place, weights_ring)
        block = lax.axis_index("fsdp")
        for_partner[...] = (by_place[0, block] + by_place[1, block]) + (
            by_place[2, block] + by_place[3, block]
        )
        copy = copies.start(for_partner, partners, ring.partner)
        yield
        copy.wait_recv()
        by_column[lax.rem(ring.place, side)] = for_partner[...] + partners[...]
        yield from around(by_column, ring)
        gains[...] = (by_column[0] + by_column[1]) + (by_column[2] + by_column[3])

    beside(
        in_step(*(gather_walk(ring, copies, own, out, cut, CHUNKS) for own, out, cut in arrays)),
        (sum_gains(), range(1, 9)),
    )
    copies.finish()
    for copy in kept:
        copy.wait()


def finish_grads(gate_up, down, small, gain_one, gain_two, number):
    ranks, owners = lax.axis_size("seq"), lax.axis_size("fsdp")
    blocks = (gate_up, down, small)
    lanes = gain_one.shape[1] // owners
    count = len(blocks) * gather_copies(CHUNKS) + 1 + 1 + 3 + 1 + 3

    def table(*shape):
        return pltpu.VMEM((*shape, 8, lanes), jnp.float32)

    return pl.pallas_call(
        finish_kernel,
        out_shape=[jax.ShapeDtypeStruct((ranks, *block.shape), block.dtype) for block in blocks]
        + [jax.ShapeDtypeStruct((8, lanes), jnp.float32)],
        in_specs=[ANYWHERE] * 3 + [VMEM] * 2,
        out_specs=[ANYWHERE] * 3 + [VMEM],
        scratch_shapes=[
            table(owners),
            table(owners),
            table(owners),
            table(owners),
            table(ranks // 2, owners),
            table(),
            table(),
            table(ranks // 2),
            pltpu.SemaphoreType.DMA((len(blocks),)),
        ]
        + semaphores(count),
        compiler_params=params(number, 32),
        name="finish_grads",
    )(*blocks, gain_one, gain_two)


def merge_lanes(first, second):
    half = first.shape[1] // 2
    low = lax.broadcasted_iota(jnp.int32, first.shape, 1) < half
    return (
        jnp.where(low, first, pltpu.roll(second, half, 1)),
        jnp.where(low, pltpu.roll(first, half, 1), second),
    )


def place_kernel(
    gate,
    up,
    down,
    query,
    pair,
    heads_low,
    heads_high,
    gate_out,
    up_out,
    down_out,
    query_out,
    key_out,
    value_out,
    heads_out,
):
    lanes = gate.shape[2]
    blocks = gate.shape[0] // 2
    for part, out in ((gate, gate_out), (up, up_out)):
        for index in range(blocks):
            low, high = merge_lanes(
                part[2 * index].astype(jnp.float32), part[2 * index + 1].astype(jnp.float32)
            )
            out[:, pl.ds(index * lanes, lanes)] = low
            out[:, pl.ds((blocks + index) * lanes, lanes)] = high
    key, value = merge_lanes(pair[0].astype(jnp.float32), pair[1].astype(jnp.float32))
    key_out[...] = key
    value_out[...] = value
    down_out[...] = down[0].astype(jnp.float32)
    query_out[...] = query[0].astype(jnp.float32)
    heads_out[:, :lanes] = heads_low[0].astype(jnp.float32)
    heads_out[:, lanes:] = heads_high[0].astype(jnp.float32)


def place_grads(gate_up, down, small):
    ranks, rows, both = gate_up.shape
    lanes = 128
    steps = both // 2 // lanes
    down_rows, width = down.shape[1:]
    query_cols = width // ranks
    first = query_cols // lanes
    assert steps == ranks and lanes == 2 * HEAD_SIZE and query_cols == 2 * lanes
    real = jnp.float32
    return pl.pallas_call(
        place_kernel,
        grid=(steps,),
        out_shape=[
            jax.ShapeDtypeStruct((rows, ranks * both // 2), real),
            jax.ShapeDtypeStruct((rows, ranks * both // 2), real),
            jax.ShapeDtypeStruct((ranks * down_rows, width), real),
            jax.ShapeDtypeStruct((rows, ranks * query_cols), real),
            jax.ShapeDtypeStruct((rows, ranks * HEAD_SIZE), real),
            jax.ShapeDtypeStruct((rows, ranks * HEAD_SIZE), real),
            jax.ShapeDtypeStruct((rows, width), real),
        ],
        in_specs=[
            pl.BlockSpec((ranks, rows, lanes), lambda i: (0, 0, i)),
            pl.BlockSpec((ranks, rows, lanes), lambda i: (0, 0, steps + i)),
            pl.BlockSpec((1, down_rows, width), lambda i: (i, 0, 0)),
            pl.BlockSpec((1, rows, query_cols), lambda i: (i, 0, 0)),
            pl.BlockSpec((2, rows, lanes), lambda i: (i // 2, 0, first)),
            pl.BlockSpec((1, rows, lanes), lambda i: (i, 0, first + 1)),
            pl.BlockSpec((1, rows, lanes), lambda i: (i, 0, first + 2)),
        ],
        out_specs=[
            pl.BlockSpec((rows, ranks * lanes), lambda i: (0, i)),
            pl.BlockSpec((rows, ranks * lanes), lambda i: (0, i)),
            pl.BlockSpec((down_rows, width), lambda i: (i, 0)),
            pl.BlockSpec((rows, query_cols), lambda i: (0, i)),
            pl.BlockSpec((rows, lanes), lambda i: (0, i // 2)),
            pl.BlockSpec((rows, lanes), lambda i: (0, i // 2)),
            pl.BlockSpec((rows, query_cols), lambda i: (0, i)),
        ],
        compiler_params=pltpu.CompilerParams(vmem_limit_bytes=32 * 2**20),
        name="place_grads",
    )(gate_up, gate_up, down, small, small, small, small)


def pick_kernel(
    query, key, value, gate, up, gain_one, gain_two, qkv_out, gate_out, up_out, wide, narrow, sems
):
    rank, ranks = lax.axis_index("seq"), lax.axis_size("seq")
    rows = query.shape[0]
    lanes = 128
    owners = wide.shape[1]
    pair = lax.div(rank, 2)
    odd = lax.rem(rank, 2)
    query_cols = query.shape[1] // ranks
    stride = gate.shape[1] // owners
    count = 0
    made = []

    def fetch(source, target):
        nonlocal count
        copy = pltpu.make_async_copy(source, target, sems.at[count])
        copy.start()
        made.append(copy)
        count += 1

    fetch(
        query.at[:, pl.ds(pl.multiple_of(rank * query_cols, lanes), query_cols)],
        qkv_out.at[pl.ds(0, rows), pl.ds(0, query_cols)],
    )
    for index, source in enumerate((key, value)):
        fetch(source.at[:, pl.ds(pl.multiple_of(pair * lanes, lanes), lanes)], narrow.at[index])
    for which, source in enumerate((gate, up)):
        for owner in range(owners):
            first = pl.multiple_of(owner * stride + pair * lanes, lanes)
            fetch(source.at[:, pl.ds(first, lanes)], wide.at[which, owner])
    line = lax.broadcasted_iota(jnp.int32, (16, rows), 0)
    first, second = (gain[...].astype(jnp.float32) for gain in (gain_one, gain_two))
    gains = jnp.where(line == 0, first, jnp.where(line == 1, second, 0.0))
    qkv_out[pl.ds(rows, 32)] = jnp.zeros((32, qkv_out.shape[1]), jnp.bfloat16)
    qkv_out[pl.ds(rows, 16), pl.ds(0, rows)] = gains.astype(jnp.bfloat16)
    for copy in made:
        copy.wait()

    def chosen(first, second):
        low, high = merge_lanes(first.astype(jnp.float32), second.astype(jnp.float32))
        return jnp.where(odd == 0, low, high).astype(jnp.bfloat16)

    qkv_out[pl.ds(0, rows), pl.ds(query_cols, lanes)] = chosen(narrow[0], narrow[1])
    for which, out in enumerate((gate_out, up_out)):
        for index in range(owners // 2):
            cols = pl.ds(index * lanes, lanes)
            out[:, cols] = chosen(wide[which, 2 * index], wide[which, 2 * index + 1])


def pick_columns(query, key, value, gate, up, gain_one, gain_two):
    rows, width = query.shape
    ranks, owners = lax.axis_size("seq"), lax.axis_size("fsdp")
    lanes = 128
    assert gate.shape[1] // owners // ranks == HEAD_SIZE == lanes // 2
    return pl.pallas_call(
        pick_kernel,
        out_shape=[
            jax.ShapeDtypeStruct((rows + 32, width // ranks + lanes), jnp.bfloat16),
            jax.ShapeDtypeStruct((rows, owners // 2 * lanes), jnp.bfloat16),
            jax.ShapeDtypeStruct((rows, owners // 2 * lanes), jnp.bfloat16),
        ],
        in_specs=[ANYWHERE] * 5 + [VMEM] * 2,
        out_specs=[VMEM] * 3,
        scratch_shapes=[
            pltpu.VMEM((2, owners, rows, lanes), jnp.bfloat16),
            pltpu.VMEM((2, rows, lanes), jnp.bfloat16),
            pltpu.SemaphoreType.DMA((2 * owners + 3,)),
        ],
        compiler_params=pltpu.CompilerParams(vmem_limit_bytes=32 * 2**20),
        name="pick_columns",
    )(query, key, value, gate, up, gain_one[None], gain_two[None])


def rotate_rows(first, second, cosine, sine):
    return jnp.concatenate([first * cosine - second * sine, second * cosine + first * sine], axis=0)


def bias_tile(start_row, key_tile, query_tile, diagonal):
    keys = key_tile * TILE + lax.broadcasted_iota(jnp.int32, (TILE, TILE), 0)
    seen = keys >= start_row
    if diagonal:
        queries = query_tile * TILE + lax.broadcasted_iota(jnp.int32, (TILE, TILE), 1)
        seen = seen & (keys <= queries)
    return jnp.where(seen, 0.0, NEG)


def attend_tiles(qkv, cosine, sine, starts, attended, lse, queries, keys, key_rows, bias):
    group = queries.shape[0] // HEAD_SIZE
    half = HEAD_SIZE // 2
    tiles = qkv.shape[1] // TILE
    cos, sin = cosine[...], sine[...]

    def rotated(first):
        return rotate_rows(
            qkv[pl.ds(first, half)].astype(jnp.float32),
            qkv[pl.ds(first + half, half)].astype(jnp.float32),
            cos,
            sin,
        ).astype(jnp.bfloat16)

    for head in range(group):
        queries[pl.ds(head * HEAD_SIZE, HEAD_SIZE)] = rotated(head * HEAD_SIZE) * jnp.bfloat16(0.125)
    keys[...] = rotated(group * HEAD_SIZE)
    key_rows[...] = keys[...].T
    for tile in range(tiles):
        lanes = pl.ds(tile * TILE, TILE)
        starts_here = starts[:, lanes]
        for low in range(tile + 1):
            bias[pl.ds(low * TILE, TILE)] = bias_tile(starts_here, low, tile, low == tile)
        count = (tile + 1) * TILE

        def one_head(head, _, lanes=lanes, count=count):
            rows = pl.ds(pl.multiple_of(head * HEAD_SIZE, HEAD_SIZE), HEAD_SIZE)
            scores = jnp.dot(
                key_rows[:count], queries[rows, lanes], preferred_element_type=jnp.float32
            )
            scores += bias[:count]
            highest = jnp.max(scores, axis=0, keepdims=True)
            weights = jnp.exp(scores - highest)
            total = jnp.sum(weights, axis=0, keepdims=True)
            out = jnp.dot(
                qkv[pl.ds((group + 1) * HEAD_SIZE, HEAD_SIZE), :count],
                weights.astype(jnp.bfloat16),
                preferred_element_type=jnp.float32,
            )
            attended[rows, lanes] = (out / total).astype(jnp.bfloat16)
            lse[head, :, lanes] = jnp.broadcast_to(highest + jnp.log(total), (8, TILE))
            return 0

        lax.fori_loop(0, group, one_head, 0)


def forward_kernel(
    qkv,
    cosine,
    sine,
    starts,
    cotangent,
    heads,
    gate,
    attended,
    lse,
    queries,
    keys,
    gathered,
    heads_all,
    gate_all,
    key_rows,
    bias,
    local,
    send,
    recv,
):
    ring = seq_ring()
    weights_ring, core, mate = fsdp_ring()
    swap, apart = transposed()
    greet_also(ring.peers + weights_ring.peers + [mate], swap, apart)
    last = send.shape[0] - 1

    def exchange():
        return pltpu.make_async_remote_copy(
            src_ref=heads,
            dst_ref=heads_all.at[core],
            send_sem=send.at[last],
            recv_sem=recv.at[last],
            device_id=swap,
            device_id_type=MESH,
        )

    def keep():
        return pltpu.make_async_copy(heads, heads_all.at[core], local.at[2])

    kept = [
        pltpu.make_async_copy(cotangent, gathered.at[ring.near[0]], local.at[0]),
        pltpu.make_async_copy(gate, gate_all.at[weights_ring.near[0]], local.at[1]),
    ]
    for copy in kept:
        copy.start()
    copies = Copies(send, recv)

    def heads_walk():
        @pl.when(apart)
        def _():
            exchange().start()

        @pl.when(jnp.logical_not(apart))
        def _():
            keep().start()

        attend_tiles(qkv, cosine, sine, starts, attended, lse, queries, keys, key_rows, bias)
        yield

        @pl.when(apart)
        def _():
            exchange().wait()

        @pl.when(jnp.logical_not(apart))
        def _():
            keep().wait()

        copy = copies.start(heads_all.at[core], heads_all.at[core], mate)
        yield
        copy.wait_recv()

    beside(
        gather_walk(
            ring, copies, cotangent, gathered, by_rows(cotangent.shape[0], CHUNKS), CHUNKS
        ),
        (
            gather_walk(
                weights_ring,
                copies,
                gate,
                gate_all,
                by_rows(gate.shape[0], CHUNKS),
                CHUNKS,
                True,
                mate,
            ),
            BESIDE_GATHER,
        ),
        (heads_walk(), (0, 6, 10)),
    )
    copies.finish()
    for copy in kept:
        copy.wait()


def attend(qkv, cosine, sine, starts, cotangent, heads, gate, group, number):
    length = qkv.shape[1]
    rows, width = cotangent.shape
    ranks = lax.axis_size("seq")
    return pl.pallas_call(
        forward_kernel,
        out_shape=[
            jax.ShapeDtypeStruct((group * HEAD_SIZE, length), jnp.bfloat16),
            jax.ShapeDtypeStruct((group, 8, length), jnp.float32),
            jax.ShapeDtypeStruct((group * HEAD_SIZE, length), jnp.bfloat16),
            jax.ShapeDtypeStruct((HEAD_SIZE, length), jnp.bfloat16),
            jax.ShapeDtypeStruct((ranks, rows, width), jnp.bfloat16),
            jax.ShapeDtypeStruct((2, *heads.shape), jnp.bfloat16),
            jax.ShapeDtypeStruct((lax.axis_size("fsdp"), *gate.shape), jnp.bfloat16),
        ],
        in_specs=[VMEM] * 4 + [ANYWHERE] * 3,
        out_specs=[VMEM] * 4 + [ANYWHERE] * 3,
        scratch_shapes=[
            pltpu.VMEM((length, HEAD_SIZE), jnp.bfloat16),
            pltpu.VMEM((length, TILE), jnp.float32),
            pltpu.SemaphoreType.DMA((3,)),
        ]
        + semaphores(gather_copies(CHUNKS) + gather_copies(CHUNKS, True) + 2),
        compiler_params=params(number, 40),
        name="attend",
    )(qkv, cosine, sine, starts, cotangent, heads, gate)


def back_tiles(
    qkv,
    queries,
    keys,
    attended,
    lse,
    grads,
    cosine,
    sine,
    starts,
    out,
    key_rows,
    value_rows,
    query_rows,
    grad_rows,
    row_dots,
    key_grad,
    value_grad,
    query_grad,
    bias,
):
    group = queries.shape[0] // HEAD_SIZE
    half = HEAD_SIZE // 2
    tiles = qkv.shape[1] // TILE
    key_rows[...] = keys[...].T
    value_rows[...] = qkv[pl.ds((group + 1) * HEAD_SIZE, HEAD_SIZE)].T
    for head in range(group):
        rows = pl.ds(head * HEAD_SIZE, HEAD_SIZE)
        query_rows[head] = queries[rows].T
        grad_rows[head] = grads[rows].T
        row_dots[head] = jnp.broadcast_to(
            jnp.sum(
                grads[rows].astype(jnp.float32) * attended[rows].astype(jnp.float32),
                axis=0,
                keepdims=True,
            ),
            row_dots.shape[1:],
        )
    key_grad[...] = jnp.zeros_like(key_grad)
    value_grad[...] = jnp.zeros_like(value_grad)
    for tile in range(tiles):
        lanes = pl.ds(tile * TILE, TILE)
        starts_here = starts[:, lanes]
        for low in range(tile + 1):
            bias[low] = bias_tile(starts_here, low, tile, low == tile)

        def one_head(head, _, lanes=lanes, tile=tile):
            rows = pl.ds(pl.multiple_of(head * HEAD_SIZE, HEAD_SIZE), HEAD_SIZE)
            query, grad = queries[rows, lanes], grads[rows, lanes]
            query_row, grad_row = query_rows[head, lanes], grad_rows[head, lanes]
            lse_row = lse[head, 0:1, lanes]
            dot_row = row_dots[head, 0:1, lanes]
            total = jnp.zeros((HEAD_SIZE, TILE), jnp.float32)
            for low in range(tile + 1):
                part = pl.ds(low * TILE, TILE)
                scores = jnp.dot(key_rows[part], query, preferred_element_type=jnp.float32)
                probs = jnp.exp(scores + bias[low] - lse_row)
                grad_probs = jnp.dot(value_rows[part], grad, preferred_element_type=jnp.float32)
                grad_scores = (probs * (grad_probs - dot_row)).astype(jnp.bfloat16)
                value_grad[part] += jnp.dot(
                    probs.astype(jnp.bfloat16), grad_row, preferred_element_type=jnp.float32
                )
                key_grad[part] += jnp.dot(
                    grad_scores, query_row, preferred_element_type=jnp.float32
                )
                total += jnp.dot(keys[:, part], grad_scores, preferred_element_type=jnp.float32)
            query_grad[rows, lanes] = total * 0.125
            return 0

        lax.fori_loop(0, group, one_head, 0)
    cos, sin = cosine[...], sine[...]
    for head in range(group):
        first = head * HEAD_SIZE
        out[pl.ds(first, HEAD_SIZE)] = rotate_rows(
            query_grad[pl.ds(first, half)], query_grad[pl.ds(first + half, half)], cos, -sin
        ).astype(jnp.bfloat16)
    turned = key_grad[...].T
    out[pl.ds(group * HEAD_SIZE, HEAD_SIZE)] = rotate_rows(
        turned[:half], turned[half:], cos, -sin
    ).astype(jnp.bfloat16)
    out[pl.ds((group + 1) * HEAD_SIZE, HEAD_SIZE)] = value_grad[...].T.astype(jnp.bfloat16)


def backward_kernel(*refs):
    ins, (part_of, middle, grads), (out, layer_out, grads_share) = (
        refs[:9],
        refs[9:12],
        refs[12:15],
    )
    scratch, (fetches, send, recv), (own, other) = refs[15:24], refs[24:27], refs[27:29]
    bufs = refs[29:]
    ring = seq_ring()
    weights_ring, core, mate = fsdp_ring()
    greet(ring.peers + weights_ring.peers + [mate])
    copies = Copies(send, recv)

    def compute():
        back_tiles(*ins, out, *scratch)
        yield

    def done(rows_of, total):
        layer_out[rows_of] = (middle[rows_of] + total).astype(jnp.bfloat16)

    def owned(rows_of, total):
        grads_share[rows_of] = total.astype(jnp.bfloat16)

    pieces = ((lambda place, which: grads.at[place, which], lambda ref: ref),)
    beside(
        reduce_walk(ring, copies, part_of, bufs[7:], middle.shape[0], CHUNKS, done),
        (
            owners_walk(
                weights_ring,
                mate,
                copies,
                fetched(copies, core, mate, pieces, own, other, fetches),
                own,
                other,
                bufs[:7],
                grads_share.shape[0],
                owned,
            ),
            (0,) * 8 + (0, 0, 1, 2, 8, 8, 8, 8, 12, 12, 14, 14),
        ),
        (compute(), (0,)),
    )
    copies.finish()


def attend_back(
    qkv,
    queries,
    keys,
    attended,
    lse,
    grads,
    cosine,
    sine,
    starts,
    partial,
    middle,
    down_grad,
    number,
):
    length = qkv.shape[1]
    group = queries.shape[0] // HEAD_SIZE
    tiles = length // TILE
    rows, width = middle.shape
    ranks, owners = lax.axis_size("seq"), lax.axis_size("fsdp")
    places = owners // 2
    grad_rows = down_grad.shape[1] // 2
    return pl.pallas_call(
        backward_kernel,
        out_shape=[
            jax.ShapeDtypeStruct(qkv.shape, jnp.bfloat16),
            jax.ShapeDtypeStruct((rows, width), jnp.bfloat16),
            jax.ShapeDtypeStruct((grad_rows, width), jnp.bfloat16),
        ],
        in_specs=[VMEM] * 11 + [ANYWHERE],
        out_specs=[VMEM] * 3,
        scratch_shapes=[
            pltpu.VMEM((length, HEAD_SIZE), jnp.bfloat16),
            pltpu.VMEM((length, HEAD_SIZE), jnp.bfloat16),
            pltpu.VMEM((group, length, HEAD_SIZE), jnp.bfloat16),
            pltpu.VMEM((group, length, HEAD_SIZE), jnp.bfloat16),
            pltpu.VMEM((group, 8, length), jnp.float32),
            pltpu.VMEM((length, HEAD_SIZE), jnp.float32),
            pltpu.VMEM((length, HEAD_SIZE), jnp.float32),
            pltpu.VMEM((group * HEAD_SIZE, length), jnp.float32),
            pltpu.VMEM((tiles, TILE, TILE), jnp.float32),
        ]
        + [pltpu.SemaphoreType.DMA((places,))]
        + semaphores(reduce_copies(CHUNKS) + OWNERS_COPIES + places)
        + owners_scratch(places, grad_rows, width)
        + reduce_scratch(rows, width),
        compiler_params=params(number, 48),
        name="attend_back",
    )(
        qkv,
        queries,
        keys,
        attended,
        lse,
        grads,
        cosine,
        sine,
        starts,
        partial,
        middle,
        down_grad.reshape(places, 2, grad_rows, width),
    )


def contract_rows(left, right):
    return jnp.einsum("ta,tb->ab", left, right, preferred_element_type=jnp.float32)


def contract_cols(left, right):
    return jnp.einsum("ta,ba->tb", left, right, preferred_element_type=jnp.float32)


def matmul(left, right):
    return jnp.dot(left, right, preferred_element_type=jnp.float32)


def shards(
    tokens,
    segment_ids,
    query_weight,
    key_matrix,
    value_matrix,
    output_weight,
    gate_weight,
    up_weight,
    down_weight,
    attention_gain,
    feed_gain,
    cotangent,
):
    rank = lax.axis_index("seq")
    owner = lax.axis_index("fsdp")
    ranks = lax.axis_size("seq")
    owners = lax.axis_size("fsdp")
    rows, width = query_weight.shape
    kv_cols = key_matrix.shape[1] // ranks
    q_cols = width // ranks
    group = q_cols // kv_cols
    ff = gate_weight.shape[1]
    ff_chunk = ff // owners // ranks
    segment_row = segment_ids[0]
    length = segment_row.shape[0]

    qkv_in, gate_in, up_in = pick_columns(
        query_weight, key_matrix, value_matrix, gate_weight, up_weight, attention_gain, feed_gain
    )
    whole, qkv_got = gather_first(tokens[0], qkv_in, 0)
    qkv_all = qkv_got[:, :rows].reshape(owners * rows, -1)
    gain_one = qkv_got[:, rows, :rows].reshape(1, -1).astype(jnp.float32)
    gain_two = qkv_got[:, rows + 1, :rows].reshape(1, -1).astype(jnp.float32)
    ff_local = owners * ff_chunk
    down_in = lax.dynamic_slice_in_dim(down_weight, rank * ff_chunk, ff_chunk, 0)

    starts = (jnp.arange(length, dtype=jnp.int32) - positions_of(segment_row))[None]
    cosine, sine = (table.T for table in angles_of(segment_row, HEAD_SIZE))
    whole = whole.reshape(length, width).astype(jnp.float32)
    hidden_one = (whole * lax.rsqrt(mean_square(whole) + EPS) * gain_one).astype(jnp.bfloat16)
    qkv = jnp.einsum("tm,mc->ct", hidden_one, qkv_all, preferred_element_type=jnp.float32)
    qkv = qkv.astype(jnp.bfloat16)
    attended, lse, queries, keys, grad_out, output_all, gate_all = attend(
        qkv, cosine, sine, starts, cotangent[0], output_weight, gate_in, group, 1
    )
    gate_all = gate_all.reshape(width, ff_local)
    grad_out = grad_out.reshape(length, width)
    output_all = output_all.reshape(q_cols, width)
    middle, hidden_two, up_all, down_all = add_branch(
        contract_rows(attended, output_all).astype(jnp.bfloat16),
        tokens[0],
        gain_two,
        up_in,
        down_in,
        2,
    )
    up_all = up_all.reshape(width, ff_local)
    down_all = down_all.reshape(ff_local, width)
    hidden_two = hidden_two.reshape(length, width)

    gate = matmul(hidden_two, gate_all)
    up_proj = matmul(hidden_two, up_all)
    sig_gate = jax.nn.sigmoid(gate)
    silu_gate = gate * sig_gate
    act = (silu_gate * up_proj).astype(jnp.bfloat16)
    grad_act = contract_cols(grad_out, down_all)
    grad_gate = (grad_act * up_proj * (sig_gate * (1.0 + gate * (1.0 - sig_gate)))).astype(
        jnp.bfloat16
    )
    grad_up = (grad_act * silu_gate).astype(jnp.bfloat16)
    back_two = contract_cols(grad_gate, gate_all) + contract_cols(grad_up, up_all)
    grad_middle, grad_gain_two, grad_branch, gate_up_share, down_grad, layer_part = back_to_middle(
        back_two.astype(jnp.bfloat16),
        middle,
        gain_two,
        cotangent[0],
        hidden_two,
        grad_gate,
        grad_up,
        act,
        grad_out,
        down_all,
        3,
    )
    grad_branch = grad_branch.reshape(length, width)

    grad_attended = jnp.einsum(
        "tm,fm->ft", grad_branch, output_all, preferred_element_type=jnp.float32
    ).astype(jnp.bfloat16)
    qkv_grads, layer_out, down_share = attend_back(
        qkv,
        queries,
        keys,
        attended,
        lse,
        grad_attended,
        cosine,
        sine,
        starts,
        layer_part,
        middle,
        down_grad,
        4,
    )
    heads_grad = matmul(attended, grad_branch).astype(jnp.bfloat16)
    qkv_grad = jnp.einsum(
        "tm,ct->mc", hidden_one, qkv_grads, preferred_element_type=jnp.float32
    ).astype(jnp.bfloat16)
    grad_inputs, grad_gain_one, small_share = back_to_tokens(
        jnp.einsum("ct,mc->tm", qkv_grads, qkv_all, preferred_element_type=jnp.float32).astype(
            jnp.bfloat16
        ),
        tokens[0],
        gain_one,
        grad_middle,
        qkv_grad,
        heads_grad,
        5,
    )
    *gathered, gains = finish_grads(
        gate_up_share, down_share, small_share, grad_gain_one, grad_gain_two, 6
    )
    gate_grad, up_grad, down_total, query_grad, key_grad, value_grad, heads_total = place_grads(
        *gathered
    )
    return (
        layer_out[None],
        grad_inputs[None],
        query_grad,
        key_grad,
        value_grad,
        heads_total,
        gate_grad,
        up_grad,
        down_total,
        gains[0],
        gains[1],
    )


def solution(mesh):
    placed = (
        P("fsdp", "seq", None),
        P("fsdp", None),
        P("fsdp", None),
        P("fsdp", None),
        P("fsdp", None),
        P("fsdp", None),
        P("fsdp", None),
        P("fsdp", None),
        P("fsdp", None),
        P("fsdp"),
        P("fsdp"),
        P("fsdp", "seq", None),
    )
    return jax.shard_map(
        shards,
        mesh=mesh,
        in_specs=placed,
        out_specs=(
            P("fsdp", "seq", None),
            P("fsdp", "seq", None),
            P("fsdp", None),
            P("fsdp", None),
            P("fsdp", None),
            P("fsdp", None),
            P("fsdp", None),
            P("fsdp", None),
            P("fsdp", None),
            P("fsdp"),
            P("fsdp"),
        ),
        check_vma=False,
    )
```

```python
import math

import jax
import jax.numpy as jnp
from jax import lax
from jax.experimental import pallas as pl
from jax.experimental.pallas import tpu as pltpu
from jax.sharding import PartitionSpec as P

HEAD_SIZE = 64
EPS = 1e-05
ROPE_BASE = 500000.0
NEG = -1e30


def rope_freqs(head_dim):
    half_dim = head_dim // 2
    table = []
    for index in range(half_dim):
        inverse = 1.0 / ROPE_BASE ** (index * 2.0 / head_dim)
        wavelen = 2.0 * math.pi / inverse
        blend = (8192.0 / wavelen - 1.0) / 3.0
        mixed = (1.0 - blend) * inverse / 32.0 + blend * inverse
        entry = inverse if wavelen < 2048.0 else inverse / 32.0 if wavelen > 8192.0 else mixed
        table.append(entry)
    return jnp.asarray(table, dtype=jnp.float32)


def positions_of(segment_row):
    indices = jnp.arange(segment_row.shape[0], dtype=jnp.int32)
    begins = jnp.concatenate(
        [jnp.ones((1,), dtype=jnp.int32), (segment_row[1:] != segment_row[:-1]).astype(jnp.int32)]
    )
    starts_at = lax.cummax(jnp.where(begins > 0, indices, 0), axis=0)
    return indices - starts_at


def angles_of(segment_row, head_dim):
    positions = positions_of(segment_row)
    phase = positions.astype(jnp.float32)[:, None] * rope_freqs(head_dim)[None, :]
    return (jnp.cos(phase), jnp.sin(phase))


MESH = pl.DeviceIdType.MESH
CHUNKS = 4
TILE = 256


class Ring:
    def __init__(self, place, count, index_of, device_of):
        side = count // 2
        self.place = place
        row, col = lax.div(place, side), lax.rem(place, side)

        def at(which, step):
            return index_of(which * side + lax.rem(col + step, side))

        self.near = [at(row, step) for step in range(side)]
        self.far = [at(1 - row, step) for step in range(side)]
        self.right = device_of(self.near[1])
        self.left = device_of(self.near[3])
        self.partner = device_of(self.far[0])
        self.peers = [self.right, self.left, self.partner]
        self.remote = [device_of(index) for index in (self.near[2], *self.far[1:])]
        self.device_of = device_of


def seq_ring():
    rank, owner = lax.axis_index("seq"), lax.axis_index("fsdp")
    return Ring(rank, lax.axis_size("seq"), lambda place: place, lambda index: (index, owner))


def fsdp_ring():
    rank, owner = lax.axis_index("seq"), lax.axis_index("fsdp")
    core = lax.rem(owner, 2)
    ring = Ring(
        lax.div(owner, 2),
        lax.axis_size("fsdp") // 2,
        lambda place: 2 * place + core,
        lambda index: (rank, index),
    )
    return ring, core, (rank, owner + 1 - 2 * core)


def greet(peers):
    barrier = pltpu.get_barrier_semaphore()
    for peer in peers:
        pl.semaphore_signal(barrier, inc=1, device_id=peer, device_id_type=MESH)
    pl.semaphore_wait(barrier, len(peers))


def in_step(*walks):
    left = list(walks)
    while left:
        left = [walk for walk in left if next(walk, walk) is not walk]
        yield


def beside(main, *sides):
    sides = [(walk, list(places)) for walk, places in sides]
    step = 0
    for _ in main:
        for walk, places in sides:
            while places and places[0] <= step:
                places.pop(0)
                next(walk, None)
        step += 1
    for _ in in_step(*(walk for walk, _ in sides)):
        pass


class Copies:
    def __init__(self, send, recv):
        self.send, self.recv = send, recv
        self.made = []

    def start(self, source, target, peer):
        number = len(self.made)
        copy = pltpu.make_async_remote_copy(
            src_ref=source,
            dst_ref=target,
            send_sem=self.send.at[number],
            recv_sem=self.recv.at[number],
            device_id=peer,
            device_id_type=MESH,
        )
        copy.start()
        self.made.append(copy)
        return copy

    def finish(self):
        for copy in self.made:
            copy.wait_send()


def by_rows(rows, chunks):
    size = rows // chunks
    return lambda ref, index: ref.at[pl.ds(index * size, size)]


def by_columns(columns, chunks):
    size = columns // chunks
    return lambda ref, index: ref.at[:, pl.ds(index * size, size)]


def chunk_rows(rows, index):
    size = rows // CHUNKS
    return pl.ds(index * size, size)


def exchange_all(ring, copies, piece, target):
    made = []
    for index in (*ring.far[1:], ring.near[2], ring.far[0], ring.near[1], ring.near[3]):
        made.append(copies.start(piece(index), target, ring.device_of(index)))
    return made


def gather_walk(ring, copies, own, out, cut, chunks, deep=False, mate=None):
    me, right, opposite, left = ring.near
    partner, far_right, _, far_left = ring.far
    half = chunks // 2
    passed = []

    def share(place, index):
        if mate is not None:
            block = cut(out.at[place], index)
            passed.append(copies.start(block, block, mate))

    to_right, to_left, to_far, on = {}, {}, {}, {}
    for step in range(chunks):
        back = chunks - 1 - step
        if not deep:
            to_far[step] = copies.start(cut(own, step), cut(out.at[me], step), ring.partner)
        to_right[step] = copies.start(cut(own, step), cut(out.at[me], step), ring.right)
        to_left[back] = copies.start(cut(own, back), cut(out.at[me], back), ring.left)
        if mate is not None:
            passed.append(copies.start(cut(own, step), cut(out.at[me], step), mate))
    yield
    if deep:
        for step in range(chunks):
            to_far[step] = copies.start(cut(own, step), cut(out.at[me], step), ring.partner)
        yield
    for step in range(half):
        back = chunks - 1 - step
        to_right[step].wait_recv()
        block = cut(out.at[left], step)
        on[step] = copies.start(block, block, ring.right)
        share(left, step)
        to_left[back].wait_recv()
        block = cut(out.at[right], back)
        on[back] = copies.start(block, block, ring.left)
        share(right, back)
        yield
    far_on, rest = {}, []
    for step in range(chunks):
        to_far[step].wait_recv()
        block = cut(out.at[partner], step)
        far_on[0, step] = copies.start(block, block, ring.right)
        far_on[1, step] = copies.start(block, block, ring.left)
        share(partner, step)
        yield
    if deep:
        for step in range(half):
            back = chunks - 1 - step
            far_on[0, step].wait_recv()
            block = cut(out.at[far_left], step)
            rest.append((step, copies.start(block, block, ring.right)))
            share(far_left, step)
            far_on[1, back].wait_recv()
            block = cut(out.at[far_right], back)
            rest.append((back, copies.start(block, block, ring.left)))
            share(far_right, back)
            yield
    for step in range(half):
        for index in (step, chunks - 1 - step):
            on[index].wait_recv()
            if not deep:
                block = cut(out.at[opposite], index)
                rest.append((index, copies.start(block, block, ring.partner)))
            share(opposite, index)
        yield
    for step in range(half):
        back = chunks - 1 - step
        to_right[back].wait_recv()
        share(left, back)
        to_left[step].wait_recv()
        share(right, step)
        if deep:
            far_on[0, back].wait_recv()
            share(far_left, back)
            far_on[1, step].wait_recv()
            share(far_right, step)
        yield
    if not deep:
        for copy in far_on.values():
            copy.wait_recv()
    for index, copy in rest:
        copy.wait_recv()
        share(ring.far[2], index)
    yield
    for copy in passed:
        copy.wait_recv()


def gather_copies(chunks, mate=False):
    return 7 * chunks + (8 * chunks if mate else 0)


def reduce_walk(ring, copies, part_of, bufs, cut, chunks, done, ready=None):
    me, right, opposite, left = ring.near
    partner, far_right, far_opposite, far_left = ring.far
    from_left, from_right, from_far, mid, end_left, end_right, end_far = bufs
    half = chunks // 2

    def wide(ref, index):
        return cut(ref, index)[...].astype(jnp.float32)

    def keep(ref, index, value):
        cut(ref, index)[...] = value.astype(jnp.bfloat16)

    def send(block, index, target, device):
        return copies.start(cut(block, index), cut(target, index), device)

    order = [x for step in range(half) for x in (step, chunks - 1 - step)]
    one_right, one_left, one_far, last_right, last_left, last_far = ({} for _ in range(6))
    if ready is None:
        for index in order:
            one_far[index] = send(part_of.at[far_opposite], index, from_far, ring.partner)
            one_right[index] = send(part_of.at[far_right], index, from_left, ring.right)
            one_left[index] = send(part_of.at[far_left], index, from_right, ring.left)
    else:
        ready(far_right, far_left)
        for index in order:
            one_right[index] = send(part_of.at[far_right], index, from_left, ring.right)
            one_left[index] = send(part_of.at[far_left], index, from_right, ring.left)
        yield
        ready(far_opposite, right)
        for index in order:
            one_far[index] = send(part_of.at[far_opposite], index, from_far, ring.partner)
    for index in range(half):
        last_right[index] = send(part_of.at[right], index, end_left, ring.right)
    if ready is not None:
        yield
        ready(left, opposite)
    for index in range(half):
        back = chunks - 1 - index
        last_left[back] = send(part_of.at[left], back, end_right, ring.left)
    if ready is not None:
        yield
        ready(partner, me)
    yield
    two = {}
    for index in order:
        one_far[index].wait_recv()
        keep(from_far, index, wide(from_far, index) + wide(part_of.at[opposite], index))
        two[index] = send(from_far, index, mid, ring.left if index < half else ring.right)
        yield
    for index in order:
        one_right[index].wait_recv()
        one_left[index].wait_recv()
        total = wide(from_left, index) + wide(from_right, index)
        keep(from_left, index, total + wide(part_of.at[partner], index))
        last_far[index] = send(from_left, index, end_far, ring.partner)
        yield
    for index in order:
        two[index].wait_recv()
        if index < half:
            keep(mid, index, wide(mid, index) + wide(part_of.at[left], index))
            last_left[index] = send(mid, index, end_right, ring.left)
        else:
            keep(mid, index, wide(mid, index) + wide(part_of.at[right], index))
            last_right[index] = send(mid, index, end_left, ring.right)
        yield
    for index in order:
        last_far[index].wait_recv()
        last_left[index].wait_recv()
        last_right[index].wait_recv()
        total = wide(part_of.at[me], index) + wide(end_left, index)
        done(index, total + wide(end_right, index) + wide(end_far, index))
        yield


def reduce_copies(chunks):
    return 3 * chunks + 2 * chunks + chunks + chunks


def owners_walk(ring, mate, copies, produce, own, other, bufs, rows, done):
    mids, from_lefts, from_rights, from_far = bufs[:2], bufs[2:4], bufs[4:6], bufs[6]
    half = rows // 2
    low, high = pl.ds(0, half), pl.ds(half, half)
    near, far = ([lax.div(index, 2) for index in row] for row in (ring.near, ring.far))
    order = [far[2], near[2], far[1], far[3], near[1], near[3], far[0], near[0]]
    awaited = []

    def wide(ref):
        return ref.astype(jnp.float32)

    def add(*numbers):
        for number in numbers:
            for wait in awaited[number]:
                wait()
            place = order[number]
            own[place] = (wide(own[place]) + wide(other[place])).astype(jnp.bfloat16)

    def make(number):
        awaited.append(produce(order[number]))

    make(0)
    yield
    make(1)
    yield
    add(0, 1)
    on = []
    for which, row in enumerate((far, near)):
        block = own.at[row[2]]
        on.append(copies.start(block.at[low], mids[which].at[low], ring.left))
        on.append(copies.start(block.at[high], mids[which].at[high], ring.right))
    yield
    ends = []
    for which, row in enumerate((far, near)):
        make(2 + 2 * which)
        yield
        make(3 + 2 * which)
        yield
        add(2 + 2 * which, 3 + 2 * which)
        ends.append(copies.start(own.at[row[1], low], from_lefts[which].at[low], ring.right))
        ends.append(copies.start(own.at[row[3], high], from_rights[which].at[high], ring.left))
        yield
    for which, row in enumerate((far, near)):
        mid = mids[which]
        on[2 * which].wait_recv()
        mid[low] = (wide(mid[low]) + wide(own[row[3], low])).astype(jnp.bfloat16)
        ends.append(copies.start(mid.at[low], from_rights[which].at[low], ring.left))
        yield
        on[2 * which + 1].wait_recv()
        mid[high] = (wide(mid[high]) + wide(own[row[1], high])).astype(jnp.bfloat16)
        ends.append(copies.start(mid.at[high], from_lefts[which].at[high], ring.right))
        yield
    make(6)
    yield
    make(7)
    yield
    add(6, 7)
    yield
    last = []
    for number in (0, 4, 1, 5):
        ends[number].wait_recv()
    for rows_of in (low, high):
        total = (
            wide(from_lefts[0][rows_of])
            + wide(from_rights[0][rows_of])
            + wide(own[far[0], rows_of])
        )
        from_lefts[0][rows_of] = total.astype(jnp.bfloat16)
        last.append(copies.start(from_lefts[0].at[rows_of], from_far.at[rows_of], ring.partner))
    yield
    for number in (2, 6, 3, 7):
        ends[number].wait_recv()
    yield
    for rows_of, copy in zip((low, high), last):
        copy.wait_recv()
        done(
            rows_of,
            wide(from_lefts[1][rows_of])
            + wide(from_rights[1][rows_of])
            + wide(own[near[0], rows_of])
            + wide(from_far[rows_of]),
        )
        yield


OWNERS_COPIES = 4 + 4 + 4 + 2


def owners_scratch(places, rows, width):
    return [pltpu.VMEM((places, rows, width), jnp.bfloat16) for _ in range(2)] + [
        pltpu.VMEM((rows, width), jnp.bfloat16) for _ in range(7)
    ]


def fetched(copies, core, mate, pieces, own, other, sems):
    count = 0

    def produce(place):
        nonlocal count
        waits = []
        for piece, part in pieces:
            sent = copies.start(piece(place, 1 - core), part(other.at[place]), mate)
            copy = pltpu.make_async_copy(piece(place, core), part(own.at[place]), sems.at[count])
            copy.start()
            count += 1
            waits += [sent.wait_recv, copy.wait]
        return waits

    return produce


def reduce_scratch(rows, width):
    return [pltpu.VMEM((rows, width), jnp.bfloat16) for _ in range(7)]


def semaphores(count):
    return [pltpu.SemaphoreType.DMA((count,)), pltpu.SemaphoreType.DMA((count,))]


def params(number, limit):
    return pltpu.CompilerParams(
        collective_id=number, has_side_effects=True, vmem_limit_bytes=limit * 2**20
    )


VMEM = pl.BlockSpec(memory_space=pltpu.VMEM)
ANYWHERE = pl.BlockSpec(memory_space=pl.ANY)


SMALL_BESIDE = (0, 2, 2, 3, 6, 6, 6, 6, 8, 8, 9, 9, 10, 10, 11)
LARGE_BESIDE = (0, 1, 2, 3, 5, 6, 7, 7, 8, 8, 8, 8, 9, 9, 10)


def weight_walk(ring, copies, own, out, mate):
    return gather_walk(ring, copies, own, out, by_rows(own.shape[0], CHUNKS), CHUNKS, True, mate)


def gather_first(tokens, qkv, gate, number):
    blocks = (tokens, qkv, gate)
    ranks, owners = lax.axis_size("seq"), lax.axis_size("fsdp")

    def kernel(tokens, qkv, gate, tokens_all, qkv_all, gate_all, local, send, recv):
        ring = seq_ring()
        weights_ring, _, mate = fsdp_ring()
        greet(ring.peers + weights_ring.peers + [mate])
        copies = Copies(send, recv)
        here = weights_ring.near[0]
        kept = [
            pltpu.make_async_copy(tokens, tokens_all.at[ring.near[0]], local.at[0]),
            pltpu.make_async_copy(qkv, qkv_all.at[here], local.at[1]),
            pltpu.make_async_copy(gate, gate_all.at[here], local.at[2]),
        ]
        for copy in kept:
            copy.start()
        rows, weight_rows = tokens.shape[0], qkv.shape[0]
        beside(
            gather_walk(ring, copies, tokens, tokens_all, by_rows(rows, CHUNKS), CHUNKS),
            (
                gather_walk(
                    weights_ring, copies, qkv, qkv_all, by_rows(weight_rows, 2), 2, True, mate
                ),
                (0, 0, 1, 2, 2, 4, 6, 6, 8),
            ),
            (weight_walk(weights_ring, copies, gate, gate_all, mate), SMALL_BESIDE),
        )
        copies.finish()
        for copy in kept:
            copy.wait()

    count = gather_copies(CHUNKS) + gather_copies(2, True) + gather_copies(CHUNKS, True)
    return pl.pallas_call(
        kernel,
        out_shape=[
            jax.ShapeDtypeStruct((size, *block.shape), jnp.bfloat16)
            for size, block in zip((ranks, owners, owners), blocks)
        ],
        in_specs=[ANYWHERE] * 3,
        out_specs=[ANYWHERE] * 3,
        scratch_shapes=[pltpu.SemaphoreType.DMA((3,))] + semaphores(count),
        compiler_params=params(number, 32),
        name="gather_first",
    )(*blocks)


def mean_square(values):
    return jnp.mean(values * values, axis=-1, keepdims=True)


PRODUCT = 512


def product(left, right, store, size=PRODUCT):
    def columns(index, _):
        cols = pl.ds(pl.multiple_of(index * size, size), size)
        store(cols, jnp.dot(left, right[:, cols], preferred_element_type=jnp.float32))
        return 0

    lax.fori_loop(0, right.shape[1] // size, columns, 0)


def two_blocks(ref, rows, first, second):
    return jnp.concatenate(
        [ref[pl.ds(pl.multiple_of(index * rows, rows), rows)] for index in (first, second)], axis=0
    )


def split_store(for_mate, own, place, core):
    def store(cols, value):
        rows = value.shape[0] // 2
        first = core == 0
        theirs = jnp.where(first, value[rows:], value[:rows])
        for_mate[place, :, cols] = theirs.astype(jnp.bfloat16)
        ours = jnp.where(first, value[:rows], value[rows:])
        own[place, :, cols] = ours.astype(jnp.bfloat16)

    return store


def branch_kernel(
    attended,
    tokens,
    gain,
    weight,
    up,
    down,
    middle,
    hidden,
    up_all,
    down_all,
    attended_here,
    block,
    got,
    weight_here,
    local,
    send,
    recv,
):
    ring = seq_ring()
    weights_ring, _, mate = fsdp_ring()
    rows = tokens.shape[0]
    greet(ring.peers + ring.remote + weights_ring.peers + [mate])
    copies = Copies(send, recv)
    me = ring.near[0]

    def lanes_of(index):
        return attended.at[:, pl.ds(pl.multiple_of(index * rows, rows), rows)]

    arriving = exchange_all(ring, copies, lanes_of, got.at[me])
    kept = [
        pltpu.make_async_copy(up, up_all.at[weights_ring.near[0]], local.at[0]),
        pltpu.make_async_copy(down, down_all.at[weights_ring.near[0]], local.at[1]),
        pltpu.make_async_copy(block, hidden.at[me], local.at[2]),
    ]
    kept[0].start()
    kept[1].start()
    load = pltpu.make_async_copy(weight, weight_here, local.at[3])
    load.start()
    mine = pltpu.make_async_copy(lanes_of(me), got.at[me], local.at[4])
    mine.start()

    def walk():
        yield
        mine.wait()
        load.wait()
        for copy in arriving:
            copy.wait_recv()
        attended_here[...] = got[...].reshape(attended_here.shape)
        turned = attended_here[...].T

        def store(cols, value):
            middle[:, cols] = tokens[:, cols].astype(jnp.float32) + value

        product(turned, weight_here, store)
        values = middle[...]
        factor = lax.rsqrt(mean_square(values) + EPS)
        block[...] = (values * factor * gain[...]).astype(jnp.bfloat16)
        kept[2].start()
        yield from gather_walk(ring, copies, block, hidden, by_rows(rows, CHUNKS), CHUNKS)

    places = (0, 0, 0, 0, 1, 1, 1, 1, 2, 3, 5, 6, 7, 8, 9)
    beside(
        walk(),
        (weight_walk(weights_ring, copies, up, up_all, mate), places),
        (weight_walk(weights_ring, copies, down, down_all, mate), places),
    )
    copies.finish()
    for copy in kept:
        copy.wait()


def add_branch(attended, tokens, gain, weight, up, down, number):
    rows, width = tokens.shape
    ranks, owners = lax.axis_size("seq"), lax.axis_size("fsdp")
    features = attended.shape[0]
    count = ranks - 1 + gather_copies(CHUNKS) + 2 * gather_copies(CHUNKS, True)
    return pl.pallas_call(
        branch_kernel,
        out_shape=[
            jax.ShapeDtypeStruct((rows, width), jnp.float32),
            jax.ShapeDtypeStruct((ranks, rows, width), jnp.bfloat16),
            jax.ShapeDtypeStruct((owners, *up.shape), jnp.bfloat16),
            jax.ShapeDtypeStruct((owners, *down.shape), jnp.bfloat16),
            jax.ShapeDtypeStruct((ranks * features, rows), jnp.bfloat16),
        ],
        in_specs=[VMEM] * 3 + [ANYWHERE] * 3,
        out_specs=[VMEM] + [ANYWHERE] * 3 + [VMEM],
        scratch_shapes=[
            pltpu.VMEM((rows, width), jnp.bfloat16),
            pltpu.VMEM((ranks, features, rows), jnp.bfloat16),
            pltpu.VMEM(weight.shape, jnp.bfloat16),
            pltpu.SemaphoreType.DMA((5,)),
        ]
        + semaphores(count),
        compiler_params=params(number, 32),
        name="add_branch",
    )(attended, tokens, gain, weight, up, down)


def norm_back_rows(grad, gain, values):
    factor = lax.rsqrt(mean_square(values) + EPS)
    normed = values * factor
    weighted = grad * gain
    back = factor * (weighted - normed * jnp.mean(weighted * normed, axis=-1, keepdims=True))
    return back, grad * normed


def middle_kernel(
    middle,
    gain,
    cotangent,
    hidden,
    gate_grads,
    up_grads,
    gate,
    up,
    weight,
    grad_middle,
    grad_gain,
    block,
    grad_attended,
    grads_share,
    part_of,
    ff_here,
    weight_here,
    given,
    got,
    send,
    recv,
    left_wide,
    right_wide,
    for_mate,
    loads,
    own,
    other,
    *bufs,
):
    ring = seq_ring()
    weights_ring, core, mate = fsdp_ring()
    rows = middle.shape[0]
    greet(ring.peers + ring.remote + weights_ring.peers + [mate])
    copies = Copies(send, recv)
    grad_gain[...] = jnp.zeros_like(grad_gain)

    def load(source, target, number):
        return pltpu.make_async_copy(source, target, loads.at[number])

    units = gate_grads.shape[1]
    first = [
        load(hidden, left_wide, 0),
        load(gate_grads, right_wide.at[:, pl.ds(0, units)], 1),
        load(up_grads, right_wide.at[:, pl.ds(units, units)], 2),
    ]
    ff = [
        load(gate, ff_here.at[:, pl.ds(0, units)], 3),
        load(up, ff_here.at[:, pl.ds(units, units)], 4),
    ]
    weight_load = load(weight, weight_here, 5)
    for copy in first[1:] + ff + first[:1] + [weight_load]:
        copy.start()
    arrived = first[1:] + ff

    def ready(*blocks):
        while arrived:
            arrived.pop().wait()
        left = two_blocks(right_wide, rows, *blocks)

        def columns(tile, _):
            cols = pl.ds(pl.multiple_of(tile * PRODUCT, PRODUCT), PRODUCT)
            value = lax.dot_general(
                left, ff_here[cols], (((1,), (1,)), ((), ())), preferred_element_type=jnp.float32
            ).astype(jnp.bfloat16)
            part_of[blocks[0], :, cols] = value[:rows]
            part_of[blocks[1], :, cols] = value[rows:]
            return 0

        lax.fori_loop(0, ff_here.shape[0] // PRODUCT, columns, 0)

    def done(index, total):
        rows_of = chunk_rows(rows, index)
        back, terms = norm_back_rows(total, gain[...], middle[rows_of])
        grad_gain[...] += jnp.sum(terms, axis=0, keepdims=True)
        values = cotangent[rows_of].astype(jnp.float32) + back
        grad_middle[rows_of] = values
        block[rows_of] = values.astype(jnp.bfloat16)

    def owned(rows_of, total):
        grads_share[rows_of] = total.astype(jnp.bfloat16)

    me = ring.near[0]
    features = grad_attended.shape[0]

    def walk():
        yield from reduce_walk(
            ring, copies, part_of, bufs[7:], by_rows(rows, CHUNKS), CHUNKS, done, ready
        )
        weight_load.wait()

        def piece(index):
            part = pl.ds(pl.multiple_of(index * features, features), features)
            given[index] = lax.dot_general(
                weight_here[part],
                block[...],
                (((1,), (1,)), ((), ())),
                preferred_element_type=jnp.float32,
            ).astype(jnp.bfloat16)
            return given.at[index]

        arriving = exchange_all(ring, copies, piece, got.at[me])
        piece(me)
        yield
        for copy in arriving:
            copy.wait_recv()
        got[me] = given[me]
        for index in range(got.shape[0]):
            grad_attended[:, pl.ds(index * rows, rows)] = got[index]

    def produce(place):
        if first:
            first.pop(0).wait()
            first.clear()
        lanes = pl.ds(pl.multiple_of(place * 2 * rows, 2 * rows), 2 * rows)
        turned = left_wide[:, lanes].T
        product(turned, right_wide, split_store(for_mate, own, place, core), 2 * PRODUCT)
        return [copies.start(for_mate.at[place], other.at[place], mate).wait_recv]

    beside(
        walk(),
        (
            owners_walk(
                weights_ring,
                mate,
                copies,
                produce,
                own,
                other,
                bufs[:7],
                grads_share.shape[0],
                owned,
            ),
            (0, 0, 1, 2, 2, 3) + (11,) * 7 + (15, 15, 15, 20, 20, 20, 20),
        ),
    )
    copies.finish()


def back_to_middle(
    middle,
    gain,
    cotangent,
    hidden,
    gate_grads,
    up_grads,
    gate,
    up,
    weight,
    number,
):
    rows, width = middle.shape
    length = hidden.shape[0]
    ranks, owners = lax.axis_size("seq"), lax.axis_size("fsdp")
    places = owners // 2
    grad_rows, grad_cols = width // owners, 2 * gate_grads.shape[1]
    features = weight.shape[0] // ranks
    count = reduce_copies(CHUNKS) + ranks - 1 + OWNERS_COPIES + places
    return pl.pallas_call(
        middle_kernel,
        out_shape=[
            jax.ShapeDtypeStruct((rows, width), jnp.float32),
            jax.ShapeDtypeStruct((1, width), jnp.float32),
            jax.ShapeDtypeStruct((rows, width), jnp.bfloat16),
            jax.ShapeDtypeStruct((features, length), jnp.bfloat16),
            jax.ShapeDtypeStruct((grad_rows, grad_cols), jnp.bfloat16),
        ],
        in_specs=[VMEM] * 3 + [ANYWHERE] * 6,
        out_specs=[VMEM] * 5,
        scratch_shapes=[
            pltpu.VMEM((ranks, rows, width), jnp.bfloat16),
            pltpu.VMEM((width, grad_cols), jnp.bfloat16),
            pltpu.VMEM(weight.shape, jnp.bfloat16),
            pltpu.VMEM((ranks, features, rows), jnp.bfloat16),
            pltpu.VMEM((ranks, features, rows), jnp.bfloat16),
        ]
        + semaphores(count)
        + [
            pltpu.VMEM((length, width), jnp.bfloat16),
            pltpu.VMEM((length, width), jnp.bfloat16),
            pltpu.VMEM((places, grad_rows, grad_cols), jnp.bfloat16),
            pltpu.SemaphoreType.DMA((6,)),
        ]
        + owners_scratch(places, grad_rows, grad_cols)
        + reduce_scratch(rows, width),
        compiler_params=params(number, 60),
        name="back_to_middle",
    )(
        middle,
        gain,
        cotangent,
        hidden,
        gate_grads,
        up_grads,
        gate,
        up,
        weight,
    )


def heads_products(copies, core, mate, attended, branch, for_mate, own, other):
    rows = branch.shape[0]

    def produce(place):
        both = attended[pl.ds(pl.multiple_of(place * 2 * rows, 2 * rows), 2 * rows)]
        product(both, branch, split_store(for_mate, own, place, core))
        return [copies.start(for_mate.at[place], other.at[place], mate).wait_recv]

    return produce


def tokens_kernel(
    part_of,
    tokens,
    gain,
    grad_middle,
    qkv_grad,
    attended,
    branch,
    out,
    grad_gain,
    share,
    heads_share,
    fetches,
    send,
    recv,
    own,
    other,
    for_mate,
    heads_own,
    heads_other,
    *bufs,
):
    ring = seq_ring()
    weights_ring, core, mate = fsdp_ring()
    rows = tokens.shape[0]
    greet(ring.peers + weights_ring.peers + [mate])
    copies = Copies(send, recv)
    grad_gain[...] = jnp.zeros_like(grad_gain)
    pieces = ((lambda place, which: qkv_grad.at[place, which], lambda ref: ref),)

    def owned(rows_of, total):
        share[rows_of] = total.astype(jnp.bfloat16)

    def heads_owned(rows_of, total):
        heads_share[rows_of] = total.astype(jnp.bfloat16)

    def done(index, total):
        rows_of = chunk_rows(rows, index)
        back, terms = norm_back_rows(total, gain[...], tokens[rows_of].astype(jnp.float32))
        grad_gain[...] += jnp.sum(terms, axis=0, keepdims=True)
        out[rows_of] = (grad_middle[rows_of] + back).astype(jnp.bfloat16)

    beside(
        reduce_walk(ring, copies, part_of, bufs[14:], by_rows(rows, CHUNKS), CHUNKS, done),
        (
            owners_walk(
                weights_ring,
                mate,
                copies,
                fetched(copies, core, mate, pieces, own, other, fetches),
                own,
                other,
                bufs[:7],
                rows,
                owned,
            ),
            (0,) * 9 + (4,) * 7 + (8, 8, 12, 14),
        ),
        (
            owners_walk(
                weights_ring,
                mate,
                copies,
                heads_products(
                    copies, core, mate, attended, branch, for_mate, heads_own, heads_other
                ),
                heads_own,
                heads_other,
                bufs[7:14],
                rows,
                heads_owned,
            ),
            (0,) * 9 + (8,) * 7 + (12, 12, 14, 15),
        ),
    )
    copies.finish()


def back_to_tokens(partial, tokens, gain, grad_middle, qkv_grad, attended, branch, number):
    rows, width = tokens.shape
    ranks, owners = lax.axis_size("seq"), lax.axis_size("fsdp")
    places = owners // 2
    cols = qkv_grad.shape[1]
    heads_cols = branch.shape[1]
    count = reduce_copies(CHUNKS) + 2 * (OWNERS_COPIES + places)
    return pl.pallas_call(
        tokens_kernel,
        out_shape=[
            jax.ShapeDtypeStruct((rows, width), jnp.bfloat16),
            jax.ShapeDtypeStruct((1, width), jnp.float32),
            jax.ShapeDtypeStruct((rows, cols), jnp.bfloat16),
            jax.ShapeDtypeStruct((rows, heads_cols), jnp.bfloat16),
        ],
        in_specs=[VMEM] * 4 + [ANYWHERE] + [VMEM] * 2,
        out_specs=[VMEM] * 4,
        scratch_shapes=[pltpu.SemaphoreType.DMA((places,))]
        + semaphores(count)
        + owners_scratch(places, rows, cols)[:2]
        + [pltpu.VMEM((places, rows, heads_cols), jnp.bfloat16)]
        + owners_scratch(places, rows, heads_cols)[:2]
        + owners_scratch(places, rows, cols)[2:]
        + owners_scratch(places, rows, heads_cols)[2:]
        + reduce_scratch(rows, width),
        compiler_params=params(number, 40),
        name="back_to_tokens",
    )(
        partial.reshape(ranks, rows, width),
        tokens,
        gain,
        grad_middle,
        qkv_grad.reshape(places, 2, rows, cols),
        attended,
        branch,
    )


def finish_kernel(
    gate_up,
    small,
    gain_one,
    gain_two,
    heads_low,
    heads_high,
    act,
    grad_out,
    gate_up_all,
    small_all,
    heads_all,
    down_all,
    gains,
    given,
    from_mate,
    pair,
    from_partner,
    by_place,
    for_partner,
    partners,
    by_column,
    heads_part,
    heads_block,
    act_here,
    grad_out_here,
    for_mate,
    down_block,
    local,
    send,
    recv,
    own,
    other,
    *bufs,
):
    ring = seq_ring()
    me = ring.near[0]
    side = lax.axis_size("seq") // 2
    weights_ring, core, mate = fsdp_ring()
    greet(ring.peers + weights_ring.peers + [mate])
    copies = Copies(send, recv)
    loads = [
        pltpu.make_async_copy(act, act_here, local.at[0]),
        pltpu.make_async_copy(grad_out, grad_out_here, local.at[1]),
    ]
    kept = [
        pltpu.make_async_copy(gate_up, gate_up_all.at[me], local.at[2]),
        pltpu.make_async_copy(small, small_all.at[me], local.at[3]),
    ]
    for copy in loads + kept:
        copy.start()

    def keep(block, out, number):
        copy = pltpu.make_async_copy(block, out.at[me], local.at[number])
        copy.start()
        kept.append(copy)

    def around(table, ring_of):
        place = lax.rem(ring_of.place, side)
        after = lax.rem(place + 1, side)
        mine = table.at[place]
        to_right = copies.start(mine, mine, ring_of.right)
        to_left = copies.start(mine, mine, ring_of.left)
        yield
        to_right.wait_recv()
        to_left.wait_recv()
        copy = copies.start(table.at[after], table.at[after], ring_of.left)
        yield
        copy.wait_recv()

    def sum_gains():
        lanes = given.shape[2]
        for index in range(given.shape[0]):
            cols = pl.ds(index * lanes, lanes)
            given[index, 0:1] = gain_one[:, cols]
            given[index, 1:2] = gain_two[:, cols]
            given[index, 2:8] = jnp.zeros((6, lanes), jnp.float32)
        copy = copies.start(given, from_mate, mate)
        yield
        copy.wait_recv()
        pair[...] = given[...] + from_mate[...]
        copy = copies.start(pair, from_partner, weights_ring.partner)
        yield
        copy.wait_recv()
        by_place[lax.rem(weights_ring.place, side)] = pair[...] + from_partner[...]
        yield from around(by_place, weights_ring)
        block = lax.axis_index("fsdp")
        for_partner[...] = (by_place[0, block] + by_place[1, block]) + (
            by_place[2, block] + by_place[3, block]
        )
        copy = copies.start(for_partner, partners, ring.partner)
        yield
        copy.wait_recv()
        by_column[lax.rem(ring.place, side)] = for_partner[...] + partners[...]
        yield from around(by_column, ring)
        gains[...] = (by_column[0] + by_column[1]) + (by_column[2] + by_column[3])

    pieces, piece_rows, width = heads_part.shape

    def heads_walk():
        half = heads_low.shape[1]
        for index in range(pieces):
            rows_of = pl.ds(index * piece_rows, piece_rows)
            heads_part[index, :, :half] = heads_low[rows_of]
            heads_part[index, :, half:] = heads_high[rows_of]
        cut = by_columns(width, 2)

        def done(index, total):
            cut(heads_block, index)[...] = total.astype(jnp.bfloat16)

        yield from reduce_walk(ring, copies, heads_part, bufs[7:], cut, 2, done)
        keep(heads_block, heads_all, 4)
        yield from gather_walk(ring, copies, heads_block, heads_all, cut, 2)

    rows = down_block.shape[0]

    def produce(place):
        if loads:
            loads.pop(0).wait()
            loads.pop(0).wait()
        both = act_here[:, pl.ds(pl.multiple_of(place * 2 * rows, 2 * rows), 2 * rows)].T
        product(both, grad_out_here, split_store(for_mate, own, place, core))
        return [copies.start(for_mate.at[place], other.at[place], mate).wait_recv]

    def owned(rows_of, total):
        down_block[rows_of] = total.astype(jnp.bfloat16)

    def down_walk():
        yield from owners_walk(
            weights_ring, mate, copies, produce, own, other, bufs[:7], rows, owned
        )
        keep(down_block, down_all, 5)
        yield from gather_walk(
            ring, copies, down_block, down_all, by_rows(rows, CHUNKS), CHUNKS
        )

    beside(
        in_step(
            gather_walk(
                ring, copies, gate_up, gate_up_all, by_rows(gate_up.shape[0], CHUNKS), CHUNKS
            ),
            gather_walk(ring, copies, small, small_all, by_rows(small.shape[0], CHUNKS), CHUNKS),
        ),
        (heads_walk(), (0, 1, 1, 2, 2, 3, 3, 4, 4, 5, 6, 6, 7, 8, 8, 9)),
        (down_walk(), (0,) * 9 + (2,) * 7 + (6, 6, 7, 7, 7, 8, 8, 9, 9, 9, 9, 10)),
        (sum_gains(), range(1, 9)),
    )
    copies.finish()
    for copy in kept:
        copy.wait()


def finish_grads(
    gate_up, small, gain_one, gain_two, heads_low, heads_high, act, grad_out, number
):
    ranks, owners = lax.axis_size("seq"), lax.axis_size("fsdp")
    lanes = gain_one.shape[1] // owners
    rows, width = heads_low.shape[0], grad_out.shape[1]
    places = owners // 2
    pieces = rows // ranks
    down_rows = act.shape[1] // owners
    count = 3 * gather_copies(CHUNKS) + 1 + 1 + 3 + 1 + 3
    count += places + OWNERS_COPIES + reduce_copies(2) + gather_copies(2)

    def table(*shape):
        return pltpu.VMEM((*shape, 8, lanes), jnp.float32)

    return pl.pallas_call(
        finish_kernel,
        out_shape=[
            jax.ShapeDtypeStruct((ranks, *gate_up.shape), jnp.bfloat16),
            jax.ShapeDtypeStruct((ranks, *small.shape), jnp.bfloat16),
            jax.ShapeDtypeStruct((ranks, pieces, width), jnp.bfloat16),
            jax.ShapeDtypeStruct((ranks, down_rows, width), jnp.bfloat16),
            jax.ShapeDtypeStruct((8, lanes), jnp.float32),
        ],
        in_specs=[ANYWHERE] * 2 + [VMEM] * 4 + [ANYWHERE] * 2,
        out_specs=[ANYWHERE] * 4 + [VMEM],
        scratch_shapes=[
            table(owners),
            table(owners),
            table(owners),
            table(owners),
            table(ranks // 2, owners),
            table(),
            table(),
            table(ranks // 2),
            pltpu.VMEM((ranks, pieces, width), jnp.bfloat16),
            pltpu.VMEM((pieces, width), jnp.bfloat16),
            pltpu.VMEM(act.shape, jnp.bfloat16),
            pltpu.VMEM(grad_out.shape, jnp.bfloat16),
            pltpu.VMEM((places, down_rows, width), jnp.bfloat16),
            pltpu.VMEM((down_rows, width), jnp.bfloat16),
            pltpu.SemaphoreType.DMA((6,)),
        ]
        + semaphores(count)
        + owners_scratch(places, down_rows, width)
        + reduce_scratch(pieces, width),
        compiler_params=params(number, 48),
        name="finish_grads",
    )(gate_up, small, gain_one, gain_two, heads_low, heads_high, act, grad_out)


def merge_lanes(first, second):
    half = first.shape[1] // 2
    low = lax.broadcasted_iota(jnp.int32, first.shape, 1) < half
    return (
        jnp.where(low, first, pltpu.roll(second, half, 1)),
        jnp.where(low, pltpu.roll(first, half, 1), second),
    )


def place_kernel(
    gate,
    up,
    down,
    query,
    pair,
    heads,
    gate_out,
    up_out,
    down_out,
    query_out,
    key_out,
    value_out,
    heads_out,
):
    lanes = gate.shape[2]
    blocks = gate.shape[0] // 2
    for part, out in ((gate, gate_out), (up, up_out)):
        for index in range(blocks):
            low, high = merge_lanes(
                part[2 * index].astype(jnp.float32), part[2 * index + 1].astype(jnp.float32)
            )
            out[:, pl.ds(index * lanes, lanes)] = low
            out[:, pl.ds((blocks + index) * lanes, lanes)] = high
    key, value = merge_lanes(pair[0].astype(jnp.float32), pair[1].astype(jnp.float32))
    key_out[...] = key
    value_out[...] = value
    down_out[...] = down[0].astype(jnp.float32)
    query_out[...] = query[0].astype(jnp.float32)
    heads_out[...] = heads[0].astype(jnp.float32)


def place_grads(gate_up, small, heads, down):
    ranks, rows, both = gate_up.shape
    lanes = 128
    steps = both // 2 // lanes
    down_rows, width = down.shape[1:]
    query_cols = width // ranks
    head_rows = heads.shape[1]
    first = query_cols // lanes
    assert steps == ranks and lanes == 2 * HEAD_SIZE and query_cols == 2 * lanes
    real = jnp.float32
    return pl.pallas_call(
        place_kernel,
        grid=(steps,),
        out_shape=[
            jax.ShapeDtypeStruct((rows, ranks * both // 2), real),
            jax.ShapeDtypeStruct((rows, ranks * both // 2), real),
            jax.ShapeDtypeStruct((ranks * down_rows, width), real),
            jax.ShapeDtypeStruct((rows, ranks * query_cols), real),
            jax.ShapeDtypeStruct((rows, ranks * HEAD_SIZE), real),
            jax.ShapeDtypeStruct((rows, ranks * HEAD_SIZE), real),
            jax.ShapeDtypeStruct((rows, width), real),
        ],
        in_specs=[
            pl.BlockSpec((ranks, rows, lanes), lambda i: (0, 0, i)),
            pl.BlockSpec((ranks, rows, lanes), lambda i: (0, 0, steps + i)),
            pl.BlockSpec((1, down_rows, width), lambda i: (i, 0, 0)),
            pl.BlockSpec((1, rows, query_cols), lambda i: (i, 0, 0)),
            pl.BlockSpec((2, rows, lanes), lambda i: (i // 2, 0, first)),
            pl.BlockSpec((1, head_rows, width), lambda i: (i, 0, 0)),
        ],
        out_specs=[
            pl.BlockSpec((rows, ranks * lanes), lambda i: (0, i)),
            pl.BlockSpec((rows, ranks * lanes), lambda i: (0, i)),
            pl.BlockSpec((down_rows, width), lambda i: (i, 0)),
            pl.BlockSpec((rows, query_cols), lambda i: (0, i)),
            pl.BlockSpec((rows, lanes), lambda i: (0, i // 2)),
            pl.BlockSpec((rows, lanes), lambda i: (0, i // 2)),
            pl.BlockSpec((head_rows, width), lambda i: (i, 0)),
        ],
        compiler_params=pltpu.CompilerParams(vmem_limit_bytes=32 * 2**20),
        name="place_grads",
    )(gate_up, gate_up, down, small, small, heads)


def pick_kernel(
    query, key, value, gate, up, gain_one, gain_two, qkv_out, gate_out, up_out, wide, narrow, sems
):
    rank, ranks = lax.axis_index("seq"), lax.axis_size("seq")
    rows = query.shape[0]
    lanes = 128
    owners = wide.shape[1]
    pair = lax.div(rank, 2)
    odd = lax.rem(rank, 2)
    query_cols = query.shape[1] // ranks
    stride = gate.shape[1] // owners
    count = 0
    made = []

    def fetch(source, target):
        nonlocal count
        copy = pltpu.make_async_copy(source, target, sems.at[count])
        copy.start()
        made.append(copy)
        count += 1

    fetch(
        query.at[:, pl.ds(pl.multiple_of(rank * query_cols, lanes), query_cols)],
        qkv_out.at[pl.ds(0, rows), pl.ds(0, query_cols)],
    )
    for index, source in enumerate((key, value)):
        fetch(source.at[:, pl.ds(pl.multiple_of(pair * lanes, lanes), lanes)], narrow.at[index])
    for which, source in enumerate((gate, up)):
        for owner in range(owners):
            first = pl.multiple_of(owner * stride + pair * lanes, lanes)
            fetch(source.at[:, pl.ds(first, lanes)], wide.at[which, owner])
    line = lax.broadcasted_iota(jnp.int32, (16, rows), 0)
    first, second = (gain[...].astype(jnp.float32) for gain in (gain_one, gain_two))
    gains = jnp.where(line == 0, first, jnp.where(line == 1, second, 0.0))
    qkv_out[pl.ds(rows, 32)] = jnp.zeros((32, qkv_out.shape[1]), jnp.bfloat16)
    qkv_out[pl.ds(rows, 16), pl.ds(0, rows)] = gains.astype(jnp.bfloat16)
    for copy in made:
        copy.wait()

    def chosen(first, second):
        low, high = merge_lanes(first.astype(jnp.float32), second.astype(jnp.float32))
        return jnp.where(odd == 0, low, high).astype(jnp.bfloat16)

    qkv_out[pl.ds(0, rows), pl.ds(query_cols, lanes)] = chosen(narrow[0], narrow[1])
    for which, out in enumerate((gate_out, up_out)):
        for index in range(owners // 2):
            cols = pl.ds(index * lanes, lanes)
            out[:, cols] = chosen(wide[which, 2 * index], wide[which, 2 * index + 1])


def pick_columns(query, key, value, gate, up, gain_one, gain_two):
    rows, width = query.shape
    ranks, owners = lax.axis_size("seq"), lax.axis_size("fsdp")
    lanes = 128
    assert gate.shape[1] // owners // ranks == HEAD_SIZE == lanes // 2
    return pl.pallas_call(
        pick_kernel,
        out_shape=[
            jax.ShapeDtypeStruct((rows + 32, width // ranks + lanes), jnp.bfloat16),
            jax.ShapeDtypeStruct((rows, owners // 2 * lanes), jnp.bfloat16),
            jax.ShapeDtypeStruct((rows, owners // 2 * lanes), jnp.bfloat16),
        ],
        in_specs=[ANYWHERE] * 5 + [VMEM] * 2,
        out_specs=[VMEM] * 3,
        scratch_shapes=[
            pltpu.VMEM((2, owners, rows, lanes), jnp.bfloat16),
            pltpu.VMEM((2, rows, lanes), jnp.bfloat16),
            pltpu.SemaphoreType.DMA((2 * owners + 3,)),
        ],
        compiler_params=pltpu.CompilerParams(vmem_limit_bytes=32 * 2**20),
        name="pick_columns",
    )(query, key, value, gate, up, gain_one[None], gain_two[None])


def rotate_rows(first, second, cosine, sine):
    return jnp.concatenate([first * cosine - second * sine, second * cosine + first * sine], axis=0)


def bias_tile(start_row, key_tile, query_tile, diagonal):
    keys = key_tile * TILE + lax.broadcasted_iota(jnp.int32, (TILE, TILE), 0)
    seen = keys >= start_row
    if diagonal:
        queries = query_tile * TILE + lax.broadcasted_iota(jnp.int32, (TILE, TILE), 1)
        seen = seen & (keys <= queries)
    return jnp.where(seen, 0.0, NEG)


def attend_tiles(qkv, cosine, sine, starts, attended, lse, queries, keys, key_rows, bias):
    group = queries.shape[0] // HEAD_SIZE
    half = HEAD_SIZE // 2
    tiles = qkv.shape[1] // TILE
    cos, sin = cosine[...], sine[...]

    def rotated(first):
        return rotate_rows(
            qkv[pl.ds(first, half)].astype(jnp.float32),
            qkv[pl.ds(first + half, half)].astype(jnp.float32),
            cos,
            sin,
        ).astype(jnp.bfloat16)

    for head in range(group):
        queries[pl.ds(head * HEAD_SIZE, HEAD_SIZE)] = rotated(head * HEAD_SIZE) * jnp.bfloat16(0.125)
    keys[...] = rotated(group * HEAD_SIZE)
    key_rows[...] = keys[...].T
    for tile in range(tiles):
        lanes = pl.ds(tile * TILE, TILE)
        starts_here = starts[:, lanes]
        for low in range(tile + 1):
            bias[pl.ds(low * TILE, TILE)] = bias_tile(starts_here, low, tile, low == tile)
        count = (tile + 1) * TILE

        def one_head(head, _, lanes=lanes, count=count):
            rows = pl.ds(pl.multiple_of(head * HEAD_SIZE, HEAD_SIZE), HEAD_SIZE)
            scores = jnp.dot(
                key_rows[:count], queries[rows, lanes], preferred_element_type=jnp.float32
            )
            scores += bias[:count]
            highest = jnp.max(scores, axis=0, keepdims=True)
            weights = jnp.exp(scores - highest)
            total = jnp.sum(weights, axis=0, keepdims=True)
            out = jnp.dot(
                qkv[pl.ds((group + 1) * HEAD_SIZE, HEAD_SIZE), :count],
                weights.astype(jnp.bfloat16),
                preferred_element_type=jnp.float32,
            )
            attended[rows, lanes] = (out / total).astype(jnp.bfloat16)
            lse[head, :, lanes] = jnp.broadcast_to(highest + jnp.log(total), (8, TILE))
            return 0

        lax.fori_loop(0, group, one_head, 0)


def forward_kernel(
    qkv,
    cosine,
    sine,
    starts,
    cotangent,
    heads,
    attended,
    lse,
    queries,
    keys,
    gathered,
    heads_all,
    key_rows,
    bias,
    local,
    send,
    recv,
):
    ring = seq_ring()
    weights_ring, _, mate = fsdp_ring()
    greet(ring.peers + weights_ring.peers + [mate])
    kept = [
        pltpu.make_async_copy(cotangent, gathered.at[ring.near[0]], local.at[0]),
        pltpu.make_async_copy(heads, heads_all.at[weights_ring.near[0]], local.at[1]),
    ]
    for copy in kept:
        copy.start()
    copies = Copies(send, recv)

    def compute():
        attend_tiles(qkv, cosine, sine, starts, attended, lse, queries, keys, key_rows, bias)
        yield

    beside(
        gather_walk(
            ring, copies, cotangent, gathered, by_rows(cotangent.shape[0], CHUNKS), CHUNKS
        ),
        (weight_walk(weights_ring, copies, heads, heads_all, mate), LARGE_BESIDE),
        (compute(), (0,)),
    )
    copies.finish()
    for copy in kept:
        copy.wait()


def attend(qkv, cosine, sine, starts, cotangent, heads, group, number):
    length = qkv.shape[1]
    rows, width = cotangent.shape
    ranks = lax.axis_size("seq")
    return pl.pallas_call(
        forward_kernel,
        out_shape=[
            jax.ShapeDtypeStruct((group * HEAD_SIZE, length), jnp.bfloat16),
            jax.ShapeDtypeStruct((group, 8, length), jnp.float32),
            jax.ShapeDtypeStruct((group * HEAD_SIZE, length), jnp.bfloat16),
            jax.ShapeDtypeStruct((HEAD_SIZE, length), jnp.bfloat16),
            jax.ShapeDtypeStruct((ranks, rows, width), jnp.bfloat16),
            jax.ShapeDtypeStruct((lax.axis_size("fsdp"), *heads.shape), jnp.bfloat16),
        ],
        in_specs=[VMEM] * 4 + [ANYWHERE] * 2,
        out_specs=[VMEM] * 4 + [ANYWHERE] * 2,
        scratch_shapes=[
            pltpu.VMEM((length, HEAD_SIZE), jnp.bfloat16),
            pltpu.VMEM((length, TILE), jnp.float32),
            pltpu.SemaphoreType.DMA((2,)),
        ]
        + semaphores(gather_copies(CHUNKS) + gather_copies(CHUNKS, True)),
        compiler_params=params(number, 40),
        name="attend",
    )(qkv, cosine, sine, starts, cotangent, heads)


def back_tiles(
    qkv,
    queries,
    keys,
    attended,
    lse,
    grads,
    cosine,
    sine,
    starts,
    out,
    key_rows,
    value_rows,
    query_rows,
    grad_rows,
    row_dots,
    key_grad,
    value_grad,
    query_grad,
    bias,
):
    group = queries.shape[0] // HEAD_SIZE
    half = HEAD_SIZE // 2
    tiles = qkv.shape[1] // TILE
    key_rows[...] = keys[...].T
    value_rows[...] = qkv[pl.ds((group + 1) * HEAD_SIZE, HEAD_SIZE)].T
    for head in range(group):
        rows = pl.ds(head * HEAD_SIZE, HEAD_SIZE)
        query_rows[head] = queries[rows].T
        grad_rows[head] = grads[rows].T
        row_dots[head] = jnp.broadcast_to(
            jnp.sum(
                grads[rows].astype(jnp.float32) * attended[rows].astype(jnp.float32),
                axis=0,
                keepdims=True,
            ),
            row_dots.shape[1:],
        )
    key_grad[...] = jnp.zeros_like(key_grad)
    value_grad[...] = jnp.zeros_like(value_grad)
    for tile in range(tiles):
        lanes = pl.ds(tile * TILE, TILE)
        starts_here = starts[:, lanes]
        for low in range(tile + 1):
            bias[low] = bias_tile(starts_here, low, tile, low == tile)

        def one_head(head, _, lanes=lanes, tile=tile):
            rows = pl.ds(pl.multiple_of(head * HEAD_SIZE, HEAD_SIZE), HEAD_SIZE)
            query, grad = queries[rows, lanes], grads[rows, lanes]
            query_row, grad_row = query_rows[head, lanes], grad_rows[head, lanes]
            lse_row = lse[head, 0:1, lanes]
            dot_row = row_dots[head, 0:1, lanes]
            total = jnp.zeros((HEAD_SIZE, TILE), jnp.float32)
            for low in range(tile + 1):
                part = pl.ds(low * TILE, TILE)
                scores = jnp.dot(key_rows[part], query, preferred_element_type=jnp.float32)
                probs = jnp.exp(scores + bias[low] - lse_row)
                grad_probs = jnp.dot(value_rows[part], grad, preferred_element_type=jnp.float32)
                grad_scores = (probs * (grad_probs - dot_row)).astype(jnp.bfloat16)
                value_grad[part] += jnp.dot(
                    probs.astype(jnp.bfloat16), grad_row, preferred_element_type=jnp.float32
                )
                key_grad[part] += jnp.dot(
                    grad_scores, query_row, preferred_element_type=jnp.float32
                )
                total += jnp.dot(keys[:, part], grad_scores, preferred_element_type=jnp.float32)
            query_grad[rows, lanes] = total * 0.125
            return 0

        lax.fori_loop(0, group, one_head, 0)
        yield
    cos, sin = cosine[...], sine[...]
    for head in range(group):
        first = head * HEAD_SIZE
        out[pl.ds(first, HEAD_SIZE)] = rotate_rows(
            query_grad[pl.ds(first, half)], query_grad[pl.ds(first + half, half)], cos, -sin
        ).astype(jnp.bfloat16)
    turned = key_grad[...].T
    out[pl.ds(group * HEAD_SIZE, HEAD_SIZE)] = rotate_rows(
        turned[:half], turned[half:], cos, -sin
    ).astype(jnp.bfloat16)
    out[pl.ds((group + 1) * HEAD_SIZE, HEAD_SIZE)] = value_grad[...].T.astype(jnp.bfloat16)


def backward_kernel(*refs):
    ins, (act, down, middle, attended, branch) = refs[:9], refs[9:14]
    (out, layer_out, heads_share), scratch = refs[14:17], refs[17:26]
    part_of, act_here, down_here, loads, send, recv = refs[26:32]
    for_mate, own, other = refs[32:35]
    bufs = refs[35:]
    ring = seq_ring()
    weights_ring, core, mate = fsdp_ring()
    greet(ring.peers + weights_ring.peers + [mate])
    copies = Copies(send, recv)
    rows = middle.shape[0]
    first = [
        pltpu.make_async_copy(act, act_here, loads.at[0]),
        pltpu.make_async_copy(down, down_here, loads.at[1]),
    ]
    for copy in first:
        copy.start()

    def ready(*blocks):
        while first:
            first.pop().wait()

        def store(cols, value):
            part_of[blocks[0], :, cols] = value[:rows].astype(jnp.bfloat16)
            part_of[blocks[1], :, cols] = value[rows:].astype(jnp.bfloat16)

        product(two_blocks(act_here, rows, *blocks), down_here, store)

    def done(index, total):
        rows_of = chunk_rows(rows, index)
        layer_out[rows_of] = (middle[rows_of] + total).astype(jnp.bfloat16)

    def owned(rows_of, total):
        heads_share[rows_of] = total.astype(jnp.bfloat16)

    beside(
        reduce_walk(
            ring, copies, part_of, bufs[7:], by_rows(rows, CHUNKS), CHUNKS, done, ready
        ),
        (
            owners_walk(
                weights_ring,
                mate,
                copies,
                heads_products(copies, core, mate, attended, branch, for_mate, own, other),
                own,
                other,
                bufs[:7],
                rows,
                owned,
            ),
            (0, 0, 1, 2, 2, 2, 3, 3, 3) + (11,) * 8 + (15, 15, 19),
        ),
        (back_tiles(*ins, out, *scratch), (3, 3, 11, 11, 15)),
    )
    copies.finish()


def attend_back(
    qkv,
    queries,
    keys,
    attended,
    lse,
    grads,
    cosine,
    sine,
    starts,
    act,
    down,
    middle,
    attended_here,
    branch,
    number,
):
    length = qkv.shape[1]
    group = queries.shape[0] // HEAD_SIZE
    tiles = length // TILE
    rows, width = middle.shape
    ranks, owners = lax.axis_size("seq"), lax.axis_size("fsdp")
    places = owners // 2
    cols = branch.shape[1]
    return pl.pallas_call(
        backward_kernel,
        out_shape=[
            jax.ShapeDtypeStruct(qkv.shape, jnp.bfloat16),
            jax.ShapeDtypeStruct((rows, width), jnp.bfloat16),
            jax.ShapeDtypeStruct((rows, cols), jnp.bfloat16),
        ],
        in_specs=[VMEM] * 9 + [ANYWHERE] * 2 + [VMEM] * 3,
        out_specs=[VMEM] * 3,
        scratch_shapes=[
            pltpu.VMEM((length, HEAD_SIZE), jnp.bfloat16),
            pltpu.VMEM((length, HEAD_SIZE), jnp.bfloat16),
            pltpu.VMEM((group, length, HEAD_SIZE), jnp.bfloat16),
            pltpu.VMEM((group, length, HEAD_SIZE), jnp.bfloat16),
            pltpu.VMEM((group, 8, length), jnp.float32),
            pltpu.VMEM((length, HEAD_SIZE), jnp.float32),
            pltpu.VMEM((length, HEAD_SIZE), jnp.float32),
            pltpu.VMEM((group * HEAD_SIZE, length), jnp.float32),
            pltpu.VMEM((tiles, TILE, TILE), jnp.float32),
            pltpu.VMEM((ranks, rows, width), jnp.bfloat16),
            pltpu.VMEM(act.shape, jnp.bfloat16),
            pltpu.VMEM(down.shape, jnp.bfloat16),
            pltpu.SemaphoreType.DMA((2,)),
        ]
        + semaphores(reduce_copies(CHUNKS) + OWNERS_COPIES + places)
        + [pltpu.VMEM((places, rows, cols), jnp.bfloat16)]
        + owners_scratch(places, rows, cols)
        + reduce_scratch(rows, width),
        compiler_params=params(number, 52),
        name="attend_back",
    )(
        qkv,
        queries,
        keys,
        attended,
        lse,
        grads,
        cosine,
        sine,
        starts,
        act,
        down,
        middle,
        attended_here,
        branch,
    )


def contract_rows(left, right):
    return jnp.einsum("ta,tb->ab", left, right, preferred_element_type=jnp.float32)


def contract_cols(left, right):
    return jnp.einsum("ta,ba->tb", left, right, preferred_element_type=jnp.float32)


def matmul(left, right):
    return jnp.dot(left, right, preferred_element_type=jnp.float32)


def shards(
    tokens,
    segment_ids,
    query_weight,
    key_matrix,
    value_matrix,
    output_weight,
    gate_weight,
    up_weight,
    down_weight,
    attention_gain,
    feed_gain,
    cotangent,
):
    rank = lax.axis_index("seq")
    owner = lax.axis_index("fsdp")
    ranks = lax.axis_size("seq")
    owners = lax.axis_size("fsdp")
    rows, width = query_weight.shape
    kv_cols = key_matrix.shape[1] // ranks
    q_cols = width // ranks
    group = q_cols // kv_cols
    ff = gate_weight.shape[1]
    ff_chunk = ff // owners // ranks
    ff_local = owners * ff_chunk
    segment_row = segment_ids[0]
    length = segment_row.shape[0]

    qkv_in, gate_in, up_in = pick_columns(
        query_weight, key_matrix, value_matrix, gate_weight, up_weight, attention_gain, feed_gain
    )
    whole, qkv_got, gate_all = gather_first(tokens[0], qkv_in, gate_in, 0)
    gate_all = gate_all.reshape(width, ff_local)
    qkv_all = qkv_got[:, :rows].reshape(owners * rows, -1)
    gain_one = qkv_got[:, rows, :rows].reshape(1, -1).astype(jnp.float32)
    gain_two = qkv_got[:, rows + 1, :rows].reshape(1, -1).astype(jnp.float32)
    down_in = lax.dynamic_slice_in_dim(down_weight, rank * ff_chunk, ff_chunk, 0)

    starts = (jnp.arange(length, dtype=jnp.int32) - positions_of(segment_row))[None]
    cosine, sine = (table.T for table in angles_of(segment_row, HEAD_SIZE))
    whole = whole.reshape(length, width).astype(jnp.float32)
    hidden_one = (whole * lax.rsqrt(mean_square(whole) + EPS) * gain_one).astype(jnp.bfloat16)
    qkv = jnp.einsum("tm,mc->ct", hidden_one, qkv_all, preferred_element_type=jnp.float32)
    qkv = qkv.astype(jnp.bfloat16)
    attended, lse, queries, keys, grad_out, output_all = attend(
        qkv, cosine, sine, starts, cotangent[0], output_weight, group, 1
    )
    grad_out = grad_out.reshape(length, width)
    output_all = output_all.reshape(-1, width)
    middle, hidden_two, up_all, down_all, attended_here = add_branch(
        attended, tokens[0], gain_two, output_all, up_in, down_in, 2
    )
    up_all = up_all.reshape(width, ff_local)
    down_all = down_all.reshape(ff_local, width)
    hidden_two = hidden_two.reshape(length, width)

    gate = matmul(hidden_two, gate_all)
    up_proj = matmul(hidden_two, up_all)
    sig_gate = jax.nn.sigmoid(gate)
    silu_gate = gate * sig_gate
    act = (silu_gate * up_proj).astype(jnp.bfloat16)
    grad_act = contract_cols(grad_out, down_all)
    grad_gate = (grad_act * up_proj * (sig_gate * (1.0 + gate * (1.0 - sig_gate)))).astype(
        jnp.bfloat16
    )
    grad_up = (grad_act * silu_gate).astype(jnp.bfloat16)
    (
        grad_middle,
        grad_gain_two,
        grad_branch,
        grad_attended,
        gate_up_share,
    ) = back_to_middle(
        middle,
        gain_two,
        cotangent[0],
        hidden_two,
        grad_gate,
        grad_up,
        gate_all,
        up_all,
        output_all,
        3,
    )

    half = width // 2
    qkv_grads, layer_out, heads_low = attend_back(
        qkv,
        queries,
        keys,
        attended,
        lse,
        grad_attended,
        cosine,
        sine,
        starts,
        act,
        down_all,
        middle,
        attended_here,
        grad_branch[:, :half],
        4,
    )
    qkv_grad = jnp.einsum(
        "tm,ct->mc", hidden_one, qkv_grads, preferred_element_type=jnp.float32
    ).astype(jnp.bfloat16)
    grad_inputs, grad_gain_one, small_share, heads_high = back_to_tokens(
        jnp.einsum("ct,mc->tm", qkv_grads, qkv_all, preferred_element_type=jnp.float32).astype(
            jnp.bfloat16
        ),
        tokens[0],
        gain_one,
        grad_middle,
        qkv_grad,
        attended_here,
        grad_branch[:, half:],
        5,
    )
    *gathered, gains = finish_grads(
        gate_up_share,
        small_share,
        grad_gain_one,
        grad_gain_two,
        heads_low,
        heads_high,
        act,
        grad_out,
        6,
    )
    gate_grad, up_grad, down_total, query_grad, key_grad, value_grad, heads_total = place_grads(
        *gathered
    )
    return (
        layer_out[None],
        grad_inputs[None],
        query_grad,
        key_grad,
        value_grad,
        heads_total,
        gate_grad,
        up_grad,
        down_total,
        gains[0],
        gains[1],
    )


def solution(mesh):
    placed = (
        P("fsdp", "seq", None),
        P("fsdp", None),
        P("fsdp", None),
        P("fsdp", None),
        P("fsdp", None),
        P("fsdp", None),
        P("fsdp", None),
        P("fsdp", None),
        P("fsdp", None),
        P("fsdp"),
        P("fsdp"),
        P("fsdp", "seq", None),
    )
    return jax.shard_map(
        shards,
        mesh=mesh,
        in_specs=placed,
        out_specs=(
            P("fsdp", "seq", None),
            P("fsdp", "seq", None),
            P("fsdp", None),
            P("fsdp", None),
            P("fsdp", None),
            P("fsdp", None),
            P("fsdp", None),
            P("fsdp", None),
            P("fsdp", None),
            P("fsdp"),
            P("fsdp"),
        ),
        check_vma=False,
    )
```

```python
import math

import jax
import jax.numpy as jnp
from jax import lax
from jax.experimental import pallas as pl
from jax.experimental.pallas import tpu as pltpu
from jax.sharding import PartitionSpec as P

HEAD_SIZE = 64
EPS = 1e-05
ROPE_BASE = 500000.0
NEG = -1e30


def rope_freqs(head_dim):
    half_dim = head_dim // 2
    table = []
    for index in range(half_dim):
        inverse = 1.0 / ROPE_BASE ** (index * 2.0 / head_dim)
        wavelen = 2.0 * math.pi / inverse
        blend = (8192.0 / wavelen - 1.0) / 3.0
        mixed = (1.0 - blend) * inverse / 32.0 + blend * inverse
        entry = inverse if wavelen < 2048.0 else inverse / 32.0 if wavelen > 8192.0 else mixed
        table.append(entry)
    return jnp.asarray(table, dtype=jnp.float32)


MESH = pl.DeviceIdType.MESH
CHUNKS = 4
TILE = 256


class Ring:
    def __init__(self, place, count, index_of, device_of):
        side = count // 2
        self.place = place
        row, col = lax.div(place, side), lax.rem(place, side)

        def at(which, step):
            return index_of(which * side + lax.rem(col + step, side))

        self.near = [at(row, step) for step in range(side)]
        self.far = [at(1 - row, step) for step in range(side)]
        self.right = device_of(self.near[1])
        self.left = device_of(self.near[3])
        self.partner = device_of(self.far[0])
        self.peers = [self.right, self.left, self.partner]
        self.remote = [device_of(index) for index in (self.near[2], *self.far[1:])]
        self.device_of = device_of


def seq_ring():
    rank, owner = lax.axis_index("seq"), lax.axis_index("fsdp")
    return Ring(rank, lax.axis_size("seq"), lambda place: place, lambda index: (index, owner))


def fsdp_ring():
    rank, owner = lax.axis_index("seq"), lax.axis_index("fsdp")
    core = lax.rem(owner, 2)
    ring = Ring(
        lax.div(owner, 2),
        lax.axis_size("fsdp") // 2,
        lambda place: 2 * place + core,
        lambda index: (rank, index),
    )
    return ring, core, (rank, owner + 1 - 2 * core)


def greet(peers):
    barrier = pltpu.get_barrier_semaphore()
    for peer in peers:
        pl.semaphore_signal(barrier, inc=1, device_id=peer, device_id_type=MESH)
    pl.semaphore_wait(barrier, len(peers))


def in_step(*walks):
    left = list(walks)
    while left:
        left = [walk for walk in left if next(walk, walk) is not walk]
        yield


def beside(main, *sides):
    sides = [(walk, list(places)) for walk, places in sides]
    step = 0
    for _ in main:
        for walk, places in sides:
            while places and places[0] <= step:
                places.pop(0)
                next(walk, None)
        step += 1
    for _ in in_step(*(walk for walk, _ in sides)):
        pass


class Copies:
    def __init__(self, send, recv):
        self.send, self.recv = send, recv
        self.made = []

    def start(self, source, target, peer):
        number = len(self.made)
        copy = pltpu.make_async_remote_copy(
            src_ref=source,
            dst_ref=target,
            send_sem=self.send.at[number],
            recv_sem=self.recv.at[number],
            device_id=peer,
            device_id_type=MESH,
        )
        copy.start()
        self.made.append(copy)
        return copy

    def finish(self):
        for copy in self.made:
            copy.wait_send()


def by_rows(rows, chunks):
    size = rows // chunks
    return lambda ref, index: ref.at[pl.ds(index * size, size)]


def by_columns(columns, chunks):
    size = columns // chunks
    return lambda ref, index: ref.at[:, pl.ds(index * size, size)]


def chunk_rows(rows, index):
    size = rows // CHUNKS
    return pl.ds(index * size, size)


def exchange_all(ring, copies, piece, target):
    made = []
    for index in (*ring.far[1:], ring.near[2], ring.far[0], ring.near[1], ring.near[3]):
        made.append(copies.start(piece(index), target, ring.device_of(index)))
    return made


def gather_walk(ring, copies, own, out, cut, chunks, deep=False, mate=None):
    me, right, opposite, left = ring.near
    partner, far_right, _, far_left = ring.far
    half = chunks // 2
    passed = []

    def share(place, index):
        if mate is not None:
            block = cut(out.at[place], index)
            passed.append(copies.start(block, block, mate))

    to_right, to_left, to_far, on = {}, {}, {}, {}
    for step in range(chunks):
        back = chunks - 1 - step
        if not deep:
            to_far[step] = copies.start(cut(own, step), cut(out.at[me], step), ring.partner)
        to_right[step] = copies.start(cut(own, step), cut(out.at[me], step), ring.right)
        to_left[back] = copies.start(cut(own, back), cut(out.at[me], back), ring.left)
        if mate is not None:
            passed.append(copies.start(cut(own, step), cut(out.at[me], step), mate))
    yield
    if deep:
        for step in range(chunks):
            to_far[step] = copies.start(cut(own, step), cut(out.at[me], step), ring.partner)
        yield
    for step in range(half):
        back = chunks - 1 - step
        to_right[step].wait_recv()
        block = cut(out.at[left], step)
        on[step] = copies.start(block, block, ring.right)
        share(left, step)
        to_left[back].wait_recv()
        block = cut(out.at[right], back)
        on[back] = copies.start(block, block, ring.left)
        share(right, back)
        yield
    far_on, rest = {}, []
    for step in range(chunks):
        to_far[step].wait_recv()
        block = cut(out.at[partner], step)
        far_on[0, step] = copies.start(block, block, ring.right)
        far_on[1, step] = copies.start(block, block, ring.left)
        share(partner, step)
        yield
    if deep:
        for step in range(half):
            back = chunks - 1 - step
            far_on[0, step].wait_recv()
            block = cut(out.at[far_left], step)
            rest.append((step, copies.start(block, block, ring.right)))
            share(far_left, step)
            far_on[1, back].wait_recv()
            block = cut(out.at[far_right], back)
            rest.append((back, copies.start(block, block, ring.left)))
            share(far_right, back)
            yield
    def finals():
        for step in range(half):
            back = chunks - 1 - step
            to_right[back].wait_recv()
            share(left, back)
            to_left[step].wait_recv()
            share(right, step)
            if deep:
                far_on[0, back].wait_recv()
                share(far_left, back)
                far_on[1, step].wait_recv()
                share(far_right, step)
            yield

    if not deep:
        yield from finals()
    for step in range(half):
        for index in (step, chunks - 1 - step):
            on[index].wait_recv()
            if not deep:
                block = cut(out.at[opposite], index)
                rest.append((index, copies.start(block, block, ring.partner)))
            share(opposite, index)
        yield
    if deep:
        yield from finals()
    else:
        for copy in far_on.values():
            copy.wait_recv()
        yield
    for index, copy in rest:
        copy.wait_recv()
        share(ring.far[2], index)
    yield
    for copy in passed:
        copy.wait_recv()


def gather_copies(chunks, mate=False):
    return 7 * chunks + (8 * chunks if mate else 0)


def reduce_walk(ring, copies, part_of, bufs, cut, chunks, done, ready=None):
    me, right, opposite, left = ring.near
    partner, far_right, far_opposite, far_left = ring.far
    from_left, from_right, from_far, mid, end_left, end_right, end_far = bufs
    half = chunks // 2

    def wide(ref, index):
        return cut(ref, index)[...].astype(jnp.float32)

    def keep(ref, index, value):
        cut(ref, index)[...] = value.astype(jnp.bfloat16)

    def send(block, index, target, device):
        return copies.start(cut(block, index), cut(target, index), device)

    order = [x for step in range(half) for x in (step, chunks - 1 - step)]
    one_right, one_left, one_far, last_right, last_left, last_far = ({} for _ in range(6))
    if ready is None:
        for index in order:
            one_far[index] = send(part_of.at[far_opposite], index, from_far, ring.partner)
            one_right[index] = send(part_of.at[far_right], index, from_left, ring.right)
            one_left[index] = send(part_of.at[far_left], index, from_right, ring.left)
    else:
        ready(far_right, far_left)
        for index in order:
            one_right[index] = send(part_of.at[far_right], index, from_left, ring.right)
            one_left[index] = send(part_of.at[far_left], index, from_right, ring.left)
        yield
        ready(far_opposite, right)
        for index in order:
            one_far[index] = send(part_of.at[far_opposite], index, from_far, ring.partner)
    for index in range(half):
        last_right[index] = send(part_of.at[right], index, end_left, ring.right)
    if ready is not None:
        yield
        ready(left, opposite)
    for index in range(half):
        back = chunks - 1 - index
        last_left[back] = send(part_of.at[left], back, end_right, ring.left)
    if ready is not None:
        yield
        ready(partner, me)
    yield
    two = {}
    for index in order:
        one_far[index].wait_recv()
        keep(from_far, index, wide(from_far, index) + wide(part_of.at[opposite], index))
        two[index] = send(from_far, index, mid, ring.left if index < half else ring.right)
        yield
    for index in order:
        one_right[index].wait_recv()
        one_left[index].wait_recv()
        total = wide(from_left, index) + wide(from_right, index)
        keep(from_left, index, total + wide(part_of.at[partner], index))
        last_far[index] = send(from_left, index, end_far, ring.partner)
        yield
    for index in order:
        two[index].wait_recv()
        if index < half:
            keep(mid, index, wide(mid, index) + wide(part_of.at[left], index))
            last_left[index] = send(mid, index, end_right, ring.left)
        else:
            keep(mid, index, wide(mid, index) + wide(part_of.at[right], index))
            last_right[index] = send(mid, index, end_left, ring.right)
        yield
    for index in order:
        last_far[index].wait_recv()
        last_left[index].wait_recv()
        last_right[index].wait_recv()
        total = wide(part_of.at[me], index) + wide(end_left, index)
        done(index, total + wide(end_right, index) + wide(end_far, index))
        yield


def reduce_copies(chunks):
    return 3 * chunks + 2 * chunks + chunks + chunks


def owners_walk(ring, mate, copies, produce, own, other, bufs, rows, done):
    mids, from_lefts, from_rights, from_far = bufs[:2], bufs[2:4], bufs[4:6], bufs[6]
    half = rows // 2
    low, high = pl.ds(0, half), pl.ds(half, half)
    near, far = ([lax.div(index, 2) for index in row] for row in (ring.near, ring.far))
    order = [far[2], far[1], far[3], near[2], near[1], near[3], far[0], near[0]]
    awaited = []

    def wide(ref):
        return ref.astype(jnp.float32)

    def add(*numbers):
        for number in numbers:
            for wait in awaited[number]:
                wait()
            place = order[number]
            own[place] = (wide(own[place]) + wide(other[place])).astype(jnp.bfloat16)

    def make(number):
        awaited.append(produce(order[number]))

    on, ends = ([], []), ([], [])

    def half_way(which):
        block = own.at[(far, near)[which][2]]
        on[which].append(copies.start(block.at[low], mids[which].at[low], ring.left))
        on[which].append(copies.start(block.at[high], mids[which].at[high], ring.right))

    def sides(which):
        row = (far, near)[which]
        ends[which].append(
            copies.start(own.at[row[1], low], from_lefts[which].at[low], ring.right)
        )
        ends[which].append(
            copies.start(own.at[row[3], high], from_rights[which].at[high], ring.left)
        )

    def other_sides(which):
        row, mid = (far, near)[which], mids[which]
        on[which][0].wait_recv()
        mid[low] = (wide(mid[low]) + wide(own[row[3], low])).astype(jnp.bfloat16)
        ends[which].append(copies.start(mid.at[low], from_rights[which].at[low], ring.left))
        on[which][1].wait_recv()
        mid[high] = (wide(mid[high]) + wide(own[row[1], high])).astype(jnp.bfloat16)
        ends[which].append(copies.start(mid.at[high], from_lefts[which].at[high], ring.right))

    make(0)
    yield
    make(1)
    yield
    add(0)
    half_way(0)
    yield
    make(2)
    yield
    add(1, 2)
    sides(0)
    yield
    make(3)
    yield
    make(4)
    yield
    other_sides(0)
    yield
    add(3)
    half_way(1)
    yield
    make(5)
    yield
    add(4, 5)
    sides(1)
    yield
    make(6)
    yield
    make(7)
    yield
    add(6, 7)
    yield
    last = []
    for copy in ends[0]:
        copy.wait_recv()
    for rows_of in (low, high):
        total = (
            wide(from_lefts[0][rows_of])
            + wide(from_rights[0][rows_of])
            + wide(own[far[0], rows_of])
        )
        from_lefts[0][rows_of] = total.astype(jnp.bfloat16)
        last.append(copies.start(from_lefts[0].at[rows_of], from_far.at[rows_of], ring.partner))
    yield
    other_sides(1)
    yield
    for copy in ends[1]:
        copy.wait_recv()
    yield
    for rows_of, copy in zip((low, high), last):
        copy.wait_recv()
        done(
            rows_of,
            wide(from_lefts[1][rows_of])
            + wide(from_rights[1][rows_of])
            + wide(own[near[0], rows_of])
            + wide(from_far[rows_of]),
        )
        yield


OWNERS_COPIES = 4 + 4 + 4 + 2


def owners_scratch(places, rows, width):
    return [pltpu.VMEM((places, rows, width), jnp.bfloat16) for _ in range(2)] + [
        pltpu.VMEM((rows, width), jnp.bfloat16) for _ in range(7)
    ]


def reduce_scratch(rows, width):
    return [pltpu.VMEM((rows, width), jnp.bfloat16) for _ in range(7)]


def semaphores(count):
    return [pltpu.SemaphoreType.DMA((count,)), pltpu.SemaphoreType.DMA((count,))]


def params(number, limit):
    return pltpu.CompilerParams(
        collective_id=number, has_side_effects=True, vmem_limit_bytes=limit * 2**20
    )


VMEM = pl.BlockSpec(memory_space=pltpu.VMEM)
ANYWHERE = pl.BlockSpec(memory_space=pl.ANY)


SMALL_BESIDE = (0, 2, 2, 3, 6, 6, 6, 6, 8, 8, 9, 9, 10, 10, 11)
LARGE_BESIDE = (0, 1, 2, 3, 5, 6, 7, 7, 8, 8, 8, 8, 9, 9, 10)


def weight_walk(ring, copies, own, out, mate):
    return gather_walk(ring, copies, own, out, by_rows(own.shape[0], CHUNKS), CHUNKS, True, mate)


def chosen_half(first, second, odd):
    low, high = merge_lanes(first.astype(jnp.float32), second.astype(jnp.float32))
    return jnp.where(odd == 0, low, high).astype(jnp.bfloat16)


class Pick:
    def __init__(self, sems, wide, narrow, rank):
        self.sems, self.wide, self.narrow = sems, wide, narrow
        self.pair, self.odd = lax.div(rank, 2), lax.rem(rank, 2)
        self.rank = rank
        self.count = 0

    def fetch(self, source, target):
        copy = pltpu.make_async_copy(source, target, self.sems.at[self.count])
        copy.start()
        self.count += 1
        return copy

    def lanes(self, first):
        return pl.ds(pl.multiple_of(first + self.pair * LANES, LANES), LANES)

    def start_units(self, which, source):
        owners = self.wide.shape[1]
        stride = source.shape[1] // owners
        return [
            self.fetch(source.at[:, self.lanes(owner * stride)], self.wide.at[which, owner])
            for owner in range(owners)
        ]

    def finish_units(self, which, made, out):
        for copy in made:
            copy.wait()
        for index in range(self.wide.shape[1] // 2):
            out[:, pl.ds(index * LANES, LANES)] = chosen_half(
                self.wide[which, 2 * index], self.wide[which, 2 * index + 1], self.odd
            )

    def start_heads(self, query, key, value, out):
        rows, cols = query.shape[0], out.shape[1] - LANES
        first = pl.multiple_of(self.rank * cols, LANES)
        return [
            self.fetch(query.at[:, pl.ds(first, cols)], out.at[pl.ds(0, rows), pl.ds(0, cols)]),
            self.fetch(key.at[:, self.lanes(0)], self.narrow.at[0]),
            self.fetch(value.at[:, self.lanes(0)], self.narrow.at[1]),
        ]

    def finish_heads(self, made, gain_one, gain_two, out):
        rows = self.narrow.shape[1]
        line = lax.broadcasted_iota(jnp.int32, (16, rows), 0)
        first, second = (gain[...].astype(jnp.float32) for gain in (gain_one, gain_two))
        gains = jnp.where(line == 0, first, jnp.where(line == 1, second, 0.0))
        out[pl.ds(rows, 32)] = jnp.zeros((32, out.shape[1]), jnp.bfloat16)
        out[pl.ds(rows, 16), pl.ds(0, rows)] = gains.astype(jnp.bfloat16)
        for copy in made:
            copy.wait()
        out[pl.ds(0, rows), pl.ds(out.shape[1] - LANES, LANES)] = chosen_half(
            self.narrow[0], self.narrow[1], self.odd
        )


def first_positions(segments):
    index = lax.broadcasted_iota(jnp.int32, segments.shape, 1)
    begins = (index == 0) | (segments != pltpu.roll(segments, 1, 1))
    starts = jnp.where(begins, index, 0)
    shift = 1
    while shift < segments.shape[1]:
        starts = jnp.maximum(starts, jnp.where(index >= shift, pltpu.roll(starts, shift, 1), 0))
        shift *= 2
    return starts, index


def first_kernel(
    tokens,
    query,
    key,
    value,
    gate,
    up,
    gain_one,
    gain_two,
    segments,
    freqs,
    hidden,
    qkv,
    heads_turned,
    gate_all,
    up_own,
    cosine,
    sine,
    starts,
    gain_one_all,
    gain_two_all,
    tokens_here,
    hidden_here,
    heads_own,
    heads_all,
    gate_own,
    wide,
    narrow,
    picks,
    stores,
    local,
    send,
    recv,
):
    ring = seq_ring()
    weights_ring, _, mate = fsdp_ring()
    greet(ring.peers + weights_ring.peers + [mate])
    copies = Copies(send, recv)
    me, here = ring.near[0], weights_ring.near[0]
    rows = tokens.shape[0]
    kept = [pltpu.make_async_copy(tokens, tokens_here.at[me], local.at[0])]
    kept[0].start()
    pick = Pick(picks, wide, narrow, lax.axis_index("seq"))
    heads_made = pick.start_heads(query, key, value, heads_own)
    gate_made = pick.start_units(0, gate)
    up_made = pick.start_units(1, up)

    def heads_walk():
        pick.finish_heads(heads_made, gain_one, gain_two, heads_own)
        copy = pltpu.make_async_copy(heads_own, heads_all.at[here], local.at[1])
        copy.start()
        kept.append(copy)
        yield from gather_walk(
            weights_ring,
            copies,
            heads_own,
            heads_all,
            by_rows(heads_own.shape[0], 2),
            2,
            True,
            mate,
        )

    def gate_walk():
        pick.finish_units(0, gate_made, gate_own)
        copy = pltpu.make_async_copy(gate_own, gate_all.at[here], local.at[2])
        copy.start()
        kept.append(copy)
        yield from weight_walk(weights_ring, copies, gate_own, gate_all, mate)

    def project(index):
        values = tokens_here[index].astype(jnp.float32)
        factor = lax.rsqrt(mean_square(values) + EPS)
        hidden_here[index] = (values * factor * gain_one_all[...]).astype(jnp.bfloat16)
        copy = pltpu.make_async_copy(hidden_here.at[index], hidden.at[index], stores.at[len(stored)])
        copy.start()
        stored.append(copy)
        lanes = pl.ds(pl.multiple_of(index * rows, rows), rows)
        qkv[:, lanes] = lax.dot_general(
            heads_turned[...],
            hidden_here[index],
            (((1,), (1,)), ((), ())),
            preferred_element_type=jnp.float32,
        ).astype(jnp.bfloat16)

    stored = []

    def compute():
        pick.finish_units(1, up_made, up_own)
        first, index = first_positions(segments[...])
        starts[...] = first
        phase = (index - first).astype(jnp.float32) * freqs[...]
        cosine[...] = jnp.cos(phase)
        sine[...] = jnp.sin(phase)
        yield
        for copy in kept:
            copy.wait()
        for owner in range(heads_all.shape[0]):
            cols = pl.ds(owner * rows, rows)
            heads_turned[:, cols] = heads_all[owner, :rows].T
            gains = heads_all[owner, pl.ds(rows, 16), pl.ds(0, rows)].astype(jnp.float32)
            gain_one_all[:, cols] = gains[0:1]
            gain_two_all[:, cols] = gains[1:2]
        project(me)
        yield
        project(ring.far[0])
        yield
        for place in (ring.near[1], ring.near[3], ring.near[2]):
            project(place)
        yield
        project(ring.far[1])
        project(ring.far[3])
        yield
        project(ring.far[2])

    beside(
        gather_walk(ring, copies, tokens, tokens_here, by_rows(rows, CHUNKS), CHUNKS),
        (heads_walk(), (0, 0, 1, 2, 2, 4, 6, 6, 6, 7)),
        (gate_walk(), SMALL_BESIDE),
        (compute(), (0, 7, 8, 10, 11, 12)),
    )
    copies.finish()
    for copy in stored:
        copy.wait()


LANES = 128


def gather_first(tokens, query, key, value, gate, up, gain_one, gain_two, segments, freqs, number):
    rows, width = tokens.shape
    ranks, owners = lax.axis_size("seq"), lax.axis_size("fsdp")
    length = segments.shape[1]
    cols = width // ranks + LANES
    units = owners // 2 * LANES
    assert gate.shape[1] // owners // ranks == HEAD_SIZE == LANES // 2
    count = gather_copies(CHUNKS) + gather_copies(2, True) + gather_copies(CHUNKS, True)
    low, real = jnp.bfloat16, jnp.float32
    return pl.pallas_call(
        first_kernel,
        out_shape=[
            jax.ShapeDtypeStruct((ranks, rows, width), low),
            jax.ShapeDtypeStruct((cols, length), low),
            jax.ShapeDtypeStruct((cols, width), low),
            jax.ShapeDtypeStruct((owners, rows, units), low),
            jax.ShapeDtypeStruct((rows, units), low),
            jax.ShapeDtypeStruct((freqs.shape[0], length), real),
            jax.ShapeDtypeStruct((freqs.shape[0], length), real),
            jax.ShapeDtypeStruct((1, length), jnp.int32),
            jax.ShapeDtypeStruct((1, width), real),
            jax.ShapeDtypeStruct((1, width), real),
        ],
        in_specs=[ANYWHERE] * 6 + [VMEM] * 4,
        out_specs=[ANYWHERE, VMEM, VMEM, ANYWHERE] + [VMEM] * 6,
        scratch_shapes=[
            pltpu.VMEM((ranks, rows, width), low),
            pltpu.VMEM((ranks, rows, width), low),
            pltpu.VMEM((rows + 32, cols), low),
            pltpu.VMEM((owners, rows + 32, cols), low),
            pltpu.VMEM((rows, units), low),
            pltpu.VMEM((2, owners, rows, LANES), low),
            pltpu.VMEM((2, rows, LANES), low),
            pltpu.SemaphoreType.DMA((2 * owners + 3,)),
            pltpu.SemaphoreType.DMA((ranks,)),
            pltpu.SemaphoreType.DMA((3,)),
        ]
        + semaphores(count),
        compiler_params=params(number, 40),
        name="gather_first",
    )(tokens, query, key, value, gate, up, gain_one[None], gain_two[None], segments, freqs)


def mean_square(values):
    return jnp.mean(values * values, axis=-1, keepdims=True)


PRODUCT = 512


def product(left, right, store, size=PRODUCT):
    def columns(index, _):
        cols = pl.ds(pl.multiple_of(index * size, size), size)
        store(cols, jnp.dot(left, right[:, cols], preferred_element_type=jnp.float32))
        return 0

    lax.fori_loop(0, right.shape[1] // size, columns, 0)


def two_blocks(ref, rows, first, second):
    return jnp.concatenate(
        [ref[pl.ds(pl.multiple_of(index * rows, rows), rows)] for index in (first, second)], axis=0
    )


def split_store(for_mate, own, place, core):
    def store(cols, value):
        rows = value.shape[0] // 2
        first = core == 0
        theirs = jnp.where(first, value[rows:], value[:rows])
        for_mate[place, :, cols] = theirs.astype(jnp.bfloat16)
        ours = jnp.where(first, value[:rows], value[rows:])
        own[place, :, cols] = ours.astype(jnp.bfloat16)

    return store


def branch_kernel(
    attended,
    tokens,
    gain,
    weight,
    gate,
    up,
    down,
    grad_out,
    middle,
    attended_here,
    hidden,
    up_all,
    down_all,
    act_out,
    gate_out,
    up_out,
    block,
    got,
    weight_here,
    gate_here,
    up_here,
    down_here,
    grad_out_here,
    hidden_here,
    gated,
    upped,
    grad_act,
    act,
    grad_gate,
    grad_up,
    stores,
    local,
    send,
    recv,
):
    ring = seq_ring()
    weights_ring, _, mate = fsdp_ring()
    rows = tokens.shape[0]
    greet(ring.peers + ring.remote + weights_ring.peers + [mate])
    copies = Copies(send, recv)
    me, here = ring.near[0], weights_ring.near[0]

    def lanes_of(index):
        return attended.at[:, pl.ds(pl.multiple_of(index * rows, rows), rows)]

    arriving = exchange_all(ring, copies, lanes_of, got.at[me])
    load = pltpu.make_async_copy(weight, weight_here, local.at[0])
    load.start()
    mine = pltpu.make_async_copy(lanes_of(me), got.at[me], local.at[1])
    mine.start()
    kept = [
        pltpu.make_async_copy(up, up_here.at[here], local.at[2]),
        pltpu.make_async_copy(down, down_here.at[here], local.at[3]),
        pltpu.make_async_copy(gate, gate_here, local.at[4]),
        pltpu.make_async_copy(grad_out, grad_out_here, local.at[5]),
    ]
    for copy in kept:
        copy.start()
    stored = []

    def store(source, target):
        copy = pltpu.make_async_copy(source, target, stores.at[len(stored)])
        copy.start()
        stored.append(copy)

    def walk():
        yield
        mine.wait()
        load.wait()
        for copy in arriving:
            copy.wait_recv()
        attended_here[...] = got[...].reshape(attended_here.shape)
        turned = attended_here[...].T

        def add(cols, value):
            middle[:, cols] = tokens[:, cols].astype(jnp.float32) + value

        product(turned, weight_here, add)
        values = middle[...]
        factor = lax.rsqrt(mean_square(values) + EPS)
        block[...] = (values * factor * gain[...]).astype(jnp.bfloat16)
        hidden_here[me] = block[...]
        yield from gather_walk(
            ring, copies, block, hidden_here, by_rows(rows, CHUNKS), CHUNKS
        )

    units = gated.shape[2]

    def both(ref, pair):
        return jnp.concatenate([ref[index] for index in pair], axis=0)

    def times(pair, matrix, out):
        left = both(hidden_here, pair)

        def columns(tile, _):
            cols = pl.ds(pl.multiple_of(tile * PRODUCT, PRODUCT), PRODUCT)
            right = matrix[:, :, cols].reshape(-1, PRODUCT)
            value = jnp.dot(left, right, preferred_element_type=jnp.float32)
            out[pair[0], :, cols] = value[:rows]
            out[pair[1], :, cols] = value[rows:]
            return 0

        lax.fori_loop(0, units // PRODUCT, columns, 0)

    def back(pair):
        left = both(grad_out_here, pair)
        share = PRODUCT // down_here.shape[1]

        def columns(tile, _):
            cols = pl.ds(pl.multiple_of(tile * PRODUCT, PRODUCT), PRODUCT)
            right = down_here[pl.ds(tile * share, share)].reshape(PRODUCT, -1)
            value = lax.dot_general(
                left, right, (((1,), (1,)), ((), ())), preferred_element_type=jnp.float32
            )
            grad_act[pair[0], :, cols] = value[:rows]
            grad_act[pair[1], :, cols] = value[rows:]
            return 0

        lax.fori_loop(0, units // PRODUCT, columns, 0)

    def combine(pair):
        for index in pair:
            value, other, grad = gated[index], upped[index], grad_act[index]
            sig = jax.nn.sigmoid(value)
            silu = value * sig
            act[index] = (silu * other).astype(jnp.bfloat16)
            grad_gate[index] = (grad * other * (sig * (1.0 + value * (1.0 - sig)))).astype(
                jnp.bfloat16
            )
            grad_up[index] = (grad * silu).astype(jnp.bfloat16)
            store(act.at[index], act_out.at[index])
            store(grad_gate.at[index], gate_out.at[index])
            store(grad_up.at[index], up_out.at[index])

    near, far = ring.near, ring.far
    pairs = ((near[0], far[0]), (near[1], near[3]), (far[1], far[3]), (near[2], far[2]))

    def compute():
        kept[0].wait()
        kept[1].wait()
        kept[2].wait()
        kept[3].wait()
        store(down_here, down_all)
        back(pairs[0])
        yield
        back(pairs[1])
        yield
        back(pairs[2])
        yield
        back(pairs[3])
        yield
        times(pairs[0], gate_here, gated)
        yield
        times(pairs[1], gate_here, gated)
        yield
        store(up_here, up_all)
        times(pairs[0], up_here, upped)
        combine(pairs[0])
        yield
        times(pairs[1], up_here, upped)
        combine(pairs[1])
        yield
        for pair in pairs[2:]:
            for index in pair:
                store(hidden_here.at[index], hidden.at[index])
            times(pair, gate_here, gated)
            times(pair, up_here, upped)
            combine(pair)
            yield

    def hold():
        for index in (*pairs[0], *pairs[1]):
            store(hidden_here.at[index], hidden.at[index])
        yield

    beside(
        walk(),
        (weight_walk(weights_ring, copies, down, down_here, mate), BESIDE_FIRST),
        (weight_walk(weights_ring, copies, up, up_here, mate), BESIDE_SECOND),
        (hold(), (9,)),
        (compute(), (4, 5, 6, 7, 7, 9, 11, 11, 12, 13)),
    )
    copies.finish()
    for copy in stored:
        copy.wait()


BESIDE_FIRST = (0, 0, 0, 0, 0, 0, 0, 0, 1, 1, 1, 1, 2, 2, 3, 4)
BESIDE_SECOND = (0, 0, 1, 1, 1, 1, 2, 2, 7, 7, 7, 7, 9, 9, 10, 11)


def add_branch(attended, tokens, gain, weight, gate, up, down, grad_out, number):
    rows, width = tokens.shape
    ranks, owners = lax.axis_size("seq"), lax.axis_size("fsdp")
    features, units = attended.shape[0], up.shape[1]
    count = ranks - 1 + gather_copies(CHUNKS) + 2 * gather_copies(CHUNKS, True)
    low, real = jnp.bfloat16, jnp.float32
    return pl.pallas_call(
        branch_kernel,
        out_shape=[
            jax.ShapeDtypeStruct((rows, width), real),
            jax.ShapeDtypeStruct((ranks * features, rows), low),
            jax.ShapeDtypeStruct((ranks, rows, width), low),
            jax.ShapeDtypeStruct((owners, *up.shape), low),
            jax.ShapeDtypeStruct((owners, *down.shape), low),
        ]
        + [jax.ShapeDtypeStruct((ranks, rows, units), low)] * 3,
        in_specs=[VMEM] * 3 + [ANYWHERE] * 5,
        out_specs=[VMEM] * 2 + [ANYWHERE] * 6,
        scratch_shapes=[
            pltpu.VMEM((rows, width), low),
            pltpu.VMEM((ranks, features, rows), low),
            pltpu.VMEM(weight.shape, low),
            pltpu.VMEM(gate.shape, low),
            pltpu.VMEM((owners, *up.shape), low),
            pltpu.VMEM((owners, *down.shape), low),
            pltpu.VMEM((ranks, rows, width), low),
            pltpu.VMEM((ranks, rows, width), low),
        ]
        + [pltpu.VMEM((ranks, rows, units), real)] * 3
        + [pltpu.VMEM((ranks, rows, units), low)] * 3
        + [pltpu.SemaphoreType.DMA((4 * ranks + 2,)), pltpu.SemaphoreType.DMA((6,))]
        + semaphores(count),
        compiler_params=params(number, 60),
        name="add_branch",
    )(attended, tokens, gain, weight, gate, up, down, grad_out)


def norm_back_rows(grad, gain, values):
    factor = lax.rsqrt(mean_square(values) + EPS)
    normed = values * factor
    weighted = grad * gain
    back = factor * (weighted - normed * jnp.mean(weighted * normed, axis=-1, keepdims=True))
    return back, grad * normed


def middle_kernel(
    middle,
    gain,
    cotangent,
    hidden,
    gate_grads,
    up_grads,
    gate,
    up,
    weight,
    grad_middle,
    grad_gain,
    block,
    grad_attended,
    grads_share,
    part_of,
    ff_here,
    weight_here,
    given,
    got,
    send,
    recv,
    left_wide,
    right_wide,
    for_mate,
    loads,
    own,
    other,
    *bufs,
):
    ring = seq_ring()
    weights_ring, core, mate = fsdp_ring()
    rows = middle.shape[0]
    greet(ring.peers + ring.remote + weights_ring.peers + [mate])
    copies = Copies(send, recv)
    grad_gain[...] = jnp.zeros_like(grad_gain)

    def load(source, target, number):
        return pltpu.make_async_copy(source, target, loads.at[number])

    units = gate_grads.shape[1]
    first = [
        load(hidden, left_wide, 0),
        load(gate_grads, right_wide.at[:, pl.ds(0, units)], 1),
        load(up_grads, right_wide.at[:, pl.ds(units, units)], 2),
    ]
    ff = [
        load(gate, ff_here.at[:, pl.ds(0, units)], 3),
        load(up, ff_here.at[:, pl.ds(units, units)], 4),
    ]
    weight_load = load(weight, weight_here, 5)
    for copy in first[1:] + ff + first[:1] + [weight_load]:
        copy.start()
    arrived = first[1:] + ff

    def ready(*blocks):
        while arrived:
            arrived.pop().wait()
        left = two_blocks(right_wide, rows, *blocks)

        def columns(tile, _):
            cols = pl.ds(pl.multiple_of(tile * PRODUCT, PRODUCT), PRODUCT)
            value = lax.dot_general(
                left, ff_here[cols], (((1,), (1,)), ((), ())), preferred_element_type=jnp.float32
            ).astype(jnp.bfloat16)
            part_of[blocks[0], :, cols] = value[:rows]
            part_of[blocks[1], :, cols] = value[rows:]
            return 0

        lax.fori_loop(0, ff_here.shape[0] // PRODUCT, columns, 0)

    def done(index, total):
        rows_of = chunk_rows(rows, index)
        back, terms = norm_back_rows(total, gain[...], middle[rows_of])
        grad_gain[...] += jnp.sum(terms, axis=0, keepdims=True)
        values = cotangent[rows_of].astype(jnp.float32) + back
        grad_middle[rows_of] = values
        block[rows_of] = values.astype(jnp.bfloat16)

    def owned(rows_of, total):
        grads_share[rows_of] = total.astype(jnp.bfloat16)

    me = ring.near[0]
    features = grad_attended.shape[0]

    def walk():
        yield from reduce_walk(
            ring, copies, part_of, bufs[7:], by_rows(rows, CHUNKS), CHUNKS, done, ready
        )
        weight_load.wait()

        def piece(index):
            part = pl.ds(pl.multiple_of(index * features, features), features)
            given[index] = lax.dot_general(
                weight_here[part],
                block[...],
                (((1,), (1,)), ((), ())),
                preferred_element_type=jnp.float32,
            ).astype(jnp.bfloat16)
            return given.at[index]

        arriving = exchange_all(ring, copies, piece, got.at[me])
        piece(me)
        yield
        for copy in arriving:
            copy.wait_recv()
        got[me] = given[me]
        for index in range(got.shape[0]):
            grad_attended[:, pl.ds(index * rows, rows)] = got[index]

    def produce(place):
        if first:
            first.pop(0).wait()
            first.clear()
        lanes = pl.ds(pl.multiple_of(place * 2 * rows, 2 * rows), 2 * rows)
        turned = left_wide[:, lanes].T
        product(turned, right_wide, split_store(for_mate, own, place, core), 2 * PRODUCT)
        return [copies.start(for_mate.at[place], other.at[place], mate).wait_recv]

    beside(
        walk(),
        (
            owners_walk(
                weights_ring,
                mate,
                copies,
                produce,
                own,
                other,
                bufs[:7],
                grads_share.shape[0],
                owned,
            ),
            (0, 0, 0, 1, 1, 11, 11, 11, 11, 15, 15, 15, 15, 15, 19, 19, 20, 20, 20),
        ),
    )
    copies.finish()


def back_to_middle(
    middle,
    gain,
    cotangent,
    hidden,
    gate_grads,
    up_grads,
    gate,
    up,
    weight,
    number,
):
    rows, width = middle.shape
    length = hidden.shape[0]
    ranks, owners = lax.axis_size("seq"), lax.axis_size("fsdp")
    places = owners // 2
    grad_rows, grad_cols = width // owners, 2 * gate_grads.shape[1]
    features = weight.shape[0] // ranks
    count = reduce_copies(CHUNKS) + ranks - 1 + OWNERS_COPIES + places
    return pl.pallas_call(
        middle_kernel,
        out_shape=[
            jax.ShapeDtypeStruct((rows, width), jnp.float32),
            jax.ShapeDtypeStruct((1, width), jnp.float32),
            jax.ShapeDtypeStruct((rows, width), jnp.bfloat16),
            jax.ShapeDtypeStruct((features, length), jnp.bfloat16),
            jax.ShapeDtypeStruct((grad_rows, grad_cols), jnp.bfloat16),
        ],
        in_specs=[VMEM] * 3 + [ANYWHERE] * 6,
        out_specs=[VMEM] * 5,
        scratch_shapes=[
            pltpu.VMEM((ranks, rows, width), jnp.bfloat16),
            pltpu.VMEM((width, grad_cols), jnp.bfloat16),
            pltpu.VMEM(weight.shape, jnp.bfloat16),
            pltpu.VMEM((ranks, features, rows), jnp.bfloat16),
            pltpu.VMEM((ranks, features, rows), jnp.bfloat16),
        ]
        + semaphores(count)
        + [
            pltpu.VMEM((length, width), jnp.bfloat16),
            pltpu.VMEM((length, width), jnp.bfloat16),
            pltpu.VMEM((places, grad_rows, grad_cols), jnp.bfloat16),
            pltpu.SemaphoreType.DMA((6,)),
        ]
        + owners_scratch(places, grad_rows, grad_cols)
        + reduce_scratch(rows, width),
        compiler_params=params(number, 60),
        name="back_to_middle",
    )(
        middle,
        gain,
        cotangent,
        hidden,
        gate_grads,
        up_grads,
        gate,
        up,
        weight,
    )


def heads_products(copies, core, mate, attended, branch, for_mate, own, other):
    rows = branch.shape[0]

    def produce(place):
        both = attended[pl.ds(pl.multiple_of(place * 2 * rows, 2 * rows), 2 * rows)]
        product(both, branch, split_store(for_mate, own, place, core))
        return [copies.start(for_mate.at[place], other.at[place], mate).wait_recv]

    return produce


def last_kernel(
    tokens,
    gain,
    grad_middle,
    qkv_grads,
    heads_turned,
    attended,
    branch,
    heads_low,
    grad_gain_two,
    hidden,
    act,
    grad_out,
    gate_up,
    out,
    gate_up_all,
    pack_all,
    heads_all,
    gains,
    part_of,
    hidden_here,
    act_here,
    grad_out_here,
    pack,
    heads,
    heads_got,
    heads_mine,
    grad_gain,
    given,
    from_mate,
    summed,
    from_places,
    for_group,
    from_group,
    loads,
    local,
    send,
    recv,
    *scratch,
):
    ring = seq_ring()
    me = ring.near[0]
    weights_ring, core, mate = fsdp_ring()
    rows = tokens.shape[0]
    greet(ring.peers + ring.remote + weights_ring.peers + weights_ring.remote + [mate])
    copies = Copies(send, recv)
    reduce_bufs, scratch = scratch[:7], scratch[7:]
    qkv_scratch, down_scratch, heads_scratch = scratch[:10], scratch[10:20], scratch[20:]
    grad_gain[...] = jnp.zeros_like(grad_gain)
    hidden_load = [pltpu.make_async_copy(hidden, hidden_here, loads.at[0])]
    down_loads = [
        pltpu.make_async_copy(act, act_here, loads.at[1]),
        pltpu.make_async_copy(grad_out, grad_out_here, loads.at[2]),
    ]
    for copy in hidden_load + down_loads:
        copy.start()
    kept = []

    def keep(block, all_of):
        copy = pltpu.make_async_copy(block, all_of.at[me], local.at[len(kept)])
        copy.start()
        kept.append(copy)

    keep(gate_up, gate_up_all)

    def ready(*blocks):
        left = jnp.concatenate(
            [
                qkv_grads[:, pl.ds(pl.multiple_of(index * rows, rows), rows)]
                for index in blocks
            ],
            axis=1,
        ).T

        def store(cols, value):
            part_of[blocks[0], :, cols] = value[:rows].astype(jnp.bfloat16)
            part_of[blocks[1], :, cols] = value[rows:].astype(jnp.bfloat16)

        product(left, heads_turned, store)

    def done(index, total):
        rows_of = chunk_rows(rows, index)
        back, terms = norm_back_rows(total, gain[...], tokens[rows_of].astype(jnp.float32))
        grad_gain[...] += jnp.sum(terms, axis=0, keepdims=True)
        out[rows_of] = (grad_middle[rows_of] + back).astype(jnp.bfloat16)

    def sums(parts, produce, block_rows, owned):
        for_mate, own, other = parts[:3]
        return owners_walk(
            weights_ring, mate, copies, produce, own, other, parts[3:], block_rows, owned
        )

    qkv_cols = qkv_grads.shape[0]
    first = pack.shape[1] - qkv_cols

    def qkv_produce(place):
        while hidden_load:
            hidden_load.pop().wait()
        for_mate, own, other = qkv_scratch[:3]
        lanes = pl.ds(pl.multiple_of(place * 2 * rows, 2 * rows), 2 * rows)
        value = lax.dot_general(
            hidden_here[:, lanes].T,
            qkv_grads[...],
            (((1,), (1,)), ((), ())),
            preferred_element_type=jnp.float32,
        )
        split_store(for_mate, own, place, core)(slice(None), value)
        return [copies.start(for_mate.at[place], other.at[place], mate).wait_recv]

    def qkv_owned(rows_of, total):
        pack[rows_of, pl.ds(first, qkv_cols)] = total.astype(jnp.bfloat16)

    down_rows = rows // 2

    def down_produce(place):
        while down_loads:
            down_loads.pop().wait()
        for_mate, own, other = down_scratch[:3]
        lanes = pl.ds(pl.multiple_of(place * rows, rows), rows)
        turned = act_here[:, lanes].T
        product(turned, grad_out_here, split_store(for_mate, own, place, core), 2 * PRODUCT)
        return [copies.start(for_mate.at[place], other.at[place], mate).wait_recv]

    def down_owned(rows_of, total):
        pack[rows_of, pl.ds(0, first)] = total[:, :first].astype(jnp.bfloat16)
        under = pl.ds(rows_of.start + down_rows, rows_of.size)
        pack[under, pl.ds(0, first)] = total[:, first:].astype(jnp.bfloat16)

    half = heads_low.shape[1]
    piece_rows = heads_mine.shape[0]

    def heads_owned(rows_of, total):
        heads[rows_of, pl.ds(half, half)] = total.astype(jnp.bfloat16)

    def heads_walk():
        for_mate, own, other = heads_scratch[:3]
        produce = heads_products(copies, core, mate, attended, branch, for_mate, own, other)
        yield from sums(heads_scratch, produce, rows, heads_owned)
        heads[:, pl.ds(0, half)] = heads_low[...]

        def piece(index):
            return heads.at[pl.ds(pl.multiple_of(index * piece_rows, piece_rows), piece_rows)]

        arriving = exchange_all(ring, copies, piece, heads_got.at[me])
        heads_got[me] = piece(me)[...]
        yield
        for copy in arriving:
            copy.wait_recv()
        heads_mine[...] = sum(
            heads_got[index].astype(jnp.float32) for index in range(heads_got.shape[0])
        ).astype(jnp.bfloat16)
        keep(heads_mine, heads_all)
        arriving = exchange_all(ring, copies, lambda index: heads_mine, heads_all.at[me])
        yield
        for copy in arriving:
            copy.wait_recv()

    def sum_gains():
        lanes = given.shape[3]
        for index in range(2 * given.shape[0]):
            cols = pl.ds(index * lanes, lanes)
            place = (index // 2, index % 2)
            given[(*place, slice(0, 1))] = grad_gain[:, cols]
            given[(*place, slice(1, 2))] = grad_gain_two[:, cols]
            given[(*place, slice(2, 8))] = jnp.zeros((6, lanes), jnp.float32)
        copy = copies.start(given.at[:, 1 - core], from_mate, mate)
        yield
        copy.wait_recv()
        summed[...] = given[:, core] + from_mate[...]
        place = weights_ring.place
        arriving = exchange_all(
            weights_ring,
            copies,
            lambda index: summed.at[lax.div(index, 2)],
            from_places.at[place],
        )
        from_places[place] = summed[place]
        yield
        for copy in arriving:
            copy.wait_recv()
        for_group[...] = sum(from_places[index] for index in range(from_places.shape[0]))
        arriving = exchange_all(ring, copies, lambda index: for_group, from_group.at[me])
        from_group[me] = for_group[...]
        yield
        for copy in arriving:
            copy.wait_recv()
        gains[...] = sum(from_group[index] for index in range(from_group.shape[0]))

    def walk():
        yield from reduce_walk(
            ring, copies, part_of, reduce_bufs, by_rows(rows, CHUNKS), CHUNKS, done, ready
        )
        keep(pack, pack_all)
        yield from gather_walk(ring, copies, pack, pack_all, by_rows(rows, CHUNKS), CHUNKS)

    beside(
        walk(),
        (
            sums(down_scratch, down_produce, down_rows, down_owned),
            (3, 3, 3, 3, 3, 3, 3, 11, 11, 11, 11, 11, 11, 11, 15, 15, 15, 19, 19, 19),
        ),
        (
            gather_walk(
                ring, copies, gate_up, gate_up_all, by_rows(rows, CHUNKS), CHUNKS
            ),
            (11, 15, 15, 16, 17, 18, 19, 19, 19, 20, 20, 22, 24, 25),
        ),
        (
            sums(qkv_scratch, qkv_produce, rows, qkv_owned),
            (11,) * 14 + (15, 15, 19, 19, 19, 19),
        ),
        (heads_walk(), (11,) * 14 + (15, 19, 19, 20, 20, 23, 27)),
        (sum_gains(), (19, 21, 24)),
    )
    copies.finish()
    for copy in kept:
        copy.wait()


def finish(
    tokens,
    gain,
    grad_middle,
    qkv_grads,
    heads_turned,
    attended,
    branch,
    heads_low,
    grad_gain_two,
    hidden,
    act,
    grad_out,
    gate_up,
    number,
):
    rows, width = tokens.shape
    ranks, owners = lax.axis_size("seq"), lax.axis_size("fsdp")
    places = owners // 2
    lanes = width // owners
    qkv_cols, half = qkv_grads.shape[0], branch.shape[1]
    packed = width // 2 + qkv_cols
    pieces = rows // ranks
    assert act.shape[1] // owners == rows // 2
    count = reduce_copies(CHUNKS) + 2 * gather_copies(CHUNKS) + 3 * (OWNERS_COPIES + places)
    count += 2 * (ranks - 1) + 1 + places - 1 + ranks - 1
    low = jnp.bfloat16

    def table(*shape):
        return pltpu.VMEM((*shape, 8, lanes), jnp.float32)

    def sums(block_rows, cols):
        return [pltpu.VMEM((places, block_rows, cols), low)] + owners_scratch(
            places, block_rows, cols
        )

    return pl.pallas_call(
        last_kernel,
        out_shape=[
            jax.ShapeDtypeStruct((rows, width), low),
            jax.ShapeDtypeStruct((ranks, rows, width), low),
            jax.ShapeDtypeStruct((ranks, rows, packed), low),
            jax.ShapeDtypeStruct((ranks, pieces, width), low),
            jax.ShapeDtypeStruct((8, lanes), jnp.float32),
        ],
        in_specs=[VMEM] * 9 + [ANYWHERE] * 4,
        out_specs=[VMEM] + [ANYWHERE] * 3 + [VMEM],
        scratch_shapes=[
            pltpu.VMEM((ranks, rows, width), low),
            pltpu.VMEM(hidden.shape, low),
            pltpu.VMEM(act.shape, low),
            pltpu.VMEM(grad_out.shape, low),
            pltpu.VMEM((rows, packed), low),
            pltpu.VMEM((rows, width), low),
            pltpu.VMEM((ranks, pieces, width), low),
            pltpu.VMEM((pieces, width), low),
            pltpu.VMEM((1, width), jnp.float32),
            table(places, 2),
            table(places),
            table(places),
            table(places),
            table(),
            table(ranks),
            pltpu.SemaphoreType.DMA((3,)),
            pltpu.SemaphoreType.DMA((3,)),
        ]
        + semaphores(count)
        + reduce_scratch(rows, width)
        + sums(rows, qkv_cols)
        + sums(rows // 2, width)
        + sums(rows, half),
        compiler_params=params(number, 56),
        name="finish",
    )(
        tokens,
        gain,
        grad_middle,
        qkv_grads,
        heads_turned,
        attended,
        branch,
        heads_low,
        grad_gain_two,
        hidden,
        act,
        grad_out,
        gate_up,
    )


def merge_lanes(first, second):
    half = first.shape[1] // 2
    low = lax.broadcasted_iota(jnp.int32, first.shape, 1) < half
    return (
        jnp.where(low, first, pltpu.roll(second, half, 1)),
        jnp.where(low, pltpu.roll(first, half, 1), second),
    )


def place_kernel(
    gate,
    up,
    down,
    query,
    pair,
    heads,
    gate_out,
    up_out,
    down_out,
    query_out,
    key_out,
    value_out,
    heads_out,
):
    lanes = gate.shape[2]
    blocks = gate.shape[0] // 2
    for part, out in ((gate, gate_out), (up, up_out)):
        for index in range(blocks):
            low, high = merge_lanes(
                part[2 * index].astype(jnp.float32), part[2 * index + 1].astype(jnp.float32)
            )
            out[:, pl.ds(index * lanes, lanes)] = low
            out[:, pl.ds((blocks + index) * lanes, lanes)] = high
    key, value = merge_lanes(pair[0].astype(jnp.float32), pair[1].astype(jnp.float32))
    key_out[...] = key
    value_out[...] = value
    down_rows, cols = down_out.shape[0], down.shape[2]
    down_out[:, :cols] = down[0, :down_rows].astype(jnp.float32)
    down_out[:, cols:] = down[0, down_rows:].astype(jnp.float32)
    query_out[...] = query[0].astype(jnp.float32)
    heads_out[...] = heads[0].astype(jnp.float32)


def place_grads(gate_up, pack, heads):
    ranks, rows, units = gate_up.shape
    units //= 2
    lanes = LANES
    steps = units // lanes
    width = heads.shape[2]
    down_cols, down_rows = width // 2, rows // 2
    query_cols = width // ranks
    head_rows = heads.shape[1]
    first = (down_cols + query_cols) // lanes
    assert steps == ranks and lanes == 2 * HEAD_SIZE and query_cols == 2 * lanes
    real = jnp.float32
    return pl.pallas_call(
        place_kernel,
        grid=(steps,),
        out_shape=[
            jax.ShapeDtypeStruct((rows, ranks * units), real),
            jax.ShapeDtypeStruct((rows, ranks * units), real),
            jax.ShapeDtypeStruct((ranks * down_rows, width), real),
            jax.ShapeDtypeStruct((rows, ranks * query_cols), real),
            jax.ShapeDtypeStruct((rows, ranks * HEAD_SIZE), real),
            jax.ShapeDtypeStruct((rows, ranks * HEAD_SIZE), real),
            jax.ShapeDtypeStruct((rows, width), real),
        ],
        in_specs=[
            pl.BlockSpec((ranks, rows, lanes), lambda i: (0, 0, i)),
            pl.BlockSpec((ranks, rows, lanes), lambda i: (0, 0, steps + i)),
            pl.BlockSpec((1, rows, down_cols), lambda i: (i, 0, 0)),
            pl.BlockSpec((1, rows, query_cols), lambda i: (i, 0, down_cols // query_cols)),
            pl.BlockSpec((2, rows, lanes), lambda i: (i // 2, 0, first)),
            pl.BlockSpec((1, head_rows, width), lambda i: (i, 0, 0)),
        ],
        out_specs=[
            pl.BlockSpec((rows, ranks * lanes), lambda i: (0, i)),
            pl.BlockSpec((rows, ranks * lanes), lambda i: (0, i)),
            pl.BlockSpec((down_rows, width), lambda i: (i, 0)),
            pl.BlockSpec((rows, query_cols), lambda i: (0, i)),
            pl.BlockSpec((rows, lanes), lambda i: (0, i // 2)),
            pl.BlockSpec((rows, lanes), lambda i: (0, i // 2)),
            pl.BlockSpec((head_rows, width), lambda i: (i, 0)),
        ],
        compiler_params=pltpu.CompilerParams(vmem_limit_bytes=32 * 2**20),
        name="place_grads",
    )(gate_up, gate_up, pack, pack, pack, heads)


def rotate_rows(first, second, cosine, sine):
    return jnp.concatenate([first * cosine - second * sine, second * cosine + first * sine], axis=0)


def bias_tile(start_row, key_tile, query_tile, diagonal):
    keys = key_tile * TILE + lax.broadcasted_iota(jnp.int32, (TILE, TILE), 0)
    seen = keys >= start_row
    if diagonal:
        queries = query_tile * TILE + lax.broadcasted_iota(jnp.int32, (TILE, TILE), 1)
        seen = seen & (keys <= queries)
    return jnp.where(seen, 0.0, NEG)


def attend_tiles(qkv, cosine, sine, starts, attended, lse, queries, keys, key_rows, bias):
    group = queries.shape[0] // HEAD_SIZE
    half = HEAD_SIZE // 2
    tiles = qkv.shape[1] // TILE
    cos, sin = cosine[...], sine[...]

    def rotated(first):
        return rotate_rows(
            qkv[pl.ds(first, half)].astype(jnp.float32),
            qkv[pl.ds(first + half, half)].astype(jnp.float32),
            cos,
            sin,
        ).astype(jnp.bfloat16)

    for head in range(group):
        queries[pl.ds(head * HEAD_SIZE, HEAD_SIZE)] = rotated(head * HEAD_SIZE) * jnp.bfloat16(0.125)
    keys[...] = rotated(group * HEAD_SIZE)
    key_rows[...] = keys[...].T
    for tile in range(tiles):
        lanes = pl.ds(tile * TILE, TILE)
        starts_here = starts[:, lanes]
        for low in range(tile + 1):
            bias[pl.ds(low * TILE, TILE)] = bias_tile(starts_here, low, tile, low == tile)
        count = (tile + 1) * TILE

        def one_head(head, _, lanes=lanes, count=count):
            rows = pl.ds(pl.multiple_of(head * HEAD_SIZE, HEAD_SIZE), HEAD_SIZE)
            scores = jnp.dot(
                key_rows[:count], queries[rows, lanes], preferred_element_type=jnp.float32
            )
            scores += bias[:count]
            highest = jnp.max(scores, axis=0, keepdims=True)
            weights = jnp.exp(scores - highest)
            total = jnp.sum(weights, axis=0, keepdims=True)
            out = jnp.dot(
                qkv[pl.ds((group + 1) * HEAD_SIZE, HEAD_SIZE), :count],
                weights.astype(jnp.bfloat16),
                preferred_element_type=jnp.float32,
            )
            attended[rows, lanes] = (out / total).astype(jnp.bfloat16)
            lse[head, :, lanes] = jnp.broadcast_to(highest + jnp.log(total), (8, TILE))
            return 0

        lax.fori_loop(0, group, one_head, 0)


def forward_kernel(
    qkv,
    cosine,
    sine,
    starts,
    cotangent,
    heads,
    attended,
    lse,
    queries,
    keys,
    gathered,
    heads_all,
    key_rows,
    bias,
    local,
    send,
    recv,
):
    ring = seq_ring()
    weights_ring, _, mate = fsdp_ring()
    greet(ring.peers + weights_ring.peers + [mate])
    kept = [
        pltpu.make_async_copy(cotangent, gathered.at[ring.near[0]], local.at[0]),
        pltpu.make_async_copy(heads, heads_all.at[weights_ring.near[0]], local.at[1]),
    ]
    for copy in kept:
        copy.start()
    copies = Copies(send, recv)

    def compute():
        attend_tiles(qkv, cosine, sine, starts, attended, lse, queries, keys, key_rows, bias)
        yield

    beside(
        gather_walk(
            ring, copies, cotangent, gathered, by_rows(cotangent.shape[0], CHUNKS), CHUNKS
        ),
        (weight_walk(weights_ring, copies, heads, heads_all, mate), LARGE_BESIDE),
        (compute(), (0,)),
    )
    copies.finish()
    for copy in kept:
        copy.wait()


def attend(qkv, cosine, sine, starts, cotangent, heads, group, number):
    length = qkv.shape[1]
    rows, width = cotangent.shape
    ranks = lax.axis_size("seq")
    return pl.pallas_call(
        forward_kernel,
        out_shape=[
            jax.ShapeDtypeStruct((group * HEAD_SIZE, length), jnp.bfloat16),
            jax.ShapeDtypeStruct((group, 8, length), jnp.float32),
            jax.ShapeDtypeStruct((group * HEAD_SIZE, length), jnp.bfloat16),
            jax.ShapeDtypeStruct((HEAD_SIZE, length), jnp.bfloat16),
            jax.ShapeDtypeStruct((ranks, rows, width), jnp.bfloat16),
            jax.ShapeDtypeStruct((lax.axis_size("fsdp"), *heads.shape), jnp.bfloat16),
        ],
        in_specs=[VMEM] * 4 + [ANYWHERE] * 2,
        out_specs=[VMEM] * 4 + [ANYWHERE] * 2,
        scratch_shapes=[
            pltpu.VMEM((length, HEAD_SIZE), jnp.bfloat16),
            pltpu.VMEM((length, TILE), jnp.float32),
            pltpu.SemaphoreType.DMA((2,)),
        ]
        + semaphores(gather_copies(CHUNKS) + gather_copies(CHUNKS, True)),
        compiler_params=params(number, 40),
        name="attend",
    )(qkv, cosine, sine, starts, cotangent, heads)


def back_tiles(
    qkv,
    queries,
    keys,
    attended,
    lse,
    grads,
    cosine,
    sine,
    starts,
    out,
    key_rows,
    value_rows,
    query_rows,
    grad_rows,
    row_dots,
    key_grad,
    value_grad,
    query_grad,
    bias,
):
    group = queries.shape[0] // HEAD_SIZE
    half = HEAD_SIZE // 2
    tiles = qkv.shape[1] // TILE
    key_rows[...] = keys[...].T
    value_rows[...] = qkv[pl.ds((group + 1) * HEAD_SIZE, HEAD_SIZE)].T
    for head in range(group):
        rows = pl.ds(head * HEAD_SIZE, HEAD_SIZE)
        query_rows[head] = queries[rows].T
        grad_rows[head] = grads[rows].T
        row_dots[head] = jnp.broadcast_to(
            jnp.sum(
                grads[rows].astype(jnp.float32) * attended[rows].astype(jnp.float32),
                axis=0,
                keepdims=True,
            ),
            row_dots.shape[1:],
        )
    key_grad[...] = jnp.zeros_like(key_grad)
    value_grad[...] = jnp.zeros_like(value_grad)
    for tile in range(tiles):
        lanes = pl.ds(tile * TILE, TILE)
        starts_here = starts[:, lanes]
        for low in range(tile + 1):
            bias[low] = bias_tile(starts_here, low, tile, low == tile)

        def one_head(head, _, lanes=lanes, tile=tile):
            rows = pl.ds(pl.multiple_of(head * HEAD_SIZE, HEAD_SIZE), HEAD_SIZE)
            query, grad = queries[rows, lanes], grads[rows, lanes]
            query_row, grad_row = query_rows[head, lanes], grad_rows[head, lanes]
            lse_row = lse[head, 0:1, lanes]
            dot_row = row_dots[head, 0:1, lanes]
            total = jnp.zeros((HEAD_SIZE, TILE), jnp.float32)
            for low in range(tile + 1):
                part = pl.ds(low * TILE, TILE)
                scores = jnp.dot(key_rows[part], query, preferred_element_type=jnp.float32)
                probs = jnp.exp(scores + bias[low] - lse_row)
                grad_probs = jnp.dot(value_rows[part], grad, preferred_element_type=jnp.float32)
                grad_scores = (probs * (grad_probs - dot_row)).astype(jnp.bfloat16)
                value_grad[part] += jnp.dot(
                    probs.astype(jnp.bfloat16), grad_row, preferred_element_type=jnp.float32
                )
                key_grad[part] += jnp.dot(
                    grad_scores, query_row, preferred_element_type=jnp.float32
                )
                total += jnp.dot(keys[:, part], grad_scores, preferred_element_type=jnp.float32)
            query_grad[rows, lanes] = total * 0.125
            return 0

        lax.fori_loop(0, group, one_head, 0)
        yield
    cos, sin = cosine[...], sine[...]
    for head in range(group):
        first = head * HEAD_SIZE
        out[pl.ds(first, HEAD_SIZE)] = rotate_rows(
            query_grad[pl.ds(first, half)], query_grad[pl.ds(first + half, half)], cos, -sin
        ).astype(jnp.bfloat16)
    turned = key_grad[...].T
    out[pl.ds(group * HEAD_SIZE, HEAD_SIZE)] = rotate_rows(
        turned[:half], turned[half:], cos, -sin
    ).astype(jnp.bfloat16)
    out[pl.ds((group + 1) * HEAD_SIZE, HEAD_SIZE)] = value_grad[...].T.astype(jnp.bfloat16)


def backward_kernel(*refs):
    ins, (act, down, middle, attended, branch) = refs[:9], refs[9:14]
    (out, layer_out, heads_share), scratch = refs[14:17], refs[17:26]
    part_of, act_here, down_here, loads, send, recv = refs[26:32]
    for_mate, own, other = refs[32:35]
    bufs = refs[35:]
    ring = seq_ring()
    weights_ring, core, mate = fsdp_ring()
    greet(ring.peers + weights_ring.peers + [mate])
    copies = Copies(send, recv)
    rows = middle.shape[0]
    first = [
        pltpu.make_async_copy(act, act_here, loads.at[0]),
        pltpu.make_async_copy(down, down_here, loads.at[1]),
    ]
    for copy in first:
        copy.start()

    def ready(*blocks):
        while first:
            first.pop().wait()

        def store(cols, value):
            part_of[blocks[0], :, cols] = value[:rows].astype(jnp.bfloat16)
            part_of[blocks[1], :, cols] = value[rows:].astype(jnp.bfloat16)

        product(two_blocks(act_here, rows, *blocks), down_here, store)

    def done(index, total):
        rows_of = chunk_rows(rows, index)
        layer_out[rows_of] = (middle[rows_of] + total).astype(jnp.bfloat16)

    def owned(rows_of, total):
        heads_share[rows_of] = total.astype(jnp.bfloat16)

    beside(
        reduce_walk(
            ring, copies, part_of, bufs[7:], by_rows(rows, CHUNKS), CHUNKS, done, ready
        ),
        (back_tiles(*ins, out, *scratch), (3, 3, 11, 15, 19)),
        (
            owners_walk(
                weights_ring,
                mate,
                copies,
                heads_products(copies, core, mate, attended, branch, for_mate, own, other),
                own,
                other,
                bufs[:7],
                rows,
                owned,
            ),
            (0, 0, 0, 1, 1, 1, 1, 3, 3, 3, 3, 3, 3, 3, 11, 11, 15, 15, 19),
        ),
    )
    copies.finish()


def attend_back(
    qkv,
    queries,
    keys,
    attended,
    lse,
    grads,
    cosine,
    sine,
    starts,
    act,
    down,
    middle,
    attended_here,
    branch,
    number,
):
    length = qkv.shape[1]
    group = queries.shape[0] // HEAD_SIZE
    tiles = length // TILE
    rows, width = middle.shape
    ranks, owners = lax.axis_size("seq"), lax.axis_size("fsdp")
    places = owners // 2
    cols = branch.shape[1]
    return pl.pallas_call(
        backward_kernel,
        out_shape=[
            jax.ShapeDtypeStruct(qkv.shape, jnp.bfloat16),
            jax.ShapeDtypeStruct((rows, width), jnp.bfloat16),
            jax.ShapeDtypeStruct((rows, cols), jnp.bfloat16),
        ],
        in_specs=[VMEM] * 9 + [ANYWHERE] * 2 + [VMEM] * 3,
        out_specs=[VMEM] * 3,
        scratch_shapes=[
            pltpu.VMEM((length, HEAD_SIZE), jnp.bfloat16),
            pltpu.VMEM((length, HEAD_SIZE), jnp.bfloat16),
            pltpu.VMEM((group, length, HEAD_SIZE), jnp.bfloat16),
            pltpu.VMEM((group, length, HEAD_SIZE), jnp.bfloat16),
            pltpu.VMEM((group, 8, length), jnp.float32),
            pltpu.VMEM((length, HEAD_SIZE), jnp.float32),
            pltpu.VMEM((length, HEAD_SIZE), jnp.float32),
            pltpu.VMEM((group * HEAD_SIZE, length), jnp.float32),
            pltpu.VMEM((tiles, TILE, TILE), jnp.float32),
            pltpu.VMEM((ranks, rows, width), jnp.bfloat16),
            pltpu.VMEM(act.shape, jnp.bfloat16),
            pltpu.VMEM(down.shape, jnp.bfloat16),
            pltpu.SemaphoreType.DMA((2,)),
        ]
        + semaphores(reduce_copies(CHUNKS) + OWNERS_COPIES + places)
        + [pltpu.VMEM((places, rows, cols), jnp.bfloat16)]
        + owners_scratch(places, rows, cols)
        + reduce_scratch(rows, width),
        compiler_params=params(number, 52),
        name="attend_back",
    )(
        qkv,
        queries,
        keys,
        attended,
        lse,
        grads,
        cosine,
        sine,
        starts,
        act,
        down,
        middle,
        attended_here,
        branch,
    )


def shards(
    tokens,
    segment_ids,
    query_weight,
    key_matrix,
    value_matrix,
    output_weight,
    gate_weight,
    up_weight,
    down_weight,
    attention_gain,
    feed_gain,
    cotangent,
):
    rank = lax.axis_index("seq")
    owner = lax.axis_index("fsdp")
    ranks = lax.axis_size("seq")
    owners = lax.axis_size("fsdp")
    rows, width = query_weight.shape
    kv_cols = key_matrix.shape[1] // ranks
    q_cols = width // ranks
    group = q_cols // kv_cols
    ff = gate_weight.shape[1]
    ff_chunk = ff // owners // ranks
    ff_local = owners * ff_chunk
    segment_row = segment_ids[0]
    length = segment_row.shape[0]

    hidden_one, qkv, heads_turned, gate_all, up_in, cosine, sine, starts, gain_one, gain_two = (
        gather_first(
            tokens[0],
            query_weight,
            key_matrix,
            value_matrix,
            gate_weight,
            up_weight,
            attention_gain,
            feed_gain,
            segment_ids,
            rope_freqs(HEAD_SIZE)[:, None],
            0,
        )
    )
    hidden_one = hidden_one.reshape(length, width)
    down_in = lax.dynamic_slice_in_dim(down_weight, rank * ff_chunk, ff_chunk, 0)

    attended, lse, queries, keys, grad_out, output_all = attend(
        qkv, cosine, sine, starts, cotangent[0], output_weight, group, 1
    )
    output_all = output_all.reshape(-1, width)
    middle, attended_here, hidden_two, up_all, down_all, act, grad_gate, grad_up = add_branch(
        attended, tokens[0], gain_two, output_all, gate_all, up_in, down_in, grad_out, 2
    )
    hidden_two = hidden_two.reshape(length, width)
    gate_all = gate_all.reshape(width, ff_local)
    up_all = up_all.reshape(width, ff_local)
    down_all = down_all.reshape(ff_local, width)
    act, grad_gate, grad_up = (part.reshape(length, ff_local) for part in (act, grad_gate, grad_up))
    grad_out = grad_out.reshape(length, width)

    (
        grad_middle,
        grad_gain_two,
        grad_branch,
        grad_attended,
        gate_up_share,
    ) = back_to_middle(
        middle,
        gain_two,
        cotangent[0],
        hidden_two,
        grad_gate,
        grad_up,
        gate_all,
        up_all,
        output_all,
        3,
    )

    half = width // 2
    qkv_grads, layer_out, heads_low = attend_back(
        qkv,
        queries,
        keys,
        attended,
        lse,
        grad_attended,
        cosine,
        sine,
        starts,
        act,
        down_all,
        middle,
        attended_here,
        grad_branch[:, :half],
        4,
    )
    grad_inputs, *gathered, gains = finish(
        tokens[0],
        gain_one,
        grad_middle,
        qkv_grads,
        heads_turned,
        attended_here,
        grad_branch[:, half:],
        heads_low,
        grad_gain_two,
        hidden_one,
        act,
        grad_out,
        gate_up_share,
        5,
    )
    gate_grad, up_grad, down_total, query_grad, key_grad, value_grad, heads_total = place_grads(
        *gathered
    )
    return (
        layer_out[None],
        grad_inputs[None],
        query_grad,
        key_grad,
        value_grad,
        heads_total,
        gate_grad,
        up_grad,
        down_total,
        gains[0],
        gains[1],
    )


def solution(mesh):
    placed = (
        P("fsdp", "seq", None),
        P("fsdp", None),
        P("fsdp", None),
        P("fsdp", None),
        P("fsdp", None),
        P("fsdp", None),
        P("fsdp", None),
        P("fsdp", None),
        P("fsdp", None),
        P("fsdp"),
        P("fsdp"),
        P("fsdp", "seq", None),
    )
    return jax.shard_map(
        shards,
        mesh=mesh,
        in_specs=placed,
        out_specs=(
            P("fsdp", "seq", None),
            P("fsdp", "seq", None),
            P("fsdp", None),
            P("fsdp", None),
            P("fsdp", None),
            P("fsdp", None),
            P("fsdp", None),
            P("fsdp", None),
            P("fsdp", None),
            P("fsdp"),
            P("fsdp"),
        ),
        check_vma=False,
    )
```

```python
import math

import jax
import jax.numpy as jnp
from jax import lax
from jax.experimental import pallas as pl
from jax.experimental.pallas import tpu as pltpu
from jax.sharding import PartitionSpec as P

HEAD_SIZE = 64
EPS = 1e-05
ROPE_BASE = 500000.0
NEG = -1e30


def rope_freqs(head_dim):
    half_dim = head_dim // 2
    table = []
    for index in range(half_dim):
        inverse = 1.0 / ROPE_BASE ** (index * 2.0 / head_dim)
        wavelen = 2.0 * math.pi / inverse
        blend = (8192.0 / wavelen - 1.0) / 3.0
        mixed = (1.0 - blend) * inverse / 32.0 + blend * inverse
        entry = inverse if wavelen < 2048.0 else inverse / 32.0 if wavelen > 8192.0 else mixed
        table.append(entry)
    return jnp.asarray(table, dtype=jnp.float32)


MESH = pl.DeviceIdType.MESH
CHUNKS = 4
TILE = 256


class Ring:
    def __init__(self, place, count, index_of, device_of):
        side = count // 2
        self.place = place
        row, col = lax.div(place, side), lax.rem(place, side)

        def at(which, step):
            return index_of(which * side + lax.rem(col + step, side))

        self.near = [at(row, step) for step in range(side)]
        self.far = [at(1 - row, step) for step in range(side)]
        self.right = device_of(self.near[1])
        self.left = device_of(self.near[3])
        self.partner = device_of(self.far[0])
        self.peers = [self.right, self.left, self.partner]
        self.remote = [device_of(index) for index in (self.near[2], *self.far[1:])]
        self.device_of = device_of


def seq_ring():
    rank, owner = lax.axis_index("seq"), lax.axis_index("fsdp")
    return Ring(rank, lax.axis_size("seq"), lambda place: place, lambda index: (index, owner))


def fsdp_ring():
    rank, owner = lax.axis_index("seq"), lax.axis_index("fsdp")
    core = lax.rem(owner, 2)
    ring = Ring(
        lax.div(owner, 2),
        lax.axis_size("fsdp") // 2,
        lambda place: 2 * place + core,
        lambda index: (rank, index),
    )
    return ring, core, (rank, owner + 1 - 2 * core)


def greet(peers):
    barrier = pltpu.get_barrier_semaphore()
    for peer in peers:
        pl.semaphore_signal(barrier, inc=1, device_id=peer, device_id_type=MESH)
    pl.semaphore_wait(barrier, len(peers))


def in_step(*walks):
    left = list(walks)
    while left:
        left = [walk for walk in left if next(walk, walk) is not walk]
        yield


def beside(main, *sides):
    sides = [(walk, list(places)) for walk, places in sides]
    step = 0
    for _ in main:
        for walk, places in sides:
            while places and places[0] <= step:
                places.pop(0)
                next(walk, None)
        step += 1
    for _ in in_step(*(walk for walk, _ in sides)):
        pass


class Copies:
    def __init__(self, send, recv):
        self.send, self.recv = send, recv
        self.made = []

    def start(self, source, target, peer):
        number = len(self.made)
        copy = pltpu.make_async_remote_copy(
            src_ref=source,
            dst_ref=target,
            send_sem=self.send.at[number],
            recv_sem=self.recv.at[number],
            device_id=peer,
            device_id_type=MESH,
        )
        copy.start()
        self.made.append(copy)
        return copy

    def settle(self, copies):
        for copy in copies:
            copy.wait_send()
        gone = {id(copy) for copy in copies}
        self.made = [None if id(copy) in gone else copy for copy in self.made]

    def finish(self):
        for copy in self.made:
            if copy is not None:
                copy.wait_send()


def by_rows(rows, chunks):
    size = rows // chunks
    return lambda ref, index: ref.at[pl.ds(index * size, size)]


def by_columns(columns, chunks):
    size = columns // chunks
    return lambda ref, index: ref.at[:, pl.ds(index * size, size)]


def chunk_rows(rows, index):
    size = rows // CHUNKS
    return pl.ds(index * size, size)


def exchange_all(ring, copies, piece, target):
    made = []
    for index in (*ring.far[1:], ring.near[2], ring.far[0], ring.near[1], ring.near[3]):
        made.append(copies.start(piece(index), target, ring.device_of(index)))
    return made


def gather_walk(ring, copies, own, out, cut, chunks, deep=False, mate=None):
    me, right, opposite, left = ring.near
    partner, far_right, _, far_left = ring.far
    half = chunks // 2
    passed = []

    def share(place, index):
        if mate is not None:
            block = cut(out.at[place], index)
            passed.append(copies.start(block, block, mate))

    to_right, to_left, to_far, on = {}, {}, {}, {}
    for step in range(chunks):
        back = chunks - 1 - step
        if not deep:
            to_far[step] = copies.start(cut(own, step), cut(out.at[me], step), ring.partner)
        to_right[step] = copies.start(cut(own, step), cut(out.at[me], step), ring.right)
        to_left[back] = copies.start(cut(own, back), cut(out.at[me], back), ring.left)
        if mate is not None:
            passed.append(copies.start(cut(own, step), cut(out.at[me], step), mate))
    yield
    if deep:
        for step in range(chunks):
            to_far[step] = copies.start(cut(own, step), cut(out.at[me], step), ring.partner)
        yield
    for step in range(half):
        back = chunks - 1 - step
        to_right[step].wait_recv()
        block = cut(out.at[left], step)
        on[step] = copies.start(block, block, ring.right)
        share(left, step)
        to_left[back].wait_recv()
        block = cut(out.at[right], back)
        on[back] = copies.start(block, block, ring.left)
        share(right, back)
        yield
    far_on, rest = {}, []
    for step in range(chunks):
        to_far[step].wait_recv()
        block = cut(out.at[partner], step)
        far_on[0, step] = copies.start(block, block, ring.right)
        far_on[1, step] = copies.start(block, block, ring.left)
        share(partner, step)
        yield
    if deep:
        for step in range(half):
            back = chunks - 1 - step
            far_on[0, step].wait_recv()
            block = cut(out.at[far_left], step)
            rest.append((step, copies.start(block, block, ring.right)))
            share(far_left, step)
            far_on[1, back].wait_recv()
            block = cut(out.at[far_right], back)
            rest.append((back, copies.start(block, block, ring.left)))
            share(far_right, back)
            yield
    def finals():
        for step in range(half):
            back = chunks - 1 - step
            to_right[back].wait_recv()
            share(left, back)
            to_left[step].wait_recv()
            share(right, step)
            if deep:
                far_on[0, back].wait_recv()
                share(far_left, back)
                far_on[1, step].wait_recv()
                share(far_right, step)
            yield

    if not deep:
        yield from finals()
    for step in range(half):
        for index in (step, chunks - 1 - step):
            on[index].wait_recv()
            if not deep:
                block = cut(out.at[opposite], index)
                rest.append((index, copies.start(block, block, ring.partner)))
            share(opposite, index)
        yield
    if deep:
        yield from finals()
    else:
        for copy in far_on.values():
            copy.wait_recv()
        yield
    for index, copy in rest:
        copy.wait_recv()
        share(ring.far[2], index)
    yield
    for copy in passed:
        copy.wait_recv()


def gather_copies(chunks, mate=False):
    return 7 * chunks + (8 * chunks if mate else 0)


def reduce_walk(ring, copies, part_of, bufs, cut, chunks, done, ready=None):
    me, right, opposite, left = ring.near
    partner, far_right, far_opposite, far_left = ring.far
    from_left, from_right, from_far, mid, end_left, end_right, end_far = bufs
    half = chunks // 2

    def wide(ref, index):
        return cut(ref, index)[...].astype(jnp.float32)

    def keep(ref, index, value):
        cut(ref, index)[...] = value.astype(jnp.bfloat16)

    sent = []

    def send(block, index, target, device):
        sent.append(copies.start(cut(block, index), cut(target, index), device))
        return sent[-1]

    order = [x for step in range(half) for x in (step, chunks - 1 - step)]
    one_right, one_left, one_far, last_right, last_left, last_far = ({} for _ in range(6))
    if ready is None:
        for index in order:
            one_far[index] = send(part_of.at[far_opposite], index, from_far, ring.partner)
            one_right[index] = send(part_of.at[far_right], index, from_left, ring.right)
            one_left[index] = send(part_of.at[far_left], index, from_right, ring.left)
    else:
        ready(far_right, far_left)
        for index in order:
            one_right[index] = send(part_of.at[far_right], index, from_left, ring.right)
            one_left[index] = send(part_of.at[far_left], index, from_right, ring.left)
        yield
        ready(far_opposite, right)
        for index in order:
            one_far[index] = send(part_of.at[far_opposite], index, from_far, ring.partner)
    for index in range(half):
        last_right[index] = send(part_of.at[right], index, end_left, ring.right)
    if ready is not None:
        yield
        ready(left, opposite)
    for index in range(half):
        back = chunks - 1 - index
        last_left[back] = send(part_of.at[left], back, end_right, ring.left)
    if ready is not None:
        yield
        ready(partner, me)
    yield
    two = {}
    for index in order:
        one_far[index].wait_recv()
        keep(from_far, index, wide(from_far, index) + wide(part_of.at[opposite], index))
        two[index] = send(from_far, index, mid, ring.left if index < half else ring.right)
        yield
    for index in order:
        one_right[index].wait_recv()
        one_left[index].wait_recv()
        total = wide(from_left, index) + wide(from_right, index)
        keep(from_left, index, total + wide(part_of.at[partner], index))
        last_far[index] = send(from_left, index, end_far, ring.partner)
        yield
    for index in order:
        two[index].wait_recv()
        if index < half:
            keep(mid, index, wide(mid, index) + wide(part_of.at[left], index))
            last_left[index] = send(mid, index, end_right, ring.left)
        else:
            keep(mid, index, wide(mid, index) + wide(part_of.at[right], index))
            last_right[index] = send(mid, index, end_left, ring.right)
        yield
    for index in order:
        last_far[index].wait_recv()
        last_left[index].wait_recv()
        last_right[index].wait_recv()
        total = wide(part_of.at[me], index) + wide(end_left, index)
        done(index, total + wide(end_right, index) + wide(end_far, index))
        yield
    copies.settle(sent)


def reduce_copies(chunks):
    return 3 * chunks + 2 * chunks + chunks + chunks


def owners_walk(ring, mate, copies, produce, own, other, bufs, rows, done):
    mids, from_lefts, from_rights, from_far = bufs[:2], bufs[2:4], bufs[4:6], bufs[6]
    half = rows // 2
    low, high = pl.ds(0, half), pl.ds(half, half)
    near, far = ([lax.div(index, 2) for index in row] for row in (ring.near, ring.far))
    order = [far[2], far[1], far[3], near[2], near[1], near[3], far[0], near[0]]
    awaited = []

    def wide(ref):
        return ref.astype(jnp.float32)

    def add(*numbers):
        for number in numbers:
            for wait in awaited[number]:
                wait()
            place = order[number]
            own[place] = (wide(own[place]) + wide(other[place])).astype(jnp.bfloat16)

    def make(number):
        awaited.append(produce(order[number]))

    on, ends = ([], []), ([], [])

    def half_way(which):
        block = own.at[(far, near)[which][2]]
        on[which].append(copies.start(block.at[low], mids[which].at[low], ring.left))
        on[which].append(copies.start(block.at[high], mids[which].at[high], ring.right))

    def sides(which):
        row = (far, near)[which]
        ends[which].append(
            copies.start(own.at[row[1], low], from_lefts[which].at[low], ring.right)
        )
        ends[which].append(
            copies.start(own.at[row[3], high], from_rights[which].at[high], ring.left)
        )

    def other_sides(which):
        row, mid = (far, near)[which], mids[which]
        on[which][0].wait_recv()
        mid[low] = (wide(mid[low]) + wide(own[row[3], low])).astype(jnp.bfloat16)
        ends[which].append(copies.start(mid.at[low], from_rights[which].at[low], ring.left))
        on[which][1].wait_recv()
        mid[high] = (wide(mid[high]) + wide(own[row[1], high])).astype(jnp.bfloat16)
        ends[which].append(copies.start(mid.at[high], from_lefts[which].at[high], ring.right))

    make(0)
    yield
    make(1)
    yield
    add(0)
    half_way(0)
    yield
    make(2)
    yield
    add(1, 2)
    sides(0)
    yield
    make(3)
    yield
    make(4)
    yield
    other_sides(0)
    yield
    add(3)
    half_way(1)
    yield
    make(5)
    yield
    add(4, 5)
    sides(1)
    yield
    make(6)
    yield
    make(7)
    yield
    add(6, 7)
    yield
    last = []
    for copy in ends[0]:
        copy.wait_recv()
    for rows_of in (low, high):
        total = (
            wide(from_lefts[0][rows_of])
            + wide(from_rights[0][rows_of])
            + wide(own[far[0], rows_of])
        )
        from_lefts[0][rows_of] = total.astype(jnp.bfloat16)
        last.append(copies.start(from_lefts[0].at[rows_of], from_far.at[rows_of], ring.partner))
    yield
    other_sides(1)
    yield
    for copy in ends[1]:
        copy.wait_recv()
    yield
    for rows_of, copy in zip((low, high), last):
        copy.wait_recv()
        done(
            rows_of,
            wide(from_lefts[1][rows_of])
            + wide(from_rights[1][rows_of])
            + wide(own[near[0], rows_of])
            + wide(from_far[rows_of]),
        )
        yield


OWNERS_COPIES = 4 + 4 + 4 + 2


def owners_scratch(places, rows, width):
    return [pltpu.VMEM((places, rows, width), jnp.bfloat16) for _ in range(2)] + [
        pltpu.VMEM((rows, width), jnp.bfloat16) for _ in range(7)
    ]


def reduce_scratch(rows, width):
    return [pltpu.VMEM((rows, width), jnp.bfloat16) for _ in range(7)]


def semaphores(count):
    return [pltpu.SemaphoreType.DMA((count,)), pltpu.SemaphoreType.DMA((count,))]


def params(number, limit):
    return pltpu.CompilerParams(
        collective_id=number, has_side_effects=True, vmem_limit_bytes=limit * 2**20
    )


VMEM = pl.BlockSpec(memory_space=pltpu.VMEM)
ANYWHERE = pl.BlockSpec(memory_space=pl.ANY)


SMALL_BESIDE = (0, 2, 2, 3, 6, 6, 6, 6, 8, 8, 9, 9, 10, 10, 11)
LARGE_BESIDE = (0, 1, 2, 3, 5, 6, 7, 7, 8, 8, 8, 8, 9, 9, 10)


def weight_walk(ring, copies, own, out, mate):
    return gather_walk(ring, copies, own, out, by_rows(own.shape[0], CHUNKS), CHUNKS, True, mate)


def chosen_half(first, second, odd):
    low, high = merge_lanes(first.astype(jnp.float32), second.astype(jnp.float32))
    return jnp.where(odd == 0, low, high).astype(jnp.bfloat16)


class Pick:
    def __init__(self, sems, wide, narrow, rank):
        self.sems, self.wide, self.narrow = sems, wide, narrow
        self.pair, self.odd = lax.div(rank, 2), lax.rem(rank, 2)
        self.rank = rank
        self.count = 0

    def fetch(self, source, target):
        copy = pltpu.make_async_copy(source, target, self.sems.at[self.count])
        copy.start()
        self.count += 1
        return copy

    def lanes(self, first):
        return pl.ds(pl.multiple_of(first + self.pair * LANES, LANES), LANES)

    def start_units(self, which, source):
        owners = self.wide.shape[1]
        stride = source.shape[1] // owners
        return [
            self.fetch(source.at[:, self.lanes(owner * stride)], self.wide.at[which, owner])
            for owner in range(owners)
        ]

    def finish_units(self, which, made, out):
        for copy in made:
            copy.wait()
        for index in range(self.wide.shape[1] // 2):
            out[:, pl.ds(index * LANES, LANES)] = chosen_half(
                self.wide[which, 2 * index], self.wide[which, 2 * index + 1], self.odd
            )

    def start_heads(self, query, key, value, out):
        rows, cols = query.shape[0], out.shape[1] - LANES
        first = pl.multiple_of(self.rank * cols, LANES)
        return [
            self.fetch(query.at[:, pl.ds(first, cols)], out.at[pl.ds(0, rows), pl.ds(0, cols)]),
            self.fetch(key.at[:, self.lanes(0)], self.narrow.at[0]),
            self.fetch(value.at[:, self.lanes(0)], self.narrow.at[1]),
        ]

    def finish_heads(self, made, gain_one, gain_two, out):
        rows = self.narrow.shape[1]
        line = lax.broadcasted_iota(jnp.int32, (16, rows), 0)
        first, second = (gain[...].astype(jnp.float32) for gain in (gain_one, gain_two))
        gains = jnp.where(line == 0, first, jnp.where(line == 1, second, 0.0))
        out[pl.ds(rows, 32)] = jnp.zeros((32, out.shape[1]), jnp.bfloat16)
        out[pl.ds(rows, 16), pl.ds(0, rows)] = gains.astype(jnp.bfloat16)
        for copy in made:
            copy.wait()
        out[pl.ds(0, rows), pl.ds(out.shape[1] - LANES, LANES)] = chosen_half(
            self.narrow[0], self.narrow[1], self.odd
        )


def first_positions(segments):
    index = lax.broadcasted_iota(jnp.int32, segments.shape, 1)
    begins = (index == 0) | (segments != pltpu.roll(segments, 1, 1))
    starts = jnp.where(begins, index, 0)
    shift = 1
    while shift < segments.shape[1]:
        starts = jnp.maximum(starts, jnp.where(index >= shift, pltpu.roll(starts, shift, 1), 0))
        shift *= 2
    return starts, index


def first_kernel(
    tokens,
    query,
    key,
    value,
    gate,
    up,
    gain_one,
    gain_two,
    segments,
    freqs,
    hidden,
    qkv,
    heads_turned,
    gate_all,
    up_own,
    cosine,
    sine,
    starts,
    gain_one_all,
    gain_two_all,
    tokens_here,
    hidden_here,
    heads_own,
    heads_all,
    gate_own,
    wide,
    narrow,
    picks,
    stores,
    local,
    send,
    recv,
):
    ring = seq_ring()
    weights_ring, _, mate = fsdp_ring()
    greet(ring.peers + weights_ring.peers + [mate])
    copies = Copies(send, recv)
    me, here = ring.near[0], weights_ring.near[0]
    rows = tokens.shape[0]
    kept = [pltpu.make_async_copy(tokens, tokens_here.at[me], local.at[0])]
    kept[0].start()
    pick = Pick(picks, wide, narrow, lax.axis_index("seq"))
    heads_made = pick.start_heads(query, key, value, heads_own)
    gate_made = pick.start_units(0, gate)
    up_made = pick.start_units(1, up)

    def heads_walk():
        pick.finish_heads(heads_made, gain_one, gain_two, heads_own)
        copy = pltpu.make_async_copy(heads_own, heads_all.at[here], local.at[1])
        copy.start()
        kept.append(copy)
        yield from gather_walk(
            weights_ring,
            copies,
            heads_own,
            heads_all,
            by_rows(heads_own.shape[0], 2),
            2,
            True,
            mate,
        )

    def gate_walk():
        pick.finish_units(0, gate_made, gate_own)
        copy = pltpu.make_async_copy(gate_own, gate_all.at[here], local.at[2])
        copy.start()
        kept.append(copy)
        yield from weight_walk(weights_ring, copies, gate_own, gate_all, mate)

    def project(index):
        values = tokens_here[index].astype(jnp.float32)
        factor = lax.rsqrt(mean_square(values) + EPS)
        hidden_here[index] = (values * factor * gain_one_all[...]).astype(jnp.bfloat16)
        copy = pltpu.make_async_copy(hidden_here.at[index], hidden.at[index], stores.at[len(stored)])
        copy.start()
        stored.append(copy)
        lanes = pl.ds(pl.multiple_of(index * rows, rows), rows)
        qkv[:, lanes] = lax.dot_general(
            heads_turned[...],
            hidden_here[index],
            (((1,), (1,)), ((), ())),
            preferred_element_type=jnp.float32,
        ).astype(jnp.bfloat16)

    stored = []

    def compute():
        pick.finish_units(1, up_made, up_own)
        first, index = first_positions(segments[...])
        starts[...] = first
        phase = (index - first).astype(jnp.float32) * freqs[...]
        cosine[...] = jnp.cos(phase)
        sine[...] = jnp.sin(phase)
        yield
        for copy in kept:
            copy.wait()
        for owner in range(heads_all.shape[0]):
            cols = pl.ds(owner * rows, rows)
            heads_turned[:, cols] = heads_all[owner, :rows].T
            gains = heads_all[owner, pl.ds(rows, 16), pl.ds(0, rows)].astype(jnp.float32)
            gain_one_all[:, cols] = gains[0:1]
            gain_two_all[:, cols] = gains[1:2]
        project(me)
        yield
        project(ring.far[0])
        yield
        for place in (ring.near[1], ring.near[3], ring.near[2]):
            project(place)
        yield
        project(ring.far[1])
        project(ring.far[3])
        yield
        project(ring.far[2])

    beside(
        gather_walk(ring, copies, tokens, tokens_here, by_rows(rows, CHUNKS), CHUNKS),
        (heads_walk(), (0, 0, 1, 2, 2, 4, 6, 6, 6, 7)),
        (gate_walk(), SMALL_BESIDE),
        (compute(), (0, 7, 8, 10, 11, 12)),
    )
    copies.finish()
    for copy in stored:
        copy.wait()


LANES = 128


def gather_first(tokens, query, key, value, gate, up, gain_one, gain_two, segments, freqs, number):
    rows, width = tokens.shape
    ranks, owners = lax.axis_size("seq"), lax.axis_size("fsdp")
    length = segments.shape[1]
    cols = width // ranks + LANES
    units = owners // 2 * LANES
    assert gate.shape[1] // owners // ranks == HEAD_SIZE == LANES // 2
    count = gather_copies(CHUNKS) + gather_copies(2, True) + gather_copies(CHUNKS, True)
    low, real = jnp.bfloat16, jnp.float32
    return pl.pallas_call(
        first_kernel,
        out_shape=[
            jax.ShapeDtypeStruct((ranks, rows, width), low),
            jax.ShapeDtypeStruct((cols, length), low),
            jax.ShapeDtypeStruct((cols, width), low),
            jax.ShapeDtypeStruct((owners, rows, units), low),
            jax.ShapeDtypeStruct((rows, units), low),
            jax.ShapeDtypeStruct((freqs.shape[0], length), real),
            jax.ShapeDtypeStruct((freqs.shape[0], length), real),
            jax.ShapeDtypeStruct((1, length), jnp.int32),
            jax.ShapeDtypeStruct((1, width), real),
            jax.ShapeDtypeStruct((1, width), real),
        ],
        in_specs=[ANYWHERE] * 6 + [VMEM] * 4,
        out_specs=[ANYWHERE, VMEM, VMEM, ANYWHERE] + [VMEM] * 6,
        scratch_shapes=[
            pltpu.VMEM((ranks, rows, width), low),
            pltpu.VMEM((ranks, rows, width), low),
            pltpu.VMEM((rows + 32, cols), low),
            pltpu.VMEM((owners, rows + 32, cols), low),
            pltpu.VMEM((rows, units), low),
            pltpu.VMEM((2, owners, rows, LANES), low),
            pltpu.VMEM((2, rows, LANES), low),
            pltpu.SemaphoreType.DMA((2 * owners + 3,)),
            pltpu.SemaphoreType.DMA((ranks,)),
            pltpu.SemaphoreType.DMA((3,)),
        ]
        + semaphores(count),
        compiler_params=params(number, 62),
        name="gather_first",
    )(tokens, query, key, value, gate, up, gain_one[None], gain_two[None], segments, freqs)


def mean_square(values):
    return jnp.mean(values * values, axis=-1, keepdims=True)


PRODUCT = 512


def product(left, right, store, size=PRODUCT):
    def columns(index, _):
        cols = pl.ds(pl.multiple_of(index * size, size), size)
        store(cols, jnp.dot(left, right[:, cols], preferred_element_type=jnp.float32))
        return 0

    lax.fori_loop(0, right.shape[1] // size, columns, 0)


def two_blocks(ref, rows, first, second):
    return jnp.concatenate(
        [ref[pl.ds(pl.multiple_of(index * rows, rows), rows)] for index in (first, second)], axis=0
    )


def split_store(for_mate, own, place, core):
    def store(cols, value):
        rows = value.shape[0] // 2
        first = core == 0
        theirs = jnp.where(first, value[rows:], value[:rows])
        for_mate[place, :, cols] = theirs.astype(jnp.bfloat16)
        ours = jnp.where(first, value[:rows], value[rows:])
        own[place, :, cols] = ours.astype(jnp.bfloat16)

    return store


def branch_kernel(
    attended,
    tokens,
    gain,
    weight,
    gate,
    up,
    down,
    grad_out,
    middle,
    attended_here,
    hidden,
    up_all,
    down_all,
    act_out,
    gate_out,
    up_out,
    block,
    got,
    weight_here,
    gate_here,
    up_here,
    down_here,
    grad_out_here,
    hidden_here,
    gated,
    upped,
    grad_act,
    act,
    grad_gate,
    grad_up,
    stores,
    local,
    send,
    recv,
):
    ring = seq_ring()
    weights_ring, _, mate = fsdp_ring()
    rows = tokens.shape[0]
    greet(ring.peers + ring.remote + weights_ring.peers + [mate])
    copies = Copies(send, recv)
    me, here = ring.near[0], weights_ring.near[0]
    down_rows = down_here.shape[1]
    down = down.at[pl.ds(pl.multiple_of(me * down_rows, down_rows), down_rows)]

    def lanes_of(index):
        return attended.at[:, pl.ds(pl.multiple_of(index * rows, rows), rows)]

    arriving = exchange_all(ring, copies, lanes_of, got.at[me])
    load = pltpu.make_async_copy(weight, weight_here, local.at[0])
    load.start()
    mine = pltpu.make_async_copy(lanes_of(me), got.at[me], local.at[1])
    mine.start()
    kept = [
        pltpu.make_async_copy(up, up_here.at[here], local.at[2]),
        pltpu.make_async_copy(down, down_here.at[here], local.at[3]),
        pltpu.make_async_copy(gate, gate_here, local.at[4]),
        pltpu.make_async_copy(grad_out, grad_out_here, local.at[5]),
    ]
    for copy in kept:
        copy.start()
    stored = []

    def store(source, target):
        copy = pltpu.make_async_copy(source, target, stores.at[len(stored)])
        copy.start()
        stored.append(copy)

    def walk():
        yield
        mine.wait()
        load.wait()
        for copy in arriving:
            copy.wait_recv()
        attended_here[...] = got[...].reshape(attended_here.shape)
        turned = attended_here[...].T

        def add(cols, value):
            middle[:, cols] = tokens[:, cols].astype(jnp.float32) + value

        product(turned, weight_here, add)
        values = middle[...]
        factor = lax.rsqrt(mean_square(values) + EPS)
        block[...] = (values * factor * gain[...]).astype(jnp.bfloat16)
        hidden_here[me] = block[...]
        yield from gather_walk(
            ring, copies, block, hidden_here, by_rows(rows, CHUNKS), CHUNKS
        )

    units = gated.shape[2]

    def both(ref, pair):
        return jnp.concatenate([ref[index] for index in pair], axis=0)

    def times(pair, matrix, out):
        left = both(hidden_here, pair)

        def columns(tile, _):
            cols = pl.ds(pl.multiple_of(tile * PRODUCT, PRODUCT), PRODUCT)
            right = matrix[:, :, cols].reshape(-1, PRODUCT)
            value = jnp.dot(left, right, preferred_element_type=jnp.float32)
            out[pair[0], :, cols] = value[:rows]
            out[pair[1], :, cols] = value[rows:]
            return 0

        lax.fori_loop(0, units // PRODUCT, columns, 0)

    def back(pair):
        left = both(grad_out_here, pair)
        share = PRODUCT // down_here.shape[1]

        def columns(tile, _):
            cols = pl.ds(pl.multiple_of(tile * PRODUCT, PRODUCT), PRODUCT)
            right = down_here[pl.ds(tile * share, share)].reshape(PRODUCT, -1)
            value = lax.dot_general(
                left, right, (((1,), (1,)), ((), ())), preferred_element_type=jnp.float32
            )
            grad_act[pair[0], :, cols] = value[:rows]
            grad_act[pair[1], :, cols] = value[rows:]
            return 0

        lax.fori_loop(0, units // PRODUCT, columns, 0)

    def combine(pair):
        for index in pair:
            value, other, grad = gated[index], upped[index], grad_act[index]
            sig = jax.nn.sigmoid(value)
            silu = value * sig
            act[index] = (silu * other).astype(jnp.bfloat16)
            grad_gate[index] = (grad * other * (sig * (1.0 + value * (1.0 - sig)))).astype(
                jnp.bfloat16
            )
            grad_up[index] = (grad * silu).astype(jnp.bfloat16)
            store(act.at[index], act_out.at[index])
            store(grad_gate.at[index], gate_out.at[index])
            store(grad_up.at[index], up_out.at[index])

    near, far = ring.near, ring.far
    pairs = ((near[0], far[0]), (near[1], near[3]), (far[1], far[3]), (near[2], far[2]))

    def compute():
        kept[0].wait()
        kept[1].wait()
        kept[2].wait()
        kept[3].wait()
        store(down_here, down_all)
        back(pairs[0])
        yield
        back(pairs[1])
        yield
        back(pairs[2])
        yield
        back(pairs[3])
        yield
        times(pairs[0], gate_here, gated)
        yield
        times(pairs[1], gate_here, gated)
        yield
        store(up_here, up_all)
        times(pairs[0], up_here, upped)
        combine(pairs[0])
        yield
        times(pairs[1], up_here, upped)
        combine(pairs[1])
        yield
        for pair in pairs[2:]:
            for index in pair:
                store(hidden_here.at[index], hidden.at[index])
            times(pair, gate_here, gated)
            times(pair, up_here, upped)
            combine(pair)
            yield

    def hold():
        for index in (*pairs[0], *pairs[1]):
            store(hidden_here.at[index], hidden.at[index])
        yield

    beside(
        walk(),
        (weight_walk(weights_ring, copies, down, down_here, mate), BESIDE_FIRST),
        (weight_walk(weights_ring, copies, up, up_here, mate), BESIDE_SECOND),
        (hold(), (9,)),
        (compute(), (4, 5, 6, 7, 7, 9, 11, 11, 12, 13)),
    )
    copies.finish()
    for copy in stored:
        copy.wait()


BESIDE_FIRST = (0, 0, 0, 0, 0, 0, 0, 0, 1, 1, 1, 1, 2, 2, 3, 4)
BESIDE_SECOND = (0, 0, 1, 1, 1, 1, 2, 2, 7, 7, 7, 7, 9, 9, 10, 11)


def add_branch(attended, tokens, gain, weight, gate, up, down, grad_out, number):
    rows, width = tokens.shape
    ranks, owners = lax.axis_size("seq"), lax.axis_size("fsdp")
    features, units = attended.shape[0], up.shape[1]
    down_block = (down.shape[0] // ranks, width)
    count = ranks - 1 + gather_copies(CHUNKS) + 2 * gather_copies(CHUNKS, True)
    low, real = jnp.bfloat16, jnp.float32
    return pl.pallas_call(
        branch_kernel,
        out_shape=[
            jax.ShapeDtypeStruct((rows, width), real),
            jax.ShapeDtypeStruct((ranks * features, rows), low),
            jax.ShapeDtypeStruct((ranks, rows, width), low),
            jax.ShapeDtypeStruct((owners, *up.shape), low),
            jax.ShapeDtypeStruct((owners, *down_block), low),
        ]
        + [jax.ShapeDtypeStruct((ranks, rows, units), low)] * 3,
        in_specs=[VMEM] * 3 + [ANYWHERE] * 5,
        out_specs=[VMEM] * 2 + [ANYWHERE] * 6,
        scratch_shapes=[
            pltpu.VMEM((rows, width), low),
            pltpu.VMEM((ranks, features, rows), low),
            pltpu.VMEM(weight.shape, low),
            pltpu.VMEM(gate.shape, low),
            pltpu.VMEM((owners, *up.shape), low),
            pltpu.VMEM((owners, *down_block), low),
            pltpu.VMEM((ranks, rows, width), low),
            pltpu.VMEM((ranks, rows, width), low),
        ]
        + [pltpu.VMEM((ranks, rows, units), real)] * 3
        + [pltpu.VMEM((ranks, rows, units), low)] * 3
        + [pltpu.SemaphoreType.DMA((4 * ranks + 2,)), pltpu.SemaphoreType.DMA((6,))]
        + semaphores(count),
        compiler_params=params(number, 62),
        name="add_branch",
    )(attended, tokens, gain, weight, gate, up, down, grad_out)


def norm_back_rows(grad, gain, values):
    factor = lax.rsqrt(mean_square(values) + EPS)
    normed = values * factor
    weighted = grad * gain
    back = factor * (weighted - normed * jnp.mean(weighted * normed, axis=-1, keepdims=True))
    return back, grad * normed


def back_kernel(*refs):
    middle, gain, cotangent = refs[:3]
    qkv, queries, keys, attended, lse, cosine, sine, starts = refs[3:11]
    hidden, gate_grads, up_grads, gate, up, weight, act, down = refs[11:19]
    grad_middle, grad_gain, block, grads_share, qkv_grads, layer_out = refs[19:25]
    tiles_scratch = refs[25:34]
    part_of, big, left_wide, right_wide, for_mate, given, got, grad_attended = refs[34:42]
    loads, send, recv, own, other = refs[42:47]
    owners_bufs, first_bufs, second_bufs = refs[47:54], refs[54:61], refs[61:68]
    ring = seq_ring()
    weights_ring, core, mate = fsdp_ring()
    rows = middle.shape[0]
    greet(ring.peers + ring.remote + weights_ring.peers + [mate])
    copies = Copies(send, recv)
    grad_gain[...] = jnp.zeros_like(grad_gain)
    units = gate_grads.shape[1]
    low_cols, high_cols = pl.ds(0, units), pl.ds(units, units)
    count = [0]

    def load(source, target):
        copy = pltpu.make_async_copy(source, target, loads.at[count[0]])
        copy.start()
        count[0] += 1
        return copy

    arrived = [
        load(gate_grads, right_wide.at[:, low_cols]),
        load(up_grads, right_wide.at[:, high_cols]),
        load(gate, big.at[:, low_cols]),
        load(up, big.at[:, high_cols]),
    ]
    hidden_load = [load(hidden, left_wide)]

    def ready(*blocks):
        while arrived:
            arrived.pop().wait()
        left = two_blocks(right_wide, rows, *blocks)

        def columns(tile, _):
            cols = pl.ds(pl.multiple_of(tile * PRODUCT, PRODUCT), PRODUCT)
            value = lax.dot_general(
                left, big[cols], (((1,), (1,)), ((), ())), preferred_element_type=jnp.float32
            ).astype(jnp.bfloat16)
            part_of[blocks[0], :, cols] = value[:rows]
            part_of[blocks[1], :, cols] = value[rows:]
            return 0

        lax.fori_loop(0, big.shape[0] // PRODUCT, columns, 0)

    def done(index, total):
        rows_of = chunk_rows(rows, index)
        back, terms = norm_back_rows(total, gain[...], middle[rows_of])
        grad_gain[...] += jnp.sum(terms, axis=0, keepdims=True)
        values = cotangent[rows_of].astype(jnp.float32) + back
        grad_middle[rows_of] = values
        block[rows_of] = values.astype(jnp.bfloat16)

    def owned(rows_of, total):
        grads_share[rows_of] = total.astype(jnp.bfloat16)

    made = []

    def produce(place):
        while hidden_load:
            hidden_load.pop().wait()
        lanes = pl.ds(pl.multiple_of(place * 2 * rows, 2 * rows), 2 * rows)
        turned = left_wide[:, lanes].T
        product(turned, right_wide, split_store(for_mate, own, place, core), 2 * PRODUCT)
        made.append(place)
        return [copies.start(for_mate.at[place], other.at[place], mate).wait_recv]

    act_here = right_wide.at[:, low_cols]
    layer_loads = []

    def layer_ready(*blocks):
        assert len(made) == for_mate.shape[0]
        while layer_loads:
            layer_loads.pop().wait()

        def store(cols, value):
            part_of[blocks[0], :, cols] = value[:rows].astype(jnp.bfloat16)
            part_of[blocks[1], :, cols] = value[rows:].astype(jnp.bfloat16)

        product(two_blocks(act_here, rows, *blocks), left_wide, store)

    def layer_done(index, total):
        rows_of = chunk_rows(rows, index)
        layer_out[rows_of] = (middle[rows_of] + total).astype(jnp.bfloat16)

    me = ring.near[0]
    features = grad_attended.shape[0]

    def walk():
        cut = by_rows(rows, CHUNKS)
        step = 0
        for _ in reduce_walk(ring, copies, part_of, first_bufs, cut, CHUNKS, done, ready):
            if step == 3:
                weight_load = load(weight, big)
            step += 1
            yield
        layer_loads.append(load(act, act_here))
        layer_loads.append(load(down, left_wide))
        weight_load.wait()

        def piece(index):
            part = pl.ds(pl.multiple_of(index * features, features), features)
            given[index] = lax.dot_general(
                big[part],
                block[...],
                (((1,), (1,)), ((), ())),
                preferred_element_type=jnp.float32,
            ).astype(jnp.bfloat16)
            return given.at[index]

        arriving = exchange_all(ring, copies, piece, got.at[me])
        piece(me)
        yield
        layer = reduce_walk(
            ring, copies, part_of, second_bufs, cut, CHUNKS, layer_done, layer_ready
        )
        for _ in range(4):
            next(layer)
            yield
        for copy in arriving:
            copy.wait_recv()
        got[me] = given[me]
        for index in range(got.shape[0]):
            grad_attended[:, pl.ds(index * rows, rows)] = got[index]
        yield
        yield from layer

    tiles = back_tiles(
        qkv,
        queries,
        keys,
        attended,
        lse,
        grad_attended,
        cosine,
        sine,
        starts,
        qkv_grads,
        *tiles_scratch,
    )
    beside(
        walk(),
        (
            owners_walk(
                weights_ring,
                mate,
                copies,
                produce,
                own,
                other,
                owners_bufs,
                grads_share.shape[0],
                owned,
            ),
            BACK_OWNERS,
        ),
        (tiles, BACK_TILES),
    )
    copies.finish()


BACK_OWNERS = (0, 0, 0, 1, 1, 3, 3, 3, 3, 11, 11, 11, 11, 11, 15, 15, 20, 25, 25)
BACK_TILES = (25, 25, 33, 33, 37)


def go_back(
    middle,
    gain,
    cotangent,
    qkv,
    queries,
    keys,
    attended,
    lse,
    cosine,
    sine,
    starts,
    hidden,
    gate_grads,
    up_grads,
    gate,
    up,
    weight,
    act,
    down,
    number,
):
    rows, width = middle.shape
    length = hidden.shape[0]
    ranks, owners = lax.axis_size("seq"), lax.axis_size("fsdp")
    places = owners // 2
    group = queries.shape[0] // HEAD_SIZE
    tiles = length // TILE
    features = weight.shape[0] // ranks
    grad_rows, grad_cols = width // owners, 2 * gate_grads.shape[1]
    count = 2 * reduce_copies(CHUNKS) + ranks - 1 + OWNERS_COPIES + places
    low, real = jnp.bfloat16, jnp.float32
    return pl.pallas_call(
        back_kernel,
        out_shape=[
            jax.ShapeDtypeStruct((rows, width), real),
            jax.ShapeDtypeStruct((1, width), real),
            jax.ShapeDtypeStruct((rows, width), low),
            jax.ShapeDtypeStruct((grad_rows, grad_cols), low),
            jax.ShapeDtypeStruct(qkv.shape, low),
            jax.ShapeDtypeStruct((rows, width), low),
        ],
        in_specs=[VMEM] * 11 + [ANYWHERE] * 8,
        out_specs=[VMEM] * 6,
        scratch_shapes=[
            pltpu.VMEM((length, HEAD_SIZE), low),
            pltpu.VMEM((length, HEAD_SIZE), low),
            pltpu.VMEM((group, length, HEAD_SIZE), low),
            pltpu.VMEM((group, length, HEAD_SIZE), low),
            pltpu.VMEM((group, 8, length), real),
            pltpu.VMEM((length, HEAD_SIZE), real),
            pltpu.VMEM((length, HEAD_SIZE), real),
            pltpu.VMEM((group * HEAD_SIZE, length), real),
            pltpu.VMEM((tiles, TILE, TILE), real),
            pltpu.VMEM((ranks, rows, width), low),
            pltpu.VMEM(weight.shape, low),
            pltpu.VMEM((length, width), low),
            pltpu.VMEM((length, width), low),
            pltpu.VMEM((places, grad_rows, grad_cols), low),
            pltpu.VMEM((ranks, features, rows), low),
            pltpu.VMEM((ranks, features, rows), low),
            pltpu.VMEM((features, length), low),
            pltpu.SemaphoreType.DMA((8,)),
        ]
        + semaphores(count)
        + owners_scratch(places, grad_rows, grad_cols)
        + reduce_scratch(rows, width)
        + reduce_scratch(rows, width),
        compiler_params=params(number, 62),
        name="go_back",
    )(
        middle,
        gain,
        cotangent,
        qkv,
        queries,
        keys,
        attended,
        lse,
        cosine,
        sine,
        starts,
        hidden,
        gate_grads,
        up_grads,
        gate,
        up,
        weight,
        act,
        down,
    )


def heads_products(copies, core, mate, attended, branch, for_mate, own, other):
    rows = branch.shape[0]

    def produce(place):
        both = attended[pl.ds(pl.multiple_of(place * 2 * rows, 2 * rows), 2 * rows)]
        product(both, branch, split_store(for_mate, own, place, core))
        return [copies.start(for_mate.at[place], other.at[place], mate).wait_recv]

    return produce


def last_kernel(
    tokens,
    gain,
    grad_middle,
    qkv_grads,
    heads_turned,
    attended,
    branch,
    grad_gain_two,
    hidden,
    act,
    grad_out,
    gate_up,
    out,
    gate_up_all,
    pack_all,
    heads_all,
    gains,
    part_of,
    hidden_here,
    act_here,
    grad_out_here,
    pack,
    heads,
    heads_got,
    heads_mine,
    grad_gain,
    given,
    from_mate,
    summed,
    from_places,
    for_group,
    from_group,
    loads,
    local,
    send,
    recv,
    *scratch,
):
    ring = seq_ring()
    me = ring.near[0]
    weights_ring, core, mate = fsdp_ring()
    rows = tokens.shape[0]
    greet(ring.peers + ring.remote + weights_ring.peers + weights_ring.remote + [mate])
    copies = Copies(send, recv)
    reduce_bufs, scratch = scratch[:7], scratch[7:]
    qkv_scratch, down_scratch, heads_scratch = scratch[:10], scratch[10:20], scratch[20:]
    grad_gain[...] = jnp.zeros_like(grad_gain)
    hidden_load = [pltpu.make_async_copy(hidden, hidden_here, loads.at[0])]
    down_loads = [
        pltpu.make_async_copy(act, act_here, loads.at[1]),
        pltpu.make_async_copy(grad_out, grad_out_here, loads.at[2]),
    ]
    for copy in hidden_load + down_loads:
        copy.start()
    kept = []

    def keep(block, all_of):
        copy = pltpu.make_async_copy(block, all_of.at[me], local.at[len(kept)])
        copy.start()
        kept.append(copy)

    keep(gate_up, gate_up_all)

    def ready(*blocks):
        left = jnp.concatenate(
            [
                qkv_grads[:, pl.ds(pl.multiple_of(index * rows, rows), rows)]
                for index in blocks
            ],
            axis=1,
        ).T

        def store(cols, value):
            part_of[blocks[0], :, cols] = value[:rows].astype(jnp.bfloat16)
            part_of[blocks[1], :, cols] = value[rows:].astype(jnp.bfloat16)

        product(left, heads_turned, store)

    def done(index, total):
        rows_of = chunk_rows(rows, index)
        back, terms = norm_back_rows(total, gain[...], tokens[rows_of].astype(jnp.float32))
        grad_gain[...] += jnp.sum(terms, axis=0, keepdims=True)
        out[rows_of] = (grad_middle[rows_of] + back).astype(jnp.bfloat16)

    def sums(parts, produce, block_rows, owned):
        for_mate, own, other = parts[:3]
        return owners_walk(
            weights_ring, mate, copies, produce, own, other, parts[3:], block_rows, owned
        )

    qkv_cols = qkv_grads.shape[0]
    first = pack.shape[1] - qkv_cols

    def qkv_produce(place):
        while hidden_load:
            hidden_load.pop().wait()
        for_mate, own, other = qkv_scratch[:3]
        lanes = pl.ds(pl.multiple_of(place * 2 * rows, 2 * rows), 2 * rows)
        value = lax.dot_general(
            hidden_here[:, lanes].T,
            qkv_grads[...],
            (((1,), (1,)), ((), ())),
            preferred_element_type=jnp.float32,
        )
        split_store(for_mate, own, place, core)(slice(None), value)
        return [copies.start(for_mate.at[place], other.at[place], mate).wait_recv]

    def qkv_owned(rows_of, total):
        pack[rows_of, pl.ds(first, qkv_cols)] = total.astype(jnp.bfloat16)

    down_rows = rows // 2

    def down_produce(place):
        while down_loads:
            down_loads.pop().wait()
        for_mate, own, other = down_scratch[:3]
        lanes = pl.ds(pl.multiple_of(place * rows, rows), rows)
        turned = act_here[:, lanes].T
        product(turned, grad_out_here, split_store(for_mate, own, place, core), 2 * PRODUCT)
        return [copies.start(for_mate.at[place], other.at[place], mate).wait_recv]

    def down_owned(rows_of, total):
        pack[rows_of, pl.ds(0, first)] = total[:, :first].astype(jnp.bfloat16)
        under = pl.ds(rows_of.start + down_rows, rows_of.size)
        pack[under, pl.ds(0, first)] = total[:, first:].astype(jnp.bfloat16)

    piece_rows = heads_mine.shape[0]

    def heads_owned(rows_of, total):
        heads[rows_of] = total.astype(jnp.bfloat16)

    def heads_walk():
        for_mate, own, other = heads_scratch[:3]
        produce = heads_products(copies, core, mate, attended, branch, for_mate, own, other)
        yield from sums(heads_scratch, produce, rows, heads_owned)

        def piece(index):
            return heads.at[pl.ds(pl.multiple_of(index * piece_rows, piece_rows), piece_rows)]

        arriving = exchange_all(ring, copies, piece, heads_got.at[me])
        heads_got[me] = piece(me)[...]
        yield
        for copy in arriving:
            copy.wait_recv()
        heads_mine[...] = sum(
            heads_got[index].astype(jnp.float32) for index in range(heads_got.shape[0])
        ).astype(jnp.bfloat16)
        keep(heads_mine, heads_all)
        arriving = exchange_all(ring, copies, lambda index: heads_mine, heads_all.at[me])
        yield
        for copy in arriving:
            copy.wait_recv()

    def sum_gains():
        lanes = given.shape[3]
        for index in range(2 * given.shape[0]):
            cols = pl.ds(index * lanes, lanes)
            place = (index // 2, index % 2)
            given[(*place, slice(0, 1))] = grad_gain[:, cols]
            given[(*place, slice(1, 2))] = grad_gain_two[:, cols]
            given[(*place, slice(2, 8))] = jnp.zeros((6, lanes), jnp.float32)
        copy = copies.start(given.at[:, 1 - core], from_mate, mate)
        yield
        copy.wait_recv()
        summed[...] = given[:, core] + from_mate[...]
        place = weights_ring.place
        arriving = exchange_all(
            weights_ring,
            copies,
            lambda index: summed.at[lax.div(index, 2)],
            from_places.at[place],
        )
        from_places[place] = summed[place]
        yield
        for copy in arriving:
            copy.wait_recv()
        for_group[...] = sum(from_places[index] for index in range(from_places.shape[0]))
        arriving = exchange_all(ring, copies, lambda index: for_group, from_group.at[me])
        from_group[me] = for_group[...]
        yield
        for copy in arriving:
            copy.wait_recv()
        gains[...] = sum(from_group[index] for index in range(from_group.shape[0]))

    def walk():
        yield from reduce_walk(
            ring, copies, part_of, reduce_bufs, by_rows(rows, CHUNKS), CHUNKS, done, ready
        )
        keep(pack, pack_all)
        yield from gather_walk(ring, copies, pack, pack_all, by_rows(rows, CHUNKS), CHUNKS)

    beside(
        walk(),
        (
            sums(down_scratch, down_produce, down_rows, down_owned),
            (3, 3, 3, 3, 3, 3, 3, 11, 11, 11, 11, 11, 11, 11, 15, 15, 15, 19, 19, 19),
        ),
        (
            gather_walk(
                ring, copies, gate_up, gate_up_all, by_rows(rows, CHUNKS), CHUNKS
            ),
            (11, 15, 15, 16, 17, 18, 19, 19, 19, 20, 20, 22, 24, 25),
        ),
        (
            sums(qkv_scratch, qkv_produce, rows, qkv_owned),
            (11,) * 14 + (15, 15, 19, 19, 19, 19),
        ),
        (heads_walk(), (3,) * 14 + (11, 11, 15, 15, 15, 16, 20, 26)),
        (sum_gains(), (19, 21, 24)),
    )
    copies.finish()
    for copy in kept:
        copy.wait()


def finish(
    tokens,
    gain,
    grad_middle,
    qkv_grads,
    heads_turned,
    attended,
    branch,
    grad_gain_two,
    hidden,
    act,
    grad_out,
    gate_up,
    number,
):
    rows, width = tokens.shape
    ranks, owners = lax.axis_size("seq"), lax.axis_size("fsdp")
    places = owners // 2
    lanes = width // owners
    qkv_cols = qkv_grads.shape[0]
    packed = width // 2 + qkv_cols
    pieces = rows // ranks
    assert act.shape[1] // owners == rows // 2
    count = reduce_copies(CHUNKS) + 2 * gather_copies(CHUNKS) + 3 * (OWNERS_COPIES + places)
    count += 2 * (ranks - 1) + 1 + places - 1 + ranks - 1
    low = jnp.bfloat16

    def table(*shape):
        return pltpu.VMEM((*shape, 8, lanes), jnp.float32)

    def sums(block_rows, cols):
        return [pltpu.VMEM((places, block_rows, cols), low)] + owners_scratch(
            places, block_rows, cols
        )

    return pl.pallas_call(
        last_kernel,
        out_shape=[
            jax.ShapeDtypeStruct((rows, width), low),
            jax.ShapeDtypeStruct((ranks, rows, width), low),
            jax.ShapeDtypeStruct((ranks, rows, packed), low),
            jax.ShapeDtypeStruct((ranks, pieces, width), low),
            jax.ShapeDtypeStruct((8, lanes), jnp.float32),
        ],
        in_specs=[VMEM] * 8 + [ANYWHERE] * 4,
        out_specs=[VMEM] + [ANYWHERE] * 3 + [VMEM],
        scratch_shapes=[
            pltpu.VMEM((ranks, rows, width), low),
            pltpu.VMEM(hidden.shape, low),
            pltpu.VMEM(act.shape, low),
            pltpu.VMEM(grad_out.shape, low),
            pltpu.VMEM((rows, packed), low),
            pltpu.VMEM((rows, width), low),
            pltpu.VMEM((ranks, pieces, width), low),
            pltpu.VMEM((pieces, width), low),
            pltpu.VMEM((1, width), jnp.float32),
            table(places, 2),
            table(places),
            table(places),
            table(places),
            table(),
            table(ranks),
            pltpu.SemaphoreType.DMA((3,)),
            pltpu.SemaphoreType.DMA((3,)),
        ]
        + semaphores(count)
        + reduce_scratch(rows, width)
        + sums(rows, qkv_cols)
        + sums(rows // 2, width)
        + sums(rows, width),
        compiler_params=params(number, 62),
        name="finish",
    )(
        tokens,
        gain,
        grad_middle,
        qkv_grads,
        heads_turned,
        attended,
        branch,
        grad_gain_two,
        hidden,
        act,
        grad_out,
        gate_up,
    )


def merge_lanes(first, second):
    half = first.shape[1] // 2
    low = lax.broadcasted_iota(jnp.int32, first.shape, 1) < half
    return (
        jnp.where(low, first, pltpu.roll(second, half, 1)),
        jnp.where(low, pltpu.roll(first, half, 1), second),
    )


def place_kernel(
    gate,
    up,
    down,
    query,
    pair,
    heads,
    layer,
    tokens,
    gate_out,
    up_out,
    down_out,
    query_out,
    key_out,
    value_out,
    heads_out,
    layer_out,
    tokens_out,
):
    lanes = gate.shape[2]
    blocks = gate.shape[0] // 2
    for part, out in ((gate, gate_out), (up, up_out)):
        for index in range(blocks):
            low, high = merge_lanes(
                part[2 * index].astype(jnp.float32), part[2 * index + 1].astype(jnp.float32)
            )
            out[:, pl.ds(index * lanes, lanes)] = low
            out[:, pl.ds((blocks + index) * lanes, lanes)] = high
    key, value = merge_lanes(pair[0].astype(jnp.float32), pair[1].astype(jnp.float32))
    key_out[...] = key
    value_out[...] = value
    down_rows, cols = down_out.shape[0], down.shape[2]
    down_out[:, :cols] = down[0, :down_rows].astype(jnp.float32)
    down_out[:, cols:] = down[0, down_rows:].astype(jnp.float32)
    query_out[...] = query[0].astype(jnp.float32)
    heads_out[...] = heads[0].astype(jnp.float32)
    layer_out[...] = layer[...]
    tokens_out[...] = tokens[...]


def place_grads(gate_up, pack, heads, layer, tokens):
    ranks, rows, units = gate_up.shape
    units //= 2
    lanes = LANES
    steps = units // lanes
    width = heads.shape[2]
    down_cols, down_rows = width // 2, rows // 2
    query_cols = width // ranks
    head_rows = heads.shape[1]
    first = (down_cols + query_cols) // lanes
    assert steps == ranks and lanes == 2 * HEAD_SIZE and query_cols == 2 * lanes
    real = jnp.float32
    return pl.pallas_call(
        place_kernel,
        grid=(steps,),
        out_shape=[
            jax.ShapeDtypeStruct((rows, ranks * units), real),
            jax.ShapeDtypeStruct((rows, ranks * units), real),
            jax.ShapeDtypeStruct((ranks * down_rows, width), real),
            jax.ShapeDtypeStruct((rows, ranks * query_cols), real),
            jax.ShapeDtypeStruct((rows, ranks * HEAD_SIZE), real),
            jax.ShapeDtypeStruct((rows, ranks * HEAD_SIZE), real),
            jax.ShapeDtypeStruct((rows, width), real),
            jax.ShapeDtypeStruct((rows, width), jnp.bfloat16),
            jax.ShapeDtypeStruct((rows, width), jnp.bfloat16),
        ],
        in_specs=[
            pl.BlockSpec((ranks, rows, lanes), lambda i: (0, 0, i)),
            pl.BlockSpec((ranks, rows, lanes), lambda i: (0, 0, steps + i)),
            pl.BlockSpec((1, rows, down_cols), lambda i: (i, 0, 0)),
            pl.BlockSpec((1, rows, query_cols), lambda i: (i, 0, down_cols // query_cols)),
            pl.BlockSpec((2, rows, lanes), lambda i: (i // 2, 0, first)),
            pl.BlockSpec((1, head_rows, width), lambda i: (i, 0, 0)),
            pl.BlockSpec((head_rows, width), lambda i: (i, 0)),
            pl.BlockSpec((head_rows, width), lambda i: (i, 0)),
        ],
        out_specs=[
            pl.BlockSpec((rows, ranks * lanes), lambda i: (0, i)),
            pl.BlockSpec((rows, ranks * lanes), lambda i: (0, i)),
            pl.BlockSpec((down_rows, width), lambda i: (i, 0)),
            pl.BlockSpec((rows, query_cols), lambda i: (0, i)),
            pl.BlockSpec((rows, lanes), lambda i: (0, i // 2)),
            pl.BlockSpec((rows, lanes), lambda i: (0, i // 2)),
            pl.BlockSpec((head_rows, width), lambda i: (i, 0)),
            pl.BlockSpec((head_rows, width), lambda i: (i, 0)),
            pl.BlockSpec((head_rows, width), lambda i: (i, 0)),
        ],
        compiler_params=pltpu.CompilerParams(vmem_limit_bytes=62 * 2**20),
        name="place_grads",
    )(gate_up, gate_up, pack, pack, pack, heads, layer, tokens)


def rotate_rows(first, second, cosine, sine):
    return jnp.concatenate([first * cosine - second * sine, second * cosine + first * sine], axis=0)


def bias_tile(start_row, key_tile, query_tile, diagonal):
    keys = key_tile * TILE + lax.broadcasted_iota(jnp.int32, (TILE, TILE), 0)
    seen = keys >= start_row
    if diagonal:
        queries = query_tile * TILE + lax.broadcasted_iota(jnp.int32, (TILE, TILE), 1)
        seen = seen & (keys <= queries)
    return jnp.where(seen, 0.0, NEG)


def attend_tiles(qkv, cosine, sine, starts, attended, lse, queries, keys, key_rows, bias):
    group = queries.shape[0] // HEAD_SIZE
    half = HEAD_SIZE // 2
    tiles = qkv.shape[1] // TILE
    cos, sin = cosine[...], sine[...]

    def rotated(first):
        return rotate_rows(
            qkv[pl.ds(first, half)].astype(jnp.float32),
            qkv[pl.ds(first + half, half)].astype(jnp.float32),
            cos,
            sin,
        ).astype(jnp.bfloat16)

    for head in range(group):
        queries[pl.ds(head * HEAD_SIZE, HEAD_SIZE)] = rotated(head * HEAD_SIZE) * jnp.bfloat16(0.125)
    keys[...] = rotated(group * HEAD_SIZE)
    key_rows[...] = keys[...].T
    for tile in range(tiles):
        lanes = pl.ds(tile * TILE, TILE)
        starts_here = starts[:, lanes]
        for low in range(tile + 1):
            bias[pl.ds(low * TILE, TILE)] = bias_tile(starts_here, low, tile, low == tile)
        count = (tile + 1) * TILE

        def one_head(head, _, lanes=lanes, count=count):
            rows = pl.ds(pl.multiple_of(head * HEAD_SIZE, HEAD_SIZE), HEAD_SIZE)
            scores = jnp.dot(
                key_rows[:count], queries[rows, lanes], preferred_element_type=jnp.float32
            )
            scores += bias[:count]
            highest = jnp.max(scores, axis=0, keepdims=True)
            weights = jnp.exp(scores - highest)
            total = jnp.sum(weights, axis=0, keepdims=True)
            out = jnp.dot(
                qkv[pl.ds((group + 1) * HEAD_SIZE, HEAD_SIZE), :count],
                weights.astype(jnp.bfloat16),
                preferred_element_type=jnp.float32,
            )
            attended[rows, lanes] = (out / total).astype(jnp.bfloat16)
            lse[head, :, lanes] = jnp.broadcast_to(highest + jnp.log(total), (8, TILE))
            return 0

        lax.fori_loop(0, group, one_head, 0)


def forward_kernel(
    qkv,
    cosine,
    sine,
    starts,
    cotangent,
    heads,
    attended,
    lse,
    queries,
    keys,
    gathered,
    heads_all,
    key_rows,
    bias,
    local,
    send,
    recv,
):
    ring = seq_ring()
    weights_ring, _, mate = fsdp_ring()
    greet(ring.peers + weights_ring.peers + [mate])
    kept = [
        pltpu.make_async_copy(cotangent, gathered.at[ring.near[0]], local.at[0]),
        pltpu.make_async_copy(heads, heads_all.at[weights_ring.near[0]], local.at[1]),
    ]
    for copy in kept:
        copy.start()
    copies = Copies(send, recv)

    def compute():
        attend_tiles(qkv, cosine, sine, starts, attended, lse, queries, keys, key_rows, bias)
        yield

    beside(
        gather_walk(
            ring, copies, cotangent, gathered, by_rows(cotangent.shape[0], CHUNKS), CHUNKS
        ),
        (weight_walk(weights_ring, copies, heads, heads_all, mate), LARGE_BESIDE),
        (compute(), (0,)),
    )
    copies.finish()
    for copy in kept:
        copy.wait()


def attend(qkv, cosine, sine, starts, cotangent, heads, group, number):
    length = qkv.shape[1]
    rows, width = cotangent.shape
    ranks = lax.axis_size("seq")
    return pl.pallas_call(
        forward_kernel,
        out_shape=[
            jax.ShapeDtypeStruct((group * HEAD_SIZE, length), jnp.bfloat16),
            jax.ShapeDtypeStruct((group, 8, length), jnp.float32),
            jax.ShapeDtypeStruct((group * HEAD_SIZE, length), jnp.bfloat16),
            jax.ShapeDtypeStruct((HEAD_SIZE, length), jnp.bfloat16),
            jax.ShapeDtypeStruct((ranks, rows, width), jnp.bfloat16),
            jax.ShapeDtypeStruct((lax.axis_size("fsdp"), *heads.shape), jnp.bfloat16),
        ],
        in_specs=[VMEM] * 4 + [ANYWHERE] * 2,
        out_specs=[VMEM] * 4 + [ANYWHERE] * 2,
        scratch_shapes=[
            pltpu.VMEM((length, HEAD_SIZE), jnp.bfloat16),
            pltpu.VMEM((length, TILE), jnp.float32),
            pltpu.SemaphoreType.DMA((2,)),
        ]
        + semaphores(gather_copies(CHUNKS) + gather_copies(CHUNKS, True)),
        compiler_params=params(number, 62),
        name="attend",
    )(qkv, cosine, sine, starts, cotangent, heads)


def back_tiles(
    qkv,
    queries,
    keys,
    attended,
    lse,
    grads,
    cosine,
    sine,
    starts,
    out,
    key_rows,
    value_rows,
    query_rows,
    grad_rows,
    row_dots,
    key_grad,
    value_grad,
    query_grad,
    bias,
):
    group = queries.shape[0] // HEAD_SIZE
    half = HEAD_SIZE // 2
    tiles = qkv.shape[1] // TILE
    key_rows[...] = keys[...].T
    value_rows[...] = qkv[pl.ds((group + 1) * HEAD_SIZE, HEAD_SIZE)].T
    for head in range(group):
        rows = pl.ds(head * HEAD_SIZE, HEAD_SIZE)
        query_rows[head] = queries[rows].T
        grad_rows[head] = grads[rows].T
        row_dots[head] = jnp.broadcast_to(
            jnp.sum(
                grads[rows].astype(jnp.float32) * attended[rows].astype(jnp.float32),
                axis=0,
                keepdims=True,
            ),
            row_dots.shape[1:],
        )
    key_grad[...] = jnp.zeros_like(key_grad)
    value_grad[...] = jnp.zeros_like(value_grad)
    for tile in range(tiles):
        lanes = pl.ds(tile * TILE, TILE)
        starts_here = starts[:, lanes]
        for low in range(tile + 1):
            bias[low] = bias_tile(starts_here, low, tile, low == tile)

        def one_head(head, _, lanes=lanes, tile=tile):
            rows = pl.ds(pl.multiple_of(head * HEAD_SIZE, HEAD_SIZE), HEAD_SIZE)
            query, grad = queries[rows, lanes], grads[rows, lanes]
            query_row, grad_row = query_rows[head, lanes], grad_rows[head, lanes]
            lse_row = lse[head, 0:1, lanes]
            dot_row = row_dots[head, 0:1, lanes]
            total = jnp.zeros((HEAD_SIZE, TILE), jnp.float32)
            for low in range(tile + 1):
                part = pl.ds(low * TILE, TILE)
                scores = jnp.dot(key_rows[part], query, preferred_element_type=jnp.float32)
                probs = jnp.exp(scores + bias[low] - lse_row)
                grad_probs = jnp.dot(value_rows[part], grad, preferred_element_type=jnp.float32)
                grad_scores = (probs * (grad_probs - dot_row)).astype(jnp.bfloat16)
                value_grad[part] += jnp.dot(
                    probs.astype(jnp.bfloat16), grad_row, preferred_element_type=jnp.float32
                )
                key_grad[part] += jnp.dot(
                    grad_scores, query_row, preferred_element_type=jnp.float32
                )
                total += jnp.dot(keys[:, part], grad_scores, preferred_element_type=jnp.float32)
            query_grad[rows, lanes] = total * 0.125
            return 0

        lax.fori_loop(0, group, one_head, 0)
        yield
    cos, sin = cosine[...], sine[...]
    for head in range(group):
        first = head * HEAD_SIZE
        out[pl.ds(first, HEAD_SIZE)] = rotate_rows(
            query_grad[pl.ds(first, half)], query_grad[pl.ds(first + half, half)], cos, -sin
        ).astype(jnp.bfloat16)
    turned = key_grad[...].T
    out[pl.ds(group * HEAD_SIZE, HEAD_SIZE)] = rotate_rows(
        turned[:half], turned[half:], cos, -sin
    ).astype(jnp.bfloat16)
    out[pl.ds((group + 1) * HEAD_SIZE, HEAD_SIZE)] = value_grad[...].T.astype(jnp.bfloat16)


def shards(
    tokens,
    segment_ids,
    query_weight,
    key_matrix,
    value_matrix,
    output_weight,
    gate_weight,
    up_weight,
    down_weight,
    attention_gain,
    feed_gain,
    cotangent,
):
    rank = lax.axis_index("seq")
    owner = lax.axis_index("fsdp")
    ranks = lax.axis_size("seq")
    owners = lax.axis_size("fsdp")
    rows, width = query_weight.shape
    kv_cols = key_matrix.shape[1] // ranks
    q_cols = width // ranks
    group = q_cols // kv_cols
    ff = gate_weight.shape[1]
    ff_chunk = ff // owners // ranks
    ff_local = owners * ff_chunk
    segment_row = segment_ids[0]
    length = segment_row.shape[0]

    hidden_one, qkv, heads_turned, gate_all, up_in, cosine, sine, starts, gain_one, gain_two = (
        gather_first(
            tokens[0],
            query_weight,
            key_matrix,
            value_matrix,
            gate_weight,
            up_weight,
            attention_gain,
            feed_gain,
            segment_ids,
            rope_freqs(HEAD_SIZE)[:, None],
            0,
        )
    )
    hidden_one = hidden_one.reshape(length, width)

    attended, lse, queries, keys, grad_out, output_all = attend(
        qkv, cosine, sine, starts, cotangent[0], output_weight, group, 1
    )
    output_all = output_all.reshape(-1, width)
    middle, attended_here, hidden_two, up_all, down_all, act, grad_gate, grad_up = add_branch(
        attended, tokens[0], gain_two, output_all, gate_all, up_in, down_weight, grad_out, 2
    )
    hidden_two = hidden_two.reshape(length, width)
    gate_all = gate_all.reshape(width, ff_local)
    up_all = up_all.reshape(width, ff_local)
    down_all = down_all.reshape(ff_local, width)
    act, grad_gate, grad_up = (part.reshape(length, ff_local) for part in (act, grad_gate, grad_up))
    grad_out = grad_out.reshape(length, width)

    grad_middle, grad_gain_two, grad_branch, gate_up_share, qkv_grads, layer_out = go_back(
        middle,
        gain_two,
        cotangent[0],
        qkv,
        queries,
        keys,
        attended,
        lse,
        cosine,
        sine,
        starts,
        hidden_two,
        grad_gate,
        grad_up,
        gate_all,
        up_all,
        output_all,
        act,
        down_all,
        3,
    )
    grad_inputs, *gathered, gains = finish(
        tokens[0],
        gain_one,
        grad_middle,
        qkv_grads,
        heads_turned,
        attended_here,
        grad_branch,
        grad_gain_two,
        hidden_one,
        act,
        grad_out,
        gate_up_share,
        4,
    )
    gate_grad, up_grad, down_total, query_grad, key_grad, value_grad, heads_total, *activations = (
        place_grads(*gathered, layer_out, grad_inputs)
    )
    layer_out, grad_inputs = activations
    return (
        layer_out[None],
        grad_inputs[None],
        query_grad,
        key_grad,
        value_grad,
        heads_total,
        gate_grad,
        up_grad,
        down_total,
        gains[0],
        gains[1],
    )


def solution(mesh):
    placed = (
        P("fsdp", "seq", None),
        P("fsdp", None),
        P("fsdp", None),
        P("fsdp", None),
        P("fsdp", None),
        P("fsdp", None),
        P("fsdp", None),
        P("fsdp", None),
        P("fsdp", None),
        P("fsdp"),
        P("fsdp"),
        P("fsdp", "seq", None),
    )
    return jax.shard_map(
        shards,
        mesh=mesh,
        in_specs=placed,
        out_specs=(
            P("fsdp", "seq", None),
            P("fsdp", "seq", None),
            P("fsdp", None),
            P("fsdp", None),
            P("fsdp", None),
            P("fsdp", None),
            P("fsdp", None),
            P("fsdp", None),
            P("fsdp", None),
            P("fsdp"),
            P("fsdp"),
        ),
        check_vma=False,
    )
```

```python
import math

import jax
import jax.numpy as jnp
from jax import lax
from jax.experimental import pallas as pl
from jax.experimental.pallas import tpu as pltpu
from jax.sharding import PartitionSpec as P

HEAD_SIZE = 64
EPS = 1e-05
ROPE_BASE = 500000.0
NEG = -1e30


def rope_freqs(head_dim):
    half_dim = head_dim // 2
    table = []
    for index in range(half_dim):
        inverse = 1.0 / ROPE_BASE ** (index * 2.0 / head_dim)
        wavelen = 2.0 * math.pi / inverse
        blend = (8192.0 / wavelen - 1.0) / 3.0
        mixed = (1.0 - blend) * inverse / 32.0 + blend * inverse
        entry = inverse if wavelen < 2048.0 else inverse / 32.0 if wavelen > 8192.0 else mixed
        table.append(entry)
    return jnp.asarray(table, dtype=jnp.float32)


MESH = pl.DeviceIdType.MESH
CHUNKS = 4
TILE = 256


class Ring:
    def __init__(self, place, count, index_of, device_of):
        side = count // 2
        self.place = place
        row, col = lax.div(place, side), lax.rem(place, side)

        def at(which, step):
            return index_of(which * side + lax.rem(col + step, side))

        self.near = [at(row, step) for step in range(side)]
        self.far = [at(1 - row, step) for step in range(side)]
        self.right = device_of(self.near[1])
        self.left = device_of(self.near[3])
        self.partner = device_of(self.far[0])
        self.peers = [self.right, self.left, self.partner]
        self.remote = [device_of(index) for index in (self.near[2], *self.far[1:])]
        self.device_of = device_of


def seq_ring():
    rank, owner = lax.axis_index("seq"), lax.axis_index("fsdp")
    return Ring(rank, lax.axis_size("seq"), lambda place: place, lambda index: (index, owner))


def fsdp_ring():
    rank, owner = lax.axis_index("seq"), lax.axis_index("fsdp")
    core = lax.rem(owner, 2)
    ring = Ring(
        lax.div(owner, 2),
        lax.axis_size("fsdp") // 2,
        lambda place: 2 * place + core,
        lambda index: (rank, index),
    )
    return ring, core, (rank, owner + 1 - 2 * core)


def greet(peers):
    barrier = pltpu.get_barrier_semaphore()
    for peer in peers:
        pl.semaphore_signal(barrier, inc=1, device_id=peer, device_id_type=MESH)
    pl.semaphore_wait(barrier, len(peers))


def in_step(*walks):
    left = list(walks)
    while left:
        left = [walk for walk in left if next(walk, walk) is not walk]
        yield


def beside(main, *sides):
    sides = [(walk, list(places)) for walk, places in sides]
    step = 0
    for _ in main:
        for walk, places in sides:
            while places and places[0] <= step:
                places.pop(0)
                next(walk, None)
        step += 1
    for _ in in_step(*(walk for walk, _ in sides)):
        pass


class Copies:
    def __init__(self, send, recv):
        self.send, self.recv = send, recv
        self.made = []

    def start(self, source, target, peer):
        number = len(self.made)
        copy = pltpu.make_async_remote_copy(
            src_ref=source,
            dst_ref=target,
            send_sem=self.send.at[number],
            recv_sem=self.recv.at[number],
            device_id=peer,
            device_id_type=MESH,
        )
        copy.start()
        self.made.append(copy)
        return copy

    def settle(self, copies):
        for copy in copies:
            copy.wait_send()
        gone = {id(copy) for copy in copies}
        self.made = [None if id(copy) in gone else copy for copy in self.made]

    def finish(self):
        for copy in self.made:
            if copy is not None:
                copy.wait_send()


def by_rows(rows, chunks):
    size = rows // chunks
    return lambda ref, index: ref.at[pl.ds(index * size, size)]


def by_columns(columns, chunks):
    size = columns // chunks
    return lambda ref, index: ref.at[:, pl.ds(index * size, size)]


def chunk_rows(rows, index):
    size = rows // CHUNKS
    return pl.ds(index * size, size)


def exchange_all(ring, copies, piece, target):
    made = []
    for index in (*ring.far[1:], ring.near[2], ring.far[0], ring.near[1], ring.near[3]):
        made.append(copies.start(piece(index), target, ring.device_of(index)))
    return made


def gather_walk(ring, copies, own, out, cut, chunks, deep=False, mate=None):
    me, right, opposite, left = ring.near
    partner, far_right, _, far_left = ring.far
    half = chunks // 2
    passed = []

    def share(place, index):
        if mate is not None:
            block = cut(out.at[place], index)
            passed.append(copies.start(block, block, mate))

    to_right, to_left, to_far, on = {}, {}, {}, {}
    for step in range(chunks):
        back = chunks - 1 - step
        if not deep:
            to_far[step] = copies.start(cut(own, step), cut(out.at[me], step), ring.partner)
        to_right[step] = copies.start(cut(own, step), cut(out.at[me], step), ring.right)
        to_left[back] = copies.start(cut(own, back), cut(out.at[me], back), ring.left)
        if mate is not None:
            passed.append(copies.start(cut(own, step), cut(out.at[me], step), mate))
    yield
    if deep:
        for step in range(chunks):
            to_far[step] = copies.start(cut(own, step), cut(out.at[me], step), ring.partner)
        yield
    for step in range(half):
        back = chunks - 1 - step
        to_right[step].wait_recv()
        block = cut(out.at[left], step)
        on[step] = copies.start(block, block, ring.right)
        share(left, step)
        to_left[back].wait_recv()
        block = cut(out.at[right], back)
        on[back] = copies.start(block, block, ring.left)
        share(right, back)
        yield
    far_on, rest = {}, []
    for step in range(chunks):
        to_far[step].wait_recv()
        block = cut(out.at[partner], step)
        far_on[0, step] = copies.start(block, block, ring.right)
        far_on[1, step] = copies.start(block, block, ring.left)
        share(partner, step)
        yield
    if deep:
        for step in range(half):
            back = chunks - 1 - step
            far_on[0, step].wait_recv()
            block = cut(out.at[far_left], step)
            rest.append((step, copies.start(block, block, ring.right)))
            share(far_left, step)
            far_on[1, back].wait_recv()
            block = cut(out.at[far_right], back)
            rest.append((back, copies.start(block, block, ring.left)))
            share(far_right, back)
            yield
    def finals():
        for step in range(half):
            back = chunks - 1 - step
            to_right[back].wait_recv()
            share(left, back)
            to_left[step].wait_recv()
            share(right, step)
            if deep:
                far_on[0, back].wait_recv()
                share(far_left, back)
                far_on[1, step].wait_recv()
                share(far_right, step)
            yield

    if not deep:
        yield from finals()
    for step in range(half):
        for index in (step, chunks - 1 - step):
            on[index].wait_recv()
            if not deep:
                block = cut(out.at[opposite], index)
                rest.append((index, copies.start(block, block, ring.partner)))
            share(opposite, index)
        yield
    if deep:
        yield from finals()
    else:
        for copy in far_on.values():
            copy.wait_recv()
        yield
    for index, copy in rest:
        copy.wait_recv()
        share(ring.far[2], index)
    yield
    for copy in passed:
        copy.wait_recv()


def gather_copies(chunks, mate=False):
    return 7 * chunks + (8 * chunks if mate else 0)


def reduce_walk(ring, copies, part_of, bufs, cut, chunks, done, ready=None):
    me, right, opposite, left = ring.near
    partner, far_right, far_opposite, far_left = ring.far
    from_left, from_right, from_far, mid, end_left, end_right, end_far = bufs
    half = chunks // 2

    def wide(ref, index):
        return cut(ref, index)[...].astype(jnp.float32)

    def keep(ref, index, value):
        cut(ref, index)[...] = value.astype(jnp.bfloat16)

    sent = []

    def send(block, index, target, device):
        sent.append(copies.start(cut(block, index), cut(target, index), device))
        return sent[-1]

    order = [x for step in range(half) for x in (step, chunks - 1 - step)]
    one_right, one_left, one_far, last_right, last_left, last_far = ({} for _ in range(6))
    if ready is None:
        for index in order:
            one_far[index] = send(part_of.at[far_opposite], index, from_far, ring.partner)
            one_right[index] = send(part_of.at[far_right], index, from_left, ring.right)
            one_left[index] = send(part_of.at[far_left], index, from_right, ring.left)
    else:
        ready(far_right, far_left)
        for index in order:
            one_right[index] = send(part_of.at[far_right], index, from_left, ring.right)
            one_left[index] = send(part_of.at[far_left], index, from_right, ring.left)
        yield
        ready(far_opposite, right)
        for index in order:
            one_far[index] = send(part_of.at[far_opposite], index, from_far, ring.partner)
    for index in range(half):
        last_right[index] = send(part_of.at[right], index, end_left, ring.right)
    if ready is not None:
        yield
        ready(left, opposite)
    for index in range(half):
        back = chunks - 1 - index
        last_left[back] = send(part_of.at[left], back, end_right, ring.left)
    if ready is not None:
        yield
        ready(partner, me)
    yield
    two = {}
    for index in order:
        one_far[index].wait_recv()
        keep(from_far, index, wide(from_far, index) + wide(part_of.at[opposite], index))
        two[index] = send(from_far, index, mid, ring.left if index < half else ring.right)
        yield
    for index in order:
        one_right[index].wait_recv()
        one_left[index].wait_recv()
        total = wide(from_left, index) + wide(from_right, index)
        keep(from_left, index, total + wide(part_of.at[partner], index))
        last_far[index] = send(from_left, index, end_far, ring.partner)
        yield
    for index in order:
        two[index].wait_recv()
        if index < half:
            keep(mid, index, wide(mid, index) + wide(part_of.at[left], index))
            last_left[index] = send(mid, index, end_right, ring.left)
        else:
            keep(mid, index, wide(mid, index) + wide(part_of.at[right], index))
            last_right[index] = send(mid, index, end_left, ring.right)
        yield
    for index in order:
        last_far[index].wait_recv()
        last_left[index].wait_recv()
        last_right[index].wait_recv()
        total = wide(part_of.at[me], index) + wide(end_left, index)
        done(index, total + wide(end_right, index) + wide(end_far, index))
        yield
    copies.settle(sent)


def reduce_copies(chunks):
    return 3 * chunks + 2 * chunks + chunks + chunks


def owners_walk(ring, mate, copies, produce, own, other, bufs, rows, done):
    mids, from_lefts, from_rights, from_far = bufs[:2], bufs[2:4], bufs[4:6], bufs[6]
    half = rows // 2
    low, high = pl.ds(0, half), pl.ds(half, half)
    near, far = ([lax.div(index, 2) for index in row] for row in (ring.near, ring.far))
    order = [far[2], far[1], far[3], near[2], near[1], near[3], far[0], near[0]]
    awaited = []

    def wide(ref):
        return ref.astype(jnp.float32)

    def add(*numbers):
        for number in numbers:
            for wait in awaited[number]:
                wait()
            if other is not None:
                place = order[number]
                own[place] = (wide(own[place]) + wide(other[place])).astype(jnp.bfloat16)

    def make(number):
        awaited.append(produce(order[number]))

    on, ends = ([], []), ([], [])

    def half_way(which):
        block = own.at[(far, near)[which][2]]
        on[which].append(copies.start(block.at[low], mids[which].at[low], ring.left))
        on[which].append(copies.start(block.at[high], mids[which].at[high], ring.right))

    def sides(which):
        row = (far, near)[which]
        ends[which].append(
            copies.start(own.at[row[1], low], from_lefts[which].at[low], ring.right)
        )
        ends[which].append(
            copies.start(own.at[row[3], high], from_rights[which].at[high], ring.left)
        )

    def other_sides(which):
        row, mid = (far, near)[which], mids[which]
        on[which][0].wait_recv()
        mid[low] = (wide(mid[low]) + wide(own[row[3], low])).astype(jnp.bfloat16)
        ends[which].append(copies.start(mid.at[low], from_rights[which].at[low], ring.left))
        on[which][1].wait_recv()
        mid[high] = (wide(mid[high]) + wide(own[row[1], high])).astype(jnp.bfloat16)
        ends[which].append(copies.start(mid.at[high], from_lefts[which].at[high], ring.right))

    make(0)
    yield
    make(1)
    yield
    add(0)
    half_way(0)
    yield
    make(2)
    yield
    add(1, 2)
    sides(0)
    yield
    make(3)
    yield
    make(4)
    yield
    other_sides(0)
    yield
    add(3)
    half_way(1)
    yield
    make(5)
    yield
    add(4, 5)
    sides(1)
    yield
    make(6)
    yield
    make(7)
    yield
    add(6, 7)
    yield
    last = []
    for copy in ends[0]:
        copy.wait_recv()
    for rows_of in (low, high):
        total = (
            wide(from_lefts[0][rows_of])
            + wide(from_rights[0][rows_of])
            + wide(own[far[0], rows_of])
        )
        from_lefts[0][rows_of] = total.astype(jnp.bfloat16)
        last.append(copies.start(from_lefts[0].at[rows_of], from_far.at[rows_of], ring.partner))
    yield
    other_sides(1)
    yield
    for copy in ends[1]:
        copy.wait_recv()
    yield
    for rows_of, copy in zip((low, high), last):
        copy.wait_recv()
        done(
            rows_of,
            wide(from_lefts[1][rows_of])
            + wide(from_rights[1][rows_of])
            + wide(own[near[0], rows_of])
            + wide(from_far[rows_of]),
        )
        yield


OWNERS_COPIES = 4 + 4 + 4 + 2


def owners_scratch(places, rows, width):
    return [pltpu.VMEM((places, rows, width), jnp.bfloat16) for _ in range(2)] + [
        pltpu.VMEM((rows, width), jnp.bfloat16) for _ in range(7)
    ]


def reduce_scratch(rows, width):
    return [pltpu.VMEM((rows, width), jnp.bfloat16) for _ in range(7)]


def semaphores(count):
    return [pltpu.SemaphoreType.DMA((count,)), pltpu.SemaphoreType.DMA((count,))]


def params(number, limit):
    return pltpu.CompilerParams(
        collective_id=number, has_side_effects=True, vmem_limit_bytes=limit * 2**20
    )


VMEM = pl.BlockSpec(memory_space=pltpu.VMEM)
ANYWHERE = pl.BlockSpec(memory_space=pl.ANY)


SMALL_BESIDE = (0, 2, 2, 3, 6, 6, 6, 6, 8, 8, 9, 9, 10, 10, 11)
LARGE_BESIDE = (0, 0, 1, 2, 3, 4, 5, 6, 7, 8, 9, 9, 10, 10, 11)


def weight_walk(ring, copies, own, out, mate):
    return gather_walk(ring, copies, own, out, by_rows(own.shape[0], CHUNKS), CHUNKS, True, mate)


def chosen_half(first, second, odd):
    low, high = merge_lanes(first.astype(jnp.float32), second.astype(jnp.float32))
    return jnp.where(odd == 0, low, high).astype(jnp.bfloat16)


class Pick:
    def __init__(self, sems, wide, narrow, rank):
        self.sems, self.wide, self.narrow = sems, wide, narrow
        self.pair, self.odd = lax.div(rank, 2), lax.rem(rank, 2)
        self.rank = rank
        self.count = 0

    def fetch(self, source, target):
        copy = pltpu.make_async_copy(source, target, self.sems.at[self.count])
        copy.start()
        self.count += 1
        return copy

    def lanes(self, first):
        return pl.ds(pl.multiple_of(first + self.pair * LANES, LANES), LANES)

    def start_units(self, which, source):
        owners = self.wide.shape[1]
        stride = source.shape[1] // owners
        return [
            self.fetch(source.at[:, self.lanes(owner * stride)], self.wide.at[which, owner])
            for owner in range(owners)
        ]

    def finish_units(self, which, made, out):
        for copy in made:
            copy.wait()
        for index in range(self.wide.shape[1] // 2):
            out[:, pl.ds(index * LANES, LANES)] = chosen_half(
                self.wide[which, 2 * index], self.wide[which, 2 * index + 1], self.odd
            )

    def start_heads(self, query, key, value, out):
        rows, cols = query.shape[0], out.shape[1] - LANES
        first = pl.multiple_of(self.rank * cols, LANES)
        return [
            self.fetch(query.at[:, pl.ds(first, cols)], out.at[pl.ds(0, rows), pl.ds(0, cols)]),
            self.fetch(key.at[:, self.lanes(0)], self.narrow.at[0]),
            self.fetch(value.at[:, self.lanes(0)], self.narrow.at[1]),
        ]

    def finish_heads(self, made, gain_one, gain_two, out):
        rows = self.narrow.shape[1]
        line = lax.broadcasted_iota(jnp.int32, (16, rows), 0)
        first, second = (gain[...].astype(jnp.float32) for gain in (gain_one, gain_two))
        gains = jnp.where(line == 0, first, jnp.where(line == 1, second, 0.0))
        out[pl.ds(rows, 32)] = jnp.zeros((32, out.shape[1]), jnp.bfloat16)
        out[pl.ds(rows, 16), pl.ds(0, rows)] = gains.astype(jnp.bfloat16)
        for copy in made:
            copy.wait()
        out[pl.ds(0, rows), pl.ds(out.shape[1] - LANES, LANES)] = chosen_half(
            self.narrow[0], self.narrow[1], self.odd
        )


def first_positions(segments):
    index = lax.broadcasted_iota(jnp.int32, segments.shape, 1)
    begins = (index == 0) | (segments != pltpu.roll(segments, 1, 1))
    starts = jnp.where(begins, index, 0)
    shift = 1
    while shift < segments.shape[1]:
        starts = jnp.maximum(starts, jnp.where(index >= shift, pltpu.roll(starts, shift, 1), 0))
        shift *= 2
    return starts, index


def first_kernel(
    tokens,
    query,
    key,
    value,
    gate,
    up,
    gain_one,
    gain_two,
    segments,
    freqs,
    hidden,
    qkv,
    heads_turned,
    gate_all,
    up_own,
    cosine,
    sine,
    starts,
    gain_one_all,
    gain_two_all,
    tokens_here,
    hidden_here,
    heads_own,
    heads_all,
    gate_own,
    wide,
    narrow,
    picks,
    stores,
    local,
    send,
    recv,
):
    ring = seq_ring()
    weights_ring, _, mate = fsdp_ring()
    greet(ring.peers + weights_ring.peers + [mate])
    copies = Copies(send, recv)
    me, here = ring.near[0], weights_ring.near[0]
    rows = tokens.shape[0]
    kept = [pltpu.make_async_copy(tokens, tokens_here.at[me], local.at[0])]
    kept[0].start()
    pick = Pick(picks, wide, narrow, lax.axis_index("seq"))
    heads_made = pick.start_heads(query, key, value, heads_own)
    gate_made = pick.start_units(0, gate)
    up_made = pick.start_units(1, up)

    def heads_walk():
        pick.finish_heads(heads_made, gain_one, gain_two, heads_own)
        copy = pltpu.make_async_copy(heads_own, heads_all.at[here], local.at[1])
        copy.start()
        kept.append(copy)
        yield from gather_walk(
            weights_ring,
            copies,
            heads_own,
            heads_all,
            by_rows(heads_own.shape[0], 2),
            2,
            True,
            mate,
        )

    def gate_walk():
        pick.finish_units(0, gate_made, gate_own)
        copy = pltpu.make_async_copy(gate_own, gate_all.at[here], local.at[2])
        copy.start()
        kept.append(copy)
        yield from weight_walk(weights_ring, copies, gate_own, gate_all, mate)

    def project(index):
        values = tokens_here[index].astype(jnp.float32)
        factor = lax.rsqrt(mean_square(values) + EPS)
        hidden_here[index] = (values * factor * gain_one_all[...]).astype(jnp.bfloat16)
        copy = pltpu.make_async_copy(hidden_here.at[index], hidden.at[index], stores.at[len(stored)])
        copy.start()
        stored.append(copy)
        lanes = pl.ds(pl.multiple_of(index * rows, rows), rows)
        qkv[:, lanes] = lax.dot_general(
            heads_turned[...],
            hidden_here[index],
            (((1,), (1,)), ((), ())),
            preferred_element_type=jnp.float32,
        ).astype(jnp.bfloat16)

    stored = []

    def compute():
        pick.finish_units(1, up_made, up_own)
        first, index = first_positions(segments[...])
        starts[...] = first
        phase = (index - first).astype(jnp.float32) * freqs[...]
        cosine[...] = jnp.cos(phase)
        sine[...] = jnp.sin(phase)
        yield
        for copy in kept:
            copy.wait()
        for owner in range(heads_all.shape[0]):
            cols = pl.ds(owner * rows, rows)
            heads_turned[:, cols] = heads_all[owner, :rows].T
            gains = heads_all[owner, pl.ds(rows, 16), pl.ds(0, rows)].astype(jnp.float32)
            gain_one_all[:, cols] = gains[0:1]
            gain_two_all[:, cols] = gains[1:2]
        project(me)
        yield
        project(ring.far[0])
        yield
        for place in (ring.near[1], ring.near[3], ring.near[2]):
            project(place)
        yield
        project(ring.far[1])
        project(ring.far[3])
        yield
        project(ring.far[2])

    beside(
        gather_walk(ring, copies, tokens, tokens_here, by_rows(rows, CHUNKS), CHUNKS),
        (heads_walk(), (0, 0, 1, 2, 2, 4, 6, 6, 6, 7)),
        (gate_walk(), SMALL_BESIDE),
        (compute(), (0, 7, 8, 10, 11, 12)),
    )
    copies.finish()
    for copy in stored:
        copy.wait()


LANES = 128


def gather_first(tokens, query, key, value, gate, up, gain_one, gain_two, segments, freqs, number):
    rows, width = tokens.shape
    ranks, owners = lax.axis_size("seq"), lax.axis_size("fsdp")
    length = segments.shape[1]
    cols = width // ranks + LANES
    units = owners // 2 * LANES
    assert gate.shape[1] // owners // ranks == HEAD_SIZE == LANES // 2
    count = gather_copies(CHUNKS) + gather_copies(2, True) + gather_copies(CHUNKS, True)
    low, real = jnp.bfloat16, jnp.float32
    return pl.pallas_call(
        first_kernel,
        out_shape=[
            jax.ShapeDtypeStruct((ranks, rows, width), low),
            jax.ShapeDtypeStruct((cols, length), low),
            jax.ShapeDtypeStruct((cols, width), low),
            jax.ShapeDtypeStruct((owners, rows, units), low),
            jax.ShapeDtypeStruct((rows, units), low),
            jax.ShapeDtypeStruct((freqs.shape[0], length), real),
            jax.ShapeDtypeStruct((freqs.shape[0], length), real),
            jax.ShapeDtypeStruct((1, length), jnp.int32),
            jax.ShapeDtypeStruct((1, width), real),
            jax.ShapeDtypeStruct((1, width), real),
        ],
        in_specs=[ANYWHERE] * 6 + [VMEM] * 4,
        out_specs=[ANYWHERE, VMEM, VMEM, ANYWHERE] + [VMEM] * 6,
        scratch_shapes=[
            pltpu.VMEM((ranks, rows, width), low),
            pltpu.VMEM((ranks, rows, width), low),
            pltpu.VMEM((rows + 32, cols), low),
            pltpu.VMEM((owners, rows + 32, cols), low),
            pltpu.VMEM((rows, units), low),
            pltpu.VMEM((2, owners, rows, LANES), low),
            pltpu.VMEM((2, rows, LANES), low),
            pltpu.SemaphoreType.DMA((2 * owners + 3,)),
            pltpu.SemaphoreType.DMA((ranks,)),
            pltpu.SemaphoreType.DMA((3,)),
        ]
        + semaphores(count),
        compiler_params=params(number, 62),
        name="gather_first",
    )(tokens, query, key, value, gate, up, gain_one[None], gain_two[None], segments, freqs)


def mean_square(values):
    return jnp.mean(values * values, axis=-1, keepdims=True)


PRODUCT = 512


def product(left, right, store, size=PRODUCT):
    def columns(index, _):
        cols = pl.ds(pl.multiple_of(index * size, size), size)
        store(cols, jnp.dot(left, right[:, cols], preferred_element_type=jnp.float32))
        return 0

    lax.fori_loop(0, right.shape[1] // size, columns, 0)


def two_blocks(ref, rows, first, second):
    return jnp.concatenate(
        [ref[pl.ds(pl.multiple_of(index * rows, rows), rows)] for index in (first, second)], axis=0
    )


def split_store(for_mate, own, place, core):
    def store(cols, value):
        rows = value.shape[0] // 2
        first = core == 0
        theirs = jnp.where(first, value[rows:], value[:rows])
        for_mate[place, :, cols] = theirs.astype(jnp.bfloat16)
        ours = jnp.where(first, value[:rows], value[rows:])
        own[place, :, cols] = ours.astype(jnp.bfloat16)

    return store


def branch_kernel(
    attended,
    tokens,
    gain,
    weight,
    gate,
    up,
    down,
    grad_out,
    middle,
    attended_here,
    hidden,
    up_all,
    down_all,
    act_out,
    gate_out,
    up_out,
    block,
    got,
    weight_here,
    gate_here,
    up_here,
    down_here,
    grad_out_here,
    hidden_here,
    gated,
    upped,
    grad_act,
    act,
    grad_gate,
    grad_up,
    stores,
    local,
    send,
    recv,
):
    ring = seq_ring()
    weights_ring, _, mate = fsdp_ring()
    rows = tokens.shape[0]
    greet(ring.peers + ring.remote + weights_ring.peers + [mate])
    copies = Copies(send, recv)
    me, here = ring.near[0], weights_ring.near[0]
    down_rows = down_here.shape[1]
    down = down.at[pl.ds(pl.multiple_of(me * down_rows, down_rows), down_rows)]

    def lanes_of(index):
        return attended.at[:, pl.ds(pl.multiple_of(index * rows, rows), rows)]

    arriving = exchange_all(ring, copies, lanes_of, got.at[me])
    load = pltpu.make_async_copy(weight, weight_here, local.at[0])
    load.start()
    mine = pltpu.make_async_copy(lanes_of(me), got.at[me], local.at[1])
    mine.start()
    kept = [
        pltpu.make_async_copy(up, up_here.at[here], local.at[2]),
        pltpu.make_async_copy(down, down_here.at[here], local.at[3]),
        pltpu.make_async_copy(gate, gate_here, local.at[4]),
        pltpu.make_async_copy(grad_out, grad_out_here, local.at[5]),
    ]
    for copy in kept:
        copy.start()
    stored = []

    def store(source, target):
        copy = pltpu.make_async_copy(source, target, stores.at[len(stored)])
        copy.start()
        stored.append(copy)

    def walk():
        yield
        mine.wait()
        load.wait()
        for copy in arriving:
            copy.wait_recv()
        attended_here[...] = got[...].reshape(attended_here.shape)
        turned = attended_here[...].T

        def add(cols, value):
            middle[:, cols] = tokens[:, cols].astype(jnp.float32) + value

        product(turned, weight_here, add)
        values = middle[...]
        factor = lax.rsqrt(mean_square(values) + EPS)
        block[...] = (values * factor * gain[...]).astype(jnp.bfloat16)
        hidden_here[me] = block[...]
        yield from gather_walk(
            ring, copies, block, hidden_here, by_rows(rows, CHUNKS), CHUNKS
        )

    units = gated.shape[2]

    def both(ref, pair):
        return jnp.concatenate([ref[index] for index in pair], axis=0)

    def times(pair, matrix, out):
        left = both(hidden_here, pair)

        def columns(tile, _):
            cols = pl.ds(pl.multiple_of(tile * PRODUCT, PRODUCT), PRODUCT)
            right = matrix[:, :, cols].reshape(-1, PRODUCT)
            value = jnp.dot(left, right, preferred_element_type=jnp.float32)
            out[pair[0], :, cols] = value[:rows]
            out[pair[1], :, cols] = value[rows:]
            return 0

        lax.fori_loop(0, units // PRODUCT, columns, 0)

    def back(pair):
        left = both(grad_out_here, pair)
        share = PRODUCT // down_here.shape[1]

        def columns(tile, _):
            cols = pl.ds(pl.multiple_of(tile * PRODUCT, PRODUCT), PRODUCT)
            right = down_here[pl.ds(tile * share, share)].reshape(PRODUCT, -1)
            value = lax.dot_general(
                left, right, (((1,), (1,)), ((), ())), preferred_element_type=jnp.float32
            )
            grad_act[pair[0], :, cols] = value[:rows]
            grad_act[pair[1], :, cols] = value[rows:]
            return 0

        lax.fori_loop(0, units // PRODUCT, columns, 0)

    def combine(pair):
        for index in pair:
            value, other, grad = gated[index], upped[index], grad_act[index]
            sig = jax.nn.sigmoid(value)
            silu = value * sig
            act[index] = (silu * other).astype(jnp.bfloat16)
            grad_gate[index] = (grad * other * (sig * (1.0 + value * (1.0 - sig)))).astype(
                jnp.bfloat16
            )
            grad_up[index] = (grad * silu).astype(jnp.bfloat16)
            store(act.at[index], act_out.at[index])
            store(grad_gate.at[index], gate_out.at[index])
            store(grad_up.at[index], up_out.at[index])

    near, far = ring.near, ring.far
    pairs = ((near[0], far[0]), (near[1], near[3]), (far[1], far[3]), (near[2], far[2]))

    def compute():
        kept[0].wait()
        kept[1].wait()
        kept[2].wait()
        kept[3].wait()
        store(down_here, down_all)
        back(pairs[0])
        yield
        back(pairs[1])
        yield
        back(pairs[2])
        yield
        back(pairs[3])
        yield
        times(pairs[0], gate_here, gated)
        yield
        times(pairs[1], gate_here, gated)
        yield
        store(up_here, up_all)
        times(pairs[0], up_here, upped)
        combine(pairs[0])
        yield
        times(pairs[1], up_here, upped)
        combine(pairs[1])
        yield
        for pair in pairs[2:]:
            for index in pair:
                store(hidden_here.at[index], hidden.at[index])
            times(pair, gate_here, gated)
            times(pair, up_here, upped)
            combine(pair)
            yield

    def hold():
        for index in (*pairs[0], *pairs[1]):
            store(hidden_here.at[index], hidden.at[index])
        yield

    beside(
        walk(),
        (weight_walk(weights_ring, copies, down, down_here, mate), BESIDE_FIRST),
        (weight_walk(weights_ring, copies, up, up_here, mate), BESIDE_SECOND),
        (hold(), (9,)),
        (compute(), (4, 5, 6, 7, 7, 9, 11, 11, 12, 13)),
    )
    copies.finish()
    for copy in stored:
        copy.wait()


BESIDE_FIRST = (0, 0, 0, 0, 0, 0, 0, 0, 1, 1, 1, 1, 2, 2, 3, 4)
BESIDE_SECOND = (0, 0, 1, 1, 1, 1, 2, 2, 7, 7, 7, 7, 9, 9, 10, 11)


def add_branch(attended, tokens, gain, weight, gate, up, down, grad_out, number):
    rows, width = tokens.shape
    ranks, owners = lax.axis_size("seq"), lax.axis_size("fsdp")
    features, units = attended.shape[0], up.shape[1]
    down_block = (down.shape[0] // ranks, width)
    count = ranks - 1 + gather_copies(CHUNKS) + 2 * gather_copies(CHUNKS, True)
    low, real = jnp.bfloat16, jnp.float32
    return pl.pallas_call(
        branch_kernel,
        out_shape=[
            jax.ShapeDtypeStruct((rows, width), real),
            jax.ShapeDtypeStruct((ranks * features, rows), low),
            jax.ShapeDtypeStruct((ranks, rows, width), low),
            jax.ShapeDtypeStruct((owners, *up.shape), low),
            jax.ShapeDtypeStruct((owners, *down_block), low),
        ]
        + [jax.ShapeDtypeStruct((ranks, rows, units), low)] * 3,
        in_specs=[VMEM] * 3 + [ANYWHERE] * 5,
        out_specs=[VMEM] * 2 + [ANYWHERE] * 6,
        scratch_shapes=[
            pltpu.VMEM((rows, width), low),
            pltpu.VMEM((ranks, features, rows), low),
            pltpu.VMEM(weight.shape, low),
            pltpu.VMEM(gate.shape, low),
            pltpu.VMEM((owners, *up.shape), low),
            pltpu.VMEM((owners, *down_block), low),
            pltpu.VMEM((ranks, rows, width), low),
            pltpu.VMEM((ranks, rows, width), low),
        ]
        + [pltpu.VMEM((ranks, rows, units), real)] * 3
        + [pltpu.VMEM((ranks, rows, units), low)] * 3
        + [pltpu.SemaphoreType.DMA((4 * ranks + 2,)), pltpu.SemaphoreType.DMA((6,))]
        + semaphores(count),
        compiler_params=params(number, 62),
        name="add_branch",
    )(attended, tokens, gain, weight, gate, up, down, grad_out)


def norm_back_rows(grad, gain, values):
    factor = lax.rsqrt(mean_square(values) + EPS)
    normed = values * factor
    weighted = grad * gain
    back = factor * (weighted - normed * jnp.mean(weighted * normed, axis=-1, keepdims=True))
    return back, grad * normed


def back_kernel(*refs):
    middle, gain, cotangent = refs[:3]
    qkv, queries, keys, attended, lse, cosine, sine, starts = refs[3:11]
    hidden, gate_grads, up_grads, gate, up, weight, act, down = refs[11:19]
    grad_middle, grad_gain, block, grads_share, qkv_grads, layer_out = refs[19:25]
    tiles_scratch = refs[25:34]
    part_of, big, left_wide, right_wide, for_mate, given, got, grad_attended = refs[34:42]
    loads, send, recv, own, other = refs[42:47]
    owners_bufs, first_bufs, second_bufs = refs[47:54], refs[54:61], refs[61:68]
    ring = seq_ring()
    weights_ring, core, mate = fsdp_ring()
    rows = middle.shape[0]
    greet(ring.peers + ring.remote + weights_ring.peers + [mate])
    copies = Copies(send, recv)
    grad_gain[...] = jnp.zeros_like(grad_gain)
    units = gate_grads.shape[1]
    low_cols, high_cols = pl.ds(0, units), pl.ds(units, units)
    count = [0]

    def load(source, target):
        copy = pltpu.make_async_copy(source, target, loads.at[count[0]])
        copy.start()
        count[0] += 1
        return copy

    arrived = [
        load(gate_grads, right_wide.at[:, low_cols]),
        load(up_grads, right_wide.at[:, high_cols]),
        load(gate, big.at[:, low_cols]),
        load(up, big.at[:, high_cols]),
    ]
    hidden_load = [load(hidden, left_wide)]

    def ready(*blocks):
        while arrived:
            arrived.pop().wait()
        left = two_blocks(right_wide, rows, *blocks)

        def columns(tile, _):
            cols = pl.ds(pl.multiple_of(tile * PRODUCT, PRODUCT), PRODUCT)
            value = lax.dot_general(
                left, big[cols], (((1,), (1,)), ((), ())), preferred_element_type=jnp.float32
            ).astype(jnp.bfloat16)
            part_of[blocks[0], :, cols] = value[:rows]
            part_of[blocks[1], :, cols] = value[rows:]
            return 0

        lax.fori_loop(0, big.shape[0] // PRODUCT, columns, 0)

    def done(index, total):
        rows_of = chunk_rows(rows, index)
        back, terms = norm_back_rows(total, gain[...], middle[rows_of])
        grad_gain[...] += jnp.sum(terms, axis=0, keepdims=True)
        values = cotangent[rows_of].astype(jnp.float32) + back
        grad_middle[rows_of] = values
        block[rows_of] = values.astype(jnp.bfloat16)

    def owned(rows_of, total):
        grads_share[rows_of] = total.astype(jnp.bfloat16)

    made = []

    def produce(place):
        while hidden_load:
            hidden_load.pop().wait()
        lanes = pl.ds(pl.multiple_of(place * 2 * rows, 2 * rows), 2 * rows)
        turned = left_wide[:, lanes].T
        product(turned, right_wide, split_store(for_mate, own, place, core), 2 * PRODUCT)
        made.append(place)
        return [copies.start(for_mate.at[place], other.at[place], mate).wait_recv]

    act_here = right_wide.at[:, low_cols]
    layer_loads = []

    def layer_ready(*blocks):
        assert len(made) == for_mate.shape[0]
        while layer_loads:
            layer_loads.pop().wait()

        def store(cols, value):
            part_of[blocks[0], :, cols] = value[:rows].astype(jnp.bfloat16)
            part_of[blocks[1], :, cols] = value[rows:].astype(jnp.bfloat16)

        product(two_blocks(act_here, rows, *blocks), left_wide, store)

    def layer_done(index, total):
        rows_of = chunk_rows(rows, index)
        layer_out[rows_of] = (middle[rows_of] + total).astype(jnp.bfloat16)

    me = ring.near[0]
    features = grad_attended.shape[0]

    def walk():
        cut = by_rows(rows, CHUNKS)
        step = 0
        for _ in reduce_walk(ring, copies, part_of, first_bufs, cut, CHUNKS, done, ready):
            if step == 3:
                weight_load = load(weight, big)
            step += 1
            yield
        layer_loads.append(load(act, act_here))
        layer_loads.append(load(down, left_wide))
        weight_load.wait()

        def piece(index):
            part = pl.ds(pl.multiple_of(index * features, features), features)
            given[index] = lax.dot_general(
                big[part],
                block[...],
                (((1,), (1,)), ((), ())),
                preferred_element_type=jnp.float32,
            ).astype(jnp.bfloat16)
            return given.at[index]

        arriving = exchange_all(ring, copies, piece, got.at[me])
        piece(me)
        yield
        layer = reduce_walk(
            ring, copies, part_of, second_bufs, cut, CHUNKS, layer_done, layer_ready
        )
        for _ in range(4):
            next(layer)
            yield
        for copy in arriving:
            copy.wait_recv()
        got[me] = given[me]
        for index in range(got.shape[0]):
            grad_attended[:, pl.ds(index * rows, rows)] = got[index]
        yield
        yield from layer

    tiles = back_tiles(
        qkv,
        queries,
        keys,
        attended,
        lse,
        grad_attended,
        cosine,
        sine,
        starts,
        qkv_grads,
        *tiles_scratch,
    )
    beside(
        walk(),
        (
            owners_walk(
                weights_ring,
                mate,
                copies,
                produce,
                own,
                other,
                owners_bufs,
                grads_share.shape[0],
                owned,
            ),
            BACK_OWNERS,
        ),
        (tiles, BACK_TILES),
    )
    copies.finish()


BACK_OWNERS = (0, 0, 0, 1, 1, 3, 3, 3, 3, 11, 11, 11, 11, 11, 15, 15, 20, 25, 25)
BACK_TILES = (25, 25, 25, 33, 37)


def go_back(
    middle,
    gain,
    cotangent,
    qkv,
    queries,
    keys,
    attended,
    lse,
    cosine,
    sine,
    starts,
    hidden,
    gate_grads,
    up_grads,
    gate,
    up,
    weight,
    act,
    down,
    number,
):
    rows, width = middle.shape
    length = hidden.shape[0]
    ranks, owners = lax.axis_size("seq"), lax.axis_size("fsdp")
    places = owners // 2
    group = queries.shape[0] // HEAD_SIZE
    tiles = length // TILE
    features = weight.shape[0] // ranks
    grad_rows, grad_cols = width // owners, 2 * gate_grads.shape[1]
    count = 2 * reduce_copies(CHUNKS) + ranks - 1 + OWNERS_COPIES + places
    low, real = jnp.bfloat16, jnp.float32
    return pl.pallas_call(
        back_kernel,
        out_shape=[
            jax.ShapeDtypeStruct((rows, width), real),
            jax.ShapeDtypeStruct((1, width), real),
            jax.ShapeDtypeStruct((rows, width), low),
            jax.ShapeDtypeStruct((grad_rows, grad_cols), low),
            jax.ShapeDtypeStruct(qkv.shape, low),
            jax.ShapeDtypeStruct((rows, width), low),
        ],
        in_specs=[VMEM] * 11 + [ANYWHERE] * 8,
        out_specs=[VMEM] * 6,
        scratch_shapes=[
            pltpu.VMEM((length, HEAD_SIZE), low),
            pltpu.VMEM((length, HEAD_SIZE), low),
            pltpu.VMEM((group, length, HEAD_SIZE), low),
            pltpu.VMEM((group, length, HEAD_SIZE), low),
            pltpu.VMEM((group, 8, length), real),
            pltpu.VMEM((length, HEAD_SIZE), real),
            pltpu.VMEM((length, HEAD_SIZE), real),
            pltpu.VMEM((group * HEAD_SIZE, length), real),
            pltpu.VMEM((tiles, TILE, TILE), real),
            pltpu.VMEM((ranks, rows, width), low),
            pltpu.VMEM(weight.shape, low),
            pltpu.VMEM((length, width), low),
            pltpu.VMEM((length, width), low),
            pltpu.VMEM((places, grad_rows, grad_cols), low),
            pltpu.VMEM((ranks, features, rows), low),
            pltpu.VMEM((ranks, features, rows), low),
            pltpu.VMEM((features, length), low),
            pltpu.SemaphoreType.DMA((8,)),
        ]
        + semaphores(count)
        + owners_scratch(places, grad_rows, grad_cols)
        + reduce_scratch(rows, width)
        + reduce_scratch(rows, width),
        compiler_params=params(number, 62),
        name="go_back",
    )(
        middle,
        gain,
        cotangent,
        qkv,
        queries,
        keys,
        attended,
        lse,
        cosine,
        sine,
        starts,
        hidden,
        gate_grads,
        up_grads,
        gate,
        up,
        weight,
        act,
        down,
    )


def last_kernel(
    tokens,
    gain,
    grad_middle,
    qkv_grads,
    heads_turned,
    attended,
    branch,
    grad_gain_two,
    hidden,
    act,
    grad_out,
    gate_up,
    out,
    gate_up_all,
    pack_all,
    heads_all,
    gains,
    part_of,
    hidden_here,
    act_here,
    grad_out_here,
    pack,
    heads,
    heads_got,
    heads_mine,
    attended_pair,
    branch_pair,
    grad_gain,
    given,
    from_mate,
    summed,
    from_places,
    for_group,
    from_group,
    loads,
    local,
    send,
    recv,
    *scratch,
):
    ring = seq_ring()
    me = ring.near[0]
    weights_ring, core, mate = fsdp_ring()
    rows = tokens.shape[0]
    greet(ring.peers + ring.remote + weights_ring.peers + weights_ring.remote + [mate])
    copies = Copies(send, recv)
    reduce_bufs, scratch = scratch[:7], scratch[7:]
    qkv_scratch, down_scratch, heads_scratch = scratch[:10], scratch[10:20], scratch[20:]
    grad_gain[...] = jnp.zeros_like(grad_gain)
    swapped = [
        copies.start(attended, attended_pair.at[core], mate),
        copies.start(branch, branch_pair.at[core], mate),
    ]
    attended_pair[core] = attended[...]
    branch_pair[core] = branch[...]
    hidden_load = [pltpu.make_async_copy(hidden, hidden_here, loads.at[0])]
    down_loads = [
        pltpu.make_async_copy(act, act_here, loads.at[1]),
        pltpu.make_async_copy(grad_out, grad_out_here, loads.at[2]),
    ]
    for copy in hidden_load + down_loads:
        copy.start()
    kept = []

    def keep(block, all_of):
        copy = pltpu.make_async_copy(block, all_of.at[me], local.at[len(kept)])
        copy.start()
        kept.append(copy)

    keep(gate_up, gate_up_all)

    def ready(*blocks):
        left = jnp.concatenate(
            [
                qkv_grads[:, pl.ds(pl.multiple_of(index * rows, rows), rows)]
                for index in blocks
            ],
            axis=1,
        ).T

        def store(cols, value):
            part_of[blocks[0], :, cols] = value[:rows].astype(jnp.bfloat16)
            part_of[blocks[1], :, cols] = value[rows:].astype(jnp.bfloat16)

        product(left, heads_turned, store)

    def done(index, total):
        rows_of = chunk_rows(rows, index)
        back, terms = norm_back_rows(total, gain[...], tokens[rows_of].astype(jnp.float32))
        grad_gain[...] += jnp.sum(terms, axis=0, keepdims=True)
        out[rows_of] = (grad_middle[rows_of] + back).astype(jnp.bfloat16)

    def sums(parts, produce, block_rows, owned):
        for_mate, own, other = parts[:3]
        return owners_walk(
            weights_ring, mate, copies, produce, own, other, parts[3:], block_rows, owned
        )

    qkv_cols = qkv_grads.shape[0]
    first = pack.shape[1] - qkv_cols

    def qkv_produce(place):
        while hidden_load:
            hidden_load.pop().wait()
        for_mate, own, other = qkv_scratch[:3]
        lanes = pl.ds(pl.multiple_of(place * 2 * rows, 2 * rows), 2 * rows)
        value = lax.dot_general(
            hidden_here[:, lanes].T,
            qkv_grads[...],
            (((1,), (1,)), ((), ())),
            preferred_element_type=jnp.float32,
        )
        split_store(for_mate, own, place, core)(slice(None), value)
        return [copies.start(for_mate.at[place], other.at[place], mate).wait_recv]

    def qkv_owned(rows_of, total):
        pack[rows_of, pl.ds(first, qkv_cols)] = total.astype(jnp.bfloat16)

    down_rows = rows // 2

    def down_produce(place):
        while down_loads:
            down_loads.pop().wait()
        for_mate, own, other = down_scratch[:3]
        lanes = pl.ds(pl.multiple_of(place * rows, rows), rows)
        turned = act_here[:, lanes].T
        product(turned, grad_out_here, split_store(for_mate, own, place, core), 2 * PRODUCT)
        return [copies.start(for_mate.at[place], other.at[place], mate).wait_recv]

    def down_owned(rows_of, total):
        pack[rows_of, pl.ds(0, first)] = total[:, :first].astype(jnp.bfloat16)
        under = pl.ds(rows_of.start + down_rows, rows_of.size)
        pack[under, pl.ds(0, first)] = total[:, first:].astype(jnp.bfloat16)

    piece_rows = heads_mine.shape[0]

    def heads_owned(rows_of, total):
        heads[rows_of] = total.astype(jnp.bfloat16)

    def heads_walk():
        own = heads_scratch[0]

        def produce(place):
            while swapped:
                swapped.pop().wait_recv()
            part = pl.ds(pl.multiple_of((2 * place + core) * rows, rows), rows)
            left = jnp.concatenate([attended_pair[0, part], attended_pair[1, part]], axis=1)

            def store(cols, value):
                own[place, :, cols] = value.astype(jnp.bfloat16)

            def columns(index, _):
                cols = pl.ds(pl.multiple_of(index * PRODUCT, PRODUCT), PRODUCT)
                right = branch_pair[:, :, cols].reshape(-1, PRODUCT)
                store(cols, jnp.dot(left, right, preferred_element_type=jnp.float32))
                return 0

            lax.fori_loop(0, branch_pair.shape[2] // PRODUCT, columns, 0)
            return []

        yield from owners_walk(
            weights_ring, mate, copies, produce, own, None, heads_scratch[1:], rows, heads_owned
        )

        def piece(index):
            return heads.at[pl.ds(pl.multiple_of(index * piece_rows, piece_rows), piece_rows)]

        arriving = exchange_all(ring, copies, piece, heads_got.at[me])
        heads_got[me] = piece(me)[...]
        yield
        for copy in arriving:
            copy.wait_recv()
        heads_mine[...] = sum(
            heads_got[index].astype(jnp.float32) for index in range(heads_got.shape[0])
        ).astype(jnp.bfloat16)
        keep(heads_mine, heads_all)
        arriving = exchange_all(ring, copies, lambda index: heads_mine, heads_all.at[me])
        yield
        for copy in arriving:
            copy.wait_recv()

    def sum_gains():
        lanes = given.shape[3]
        for index in range(2 * given.shape[0]):
            cols = pl.ds(index * lanes, lanes)
            place = (index // 2, index % 2)
            given[(*place, slice(0, 1))] = grad_gain[:, cols]
            given[(*place, slice(1, 2))] = grad_gain_two[:, cols]
            given[(*place, slice(2, 8))] = jnp.zeros((6, lanes), jnp.float32)
        copy = copies.start(given.at[:, 1 - core], from_mate, mate)
        yield
        copy.wait_recv()
        summed[...] = given[:, core] + from_mate[...]
        place = weights_ring.place
        arriving = exchange_all(
            weights_ring,
            copies,
            lambda index: summed.at[lax.div(index, 2)],
            from_places.at[place],
        )
        from_places[place] = summed[place]
        yield
        for copy in arriving:
            copy.wait_recv()
        for_group[...] = sum(from_places[index] for index in range(from_places.shape[0]))
        arriving = exchange_all(ring, copies, lambda index: for_group, from_group.at[me])
        from_group[me] = for_group[...]
        yield
        for copy in arriving:
            copy.wait_recv()
        gains[...] = sum(from_group[index] for index in range(from_group.shape[0]))

    def walk():
        yield from reduce_walk(
            ring, copies, part_of, reduce_bufs, by_rows(rows, CHUNKS), CHUNKS, done, ready
        )
        for _ in range(LAST_PAUSE):
            yield
        keep(pack, pack_all)
        yield from gather_walk(ring, copies, pack, pack_all, by_rows(rows, CHUNKS), CHUNKS)

    beside(
        walk(),
        (heads_walk(), LAST_HEADS),
        (
            gather_walk(ring, copies, gate_up, gate_up_all, by_rows(rows, CHUNKS), CHUNKS),
            LAST_GATE_UP,
        ),
        (sums(qkv_scratch, qkv_produce, rows, qkv_owned), LAST_QKV),
        (sums(down_scratch, down_produce, down_rows, down_owned), LAST_DOWN),
        (sum_gains(), LAST_GAINS),
    )
    copies.finish()
    for copy in kept:
        copy.wait()


LAST_PAUSE = 5
LAST_HEADS = (3,) * 14 + (13, 15, 19, 20, 20, 21, 24, 32)
LAST_GATE_UP = (11, 17, 18, 19, 19, 20, 20, 21, 21, 22, 23, 24, 27, 28)
LAST_QKV = (13,) * 9 + (15,) * 5 + (20, 20, 22, 23, 23, 23)
LAST_DOWN = (15,) * 7 + (20,) * 7 + (22, 22, 23, 23, 23, 23)
LAST_GAINS = (19, 22, 25)


def finish(
    tokens,
    gain,
    grad_middle,
    qkv_grads,
    heads_turned,
    attended,
    branch,
    grad_gain_two,
    hidden,
    act,
    grad_out,
    gate_up,
    number,
):
    rows, width = tokens.shape
    ranks, owners = lax.axis_size("seq"), lax.axis_size("fsdp")
    places = owners // 2
    lanes = width // owners
    qkv_cols = qkv_grads.shape[0]
    packed = width // 2 + qkv_cols
    pieces = rows // ranks
    assert act.shape[1] // owners == rows // 2
    count = reduce_copies(CHUNKS) + 2 * gather_copies(CHUNKS) + 3 * OWNERS_COPIES + 2 * places + 2
    count += 2 * (ranks - 1) + 1 + places - 1 + ranks - 1
    low = jnp.bfloat16

    def table(*shape):
        return pltpu.VMEM((*shape, 8, lanes), jnp.float32)

    def sums(block_rows, cols):
        return [pltpu.VMEM((places, block_rows, cols), low)] + owners_scratch(
            places, block_rows, cols
        )

    return pl.pallas_call(
        last_kernel,
        out_shape=[
            jax.ShapeDtypeStruct((rows, width), low),
            jax.ShapeDtypeStruct((ranks, rows, width), low),
            jax.ShapeDtypeStruct((ranks, rows, packed), low),
            jax.ShapeDtypeStruct((ranks, pieces, width), low),
            jax.ShapeDtypeStruct((8, lanes), jnp.float32),
        ],
        in_specs=[VMEM] * 8 + [ANYWHERE] * 4,
        out_specs=[VMEM] + [ANYWHERE] * 3 + [VMEM],
        scratch_shapes=[
            pltpu.VMEM((ranks, rows, width), low),
            pltpu.VMEM(hidden.shape, low),
            pltpu.VMEM(act.shape, low),
            pltpu.VMEM(grad_out.shape, low),
            pltpu.VMEM((rows, packed), low),
            pltpu.VMEM((rows, width), low),
            pltpu.VMEM((ranks, pieces, width), low),
            pltpu.VMEM((pieces, width), low),
            pltpu.VMEM((2, *attended.shape), low),
            pltpu.VMEM((2, *branch.shape), low),
            pltpu.VMEM((1, width), jnp.float32),
            table(places, 2),
            table(places),
            table(places),
            table(places),
            table(),
            table(ranks),
            pltpu.SemaphoreType.DMA((3,)),
            pltpu.SemaphoreType.DMA((3,)),
        ]
        + semaphores(count)
        + reduce_scratch(rows, width)
        + sums(rows, qkv_cols)
        + sums(rows // 2, width)
        + owners_scratch(places, rows, width)[1:],
        compiler_params=params(number, 62),
        name="finish",
    )(
        tokens,
        gain,
        grad_middle,
        qkv_grads,
        heads_turned,
        attended,
        branch,
        grad_gain_two,
        hidden,
        act,
        grad_out,
        gate_up,
    )


def merge_lanes(first, second):
    half = first.shape[1] // 2
    low = lax.broadcasted_iota(jnp.int32, first.shape, 1) < half
    return (
        jnp.where(low, first, pltpu.roll(second, half, 1)),
        jnp.where(low, pltpu.roll(first, half, 1), second),
    )


def place_kernel(
    gate,
    up,
    down,
    query,
    pair,
    heads,
    layer,
    tokens,
    gate_out,
    up_out,
    down_out,
    query_out,
    key_out,
    value_out,
    heads_out,
    layer_out,
    tokens_out,
):
    lanes = gate.shape[2]
    blocks = gate.shape[0] // 2
    for part, out in ((gate, gate_out), (up, up_out)):
        for index in range(blocks):
            low, high = merge_lanes(
                part[2 * index].astype(jnp.float32), part[2 * index + 1].astype(jnp.float32)
            )
            out[:, pl.ds(index * lanes, lanes)] = low
            out[:, pl.ds((blocks + index) * lanes, lanes)] = high
    key, value = merge_lanes(pair[0].astype(jnp.float32), pair[1].astype(jnp.float32))
    key_out[...] = key
    value_out[...] = value
    down_rows, cols = down_out.shape[0], down.shape[2]
    down_out[:, :cols] = down[0, :down_rows].astype(jnp.float32)
    down_out[:, cols:] = down[0, down_rows:].astype(jnp.float32)
    query_out[...] = query[0].astype(jnp.float32)
    heads_out[...] = heads[0].astype(jnp.float32)
    layer_out[...] = layer[...]
    tokens_out[...] = tokens[...]


def place_grads(gate_up, pack, heads, layer, tokens):
    ranks, rows, units = gate_up.shape
    units //= 2
    lanes = LANES
    steps = units // lanes
    width = heads.shape[2]
    down_cols, down_rows = width // 2, rows // 2
    query_cols = width // ranks
    head_rows = heads.shape[1]
    first = (down_cols + query_cols) // lanes
    assert steps == ranks and lanes == 2 * HEAD_SIZE and query_cols == 2 * lanes
    real = jnp.float32
    return pl.pallas_call(
        place_kernel,
        grid=(steps,),
        out_shape=[
            jax.ShapeDtypeStruct((rows, ranks * units), real),
            jax.ShapeDtypeStruct((rows, ranks * units), real),
            jax.ShapeDtypeStruct((ranks * down_rows, width), real),
            jax.ShapeDtypeStruct((rows, ranks * query_cols), real),
            jax.ShapeDtypeStruct((rows, ranks * HEAD_SIZE), real),
            jax.ShapeDtypeStruct((rows, ranks * HEAD_SIZE), real),
            jax.ShapeDtypeStruct((rows, width), real),
            jax.ShapeDtypeStruct((rows, width), jnp.bfloat16),
            jax.ShapeDtypeStruct((rows, width), jnp.bfloat16),
        ],
        in_specs=[
            pl.BlockSpec((ranks, rows, lanes), lambda i: (0, 0, i)),
            pl.BlockSpec((ranks, rows, lanes), lambda i: (0, 0, steps + i)),
            pl.BlockSpec((1, rows, down_cols), lambda i: (i, 0, 0)),
            pl.BlockSpec((1, rows, query_cols), lambda i: (i, 0, down_cols // query_cols)),
            pl.BlockSpec((2, rows, lanes), lambda i: (i // 2, 0, first)),
            pl.BlockSpec((1, head_rows, width), lambda i: (i, 0, 0)),
            pl.BlockSpec((head_rows, width), lambda i: (i, 0)),
            pl.BlockSpec((head_rows, width), lambda i: (i, 0)),
        ],
        out_specs=[
            pl.BlockSpec((rows, ranks * lanes), lambda i: (0, i)),
            pl.BlockSpec((rows, ranks * lanes), lambda i: (0, i)),
            pl.BlockSpec((down_rows, width), lambda i: (i, 0)),
            pl.BlockSpec((rows, query_cols), lambda i: (0, i)),
            pl.BlockSpec((rows, lanes), lambda i: (0, i // 2)),
            pl.BlockSpec((rows, lanes), lambda i: (0, i // 2)),
            pl.BlockSpec((head_rows, width), lambda i: (i, 0)),
            pl.BlockSpec((head_rows, width), lambda i: (i, 0)),
            pl.BlockSpec((head_rows, width), lambda i: (i, 0)),
        ],
        compiler_params=pltpu.CompilerParams(vmem_limit_bytes=62 * 2**20),
        name="place_grads",
    )(gate_up, gate_up, pack, pack, pack, heads, layer, tokens)


def rotate_rows(first, second, cosine, sine):
    return jnp.concatenate([first * cosine - second * sine, second * cosine + first * sine], axis=0)


def bias_tile(start_row, key_tile, query_tile, diagonal):
    keys = key_tile * TILE + lax.broadcasted_iota(jnp.int32, (TILE, TILE), 0)
    seen = keys >= start_row
    if diagonal:
        queries = query_tile * TILE + lax.broadcasted_iota(jnp.int32, (TILE, TILE), 1)
        seen = seen & (keys <= queries)
    return jnp.where(seen, 0.0, NEG)


def attend_tiles(qkv, cosine, sine, starts, attended, lse, queries, keys, key_rows, bias):
    group = queries.shape[0] // HEAD_SIZE
    half = HEAD_SIZE // 2
    tiles = qkv.shape[1] // TILE
    cos, sin = cosine[...], sine[...]

    def rotated(first):
        return rotate_rows(
            qkv[pl.ds(first, half)].astype(jnp.float32),
            qkv[pl.ds(first + half, half)].astype(jnp.float32),
            cos,
            sin,
        ).astype(jnp.bfloat16)

    for head in range(group):
        queries[pl.ds(head * HEAD_SIZE, HEAD_SIZE)] = rotated(head * HEAD_SIZE) * jnp.bfloat16(0.125)
    keys[...] = rotated(group * HEAD_SIZE)
    key_rows[...] = keys[...].T
    for tile in range(tiles):
        lanes = pl.ds(tile * TILE, TILE)
        starts_here = starts[:, lanes]
        for low in range(tile + 1):
            bias[pl.ds(low * TILE, TILE)] = bias_tile(starts_here, low, tile, low == tile)
        count = (tile + 1) * TILE

        def one_head(head, _, lanes=lanes, count=count):
            rows = pl.ds(pl.multiple_of(head * HEAD_SIZE, HEAD_SIZE), HEAD_SIZE)
            scores = jnp.dot(
                key_rows[:count], queries[rows, lanes], preferred_element_type=jnp.float32
            )
            scores += bias[:count]
            highest = jnp.max(scores, axis=0, keepdims=True)
            weights = jnp.exp(scores - highest)
            total = jnp.sum(weights, axis=0, keepdims=True)
            out = jnp.dot(
                qkv[pl.ds((group + 1) * HEAD_SIZE, HEAD_SIZE), :count],
                weights.astype(jnp.bfloat16),
                preferred_element_type=jnp.float32,
            )
            attended[rows, lanes] = (out / total).astype(jnp.bfloat16)
            lse[head, :, lanes] = jnp.broadcast_to(highest + jnp.log(total), (8, TILE))
            return 0

        lax.fori_loop(0, group, one_head, 0)


def forward_kernel(
    qkv,
    cosine,
    sine,
    starts,
    cotangent,
    heads,
    attended,
    lse,
    queries,
    keys,
    gathered,
    heads_all,
    key_rows,
    bias,
    local,
    send,
    recv,
):
    ring = seq_ring()
    weights_ring, _, mate = fsdp_ring()
    greet(ring.peers + weights_ring.peers + [mate])
    kept = [
        pltpu.make_async_copy(cotangent, gathered.at[ring.near[0]], local.at[0]),
        pltpu.make_async_copy(heads, heads_all.at[weights_ring.near[0]], local.at[1]),
    ]
    for copy in kept:
        copy.start()
    copies = Copies(send, recv)

    def compute():
        attend_tiles(qkv, cosine, sine, starts, attended, lse, queries, keys, key_rows, bias)
        yield

    beside(
        gather_walk(
            ring, copies, cotangent, gathered, by_rows(cotangent.shape[0], CHUNKS), CHUNKS
        ),
        (weight_walk(weights_ring, copies, heads, heads_all, mate), LARGE_BESIDE),
        (compute(), (0,)),
    )
    copies.finish()
    for copy in kept:
        copy.wait()


def attend(qkv, cosine, sine, starts, cotangent, heads, group, number):
    length = qkv.shape[1]
    rows, width = cotangent.shape
    ranks = lax.axis_size("seq")
    return pl.pallas_call(
        forward_kernel,
        out_shape=[
            jax.ShapeDtypeStruct((group * HEAD_SIZE, length), jnp.bfloat16),
            jax.ShapeDtypeStruct((group, 8, length), jnp.float32),
            jax.ShapeDtypeStruct((group * HEAD_SIZE, length), jnp.bfloat16),
            jax.ShapeDtypeStruct((HEAD_SIZE, length), jnp.bfloat16),
            jax.ShapeDtypeStruct((ranks, rows, width), jnp.bfloat16),
            jax.ShapeDtypeStruct((lax.axis_size("fsdp"), *heads.shape), jnp.bfloat16),
        ],
        in_specs=[VMEM] * 4 + [ANYWHERE] * 2,
        out_specs=[VMEM] * 4 + [ANYWHERE] * 2,
        scratch_shapes=[
            pltpu.VMEM((length, HEAD_SIZE), jnp.bfloat16),
            pltpu.VMEM((length, TILE), jnp.float32),
            pltpu.SemaphoreType.DMA((2,)),
        ]
        + semaphores(gather_copies(CHUNKS) + gather_copies(CHUNKS, True)),
        compiler_params=params(number, 62),
        name="attend",
    )(qkv, cosine, sine, starts, cotangent, heads)


def back_tiles(
    qkv,
    queries,
    keys,
    attended,
    lse,
    grads,
    cosine,
    sine,
    starts,
    out,
    key_rows,
    value_rows,
    query_rows,
    grad_rows,
    row_dots,
    key_grad,
    value_grad,
    query_grad,
    bias,
):
    group = queries.shape[0] // HEAD_SIZE
    half = HEAD_SIZE // 2
    tiles = qkv.shape[1] // TILE
    key_rows[...] = keys[...].T
    value_rows[...] = qkv[pl.ds((group + 1) * HEAD_SIZE, HEAD_SIZE)].T
    for head in range(group):
        rows = pl.ds(head * HEAD_SIZE, HEAD_SIZE)
        query_rows[head] = queries[rows].T
        grad_rows[head] = grads[rows].T
        row_dots[head] = jnp.broadcast_to(
            jnp.sum(
                grads[rows].astype(jnp.float32) * attended[rows].astype(jnp.float32),
                axis=0,
                keepdims=True,
            ),
            row_dots.shape[1:],
        )
    key_grad[...] = jnp.zeros_like(key_grad)
    value_grad[...] = jnp.zeros_like(value_grad)
    for tile in range(tiles):
        lanes = pl.ds(tile * TILE, TILE)
        starts_here = starts[:, lanes]
        for low in range(tile + 1):
            bias[low] = bias_tile(starts_here, low, tile, low == tile)

        def one_head(head, _, lanes=lanes, tile=tile):
            rows = pl.ds(pl.multiple_of(head * HEAD_SIZE, HEAD_SIZE), HEAD_SIZE)
            query, grad = queries[rows, lanes], grads[rows, lanes]
            query_row, grad_row = query_rows[head, lanes], grad_rows[head, lanes]
            lse_row = lse[head, 0:1, lanes]
            dot_row = row_dots[head, 0:1, lanes]
            total = jnp.zeros((HEAD_SIZE, TILE), jnp.float32)
            for low in range(tile + 1):
                part = pl.ds(low * TILE, TILE)
                scores = jnp.dot(key_rows[part], query, preferred_element_type=jnp.float32)
                probs = jnp.exp(scores + bias[low] - lse_row)
                grad_probs = jnp.dot(value_rows[part], grad, preferred_element_type=jnp.float32)
                grad_scores = (probs * (grad_probs - dot_row)).astype(jnp.bfloat16)
                value_grad[part] += jnp.dot(
                    probs.astype(jnp.bfloat16), grad_row, preferred_element_type=jnp.float32
                )
                key_grad[part] += jnp.dot(
                    grad_scores, query_row, preferred_element_type=jnp.float32
                )
                total += jnp.dot(keys[:, part], grad_scores, preferred_element_type=jnp.float32)
            query_grad[rows, lanes] = total * 0.125
            return 0

        lax.fori_loop(0, group, one_head, 0)
        yield
    cos, sin = cosine[...], sine[...]
    for head in range(group):
        first = head * HEAD_SIZE
        out[pl.ds(first, HEAD_SIZE)] = rotate_rows(
            query_grad[pl.ds(first, half)], query_grad[pl.ds(first + half, half)], cos, -sin
        ).astype(jnp.bfloat16)
    turned = key_grad[...].T
    out[pl.ds(group * HEAD_SIZE, HEAD_SIZE)] = rotate_rows(
        turned[:half], turned[half:], cos, -sin
    ).astype(jnp.bfloat16)
    out[pl.ds((group + 1) * HEAD_SIZE, HEAD_SIZE)] = value_grad[...].T.astype(jnp.bfloat16)


def shards(
    tokens,
    segment_ids,
    query_weight,
    key_matrix,
    value_matrix,
    output_weight,
    gate_weight,
    up_weight,
    down_weight,
    attention_gain,
    feed_gain,
    cotangent,
):
    rank = lax.axis_index("seq")
    owner = lax.axis_index("fsdp")
    ranks = lax.axis_size("seq")
    owners = lax.axis_size("fsdp")
    rows, width = query_weight.shape
    kv_cols = key_matrix.shape[1] // ranks
    q_cols = width // ranks
    group = q_cols // kv_cols
    ff = gate_weight.shape[1]
    ff_chunk = ff // owners // ranks
    ff_local = owners * ff_chunk
    segment_row = segment_ids[0]
    length = segment_row.shape[0]

    hidden_one, qkv, heads_turned, gate_all, up_in, cosine, sine, starts, gain_one, gain_two = (
        gather_first(
            tokens[0],
            query_weight,
            key_matrix,
            value_matrix,
            gate_weight,
            up_weight,
            attention_gain,
            feed_gain,
            segment_ids,
            rope_freqs(HEAD_SIZE)[:, None],
            0,
        )
    )
    hidden_one = hidden_one.reshape(length, width)

    attended, lse, queries, keys, grad_out, output_all = attend(
        qkv, cosine, sine, starts, cotangent[0], output_weight, group, 1
    )
    output_all = output_all.reshape(-1, width)
    middle, attended_here, hidden_two, up_all, down_all, act, grad_gate, grad_up = add_branch(
        attended, tokens[0], gain_two, output_all, gate_all, up_in, down_weight, grad_out, 2
    )
    hidden_two = hidden_two.reshape(length, width)
    gate_all = gate_all.reshape(width, ff_local)
    up_all = up_all.reshape(width, ff_local)
    down_all = down_all.reshape(ff_local, width)
    act, grad_gate, grad_up = (part.reshape(length, ff_local) for part in (act, grad_gate, grad_up))
    grad_out = grad_out.reshape(length, width)

    grad_middle, grad_gain_two, grad_branch, gate_up_share, qkv_grads, layer_out = go_back(
        middle,
        gain_two,
        cotangent[0],
        qkv,
        queries,
        keys,
        attended,
        lse,
        cosine,
        sine,
        starts,
        hidden_two,
        grad_gate,
        grad_up,
        gate_all,
        up_all,
        output_all,
        act,
        down_all,
        3,
    )
    grad_inputs, *gathered, gains = finish(
        tokens[0],
        gain_one,
        grad_middle,
        qkv_grads,
        heads_turned,
        attended_here,
        grad_branch,
        grad_gain_two,
        hidden_one,
        act,
        grad_out,
        gate_up_share,
        4,
    )
    gate_grad, up_grad, down_total, query_grad, key_grad, value_grad, heads_total, *activations = (
        place_grads(*gathered, layer_out, grad_inputs)
    )
    layer_out, grad_inputs = activations
    return (
        layer_out[None],
        grad_inputs[None],
        query_grad,
        key_grad,
        value_grad,
        heads_total,
        gate_grad,
        up_grad,
        down_total,
        gains[0],
        gains[1],
    )


def solution(mesh):
    placed = (
        P("fsdp", "seq", None),
        P("fsdp", None),
        P("fsdp", None),
        P("fsdp", None),
        P("fsdp", None),
        P("fsdp", None),
        P("fsdp", None),
        P("fsdp", None),
        P("fsdp", None),
        P("fsdp"),
        P("fsdp"),
        P("fsdp", "seq", None),
    )
    return jax.shard_map(
        shards,
        mesh=mesh,
        in_specs=placed,
        out_specs=(
            P("fsdp", "seq", None),
            P("fsdp", "seq", None),
            P("fsdp", None),
            P("fsdp", None),
            P("fsdp", None),
            P("fsdp", None),
            P("fsdp", None),
            P("fsdp", None),
            P("fsdp", None),
            P("fsdp"),
            P("fsdp"),
        ),
        check_vma=False,
    )
```

```python
import math

import jax
import jax.numpy as jnp
from jax import lax
from jax.experimental import pallas as pl
from jax.experimental.pallas import tpu as pltpu
from jax.sharding import PartitionSpec as P

HEAD_SIZE = 64
EPS = 1e-05
ROPE_BASE = 500000.0
NEG = -1e30


def rope_freqs(head_dim):
    half_dim = head_dim // 2
    table = []
    for index in range(half_dim):
        inverse = 1.0 / ROPE_BASE ** (index * 2.0 / head_dim)
        wavelen = 2.0 * math.pi / inverse
        blend = (8192.0 / wavelen - 1.0) / 3.0
        mixed = (1.0 - blend) * inverse / 32.0 + blend * inverse
        entry = inverse if wavelen < 2048.0 else inverse / 32.0 if wavelen > 8192.0 else mixed
        table.append(entry)
    return jnp.asarray(table, dtype=jnp.float32)


MESH = pl.DeviceIdType.MESH
CHUNKS = 4
TILE = 256


class Ring:
    def __init__(self, place, count, index_of, device_of):
        side = count // 2
        self.place = place
        row, col = lax.div(place, side), lax.rem(place, side)

        def at(which, step):
            return index_of(which * side + lax.rem(col + step, side))

        self.near = [at(row, step) for step in range(side)]
        self.far = [at(1 - row, step) for step in range(side)]
        self.right = device_of(self.near[1])
        self.left = device_of(self.near[3])
        self.partner = device_of(self.far[0])
        self.peers = [self.right, self.left, self.partner]
        self.remote = [device_of(index) for index in (self.near[2], *self.far[1:])]
        self.device_of = device_of


def seq_ring():
    rank, owner = lax.axis_index("seq"), lax.axis_index("fsdp")
    return Ring(rank, lax.axis_size("seq"), lambda place: place, lambda index: (index, owner))


def fsdp_ring():
    rank, owner = lax.axis_index("seq"), lax.axis_index("fsdp")
    core = lax.rem(owner, 2)
    ring = Ring(
        lax.div(owner, 2),
        lax.axis_size("fsdp") // 2,
        lambda place: 2 * place + core,
        lambda index: (rank, index),
    )
    return ring, core, (rank, owner + 1 - 2 * core)


def greet(peers):
    barrier = pltpu.get_barrier_semaphore()
    for peer in peers:
        pl.semaphore_signal(barrier, inc=1, device_id=peer, device_id_type=MESH)
    pl.semaphore_wait(barrier, len(peers))


def in_step(*walks):
    left = list(walks)
    while left:
        left = [walk for walk in left if next(walk, walk) is not walk]
        yield


def beside(main, *sides):
    sides = [(walk, list(places)) for walk, places in sides]
    step = 0
    for _ in main:
        for walk, places in sides:
            while places and places[0] <= step:
                places.pop(0)
                next(walk, None)
        step += 1
    for _ in in_step(*(walk for walk, _ in sides)):
        pass


class Copies:
    def __init__(self, send, recv):
        self.send, self.recv = send, recv
        self.made = []

    def start(self, source, target, peer):
        number = len(self.made)
        copy = pltpu.make_async_remote_copy(
            src_ref=source,
            dst_ref=target,
            send_sem=self.send.at[number],
            recv_sem=self.recv.at[number],
            device_id=peer,
            device_id_type=MESH,
        )
        copy.start()
        self.made.append(copy)
        return copy

    def settle(self, copies):
        for copy in copies:
            copy.wait_send()
        gone = {id(copy) for copy in copies}
        self.made = [None if id(copy) in gone else copy for copy in self.made]

    def finish(self):
        for copy in self.made:
            if copy is not None:
                copy.wait_send()


def by_rows(rows, chunks):
    size = rows // chunks
    return lambda ref, index: ref.at[pl.ds(index * size, size)]


def by_columns(columns, chunks):
    size = columns // chunks
    return lambda ref, index: ref.at[:, pl.ds(index * size, size)]


def chunk_rows(rows, index):
    size = rows // CHUNKS
    return pl.ds(index * size, size)


def exchange_all(ring, copies, piece, target):
    made = []
    for index in (*ring.far[1:], ring.near[2], ring.far[0], ring.near[1], ring.near[3]):
        made.append(copies.start(piece(index), target, ring.device_of(index)))
    return made


def gather_walk(ring, copies, own, out, cut, chunks, deep=False, mate=None):
    me, right, opposite, left = ring.near
    partner, far_right, _, far_left = ring.far
    half = chunks // 2
    passed = []

    def share(place, index):
        if mate is not None:
            block = cut(out.at[place], index)
            passed.append(copies.start(block, block, mate))

    to_right, to_left, to_far, on = {}, {}, {}, {}
    for step in range(chunks):
        back = chunks - 1 - step
        if not deep:
            to_far[step] = copies.start(cut(own, step), cut(out.at[me], step), ring.partner)
        to_right[step] = copies.start(cut(own, step), cut(out.at[me], step), ring.right)
        to_left[back] = copies.start(cut(own, back), cut(out.at[me], back), ring.left)
        if mate is not None:
            passed.append(copies.start(cut(own, step), cut(out.at[me], step), mate))
    yield
    if deep:
        for step in range(chunks):
            to_far[step] = copies.start(cut(own, step), cut(out.at[me], step), ring.partner)
        yield
    for step in range(half):
        back = chunks - 1 - step
        to_right[step].wait_recv()
        block = cut(out.at[left], step)
        on[step] = copies.start(block, block, ring.right)
        share(left, step)
        to_left[back].wait_recv()
        block = cut(out.at[right], back)
        on[back] = copies.start(block, block, ring.left)
        share(right, back)
        yield
    far_on, rest = {}, []
    for step in range(chunks):
        to_far[step].wait_recv()
        block = cut(out.at[partner], step)
        far_on[0, step] = copies.start(block, block, ring.right)
        far_on[1, step] = copies.start(block, block, ring.left)
        share(partner, step)
        yield
    if deep:
        for step in range(half):
            back = chunks - 1 - step
            far_on[0, step].wait_recv()
            block = cut(out.at[far_left], step)
            rest.append((step, copies.start(block, block, ring.right)))
            share(far_left, step)
            far_on[1, back].wait_recv()
            block = cut(out.at[far_right], back)
            rest.append((back, copies.start(block, block, ring.left)))
            share(far_right, back)
            yield
    def finals():
        for step in range(half):
            back = chunks - 1 - step
            to_right[back].wait_recv()
            share(left, back)
            to_left[step].wait_recv()
            share(right, step)
            if deep:
                far_on[0, back].wait_recv()
                share(far_left, back)
                far_on[1, step].wait_recv()
                share(far_right, step)
            yield

    if not deep:
        yield from finals()
    for step in range(half):
        for index in (step, chunks - 1 - step):
            on[index].wait_recv()
            if not deep:
                block = cut(out.at[opposite], index)
                rest.append((index, copies.start(block, block, ring.partner)))
            share(opposite, index)
        yield
    if deep:
        yield from finals()
    else:
        for copy in far_on.values():
            copy.wait_recv()
        yield
    for index, copy in rest:
        copy.wait_recv()
        share(ring.far[2], index)
    yield
    for copy in passed:
        copy.wait_recv()


def gather_copies(chunks, mate=False):
    return 7 * chunks + (8 * chunks if mate else 0)


def reduce_walk(ring, copies, part_of, bufs, cut, chunks, done, ready=None):
    me, right, opposite, left = ring.near
    partner, far_right, far_opposite, far_left = ring.far
    from_left, from_right, from_far, mid, end_left, end_right, end_far = bufs
    half = chunks // 2

    def wide(ref, index):
        return cut(ref, index)[...].astype(jnp.float32)

    def keep(ref, index, value):
        cut(ref, index)[...] = value.astype(jnp.bfloat16)

    sent = []

    def send(block, index, target, device):
        sent.append(copies.start(cut(block, index), cut(target, index), device))
        return sent[-1]

    order = [x for step in range(half) for x in (step, chunks - 1 - step)]
    one_right, one_left, one_far, last_right, last_left, last_far = ({} for _ in range(6))
    if ready is None:
        for index in order:
            one_far[index] = send(part_of.at[far_opposite], index, from_far, ring.partner)
            one_right[index] = send(part_of.at[far_right], index, from_left, ring.right)
            one_left[index] = send(part_of.at[far_left], index, from_right, ring.left)
    else:
        ready(far_right, far_left)
        for index in order:
            one_right[index] = send(part_of.at[far_right], index, from_left, ring.right)
            one_left[index] = send(part_of.at[far_left], index, from_right, ring.left)
        yield
        ready(far_opposite, right)
        for index in order:
            one_far[index] = send(part_of.at[far_opposite], index, from_far, ring.partner)
    for index in range(half):
        last_right[index] = send(part_of.at[right], index, end_left, ring.right)
    if ready is not None:
        yield
        ready(left, opposite)
    for index in range(half):
        back = chunks - 1 - index
        last_left[back] = send(part_of.at[left], back, end_right, ring.left)
    if ready is not None:
        yield
        ready(partner, me)
    yield
    two = {}
    for index in order:
        one_far[index].wait_recv()
        keep(from_far, index, wide(from_far, index) + wide(part_of.at[opposite], index))
        two[index] = send(from_far, index, mid, ring.left if index < half else ring.right)
        yield
    for index in order:
        one_right[index].wait_recv()
        one_left[index].wait_recv()
        total = wide(from_left, index) + wide(from_right, index)
        keep(from_left, index, total + wide(part_of.at[partner], index))
        last_far[index] = send(from_left, index, end_far, ring.partner)
        yield
    for index in order:
        two[index].wait_recv()
        if index < half:
            keep(mid, index, wide(mid, index) + wide(part_of.at[left], index))
            last_left[index] = send(mid, index, end_right, ring.left)
        else:
            keep(mid, index, wide(mid, index) + wide(part_of.at[right], index))
            last_right[index] = send(mid, index, end_left, ring.right)
        yield
    for index in order:
        last_far[index].wait_recv()
        last_left[index].wait_recv()
        last_right[index].wait_recv()
        total = wide(part_of.at[me], index) + wide(end_left, index)
        done(index, total + wide(end_right, index) + wide(end_far, index))
        yield
    copies.settle(sent)


def reduce_copies(chunks):
    return 3 * chunks + 2 * chunks + chunks + chunks


def owners_walk(ring, mate, copies, produce, own, other, bufs, rows, done):
    mids, from_lefts, from_rights, from_far = bufs[:2], bufs[2:4], bufs[4:6], bufs[6]
    half = rows // 2
    low, high = pl.ds(0, half), pl.ds(half, half)
    near, far = ([lax.div(index, 2) for index in row] for row in (ring.near, ring.far))
    order = [far[2], far[1], far[3], near[2], near[1], near[3], far[0], near[0]]
    awaited = []

    def wide(ref):
        return ref.astype(jnp.float32)

    def add(*numbers):
        for number in numbers:
            for wait in awaited[number]:
                wait()
            if other is not None:
                place = order[number]
                own[place] = (wide(own[place]) + wide(other[place])).astype(jnp.bfloat16)

    def make(number):
        awaited.append(produce(order[number]))

    on, ends = ([], []), ([], [])

    def half_way(which):
        block = own.at[(far, near)[which][2]]
        on[which].append(copies.start(block.at[low], mids[which].at[low], ring.left))
        on[which].append(copies.start(block.at[high], mids[which].at[high], ring.right))

    def sides(which):
        row = (far, near)[which]
        ends[which].append(
            copies.start(own.at[row[1], low], from_lefts[which].at[low], ring.right)
        )
        ends[which].append(
            copies.start(own.at[row[3], high], from_rights[which].at[high], ring.left)
        )

    def other_sides(which):
        row, mid = (far, near)[which], mids[which]
        on[which][0].wait_recv()
        mid[low] = (wide(mid[low]) + wide(own[row[3], low])).astype(jnp.bfloat16)
        ends[which].append(copies.start(mid.at[low], from_rights[which].at[low], ring.left))
        on[which][1].wait_recv()
        mid[high] = (wide(mid[high]) + wide(own[row[1], high])).astype(jnp.bfloat16)
        ends[which].append(copies.start(mid.at[high], from_lefts[which].at[high], ring.right))

    make(0)
    yield
    make(1)
    yield
    add(0)
    half_way(0)
    yield
    make(2)
    yield
    add(1, 2)
    sides(0)
    yield
    make(3)
    yield
    make(4)
    yield
    other_sides(0)
    yield
    add(3)
    half_way(1)
    yield
    make(5)
    yield
    add(4, 5)
    sides(1)
    yield
    make(6)
    yield
    make(7)
    yield
    add(6, 7)
    yield
    last = []
    for copy in ends[0]:
        copy.wait_recv()
    for rows_of in (low, high):
        total = (
            wide(from_lefts[0][rows_of])
            + wide(from_rights[0][rows_of])
            + wide(own[far[0], rows_of])
        )
        from_lefts[0][rows_of] = total.astype(jnp.bfloat16)
        last.append(copies.start(from_lefts[0].at[rows_of], from_far.at[rows_of], ring.partner))
    yield
    other_sides(1)
    yield
    for copy in ends[1]:
        copy.wait_recv()
    yield
    for rows_of, copy in zip((low, high), last):
        copy.wait_recv()
        done(
            rows_of,
            wide(from_lefts[1][rows_of])
            + wide(from_rights[1][rows_of])
            + wide(own[near[0], rows_of])
            + wide(from_far[rows_of]),
        )
        yield


OWNERS_COPIES = 4 + 4 + 4 + 2


def owners_scratch(places, rows, width):
    return [pltpu.VMEM((places, rows, width), jnp.bfloat16) for _ in range(2)] + [
        pltpu.VMEM((rows, width), jnp.bfloat16) for _ in range(7)
    ]


def reduce_scratch(rows, width):
    return [pltpu.VMEM((rows, width), jnp.bfloat16) for _ in range(7)]


def semaphores(count):
    return [pltpu.SemaphoreType.DMA((count,)), pltpu.SemaphoreType.DMA((count,))]


def params(number, limit):
    return pltpu.CompilerParams(
        collective_id=number, has_side_effects=True, vmem_limit_bytes=limit * 2**20
    )


VMEM = pl.BlockSpec(memory_space=pltpu.VMEM)
ANYWHERE = pl.BlockSpec(memory_space=pl.ANY)


SMALL_BESIDE = (0, 2, 2, 3, 6, 6, 6, 6, 8, 8, 9, 9, 10, 10, 11)
LARGE_BESIDE = (0, 0, 1, 2, 3, 4, 5, 6, 7, 8, 9, 9, 10, 10, 11)


def weight_walk(ring, copies, own, out, mate):
    return gather_walk(ring, copies, own, out, by_rows(own.shape[0], CHUNKS), CHUNKS, True, mate)


def chosen_half(first, second, odd):
    low, high = merge_lanes(first.astype(jnp.float32), second.astype(jnp.float32))
    return jnp.where(odd == 0, low, high).astype(jnp.bfloat16)


class Pick:
    def __init__(self, sems, wide, narrow, rank):
        self.sems, self.wide, self.narrow = sems, wide, narrow
        self.pair, self.odd = lax.div(rank, 2), lax.rem(rank, 2)
        self.rank = rank
        self.count = 0

    def fetch(self, source, target):
        copy = pltpu.make_async_copy(source, target, self.sems.at[self.count])
        copy.start()
        self.count += 1
        return copy

    def lanes(self, first):
        return pl.ds(pl.multiple_of(first + self.pair * LANES, LANES), LANES)

    def start_units(self, which, source):
        owners = self.wide.shape[1]
        stride = source.shape[1] // owners
        return [
            self.fetch(source.at[:, self.lanes(owner * stride)], self.wide.at[which, owner])
            for owner in range(owners)
        ]

    def finish_units(self, which, made, out):
        for copy in made:
            copy.wait()
        for index in range(self.wide.shape[1] // 2):
            out[:, pl.ds(index * LANES, LANES)] = chosen_half(
                self.wide[which, 2 * index], self.wide[which, 2 * index + 1], self.odd
            )

    def start_heads(self, query, key, value, out):
        rows, cols = query.shape[0], out.shape[1] - LANES
        first = pl.multiple_of(self.rank * cols, LANES)
        return [
            self.fetch(query.at[:, pl.ds(first, cols)], out.at[pl.ds(0, rows), pl.ds(0, cols)]),
            self.fetch(key.at[:, self.lanes(0)], self.narrow.at[0]),
            self.fetch(value.at[:, self.lanes(0)], self.narrow.at[1]),
        ]

    def finish_heads(self, made, gain_one, gain_two, out):
        rows = self.narrow.shape[1]
        line = lax.broadcasted_iota(jnp.int32, (16, rows), 0)
        first, second = (gain[...].astype(jnp.float32) for gain in (gain_one, gain_two))
        gains = jnp.where(line == 0, first, jnp.where(line == 1, second, 0.0))
        out[pl.ds(rows, 32)] = jnp.zeros((32, out.shape[1]), jnp.bfloat16)
        out[pl.ds(rows, 16), pl.ds(0, rows)] = gains.astype(jnp.bfloat16)
        for copy in made:
            copy.wait()
        out[pl.ds(0, rows), pl.ds(out.shape[1] - LANES, LANES)] = chosen_half(
            self.narrow[0], self.narrow[1], self.odd
        )


def first_positions(segments):
    index = lax.broadcasted_iota(jnp.int32, segments.shape, 1)
    begins = (index == 0) | (segments != pltpu.roll(segments, 1, 1))
    starts = jnp.where(begins, index, 0)
    shift = 1
    while shift < segments.shape[1]:
        starts = jnp.maximum(starts, jnp.where(index >= shift, pltpu.roll(starts, shift, 1), 0))
        shift *= 2
    return starts, index


def first_kernel(
    tokens,
    query,
    key,
    value,
    gate,
    up,
    gain_one,
    gain_two,
    segments,
    freqs,
    hidden,
    qkv,
    heads_turned,
    gate_all,
    up_own,
    cosine,
    sine,
    starts,
    gain_one_all,
    gain_two_all,
    tokens_here,
    hidden_here,
    heads_own,
    heads_all,
    gate_own,
    wide,
    narrow,
    picks,
    stores,
    local,
    send,
    recv,
):
    ring = seq_ring()
    weights_ring, _, mate = fsdp_ring()
    greet(ring.peers + weights_ring.peers + [mate])
    copies = Copies(send, recv)
    me, here = ring.near[0], weights_ring.near[0]
    rows = tokens.shape[0]
    kept = [pltpu.make_async_copy(tokens, tokens_here.at[me], local.at[0])]
    kept[0].start()
    pick = Pick(picks, wide, narrow, lax.axis_index("seq"))
    heads_made = pick.start_heads(query, key, value, heads_own)
    gate_made = pick.start_units(0, gate)
    up_made = pick.start_units(1, up)

    def heads_walk():
        pick.finish_heads(heads_made, gain_one, gain_two, heads_own)
        copy = pltpu.make_async_copy(heads_own, heads_all.at[here], local.at[1])
        copy.start()
        kept.append(copy)
        yield from gather_walk(
            weights_ring,
            copies,
            heads_own,
            heads_all,
            by_rows(heads_own.shape[0], 2),
            2,
            True,
            mate,
        )

    def gate_walk():
        pick.finish_units(0, gate_made, gate_own)
        copy = pltpu.make_async_copy(gate_own, gate_all.at[here], local.at[2])
        copy.start()
        kept.append(copy)
        yield from weight_walk(weights_ring, copies, gate_own, gate_all, mate)

    def project(index):
        values = tokens_here[index].astype(jnp.float32)
        factor = lax.rsqrt(mean_square(values) + EPS)
        hidden_here[index] = (values * factor * gain_one_all[...]).astype(jnp.bfloat16)
        copy = pltpu.make_async_copy(hidden_here.at[index], hidden.at[index], stores.at[len(stored)])
        copy.start()
        stored.append(copy)
        lanes = pl.ds(pl.multiple_of(index * rows, rows), rows)
        qkv[:, lanes] = lax.dot_general(
            heads_turned[...],
            hidden_here[index],
            (((1,), (1,)), ((), ())),
            preferred_element_type=jnp.float32,
        ).astype(jnp.bfloat16)

    stored = []

    def compute():
        pick.finish_units(1, up_made, up_own)
        first, index = first_positions(segments[...])
        starts[...] = first
        phase = (index - first).astype(jnp.float32) * freqs[...]
        cosine[...] = jnp.cos(phase)
        sine[...] = jnp.sin(phase)
        yield
        for copy in kept:
            copy.wait()
        for owner in range(heads_all.shape[0]):
            cols = pl.ds(owner * rows, rows)
            heads_turned[:, cols] = heads_all[owner, :rows].T
            gains = heads_all[owner, pl.ds(rows, 16), pl.ds(0, rows)].astype(jnp.float32)
            gain_one_all[:, cols] = gains[0:1]
            gain_two_all[:, cols] = gains[1:2]
        project(me)
        yield
        project(ring.far[0])
        yield
        for place in (ring.near[1], ring.near[3], ring.near[2]):
            project(place)
        yield
        project(ring.far[1])
        project(ring.far[3])
        yield
        project(ring.far[2])

    beside(
        gather_walk(ring, copies, tokens, tokens_here, by_rows(rows, CHUNKS), CHUNKS),
        (heads_walk(), (0, 0, 1, 2, 2, 4, 6, 6, 6, 7)),
        (gate_walk(), SMALL_BESIDE),
        (compute(), (0, 7, 8, 10, 11, 12)),
    )
    copies.finish()
    for copy in stored:
        copy.wait()


LANES = 128


def gather_first(tokens, query, key, value, gate, up, gain_one, gain_two, segments, freqs, number):
    rows, width = tokens.shape
    ranks, owners = lax.axis_size("seq"), lax.axis_size("fsdp")
    length = segments.shape[1]
    cols = width // ranks + LANES
    units = owners // 2 * LANES
    assert gate.shape[1] // owners // ranks == HEAD_SIZE == LANES // 2
    count = gather_copies(CHUNKS) + gather_copies(2, True) + gather_copies(CHUNKS, True)
    low, real = jnp.bfloat16, jnp.float32
    return pl.pallas_call(
        first_kernel,
        out_shape=[
            jax.ShapeDtypeStruct((ranks, rows, width), low),
            jax.ShapeDtypeStruct((cols, length), low),
            jax.ShapeDtypeStruct((cols, width), low),
            jax.ShapeDtypeStruct((owners, rows, units), low),
            jax.ShapeDtypeStruct((rows, units), low),
            jax.ShapeDtypeStruct((freqs.shape[0], length), real),
            jax.ShapeDtypeStruct((freqs.shape[0], length), real),
            jax.ShapeDtypeStruct((1, length), jnp.int32),
            jax.ShapeDtypeStruct((1, width), real),
            jax.ShapeDtypeStruct((1, width), real),
        ],
        in_specs=[ANYWHERE] * 6 + [VMEM] * 4,
        out_specs=[ANYWHERE, VMEM, VMEM, ANYWHERE] + [VMEM] * 6,
        scratch_shapes=[
            pltpu.VMEM((ranks, rows, width), low),
            pltpu.VMEM((ranks, rows, width), low),
            pltpu.VMEM((rows + 32, cols), low),
            pltpu.VMEM((owners, rows + 32, cols), low),
            pltpu.VMEM((rows, units), low),
            pltpu.VMEM((2, owners, rows, LANES), low),
            pltpu.VMEM((2, rows, LANES), low),
            pltpu.SemaphoreType.DMA((2 * owners + 3,)),
            pltpu.SemaphoreType.DMA((ranks,)),
            pltpu.SemaphoreType.DMA((3,)),
        ]
        + semaphores(count),
        compiler_params=params(number, 62),
        name="gather_first",
    )(tokens, query, key, value, gate, up, gain_one[None], gain_two[None], segments, freqs)


def mean_square(values):
    return jnp.mean(values * values, axis=-1, keepdims=True)


PRODUCT = 512


def product(left, right, store, size=PRODUCT):
    def columns(index, _):
        cols = pl.ds(pl.multiple_of(index * size, size), size)
        store(cols, jnp.dot(left, right[:, cols], preferred_element_type=jnp.float32))
        return 0

    lax.fori_loop(0, right.shape[1] // size, columns, 0)


def two_blocks(ref, rows, first, second):
    return jnp.concatenate(
        [ref[pl.ds(pl.multiple_of(index * rows, rows), rows)] for index in (first, second)], axis=0
    )


def split_store(for_mate, own, place, core):
    def store(cols, value):
        rows = value.shape[0] // 2
        first = core == 0
        theirs = jnp.where(first, value[rows:], value[:rows])
        for_mate[place, :, cols] = theirs.astype(jnp.bfloat16)
        ours = jnp.where(first, value[:rows], value[rows:])
        own[place, :, cols] = ours.astype(jnp.bfloat16)

    return store


def branch_kernel(
    attended,
    tokens,
    gain,
    weight,
    gate,
    up,
    down,
    grad_out,
    middle,
    attended_here,
    hidden,
    up_all,
    down_all,
    act_out,
    gate_out,
    up_out,
    block,
    got,
    weight_here,
    gate_here,
    up_here,
    down_here,
    grad_out_here,
    hidden_here,
    gated,
    upped,
    grad_act,
    act,
    grad_gate,
    grad_up,
    stores,
    local,
    send,
    recv,
):
    ring = seq_ring()
    weights_ring, _, mate = fsdp_ring()
    rows = tokens.shape[0]
    greet(ring.peers + ring.remote + weights_ring.peers + [mate])
    copies = Copies(send, recv)
    me, here = ring.near[0], weights_ring.near[0]
    down_rows = down_here.shape[1]
    down = down.at[pl.ds(pl.multiple_of(me * down_rows, down_rows), down_rows)]

    def lanes_of(index):
        return attended.at[:, pl.ds(pl.multiple_of(index * rows, rows), rows)]

    arriving = exchange_all(ring, copies, lanes_of, got.at[me])
    load = pltpu.make_async_copy(weight, weight_here, local.at[0])
    load.start()
    mine = pltpu.make_async_copy(lanes_of(me), got.at[me], local.at[1])
    mine.start()
    kept = [
        pltpu.make_async_copy(up, up_here.at[here], local.at[2]),
        pltpu.make_async_copy(down, down_here.at[here], local.at[3]),
        pltpu.make_async_copy(gate, gate_here, local.at[4]),
        pltpu.make_async_copy(grad_out, grad_out_here, local.at[5]),
    ]
    for copy in kept:
        copy.start()
    stored = []

    def store(source, target):
        copy = pltpu.make_async_copy(source, target, stores.at[len(stored)])
        copy.start()
        stored.append(copy)

    def walk():
        yield
        mine.wait()
        load.wait()
        for copy in arriving:
            copy.wait_recv()
        attended_here[...] = got[...].reshape(attended_here.shape)
        turned = attended_here[...].T

        def add(cols, value):
            middle[:, cols] = tokens[:, cols].astype(jnp.float32) + value

        product(turned, weight_here, add)
        values = middle[...]
        factor = lax.rsqrt(mean_square(values) + EPS)
        block[...] = (values * factor * gain[...]).astype(jnp.bfloat16)
        hidden_here[me] = block[...]
        yield from gather_walk(
            ring, copies, block, hidden_here, by_rows(rows, CHUNKS), CHUNKS
        )

    units = gated.shape[2]

    def both(ref, pair):
        return jnp.concatenate([ref[index] for index in pair], axis=0)

    def times(pair, matrix, out):
        left = both(hidden_here, pair)

        def columns(tile, _):
            cols = pl.ds(pl.multiple_of(tile * PRODUCT, PRODUCT), PRODUCT)
            right = matrix[:, :, cols].reshape(-1, PRODUCT)
            value = jnp.dot(left, right, preferred_element_type=jnp.float32)
            out[pair[0], :, cols] = value[:rows]
            out[pair[1], :, cols] = value[rows:]
            return 0

        lax.fori_loop(0, units // PRODUCT, columns, 0)

    def back(pair):
        left = both(grad_out_here, pair)
        share = PRODUCT // down_here.shape[1]

        def columns(tile, _):
            cols = pl.ds(pl.multiple_of(tile * PRODUCT, PRODUCT), PRODUCT)
            right = down_here[pl.ds(tile * share, share)].reshape(PRODUCT, -1)
            value = lax.dot_general(
                left, right, (((1,), (1,)), ((), ())), preferred_element_type=jnp.float32
            )
            grad_act[pair[0], :, cols] = value[:rows]
            grad_act[pair[1], :, cols] = value[rows:]
            return 0

        lax.fori_loop(0, units // PRODUCT, columns, 0)

    def combine(pair):
        for index in pair:
            value, other, grad = gated[index], upped[index], grad_act[index]
            sig = jax.nn.sigmoid(value)
            silu = value * sig
            act[index] = (silu * other).astype(jnp.bfloat16)
            grad_gate[index] = (grad * other * (sig * (1.0 + value * (1.0 - sig)))).astype(
                jnp.bfloat16
            )
            grad_up[index] = (grad * silu).astype(jnp.bfloat16)
            store(act.at[index], act_out.at[index])
            store(grad_gate.at[index], gate_out.at[index])
            store(grad_up.at[index], up_out.at[index])

    near, far = ring.near, ring.far
    pairs = ((near[0], far[0]), (near[1], near[3]), (far[1], far[3]), (near[2], far[2]))

    def compute():
        kept[0].wait()
        kept[1].wait()
        kept[2].wait()
        kept[3].wait()
        store(down_here, down_all)
        back(pairs[0])
        yield
        back(pairs[1])
        yield
        back(pairs[2])
        yield
        back(pairs[3])
        yield
        times(pairs[0], gate_here, gated)
        yield
        times(pairs[1], gate_here, gated)
        yield
        store(up_here, up_all)
        times(pairs[0], up_here, upped)
        combine(pairs[0])
        yield
        times(pairs[1], up_here, upped)
        combine(pairs[1])
        yield
        for pair in pairs[2:]:
            for index in pair:
                store(hidden_here.at[index], hidden.at[index])
            times(pair, gate_here, gated)
            times(pair, up_here, upped)
            combine(pair)
            yield

    def hold():
        for index in (*pairs[0], *pairs[1]):
            store(hidden_here.at[index], hidden.at[index])
        yield

    beside(
        walk(),
        (weight_walk(weights_ring, copies, down, down_here, mate), BESIDE_FIRST),
        (weight_walk(weights_ring, copies, up, up_here, mate), BESIDE_SECOND),
        (hold(), (9,)),
        (compute(), (4, 5, 6, 7, 7, 9, 11, 11, 12, 13)),
    )
    copies.finish()
    for copy in stored:
        copy.wait()


BESIDE_FIRST = (0, 0, 0, 0, 0, 0, 0, 0, 1, 1, 1, 1, 2, 2, 3, 4)
BESIDE_SECOND = (0, 0, 1, 1, 1, 1, 2, 2, 7, 7, 7, 7, 9, 9, 10, 11)


def add_branch(attended, tokens, gain, weight, gate, up, down, grad_out, number):
    rows, width = tokens.shape
    ranks, owners = lax.axis_size("seq"), lax.axis_size("fsdp")
    features, units = attended.shape[0], up.shape[1]
    down_block = (down.shape[0] // ranks, width)
    count = ranks - 1 + gather_copies(CHUNKS) + 2 * gather_copies(CHUNKS, True)
    low, real = jnp.bfloat16, jnp.float32
    return pl.pallas_call(
        branch_kernel,
        out_shape=[
            jax.ShapeDtypeStruct((rows, width), real),
            jax.ShapeDtypeStruct((ranks * features, rows), low),
            jax.ShapeDtypeStruct((ranks, rows, width), low),
            jax.ShapeDtypeStruct((owners, *up.shape), low),
            jax.ShapeDtypeStruct((owners, *down_block), low),
        ]
        + [jax.ShapeDtypeStruct((ranks, rows, units), low)] * 3,
        in_specs=[VMEM] * 3 + [ANYWHERE] * 5,
        out_specs=[VMEM] * 2 + [ANYWHERE] * 6,
        scratch_shapes=[
            pltpu.VMEM((rows, width), low),
            pltpu.VMEM((ranks, features, rows), low),
            pltpu.VMEM(weight.shape, low),
            pltpu.VMEM(gate.shape, low),
            pltpu.VMEM((owners, *up.shape), low),
            pltpu.VMEM((owners, *down_block), low),
            pltpu.VMEM((ranks, rows, width), low),
            pltpu.VMEM((ranks, rows, width), low),
        ]
        + [pltpu.VMEM((ranks, rows, units), real)] * 3
        + [pltpu.VMEM((ranks, rows, units), low)] * 3
        + [pltpu.SemaphoreType.DMA((4 * ranks + 2,)), pltpu.SemaphoreType.DMA((6,))]
        + semaphores(count),
        compiler_params=params(number, 62),
        name="add_branch",
    )(attended, tokens, gain, weight, gate, up, down, grad_out)


def norm_back_rows(grad, gain, values):
    factor = lax.rsqrt(mean_square(values) + EPS)
    normed = values * factor
    weighted = grad * gain
    back = factor * (weighted - normed * jnp.mean(weighted * normed, axis=-1, keepdims=True))
    return back, grad * normed


def back_kernel(*refs):
    middle, gain, cotangent = refs[:3]
    qkv, queries, keys, attended, lse, cosine, sine, starts = refs[3:11]
    hidden, gate_grads, up_grads, gate, up, weight, act, down = refs[11:19]
    grad_middle, grad_gain, block, grads_share, qkv_grads, layer_out = refs[19:25]
    tiles_scratch = refs[25:34]
    part_of, big, left_wide, right_wide, for_mate, given, got, grad_attended = refs[34:42]
    loads, send, recv, own, other = refs[42:47]
    owners_bufs, first_bufs, second_bufs = refs[47:54], refs[54:61], refs[61:68]
    ring = seq_ring()
    weights_ring, core, mate = fsdp_ring()
    rows = middle.shape[0]
    greet(ring.peers + ring.remote + weights_ring.peers + [mate])
    copies = Copies(send, recv)
    grad_gain[...] = jnp.zeros_like(grad_gain)
    units = gate_grads.shape[1]
    low_cols, high_cols = pl.ds(0, units), pl.ds(units, units)
    count = [0]

    def load(source, target):
        copy = pltpu.make_async_copy(source, target, loads.at[count[0]])
        copy.start()
        count[0] += 1
        return copy

    arrived = [
        load(gate_grads, right_wide.at[:, low_cols]),
        load(up_grads, right_wide.at[:, high_cols]),
        load(gate, big.at[:, low_cols]),
        load(up, big.at[:, high_cols]),
    ]
    hidden_load = [load(hidden, left_wide)]

    def ready(*blocks):
        while arrived:
            arrived.pop().wait()
        left = two_blocks(right_wide, rows, *blocks)

        def columns(tile, _):
            cols = pl.ds(pl.multiple_of(tile * PRODUCT, PRODUCT), PRODUCT)
            value = lax.dot_general(
                left, big[cols], (((1,), (1,)), ((), ())), preferred_element_type=jnp.float32
            ).astype(jnp.bfloat16)
            part_of[blocks[0], :, cols] = value[:rows]
            part_of[blocks[1], :, cols] = value[rows:]
            return 0

        lax.fori_loop(0, big.shape[0] // PRODUCT, columns, 0)

    def done(index, total):
        rows_of = chunk_rows(rows, index)
        back, terms = norm_back_rows(total, gain[...], middle[rows_of])
        grad_gain[...] += jnp.sum(terms, axis=0, keepdims=True)
        values = cotangent[rows_of].astype(jnp.float32) + back
        grad_middle[rows_of] = values
        block[rows_of] = values.astype(jnp.bfloat16)

    def owned(rows_of, total):
        grads_share[rows_of] = total.astype(jnp.bfloat16)

    made = []

    def produce(place):
        while hidden_load:
            hidden_load.pop().wait()
        lanes = pl.ds(pl.multiple_of(place * 2 * rows, 2 * rows), 2 * rows)
        turned = left_wide[:, lanes].T
        product(turned, right_wide, split_store(for_mate, own, place, core), 2 * PRODUCT)
        made.append(place)
        return [copies.start(for_mate.at[place], other.at[place], mate).wait_recv]

    act_here = right_wide.at[:, low_cols]
    layer_loads = []

    def layer_ready(*blocks):
        assert len(made) == for_mate.shape[0]
        while layer_loads:
            layer_loads.pop().wait()

        def store(cols, value):
            part_of[blocks[0], :, cols] = value[:rows].astype(jnp.bfloat16)
            part_of[blocks[1], :, cols] = value[rows:].astype(jnp.bfloat16)

        product(two_blocks(act_here, rows, *blocks), left_wide, store)

    def layer_done(index, total):
        rows_of = chunk_rows(rows, index)
        layer_out[rows_of] = (middle[rows_of] + total).astype(jnp.bfloat16)

    me = ring.near[0]
    features = grad_attended.shape[0]

    def walk():
        cut = by_rows(rows, CHUNKS)
        step = 0
        for _ in reduce_walk(ring, copies, part_of, first_bufs, cut, CHUNKS, done, ready):
            if step == 3:
                weight_load = load(weight, big)
            step += 1
            yield
        layer_loads.append(load(act, act_here))
        layer_loads.append(load(down, left_wide))
        weight_load.wait()

        def piece(index):
            part = pl.ds(pl.multiple_of(index * features, features), features)
            given[index] = lax.dot_general(
                big[part],
                block[...],
                (((1,), (1,)), ((), ())),
                preferred_element_type=jnp.float32,
            ).astype(jnp.bfloat16)
            return given.at[index]

        arriving = exchange_all(ring, copies, piece, got.at[me])
        piece(me)
        yield
        layer = reduce_walk(
            ring, copies, part_of, second_bufs, cut, CHUNKS, layer_done, layer_ready
        )
        for _ in range(4):
            next(layer)
            yield
        for copy in arriving:
            copy.wait_recv()
        got[me] = given[me]
        for index in range(got.shape[0]):
            grad_attended[:, pl.ds(index * rows, rows)] = got[index]
        yield
        yield from layer

    tiles = back_tiles(
        qkv,
        queries,
        keys,
        attended,
        lse,
        grad_attended,
        cosine,
        sine,
        starts,
        qkv_grads,
        *tiles_scratch,
    )
    beside(
        walk(),
        (
            owners_walk(
                weights_ring,
                mate,
                copies,
                produce,
                own,
                other,
                owners_bufs,
                grads_share.shape[0],
                owned,
            ),
            BACK_OWNERS,
        ),
        (tiles, BACK_TILES),
    )
    copies.finish()


BACK_OWNERS = (0, 0, 0, 1, 1, 3, 3, 3, 3, 11, 11, 11, 11, 11, 15, 15, 20, 25, 25)
BACK_TILES = (25, 25, 25, 33, 37)


def go_back(
    middle,
    gain,
    cotangent,
    qkv,
    queries,
    keys,
    attended,
    lse,
    cosine,
    sine,
    starts,
    hidden,
    gate_grads,
    up_grads,
    gate,
    up,
    weight,
    act,
    down,
    number,
):
    rows, width = middle.shape
    length = hidden.shape[0]
    ranks, owners = lax.axis_size("seq"), lax.axis_size("fsdp")
    places = owners // 2
    group = queries.shape[0] // HEAD_SIZE
    tiles = length // TILE
    features = weight.shape[0] // ranks
    grad_rows, grad_cols = width // owners, 2 * gate_grads.shape[1]
    count = 2 * reduce_copies(CHUNKS) + ranks - 1 + OWNERS_COPIES + places
    low, real = jnp.bfloat16, jnp.float32
    return pl.pallas_call(
        back_kernel,
        out_shape=[
            jax.ShapeDtypeStruct((rows, width), real),
            jax.ShapeDtypeStruct((1, width), real),
            jax.ShapeDtypeStruct((rows, width), low),
            jax.ShapeDtypeStruct((grad_rows, grad_cols), low),
            jax.ShapeDtypeStruct(qkv.shape, low),
            jax.ShapeDtypeStruct((rows, width), low),
        ],
        in_specs=[VMEM] * 11 + [ANYWHERE] * 8,
        out_specs=[VMEM] * 6,
        scratch_shapes=[
            pltpu.VMEM((length, HEAD_SIZE), low),
            pltpu.VMEM((length, HEAD_SIZE), low),
            pltpu.VMEM((group, length, HEAD_SIZE), low),
            pltpu.VMEM((group, length, HEAD_SIZE), low),
            pltpu.VMEM((group, 8, length), real),
            pltpu.VMEM((length, HEAD_SIZE), real),
            pltpu.VMEM((length, HEAD_SIZE), real),
            pltpu.VMEM((group * HEAD_SIZE, length), real),
            pltpu.VMEM((tiles, TILE, TILE), real),
            pltpu.VMEM((ranks, rows, width), low),
            pltpu.VMEM(weight.shape, low),
            pltpu.VMEM((length, width), low),
            pltpu.VMEM((length, width), low),
            pltpu.VMEM((places, grad_rows, grad_cols), low),
            pltpu.VMEM((ranks, features, rows), low),
            pltpu.VMEM((ranks, features, rows), low),
            pltpu.VMEM((features, length), low),
            pltpu.SemaphoreType.DMA((8,)),
        ]
        + semaphores(count)
        + owners_scratch(places, grad_rows, grad_cols)
        + reduce_scratch(rows, width)
        + reduce_scratch(rows, width),
        compiler_params=params(number, 62),
        name="go_back",
    )(
        middle,
        gain,
        cotangent,
        qkv,
        queries,
        keys,
        attended,
        lse,
        cosine,
        sine,
        starts,
        hidden,
        gate_grads,
        up_grads,
        gate,
        up,
        weight,
        act,
        down,
    )


def last_kernel(
    tokens,
    gain,
    grad_middle,
    qkv_grads,
    heads_turned,
    attended,
    branch,
    grad_gain_two,
    hidden,
    act,
    grad_out,
    gate_up,
    out,
    gate_up_all,
    pack_all,
    gains,
    part_of,
    hidden_here,
    act_here,
    grad_out_here,
    pack,
    heads,
    heads_got,
    heads_mine,
    attended_pair,
    branch_pair,
    grad_gain,
    given,
    from_mate,
    summed,
    from_places,
    for_group,
    from_group,
    loads,
    local,
    send,
    recv,
    *scratch,
):
    ring = seq_ring()
    me = ring.near[0]
    weights_ring, core, mate = fsdp_ring()
    rows = tokens.shape[0]
    greet(ring.peers + ring.remote + weights_ring.peers + weights_ring.remote + [mate])
    copies = Copies(send, recv)
    reduce_bufs, scratch = scratch[:7], scratch[7:]
    qkv_scratch, down_scratch, heads_scratch = scratch[:10], scratch[10:20], scratch[20:]
    grad_gain[...] = jnp.zeros_like(grad_gain)
    swapped = [
        copies.start(attended, attended_pair.at[core], mate),
        copies.start(branch, branch_pair.at[core], mate),
    ]
    attended_pair[core] = attended[...]
    branch_pair[core] = branch[...]
    hidden_load = [pltpu.make_async_copy(hidden, hidden_here, loads.at[0])]
    down_loads = [
        pltpu.make_async_copy(act, act_here, loads.at[1]),
        pltpu.make_async_copy(grad_out, grad_out_here, loads.at[2]),
    ]
    for copy in hidden_load + down_loads:
        copy.start()
    kept = []

    def keep(block, all_of):
        copy = pltpu.make_async_copy(block, all_of.at[me], local.at[len(kept)])
        copy.start()
        kept.append(copy)

    keep(gate_up, gate_up_all)

    def ready(*blocks):
        left = jnp.concatenate(
            [
                qkv_grads[:, pl.ds(pl.multiple_of(index * rows, rows), rows)]
                for index in blocks
            ],
            axis=1,
        ).T

        def store(cols, value):
            part_of[blocks[0], :, cols] = value[:rows].astype(jnp.bfloat16)
            part_of[blocks[1], :, cols] = value[rows:].astype(jnp.bfloat16)

        product(left, heads_turned, store)

    def done(index, total):
        rows_of = chunk_rows(rows, index)
        back, terms = norm_back_rows(total, gain[...], tokens[rows_of].astype(jnp.float32))
        grad_gain[...] += jnp.sum(terms, axis=0, keepdims=True)
        out[rows_of] = (grad_middle[rows_of] + back).astype(jnp.bfloat16)

    def sums(parts, produce, block_rows, owned):
        for_mate, own, other = parts[:3]
        return owners_walk(
            weights_ring, mate, copies, produce, own, other, parts[3:], block_rows, owned
        )

    qkv_cols = qkv_grads.shape[0]
    heads_cols = heads.shape[1] // heads_got.shape[0]
    first = pack.shape[1] - qkv_cols - heads_cols

    def qkv_produce(place):
        while hidden_load:
            hidden_load.pop().wait()
        for_mate, own, other = qkv_scratch[:3]
        lanes = pl.ds(pl.multiple_of(place * 2 * rows, 2 * rows), 2 * rows)
        value = lax.dot_general(
            hidden_here[:, lanes].T,
            qkv_grads[...],
            (((1,), (1,)), ((), ())),
            preferred_element_type=jnp.float32,
        )
        split_store(for_mate, own, place, core)(slice(None), value)
        return [copies.start(for_mate.at[place], other.at[place], mate).wait_recv]

    def qkv_owned(rows_of, total):
        pack[rows_of, pl.ds(first + heads_cols, qkv_cols)] = total.astype(jnp.bfloat16)

    down_rows = rows // 2

    def down_produce(place):
        while down_loads:
            down_loads.pop().wait()
        for_mate, own, other = down_scratch[:3]
        lanes = pl.ds(pl.multiple_of(place * rows, rows), rows)
        turned = act_here[:, lanes].T
        product(turned, grad_out_here, split_store(for_mate, own, place, core), 2 * PRODUCT)
        return [copies.start(for_mate.at[place], other.at[place], mate).wait_recv]

    def down_owned(rows_of, total):
        pack[rows_of, pl.ds(0, first)] = total[:, :first].astype(jnp.bfloat16)
        under = pl.ds(rows_of.start + down_rows, rows_of.size)
        pack[under, pl.ds(0, first)] = total[:, first:].astype(jnp.bfloat16)

    piece_rows = heads_mine.shape[0]

    def heads_owned(rows_of, total):
        heads[rows_of] = total.astype(jnp.bfloat16)

    def heads_walk():
        own = heads_scratch[0]

        def produce(place):
            while swapped:
                swapped.pop().wait_recv()
            part = pl.ds(pl.multiple_of((2 * place + core) * rows, rows), rows)
            left = jnp.concatenate([attended_pair[0, part], attended_pair[1, part]], axis=1)

            def store(cols, value):
                own[place, :, cols] = value.astype(jnp.bfloat16)

            def columns(index, _):
                cols = pl.ds(pl.multiple_of(index * PRODUCT, PRODUCT), PRODUCT)
                right = branch_pair[:, :, cols].reshape(-1, PRODUCT)
                store(cols, jnp.dot(left, right, preferred_element_type=jnp.float32))
                return 0

            lax.fori_loop(0, branch_pair.shape[2] // PRODUCT, columns, 0)
            return []

        yield from owners_walk(
            weights_ring, mate, copies, produce, own, None, heads_scratch[1:], rows, heads_owned
        )

        def piece(index):
            return heads.at[pl.ds(pl.multiple_of(index * piece_rows, piece_rows), piece_rows)]

        arriving = exchange_all(ring, copies, piece, heads_got.at[me])
        heads_got[me] = piece(me)[...]
        yield
        for copy in arriving:
            copy.wait_recv()
        heads_mine[...] = sum(
            heads_got[index].astype(jnp.float32) for index in range(heads_got.shape[0])
        ).astype(jnp.bfloat16)
        for index in range(heads_got.shape[0]):
            rows_of = pl.ds(index * piece_rows, piece_rows)
            cols = pl.ds(index * heads_cols, heads_cols)
            pack[rows_of, pl.ds(first, heads_cols)] = heads_mine[:, cols]

    def sum_gains():
        lanes = given.shape[3]
        for index in range(2 * given.shape[0]):
            cols = pl.ds(index * lanes, lanes)
            place = (index // 2, index % 2)
            given[(*place, slice(0, 1))] = grad_gain[:, cols]
            given[(*place, slice(1, 2))] = grad_gain_two[:, cols]
            given[(*place, slice(2, 8))] = jnp.zeros((6, lanes), jnp.float32)
        copy = copies.start(given.at[:, 1 - core], from_mate, mate)
        yield
        copy.wait_recv()
        summed[...] = given[:, core] + from_mate[...]
        place = weights_ring.place
        arriving = exchange_all(
            weights_ring,
            copies,
            lambda index: summed.at[lax.div(index, 2)],
            from_places.at[place],
        )
        from_places[place] = summed[place]
        yield
        for copy in arriving:
            copy.wait_recv()
        for_group[...] = sum(from_places[index] for index in range(from_places.shape[0]))
        arriving = exchange_all(ring, copies, lambda index: for_group, from_group.at[me])
        from_group[me] = for_group[...]
        yield
        for copy in arriving:
            copy.wait_recv()
        gains[...] = sum(from_group[index] for index in range(from_group.shape[0]))

    def walk():
        yield from reduce_walk(
            ring, copies, part_of, reduce_bufs, by_rows(rows, CHUNKS), CHUNKS, done, ready
        )
        for _ in range(LAST_PAUSE):
            yield
        keep(pack, pack_all)
        yield from gather_walk(ring, copies, pack, pack_all, by_rows(rows, CHUNKS), CHUNKS)

    beside(
        walk(),
        (heads_walk(), LAST_HEADS),
        (
            gather_walk(ring, copies, gate_up, gate_up_all, by_rows(rows, CHUNKS), CHUNKS),
            LAST_GATE_UP,
        ),
        (sums(qkv_scratch, qkv_produce, rows, qkv_owned), LAST_QKV),
        (sums(down_scratch, down_produce, down_rows, down_owned), LAST_DOWN),
        (sum_gains(), LAST_GAINS),
    )
    copies.finish()
    for copy in kept:
        copy.wait()


LAST_PAUSE = 5
LAST_HEADS = (3,) * 14 + (13, 15, 19, 20, 20, 21, 24)
LAST_GATE_UP = (11, 17, 18, 19, 19, 20, 20, 21, 21, 22, 23, 24, 27, 28)
LAST_QKV = (13,) * 9 + (15,) * 5 + (20, 20, 22, 23, 23, 23)
LAST_DOWN = (15,) * 7 + (20,) * 7 + (22, 22, 23, 23, 23, 23)
LAST_GAINS = (19, 22, 25)


def finish(
    tokens,
    gain,
    grad_middle,
    qkv_grads,
    heads_turned,
    attended,
    branch,
    grad_gain_two,
    hidden,
    act,
    grad_out,
    gate_up,
    number,
):
    rows, width = tokens.shape
    ranks, owners = lax.axis_size("seq"), lax.axis_size("fsdp")
    places = owners // 2
    lanes = width // owners
    qkv_cols = qkv_grads.shape[0]
    packed = width // 2 + width // ranks + qkv_cols
    pieces = rows // ranks
    assert act.shape[1] // owners == rows // 2
    count = reduce_copies(CHUNKS) + 2 * gather_copies(CHUNKS) + 3 * OWNERS_COPIES + 2 * places + 2
    count += ranks - 1 + 1 + places - 1 + ranks - 1
    low = jnp.bfloat16

    def table(*shape):
        return pltpu.VMEM((*shape, 8, lanes), jnp.float32)

    def sums(block_rows, cols):
        return [pltpu.VMEM((places, block_rows, cols), low)] + owners_scratch(
            places, block_rows, cols
        )

    return pl.pallas_call(
        last_kernel,
        out_shape=[
            jax.ShapeDtypeStruct((rows, width), low),
            jax.ShapeDtypeStruct((ranks, rows, width), low),
            jax.ShapeDtypeStruct((ranks, rows, packed), low),
            jax.ShapeDtypeStruct((8, lanes), jnp.float32),
        ],
        in_specs=[VMEM] * 8 + [ANYWHERE] * 4,
        out_specs=[VMEM] + [ANYWHERE] * 2 + [VMEM],
        scratch_shapes=[
            pltpu.VMEM((ranks, rows, width), low),
            pltpu.VMEM(hidden.shape, low),
            pltpu.VMEM(act.shape, low),
            pltpu.VMEM(grad_out.shape, low),
            pltpu.VMEM((rows, packed), low),
            pltpu.VMEM((rows, width), low),
            pltpu.VMEM((ranks, pieces, width), low),
            pltpu.VMEM((pieces, width), low),
            pltpu.VMEM((2, *attended.shape), low),
            pltpu.VMEM((2, *branch.shape), low),
            pltpu.VMEM((1, width), jnp.float32),
            table(places, 2),
            table(places),
            table(places),
            table(places),
            table(),
            table(ranks),
            pltpu.SemaphoreType.DMA((3,)),
            pltpu.SemaphoreType.DMA((3,)),
        ]
        + semaphores(count)
        + reduce_scratch(rows, width)
        + sums(rows, qkv_cols)
        + sums(rows // 2, width)
        + owners_scratch(places, rows, width)[1:],
        compiler_params=params(number, 62),
        name="finish",
    )(
        tokens,
        gain,
        grad_middle,
        qkv_grads,
        heads_turned,
        attended,
        branch,
        grad_gain_two,
        hidden,
        act,
        grad_out,
        gate_up,
    )


def merge_lanes(first, second):
    half = first.shape[1] // 2
    low = lax.broadcasted_iota(jnp.int32, first.shape, 1) < half
    return (
        jnp.where(low, first, pltpu.roll(second, half, 1)),
        jnp.where(low, pltpu.roll(first, half, 1), second),
    )


def place_kernel(
    gate,
    up,
    down,
    query,
    pair,
    heads,
    layer,
    tokens,
    gate_out,
    up_out,
    down_out,
    query_out,
    key_out,
    value_out,
    heads_out,
    layer_out,
    tokens_out,
):
    lanes = gate.shape[2]
    blocks = gate.shape[0] // 2
    for part, out in ((gate, gate_out), (up, up_out)):
        for index in range(blocks):
            low, high = merge_lanes(
                part[2 * index].astype(jnp.float32), part[2 * index + 1].astype(jnp.float32)
            )
            out[:, pl.ds(index * lanes, lanes)] = low
            out[:, pl.ds((blocks + index) * lanes, lanes)] = high
    key, value = merge_lanes(pair[0].astype(jnp.float32), pair[1].astype(jnp.float32))
    key_out[...] = key
    value_out[...] = value
    down_rows, cols = down_out.shape[0], down.shape[2]
    down_out[:, :cols] = down[0, :down_rows].astype(jnp.float32)
    down_out[:, cols:] = down[0, down_rows:].astype(jnp.float32)
    query_out[...] = query[0].astype(jnp.float32)
    head_rows, head_cols = heads_out.shape[0], heads.shape[2]
    for index in range(heads.shape[1] // head_rows):
        part = heads[0, index * head_rows : (index + 1) * head_rows]
        heads_out[:, pl.ds(index * head_cols, head_cols)] = part.astype(jnp.float32)
    layer_out[...] = layer[...]
    tokens_out[...] = tokens[...]


def place_grads(gate_up, pack, layer, tokens):
    ranks, rows, units = gate_up.shape
    units //= 2
    lanes = LANES
    steps = units // lanes
    width = layer.shape[1]
    down_cols, down_rows = width // 2, rows // 2
    query_cols = width // ranks
    head_rows = rows // ranks
    first = (down_cols + 2 * query_cols) // lanes
    assert steps == ranks and lanes == 2 * HEAD_SIZE and query_cols == 2 * lanes
    real = jnp.float32
    return pl.pallas_call(
        place_kernel,
        grid=(steps,),
        out_shape=[
            jax.ShapeDtypeStruct((rows, ranks * units), real),
            jax.ShapeDtypeStruct((rows, ranks * units), real),
            jax.ShapeDtypeStruct((ranks * down_rows, width), real),
            jax.ShapeDtypeStruct((rows, ranks * query_cols), real),
            jax.ShapeDtypeStruct((rows, ranks * HEAD_SIZE), real),
            jax.ShapeDtypeStruct((rows, ranks * HEAD_SIZE), real),
            jax.ShapeDtypeStruct((rows, width), real),
            jax.ShapeDtypeStruct((rows, width), jnp.bfloat16),
            jax.ShapeDtypeStruct((rows, width), jnp.bfloat16),
        ],
        in_specs=[
            pl.BlockSpec((ranks, rows, lanes), lambda i: (0, 0, i)),
            pl.BlockSpec((ranks, rows, lanes), lambda i: (0, 0, steps + i)),
            pl.BlockSpec((1, rows, down_cols), lambda i: (i, 0, 0)),
            pl.BlockSpec((1, rows, query_cols), lambda i: (i, 0, down_cols // query_cols + 1)),
            pl.BlockSpec((2, rows, lanes), lambda i: (i // 2, 0, first)),
            pl.BlockSpec((1, rows, query_cols), lambda i: (i, 0, down_cols // query_cols)),
            pl.BlockSpec((head_rows, width), lambda i: (i, 0)),
            pl.BlockSpec((head_rows, width), lambda i: (i, 0)),
        ],
        out_specs=[
            pl.BlockSpec((rows, ranks * lanes), lambda i: (0, i)),
            pl.BlockSpec((rows, ranks * lanes), lambda i: (0, i)),
            pl.BlockSpec((down_rows, width), lambda i: (i, 0)),
            pl.BlockSpec((rows, query_cols), lambda i: (0, i)),
            pl.BlockSpec((rows, lanes), lambda i: (0, i // 2)),
            pl.BlockSpec((rows, lanes), lambda i: (0, i // 2)),
            pl.BlockSpec((head_rows, width), lambda i: (i, 0)),
            pl.BlockSpec((head_rows, width), lambda i: (i, 0)),
            pl.BlockSpec((head_rows, width), lambda i: (i, 0)),
        ],
        compiler_params=pltpu.CompilerParams(vmem_limit_bytes=62 * 2**20),
        name="place_grads",
    )(gate_up, gate_up, pack, pack, pack, pack, layer, tokens)


def rotate_rows(first, second, cosine, sine):
    return jnp.concatenate([first * cosine - second * sine, second * cosine + first * sine], axis=0)


def bias_tile(start_row, key_tile, query_tile, diagonal):
    keys = key_tile * TILE + lax.broadcasted_iota(jnp.int32, (TILE, TILE), 0)
    seen = keys >= start_row
    if diagonal:
        queries = query_tile * TILE + lax.broadcasted_iota(jnp.int32, (TILE, TILE), 1)
        seen = seen & (keys <= queries)
    return jnp.where(seen, 0.0, NEG)


def attend_tiles(qkv, cosine, sine, starts, attended, lse, queries, keys, key_rows, bias):
    group = queries.shape[0] // HEAD_SIZE
    half = HEAD_SIZE // 2
    tiles = qkv.shape[1] // TILE
    cos, sin = cosine[...], sine[...]

    def rotated(first):
        return rotate_rows(
            qkv[pl.ds(first, half)].astype(jnp.float32),
            qkv[pl.ds(first + half, half)].astype(jnp.float32),
            cos,
            sin,
        ).astype(jnp.bfloat16)

    for head in range(group):
        queries[pl.ds(head * HEAD_SIZE, HEAD_SIZE)] = rotated(head * HEAD_SIZE) * jnp.bfloat16(0.125)
    keys[...] = rotated(group * HEAD_SIZE)
    key_rows[...] = keys[...].T
    for tile in range(tiles):
        lanes = pl.ds(tile * TILE, TILE)
        starts_here = starts[:, lanes]
        for low in range(tile + 1):
            bias[pl.ds(low * TILE, TILE)] = bias_tile(starts_here, low, tile, low == tile)
        count = (tile + 1) * TILE

        def one_head(head, _, lanes=lanes, count=count):
            rows = pl.ds(pl.multiple_of(head * HEAD_SIZE, HEAD_SIZE), HEAD_SIZE)
            scores = jnp.dot(
                key_rows[:count], queries[rows, lanes], preferred_element_type=jnp.float32
            )
            scores += bias[:count]
            highest = jnp.max(scores, axis=0, keepdims=True)
            weights = jnp.exp(scores - highest)
            total = jnp.sum(weights, axis=0, keepdims=True)
            out = jnp.dot(
                qkv[pl.ds((group + 1) * HEAD_SIZE, HEAD_SIZE), :count],
                weights.astype(jnp.bfloat16),
                preferred_element_type=jnp.float32,
            )
            attended[rows, lanes] = (out / total).astype(jnp.bfloat16)
            lse[head, :, lanes] = jnp.broadcast_to(highest + jnp.log(total), (8, TILE))
            return 0

        lax.fori_loop(0, group, one_head, 0)


def forward_kernel(
    qkv,
    cosine,
    sine,
    starts,
    cotangent,
    heads,
    attended,
    lse,
    queries,
    keys,
    gathered,
    heads_all,
    key_rows,
    bias,
    local,
    send,
    recv,
):
    ring = seq_ring()
    weights_ring, _, mate = fsdp_ring()
    greet(ring.peers + weights_ring.peers + [mate])
    kept = [
        pltpu.make_async_copy(cotangent, gathered.at[ring.near[0]], local.at[0]),
        pltpu.make_async_copy(heads, heads_all.at[weights_ring.near[0]], local.at[1]),
    ]
    for copy in kept:
        copy.start()
    copies = Copies(send, recv)

    def compute():
        attend_tiles(qkv, cosine, sine, starts, attended, lse, queries, keys, key_rows, bias)
        yield

    beside(
        gather_walk(
            ring, copies, cotangent, gathered, by_rows(cotangent.shape[0], CHUNKS), CHUNKS
        ),
        (weight_walk(weights_ring, copies, heads, heads_all, mate), LARGE_BESIDE),
        (compute(), (0,)),
    )
    copies.finish()
    for copy in kept:
        copy.wait()


def attend(qkv, cosine, sine, starts, cotangent, heads, group, number):
    length = qkv.shape[1]
    rows, width = cotangent.shape
    ranks = lax.axis_size("seq")
    return pl.pallas_call(
        forward_kernel,
        out_shape=[
            jax.ShapeDtypeStruct((group * HEAD_SIZE, length), jnp.bfloat16),
            jax.ShapeDtypeStruct((group, 8, length), jnp.float32),
            jax.ShapeDtypeStruct((group * HEAD_SIZE, length), jnp.bfloat16),
            jax.ShapeDtypeStruct((HEAD_SIZE, length), jnp.bfloat16),
            jax.ShapeDtypeStruct((ranks, rows, width), jnp.bfloat16),
            jax.ShapeDtypeStruct((lax.axis_size("fsdp"), *heads.shape), jnp.bfloat16),
        ],
        in_specs=[VMEM] * 4 + [ANYWHERE] * 2,
        out_specs=[VMEM] * 4 + [ANYWHERE] * 2,
        scratch_shapes=[
            pltpu.VMEM((length, HEAD_SIZE), jnp.bfloat16),
            pltpu.VMEM((length, TILE), jnp.float32),
            pltpu.SemaphoreType.DMA((2,)),
        ]
        + semaphores(gather_copies(CHUNKS) + gather_copies(CHUNKS, True)),
        compiler_params=params(number, 62),
        name="attend",
    )(qkv, cosine, sine, starts, cotangent, heads)


def back_tiles(
    qkv,
    queries,
    keys,
    attended,
    lse,
    grads,
    cosine,
    sine,
    starts,
    out,
    key_rows,
    value_rows,
    query_rows,
    grad_rows,
    row_dots,
    key_grad,
    value_grad,
    query_grad,
    bias,
):
    group = queries.shape[0] // HEAD_SIZE
    half = HEAD_SIZE // 2
    tiles = qkv.shape[1] // TILE
    key_rows[...] = keys[...].T
    value_rows[...] = qkv[pl.ds((group + 1) * HEAD_SIZE, HEAD_SIZE)].T
    for head in range(group):
        rows = pl.ds(head * HEAD_SIZE, HEAD_SIZE)
        query_rows[head] = queries[rows].T
        grad_rows[head] = grads[rows].T
        row_dots[head] = jnp.broadcast_to(
            jnp.sum(
                grads[rows].astype(jnp.float32) * attended[rows].astype(jnp.float32),
                axis=0,
                keepdims=True,
            ),
            row_dots.shape[1:],
        )
    key_grad[...] = jnp.zeros_like(key_grad)
    value_grad[...] = jnp.zeros_like(value_grad)
    for tile in range(tiles):
        lanes = pl.ds(tile * TILE, TILE)
        starts_here = starts[:, lanes]
        for low in range(tile + 1):
            bias[low] = bias_tile(starts_here, low, tile, low == tile)

        def one_head(head, _, lanes=lanes, tile=tile):
            rows = pl.ds(pl.multiple_of(head * HEAD_SIZE, HEAD_SIZE), HEAD_SIZE)
            query, grad = queries[rows, lanes], grads[rows, lanes]
            query_row, grad_row = query_rows[head, lanes], grad_rows[head, lanes]
            lse_row = lse[head, 0:1, lanes]
            dot_row = row_dots[head, 0:1, lanes]
            total = jnp.zeros((HEAD_SIZE, TILE), jnp.float32)
            for low in range(tile + 1):
                part = pl.ds(low * TILE, TILE)
                scores = jnp.dot(key_rows[part], query, preferred_element_type=jnp.float32)
                probs = jnp.exp(scores + bias[low] - lse_row)
                grad_probs = jnp.dot(value_rows[part], grad, preferred_element_type=jnp.float32)
                grad_scores = (probs * (grad_probs - dot_row)).astype(jnp.bfloat16)
                value_grad[part] += jnp.dot(
                    probs.astype(jnp.bfloat16), grad_row, preferred_element_type=jnp.float32
                )
                key_grad[part] += jnp.dot(
                    grad_scores, query_row, preferred_element_type=jnp.float32
                )
                total += jnp.dot(keys[:, part], grad_scores, preferred_element_type=jnp.float32)
            query_grad[rows, lanes] = total * 0.125
            return 0

        lax.fori_loop(0, group, one_head, 0)
        yield
    cos, sin = cosine[...], sine[...]
    for head in range(group):
        first = head * HEAD_SIZE
        out[pl.ds(first, HEAD_SIZE)] = rotate_rows(
            query_grad[pl.ds(first, half)], query_grad[pl.ds(first + half, half)], cos, -sin
        ).astype(jnp.bfloat16)
    turned = key_grad[...].T
    out[pl.ds(group * HEAD_SIZE, HEAD_SIZE)] = rotate_rows(
        turned[:half], turned[half:], cos, -sin
    ).astype(jnp.bfloat16)
    out[pl.ds((group + 1) * HEAD_SIZE, HEAD_SIZE)] = value_grad[...].T.astype(jnp.bfloat16)


def shards(
    tokens,
    segment_ids,
    query_weight,
    key_matrix,
    value_matrix,
    output_weight,
    gate_weight,
    up_weight,
    down_weight,
    attention_gain,
    feed_gain,
    cotangent,
):
    rank = lax.axis_index("seq")
    owner = lax.axis_index("fsdp")
    ranks = lax.axis_size("seq")
    owners = lax.axis_size("fsdp")
    rows, width = query_weight.shape
    kv_cols = key_matrix.shape[1] // ranks
    q_cols = width // ranks
    group = q_cols // kv_cols
    ff = gate_weight.shape[1]
    ff_chunk = ff // owners // ranks
    ff_local = owners * ff_chunk
    segment_row = segment_ids[0]
    length = segment_row.shape[0]

    hidden_one, qkv, heads_turned, gate_all, up_in, cosine, sine, starts, gain_one, gain_two = (
        gather_first(
            tokens[0],
            query_weight,
            key_matrix,
            value_matrix,
            gate_weight,
            up_weight,
            attention_gain,
            feed_gain,
            segment_ids,
            rope_freqs(HEAD_SIZE)[:, None],
            0,
        )
    )
    hidden_one = hidden_one.reshape(length, width)

    attended, lse, queries, keys, grad_out, output_all = attend(
        qkv, cosine, sine, starts, cotangent[0], output_weight, group, 1
    )
    output_all = output_all.reshape(-1, width)
    middle, attended_here, hidden_two, up_all, down_all, act, grad_gate, grad_up = add_branch(
        attended, tokens[0], gain_two, output_all, gate_all, up_in, down_weight, grad_out, 2
    )
    hidden_two = hidden_two.reshape(length, width)
    gate_all = gate_all.reshape(width, ff_local)
    up_all = up_all.reshape(width, ff_local)
    down_all = down_all.reshape(ff_local, width)
    act, grad_gate, grad_up = (part.reshape(length, ff_local) for part in (act, grad_gate, grad_up))
    grad_out = grad_out.reshape(length, width)

    grad_middle, grad_gain_two, grad_branch, gate_up_share, qkv_grads, layer_out = go_back(
        middle,
        gain_two,
        cotangent[0],
        qkv,
        queries,
        keys,
        attended,
        lse,
        cosine,
        sine,
        starts,
        hidden_two,
        grad_gate,
        grad_up,
        gate_all,
        up_all,
        output_all,
        act,
        down_all,
        3,
    )
    grad_inputs, *gathered, gains = finish(
        tokens[0],
        gain_one,
        grad_middle,
        qkv_grads,
        heads_turned,
        attended_here,
        grad_branch,
        grad_gain_two,
        hidden_one,
        act,
        grad_out,
        gate_up_share,
        4,
    )
    gate_grad, up_grad, down_total, query_grad, key_grad, value_grad, heads_total, *activations = (
        place_grads(*gathered, layer_out, grad_inputs)
    )
    layer_out, grad_inputs = activations
    return (
        layer_out[None],
        grad_inputs[None],
        query_grad,
        key_grad,
        value_grad,
        heads_total,
        gate_grad,
        up_grad,
        down_total,
        gains[0],
        gains[1],
    )


def solution(mesh):
    placed = (
        P("fsdp", "seq", None),
        P("fsdp", None),
        P("fsdp", None),
        P("fsdp", None),
        P("fsdp", None),
        P("fsdp", None),
        P("fsdp", None),
        P("fsdp", None),
        P("fsdp", None),
        P("fsdp"),
        P("fsdp"),
        P("fsdp", "seq", None),
    )
    return jax.shard_map(
        shards,
        mesh=mesh,
        in_specs=placed,
        out_specs=(
            P("fsdp", "seq", None),
            P("fsdp", "seq", None),
            P("fsdp", None),
            P("fsdp", None),
            P("fsdp", None),
            P("fsdp", None),
            P("fsdp", None),
            P("fsdp", None),
            P("fsdp", None),
            P("fsdp"),
            P("fsdp"),
        ),
        check_vma=False,
    )
```
